32 devices in a mesh: batch: 8 (over y, x, core), head: 4 (over z).
Axes of the slice: x: 2, y: 2, z: 4, core: 2. Of those that a mesh axis runs over, the one named last changes fastest.
Arguments:
- tokens: bfloat16 [8, 1024, 2048], P('batch', 'head'), may hold values from -6 to 6
- z_weight: bfloat16 [2048, 4096], P(None, 'head'), may hold values from -0.125 to 0.125
- x_weight: bfloat16 [2048, 4096], P(None, 'head'), may hold values from -0.125 to 0.125
- bc_weight: bfloat16 [2048, 256], replicated, may hold values from -0.125 to 0.125
- dt_weight: bfloat16 [2048, 64], P(None, 'head'), may hold values from -0.125 to 0.125
- conv_weight: float32 [4, 4096], P(None, 'head'), may hold values from -3 to 3
- conv_bias: float32 [4096], P('head'), may hold values from -3 to 3
- dt_bias: float32 [64], P('head'), may hold values from -4 to -1
- a_log: float32 [64], P('head'), may hold values from -3 to 1
- skip: float32 [4096], P('head'), may hold values from 0.5 to 1.5
- norm_gain: float32 [4096], P('head'), may hold values from 0.25 to 1.75
- pre_gain: float32 [2048], replicated, may hold values from 0.25 to 1.75
- out_weight: bfloat16 [4096, 2048], P('head'), may hold values from -0.1875 to 0.1875
- cotangent: bfloat16 [4, 8, 1024, 2048], P(None, 'batch', 'head'), may hold values from -6 to 6
Outputs:
- outputs: bfloat16 [4, 8, 1024, 2048], P(None, 'batch', 'head')
- tokens_grad: bfloat16 [8, 1024, 2048], P('batch', 'head')
- z_weight_grad: float32 [2048, 4096], P(None, 'head')
- x_weight_grad: float32 [2048, 4096], P(None, 'head')
- state_proj_weight_gradient: float32 [2048, 256], replicated
- dt_weight_grad: float32 [2048, 64], P(None, 'head')
- conv_weight_grad: float32 [4, 4096], P(None, 'head')
- conv_bias_grad: float32 [4096], P('head')
- dt_bias_grad: float32 [64], P('head')
- a_log_grad: float32 [64], P('head')
- skip_grad: float32 [4096], P('head')
- norm_gain_grad: float32 [4096], P('head')
- pre_gain_grad: float32 [2048], replicated
- out_weight_grad: float32 [4096, 2048], P('head')
The draws below stay inside these ranges and needn't reach their ends.
All inputs are finite; a program needn't handle non-finite values.
Results may differ from the reference program's by a relative error of at most 0.015.
Values may be sent and summed in bfloat16 or wider, within the bound.
A program may use at most 256 MiB of HBM per device.

```python
import jax
import jax.numpy as jnp
import numpy as np
from jax import lax

D = 2048
H = 64
P_SIZE = 64
N = 128
CONVK = 4
SPAN = 128
LEN = 1024
DI = 4096
SEQS = 8
N_HEAD = 4


def block_scale(key, dims, cuts, smallest, largest):
    loudness = 1.0
    for axis_at, shards_of in cuts:
        heights = jax.random.uniform(jax.random.fold_in(jax.random.fold_in(key, 6), axis_at), (shards_of,), jnp.float32, smallest / len(cuts), largest / len(cuts))
        loudness = loudness * jnp.repeat(jnp.exp(heights), dims[axis_at] // shards_of).reshape((-1,) + (1,) * (len(dims) - 1 - axis_at))
    return loudness


def centred(key, shape, spread, most, split=(), held_as=jnp.bfloat16):
    values = jax.random.normal(key, shape, jnp.float32) * spread
    if len(split) > 0:
        values = block_scale(key, shape, split, -0.22, 0.18) * values
    return jnp.clip(values, min=-most, max=most).astype(held_as)


def setup_inputs(seed: int = 0) -> dict:
    keys = jax.random.split(jax.random.key(seed), 15)
    return {
        "tokens": centred(keys[0], (SEQS, LEN, D), 1.0, 6.0, ((0, 8), (1, 4))),
        "z_weight": centred(keys[1], (D, DI), D ** -0.5, 0.125, ((1, 4),)),
        "x_weight": centred(keys[2], (D, DI), D ** -0.5, 0.125, ((1, 4),)),
        "bc_weight": centred(keys[3], (D, 2 * N), D ** -0.5, 0.125),
        "dt_weight": centred(keys[4], (D, H), D ** -0.5, 0.125, ((1, 4),)),
        "conv_weight": centred(keys[5], (CONVK, DI), CONVK ** -0.5, 3.0, ((1, 4),), jnp.float32),
        "conv_bias": centred(keys[6], (DI,), 0.5, 3.0, ((0, 4),), jnp.float32),
        "dt_bias": jnp.clip(-4.0 + 3.0 * jax.random.uniform(keys[7], (H,), jnp.float32) ** block_scale(keys[7], (H,), ((0, 4),), -0.2, 0.2), -4.0, -1.0),
        "a_log": jnp.clip(-3.0 + 4.0 * jax.random.uniform(keys[8], (H,), jnp.float32) ** block_scale(keys[8], (H,), ((0, 4),), -0.2, 0.2), -3.0, 1.0),
        "skip": jnp.clip(0.5 + 1.0 * jax.random.uniform(keys[9], (DI,), jnp.float32) ** block_scale(keys[9], (DI,), ((0, 4),), -0.2, 0.2), 0.5, 1.5),
        "norm_gain": jnp.clip(1.0 + 0.15 * jax.random.normal(keys[10], (DI,), jnp.float32), 0.25, 1.75),
        "pre_gain": jnp.clip(1.0 + 0.15 * jax.random.normal(keys[11], (D,), jnp.float32), 0.25, 1.75),
        "out_weight": centred(keys[12], (DI, D), (DI // 4) ** -0.5, 0.1875, ((0, 4),)),
        "cotangent": centred(keys[13], (4, SEQS, LEN, D), 1.0, 6.0, ((1, 8), (2, 4))),
    }


EPSILON = 1e-05
HIGHEST = lax.Precision.HIGHEST

@jax.custom_vjp
def low(v):
    return lax.optimization_barrier(v.astype(jnp.bfloat16)).astype(jnp.float32)

@jax.custom_vjp
def low_back(v):
    return v

def low_keep(v):
    return (low(v), None)

def low_pass(kept, grad):
    return (grad,)

def back_keep(v):
    return (v, None)

def lower_backward(kept, grad):
    return (low(grad),)
low.defvjp(low_keep, low_pass)
low_back.defvjp(back_keep, lower_backward)

def scan_blocks(act_in, incoming_deltas, decay_rate, b_proj, c_proj, block_len):
    length, head_count, head_size = act_in.shape
    blocks_num = length // block_len
    act_blocks = act_in.reshape(blocks_num, block_len, head_count, head_size)
    deltas = incoming_deltas.reshape(blocks_num, block_len, head_count).transpose(0, 2, 1)
    b_blocks = b_proj.reshape(blocks_num, block_len, -1)
    c_blocks = c_proj.reshape(blocks_num, block_len, -1)
    log_decay = jnp.cumsum(deltas * decay_rate[None, :, None], axis=2)
    log_diff = log_decay[..., :, None] - log_decay[..., None, :]
    causal = jnp.tril(jnp.ones((block_len, block_len), dtype=bool))
    decay_mat = jnp.exp(jnp.where(causal, log_diff, -jnp.inf))
    inner_prod = jnp.einsum('ctn,csn->cts', c_blocks, b_blocks, precision=HIGHEST)
    weights = decay_mat * inner_prod[:, None] * deltas[:, :, None, :]
    within = jnp.einsum('chts,cshp->cthp', weights, act_blocks, precision=HIGHEST)
    tail_scale = jnp.exp(log_decay[..., -1:] - log_decay) * deltas
    scaled = act_blocks * tail_scale.transpose(0, 2, 1)[..., None]
    local_states = jnp.einsum('cshp,csn->chpn', scaled, b_blocks, precision=HIGHEST)
    totals_decay = jnp.exp(log_decay[..., -1])

    def advance(state_now, inputs):
        new_state, factor = inputs
        return (factor[:, None, None] * state_now + new_state, state_now)
    start_state = jnp.zeros((head_count, head_size, b_proj.shape[-1]), act_in.dtype)
    _, before = lax.scan(advance, start_state, (local_states, totals_decay))
    across = jnp.einsum('ctn,chpn->cthp', c_blocks, before, precision=HIGHEST)
    across = across * jnp.exp(log_decay).transpose(0, 2, 1)[..., None]
    return (within + across).reshape(length, head_count, head_size)

def mixer(gate_proj, inner_proj, bc_proj, step_raw, w_conv, b_conv, b_step, log_rate, skip_gain):
    length, channels = inner_proj.shape
    kernel_len = w_conv.shape[0]
    head_count = step_raw.shape[1]
    state_size = bc_proj.shape[1] // 2
    padded = jnp.pad(inner_proj, ((kernel_len - 1, 0), (0, 0)))
    conv_out = b_conv + sum((w_conv[offset] * padded[offset:offset + length] for offset in range(kernel_len)))
    active = jax.nn.silu(conv_out)
    step_size = jax.nn.softplus(step_raw + b_step)
    decay_rate = -jnp.exp(log_rate)
    scanned = scan_blocks(active.reshape(length, head_count, channels // head_count), step_size, decay_rate, bc_proj[:, :state_size], bc_proj[:, state_size:], SPAN)
    scanned = scanned.reshape(length, channels) + skip_gain * active
    return scanned * jax.nn.silu(gate_proj)

def reference(tokens, z_weight, x_weight, bc_weight, dt_weight, conv_weight, conv_bias, dt_bias, a_log, skip, norm_gain, pre_gain, out_weight, cotangent):
    head_share = H // N_HEAD
    rank_head = np.array([order % N_HEAD * head_share + order // N_HEAD for order in range(H)])
    channel_order = (rank_head[:, None] * P_SIZE + np.arange(P_SIZE)[None, :]).reshape(-1)
    params = tuple((item.astype(jnp.float32) for item in (z_weight, x_weight, bc_weight, dt_weight, conv_weight, conv_bias, dt_bias, a_log, skip, norm_gain, pre_gain, out_weight)))

    def forward(params, tokens_f):
        w_gate, w_inner, w_bc, w_step, w_conv, b_conv, b_step, log_rate, skip_gain, gain_norm, gain_pre, w_output = params
        gain_rank = gain_norm[channel_order]
        out_rank = w_output[channel_order]

        def one_sequence(sequence):
            inv_rms = lax.rsqrt(lax.optimization_barrier(jnp.mean(sequence * sequence, axis=-1, keepdims=True)) + EPSILON)
            normed_input = low(sequence * inv_rms * gain_pre)
            gate_proj = low_back(jnp.dot(normed_input, w_gate, precision=HIGHEST))
            inner_proj = low_back(jnp.dot(normed_input, w_inner, precision=HIGHEST))
            step_raw = low_back(jnp.dot(normed_input, w_step, precision=HIGHEST))
            bc_proj = jnp.dot(normed_input, w_bc, precision=HIGHEST)
            gated = mixer(gate_proj, inner_proj, bc_proj, step_raw, w_conv, b_conv, b_step, log_rate, skip_gain)
            gated = gated[:, channel_order]
            results = []
            for nested_widths in range(4):
                prefix_cols = DI * 2 ** nested_widths // 8
                prefix = gated[:, :prefix_cols]
                recip = lax.rsqrt(lax.optimization_barrier(jnp.mean(prefix * prefix, axis=-1, keepdims=True)) + EPSILON)
                normalized_rows = low(prefix * recip * gain_rank[:prefix_cols])
                results.append(sequence + jnp.dot(normalized_rows, out_rank[:prefix_cols], precision=HIGHEST))
            return jnp.stack(results)
        return lax.map(jax.checkpoint(one_sequence), tokens_f)
    tokens_f = tokens.astype(jnp.float32)
    layer_out, pullback = jax.vjp(forward, params, tokens_f)
    grads, tokens_grad = pullback(jnp.transpose(cotangent.astype(jnp.float32), (1, 0, 2, 3)))
    outputs = jnp.transpose(layer_out, (1, 0, 2, 3)).astype(jnp.bfloat16)
    return (outputs, tokens_grad.astype(jnp.bfloat16), grads[0], grads[1], grads[2], grads[3], grads[4], grads[5], grads[6], grads[7], grads[8], grads[9], grads[10], grads[11])
```

```python
import functools
import itertools

import jax
import jax.numpy as jnp
from jax import lax
from jax.experimental import pallas as pl
from jax.experimental.pallas import tpu as pltpu
from jax.sharding import PartitionSpec as P

SPAN = 128
ROWS = 256
EPSILON = 1e-05
BF16 = jnp.bfloat16
F32 = jnp.float32
HIGHEST = lax.Precision.HIGHEST
VMEM_BYTES = 60 * 1024 * 1024


def mm(a, b):
    return lax.dot_general(a, b, (((1,), (0,)), ((), ())), preferred_element_type=F32)


def mm_nt(a, b):
    return lax.dot_general(a, b, (((1,), (1,)), ((), ())), preferred_element_type=F32)


def mm_tn(a, b):
    return lax.dot_general(a, b, (((0,), (0,)), ((), ())), preferred_element_type=F32)


def mm_exact(a, b):
    return lax.dot_general(
        a, b, (((1,), (0,)), ((), ())), preferred_element_type=F32, precision=HIGHEST
    )


def lower_mask(shape):
    return lax.broadcasted_iota(jnp.int32, shape, 0) >= lax.broadcasted_iota(jnp.int32, shape, 1)


def softplus(v):
    return jnp.maximum(v, 0.0) + jnp.log1p(jnp.exp(-jnp.abs(v)))


def sigmoid(v):
    return 1.0 / (1.0 + jnp.exp(-v))


def pair_columns(values, pair, left):
    shape = (SPAN, 128)
    one = jnp.broadcast_to(values[:, 2 * pair : 2 * pair + 1], shape)
    two = jnp.broadcast_to(values[:, 2 * pair + 1 : 2 * pair + 2], shape)
    return one, two, jnp.where(left, one, two)


def forward_kernel(
    x_ref, zw_ref, xw_ref, bcw_ref, dtw_ref, convw_ref, convb_ref, dtb_ref, alog_ref, skip_ref,
    gated_ref, gate_ref, scan_ref, conv_ref, inner_ref, bc_ref, step_ref, prev_ref,
    state, ext, tails,
):
    rows_num, channels = gate_ref.shape
    n = state.shape[0]

    @pl.when(pl.program_id(0) == 0)
    def _():
        state[...] = jnp.zeros_like(state)
        ext[0:8, :] = jnp.zeros((8, channels), F32)

    x = x_ref[...]
    gate_ref[...] = mm(x, zw_ref[...])
    ext[8:, :] = mm(x, xw_ref[...])
    bc_ref[...] = mm(x, bcw_ref[...])
    step_ref[...] = mm(x, dtw_ref[...])
    conv = convb_ref[...] + sum(
        convw_ref[k : k + 1, :] * ext[5 + k : 5 + k + rows_num, :] for k in range(4)
    )
    conv_ref[...] = conv
    inner_ref[...] = ext[8:, :]
    ext[0:8, :] = ext[rows_num : rows_num + 8, :]
    rate = -jnp.exp(alog_ref[...])
    lower = lower_mask((SPAN, SPAN))
    lower_f = lower.astype(F32)
    left = lax.broadcasted_iota(jnp.int32, (SPAN, 128), 1) < 64

    def block(at, carry):
        rows = pl.ds(pl.multiple_of(at * SPAN, SPAN), SPAN)
        delta = softplus(step_ref[rows, :] + dtb_ref[...])
        cum = mm_exact(lower_f, delta * rate)
        cum_t = cum.T
        b_val = bc_ref[rows, :n].astype(BF16)
        c_val = bc_ref[rows, n:].astype(BF16)
        inner = jnp.where(lower, mm_nt(c_val, b_val), 0.0)
        before = state[...].astype(BF16)
        prev_ref[at] = before
        across = mm(c_val, before)
        for pair in range(channels // 128):
            cols = slice(pair * 128, pair * 128 + 128)
            c0, c1, ce = pair_columns(cum, pair, left)
            _, _, de = pair_columns(delta, pair, left)
            tot = ce[SPAN - 1 : SPAN, :]
            conv_p = conv_ref[rows, cols]
            act = conv_p * sigmoid(conv_p)
            u = act * de
            tails[:, cols] = (u * jnp.exp(tot - ce)).astype(BF16)
            u0 = jnp.where(left, u, 0.0).astype(BF16)
            u1 = jnp.where(left, 0.0, u).astype(BF16)
            p0 = (jnp.exp(jnp.minimum(c0 - cum_t[2 * pair : 2 * pair + 1, :], 0.0)) * inner).astype(BF16)
            p1 = (jnp.exp(jnp.minimum(c1 - cum_t[2 * pair + 1 : 2 * pair + 2, :], 0.0)) * inner).astype(BF16)
            within = mm(jnp.concatenate([p0, p1], axis=1), jnp.concatenate([u0, u1], axis=0))
            y = within + across[:, cols] * jnp.exp(ce) + skip_ref[:, cols] * act
            scan_ref[rows, cols] = y
            gate = gate_ref[rows, cols]
            gated_ref[rows, cols] = (y * gate * sigmoid(gate)).astype(BF16)
            state[:, cols] = state[:, cols] * jnp.exp(tot)
        state[...] += mm(bc_ref[rows, :n].T.astype(BF16), tails[...])
        return carry

    lax.fori_loop(0, rows_num // SPAN, block, 0)


def forward_call(x, zw, xw, bcw, dtw, convw, convb, dtb, alog, skip):
    length, model = x.shape
    channels = zw.shape[1]
    n = bcw.shape[1] // 2
    steps = length // ROWS
    fixed = lambda a: pl.BlockSpec(a.shape, lambda i: (0,) * a.ndim)
    rows = lambda w: pl.BlockSpec((ROWS, w), lambda i: (i, 0))
    sub = ROWS // SPAN
    shapes = (
        (channels, BF16), (channels, F32), (channels, F32), (channels, F32), (channels, F32),
        (2 * n, F32), (dtw.shape[1], F32),
    )
    return pl.pallas_call(
        forward_kernel,
        grid=(steps,),
        in_specs=[rows(model)] + [fixed(a) for a in (zw, xw, bcw, dtw, convw, convb, dtb, alog, skip)],
        out_specs=[rows(w) for w, _ in shapes]
        + [pl.BlockSpec((sub, n, channels), lambda i: (i, 0, 0))],
        out_shape=[jax.ShapeDtypeStruct((length, w), t) for w, t in shapes]
        + [jax.ShapeDtypeStruct((length // SPAN, n, channels), BF16)],
        scratch_shapes=[
            pltpu.VMEM((n, channels), F32),
            pltpu.VMEM((ROWS + 8, channels), F32),
            pltpu.VMEM((SPAN, channels), BF16),
        ],
        compiler_params=pltpu.CompilerParams(vmem_limit_bytes=VMEM_BYTES),
        cost_estimate=pl.CostEstimate(
            flops=4 * length * model * channels, bytes_accessed=32 * 2**20, transcendentals=length * channels * 8
        ),
        name="scan_forward",
    )(x, zw, xw, bcw, dtw, convw, convb, dtb, alog, skip)


def backward_kernel(
    dg_ref, gate_ref, scan_ref, conv_ref, inner_ref, bc_ref, step_ref, prev_ref,
    convw_ref, dtb_ref, alog_ref, skip_ref, hot_ref,
    dgate_ref, dinner_ref, dbc_ref, dstep_ref, vec_ref, head_ref,
    lam, dconv, dyc_s, vt_s, q_s, v_s, w_s, da_s, etot_s,
):
    rows_num, channels = gate_ref.shape
    n = lam.shape[0]
    heads = hot_ref.shape[0]

    @pl.when(pl.program_id(0) == 0)
    def _():
        lam[...] = jnp.zeros_like(lam)
        dconv[rows_num:, :] = jnp.zeros((8, channels), F32)
        vec_ref[...] = jnp.zeros_like(vec_ref)
        head_ref[...] = jnp.zeros_like(head_ref)

    rate = -jnp.exp(alog_ref[...])
    lower = lower_mask((SPAN, SPAN))
    lower_f = lower.astype(F32)
    lower_b = lower.astype(BF16)
    row_at = lax.broadcasted_iota(jnp.int32, (SPAN, SPAN), 0)
    col_at = lax.broadcasted_iota(jnp.int32, (SPAN, SPAN), 1)
    upper = row_at <= col_at
    strict = row_at < col_at
    strict_f = strict.astype(F32)
    left = lax.broadcasted_iota(jnp.int32, (SPAN, 128), 1) < 64

    def block(back, carry):
        at = rows_num // SPAN - 1 - back
        rows = pl.ds(pl.multiple_of(at * SPAN, SPAN), SPAN)
        raw = step_ref[rows, :] + dtb_ref[...]
        delta = softplus(raw)
        cum = mm_exact(lower_f, delta * rate)
        cum_t = cum.T
        delta_t = delta.T
        slope_t = sigmoid(raw).T
        rate_t = jnp.broadcast_to(rate, (SPAN, 128)).T
        b_val = bc_ref[rows, :n].astype(BF16)
        c_val = bc_ref[rows, n:].astype(BF16)
        inner = jnp.where(upper, mm_nt(b_val, c_val), 0.0)
        before = prev_ref[at]
        lam_b = lam[...].astype(BF16)
        across = mm(c_val, before)
        dtail = mm(b_val, lam_b)
        d_inner_prod = jnp.zeros((SPAN, SPAN), F32)
        for pair in range(channels // 128):
            cols = slice(pair * 128, pair * 128 + 128)
            c0, c1, ce = pair_columns(cum, pair, left)
            _, _, de = pair_columns(delta, pair, left)
            tot = ce[SPAN - 1 : SPAN, :]
            e_cum = jnp.exp(ce)
            e_tail = jnp.exp(tot - ce)
            dg = dg_ref[rows, cols].astype(F32)
            gate = gate_ref[rows, cols]
            sg = sigmoid(gate)
            sl = gate * sg
            dgate_ref[rows, cols] = (dg * scan_ref[rows, cols] * (sg + sl * (1.0 - sg))).astype(BF16)
            dy = dg * sl
            conv_p = conv_ref[rows, cols]
            sc = sigmoid(conv_p)
            act = conv_p * sc
            vec_ref[5:6, cols] += jnp.sum(dy * act, axis=0, keepdims=True)
            u = act * de
            u_b = u.astype(BF16)
            dy0 = jnp.where(left, dy, 0.0).astype(BF16)
            dy1 = jnp.where(left, 0.0, dy).astype(BF16)
            dy01 = jnp.concatenate([dy0, dy1], axis=0)
            m0 = jnp.exp(jnp.minimum(cum_t[2 * pair : 2 * pair + 1, :] - c0, 0.0))
            m1 = jnp.exp(jnp.minimum(cum_t[2 * pair + 1 : 2 * pair + 2, :] - c1, 0.0))
            p0 = m0 * inner
            p1 = m1 * inner
            du = mm(jnp.concatenate([p0.astype(BF16), p1.astype(BF16)], axis=1), dy01)
            dp = mm_nt(u_b, dy01)
            dp0, dp1 = dp[:, :SPAN], dp[:, SPAN:]
            d_inner_prod += dp0 * m0 + dp1 * m1
            e01 = jnp.concatenate([(dp0 * p0).astype(BF16), (dp1 * p1).astype(BF16)], axis=0)
            spans = mm(e01, lower_b)
            da_s[2 * pair : 2 * pair + 1, :] = jnp.sum(
                jnp.where(strict, spans[:SPAN], 0.0), axis=0, keepdims=True
            )
            da_s[2 * pair + 1 : 2 * pair + 2, :] = jnp.sum(
                jnp.where(strict, spans[SPAN:], 0.0), axis=0, keepdims=True
            )
            dut = dtail[:, cols] * e_tail
            du = du + dut
            dye = dy * e_cum
            dyc_s[:, cols] = dye.astype(BF16)
            vt_s[:, cols] = (u * e_tail).astype(BF16)
            q_s[:, cols] = (dye * across[:, cols]).astype(BF16)
            v_s[:, cols] = (u * dut).astype(BF16)
            w_s[:, cols] = (act * du).astype(BF16)
            etot_s[:, cols] = jnp.exp(tot)
            d_act = de * du + skip_ref[:, cols] * dy
            dconv[rows, cols] = d_act * (sc * (1.0 + conv_p * (1.0 - sc)))
        hot = hot_ref[...]
        over = jnp.sum(lam[...] * before.astype(F32), axis=0, keepdims=True) * etot_s[...]
        over = jnp.broadcast_to(over, (128, channels))
        over = lax.dot_general(
            hot.astype(F32), over, (((1,), (1,)), ((), ())), preferred_element_type=F32, precision=HIGHEST
        )
        da = (
            da_s[...]
            + mm_exact(mm_nt(hot, q_s[...]), lower_f)
            + mm_exact(mm_nt(hot, v_s[...]), strict_f)
            + over
        )
        d_step = mm_nt(hot, w_s[...]) + rate_t[:heads] * da
        d_raw = d_step * slope_t[:heads]
        head_ref[0:heads, :] += d_raw
        head_ref[heads : 2 * heads, :] += delta_t[:heads] * da * rate_t[:heads]
        dstep_ref[:, rows] = d_raw
        dg_b = jnp.where(upper, d_inner_prod, 0.0)
        dbc_ref[rows, :n] = mm(dg_b.astype(BF16), c_val) + mm_nt(vt_s[...], lam_b)
        dbc_ref[rows, n:] = mm(dg_b.T.astype(BF16), b_val) + mm_nt(dyc_s[...], before)
        lam[...] = lam[...] * etot_s[...] + mm(bc_ref[rows, n:].T.astype(BF16), dyc_s[...])
        return carry

    lax.fori_loop(0, rows_num // SPAN, block, 0)
    inner_v = inner_ref[...]
    d_in = jnp.zeros((rows_num, channels), F32)
    for k in range(4):
        shifted = dconv[3 - k : 3 - k + rows_num, :]
        d_in += convw_ref[k : k + 1, :] * shifted
        vec_ref[k : k + 1, :] += jnp.sum(inner_v * shifted, axis=0, keepdims=True)
    vec_ref[4:5, :] += jnp.sum(dconv[0:rows_num, :], axis=0, keepdims=True)
    dinner_ref[...] = d_in.astype(BF16)
    dconv[rows_num:, :] = dconv[0:8, :]


def backward_call(dg, gate, scan, conv, inner, bc, step, prev, convw, dtb, alog, skip, hot):
    length, channels = gate.shape
    n = bc.shape[1] // 2
    heads = hot.shape[0]
    steps = length // ROWS
    fixed = lambda a: pl.BlockSpec(a.shape, lambda i: (0,) * a.ndim)
    rows = lambda w: pl.BlockSpec((ROWS, w), lambda i: (steps - 1 - i, 0))
    sub = ROWS // SPAN
    return pl.pallas_call(
        backward_kernel,
        grid=(steps,),
        in_specs=[rows(a.shape[1]) for a in (dg, gate, scan, conv, inner, bc, step)]
        + [pl.BlockSpec((sub, n, channels), lambda i: (steps - 1 - i, 0, 0))]
        + [fixed(a) for a in (convw, dtb, alog, skip, hot)],
        out_specs=[
            rows(channels), rows(channels), rows(2 * n),
            pl.BlockSpec((heads, ROWS), lambda i: (0, steps - 1 - i)),
            pl.BlockSpec((8, channels), lambda i: (0, 0)),
            pl.BlockSpec((2 * heads, SPAN), lambda i: (0, 0)),
        ],
        out_shape=[
            jax.ShapeDtypeStruct((length, channels), BF16),
            jax.ShapeDtypeStruct((length, channels), BF16),
            jax.ShapeDtypeStruct((length, 2 * n), F32),
            jax.ShapeDtypeStruct((heads, length), F32),
            jax.ShapeDtypeStruct((8, channels), F32),
            jax.ShapeDtypeStruct((2 * heads, SPAN), F32),
        ],
        scratch_shapes=[
            pltpu.VMEM((n, channels), F32),
            pltpu.VMEM((ROWS + 8, channels), F32),
        ]
        + [pltpu.VMEM((SPAN, channels), BF16)] * 5
        + [pltpu.VMEM((heads, SPAN), F32), pltpu.VMEM((1, channels), F32)],
        compiler_params=pltpu.CompilerParams(vmem_limit_bytes=VMEM_BYTES),
        cost_estimate=pl.CostEstimate(
            flops=2**31, bytes_accessed=30 * 2**20, transcendentals=length * channels * 16
        ),
        name="scan_backward",
    )(dg, gate, scan, conv, inner, bc, step, prev, convw, dtb, alog, skip, hot)


def segments(channels):
    ends = [channels * 2**w // 8 for w in range(4)]
    return list(zip([0] + ends[:-1], ends))


def middle_kernel(g_ref, w_ref, gain_ref, tok_ref, cot_ref, out_ref, dg_ref, dy_ref, gg_ref, ggrad_ref):
    groups, rows_num, channels = g_ref.shape
    model = tok_ref.shape[1]
    segs = segments(channels)
    sums = [jnp.zeros((rows_num, 1), F32) for _ in segs]
    for j in range(groups):
        g = g_ref[j].astype(F32)
        gg_ref[j] = (g * gain_ref[j]).astype(BF16)
        for w, (lo, hi) in enumerate(segs):
            sums[w] += jnp.sum(g[:, lo:hi] * g[:, lo:hi], axis=1, keepdims=True)
    recips = []
    total = jnp.zeros((rows_num, 1), F32)
    for w, (lo, hi) in enumerate(segs):
        total = total + sums[w]
        recips.append(lax.rsqrt(total / (hi * groups) + EPSILON))
    tile = 512

    def forward(at, dots):
        cols = pl.ds(pl.multiple_of(at * tile, tile), tile)
        acc = jnp.zeros((rows_num, tile), F32)
        tok = tok_ref[:, cols].astype(F32)
        new = []
        for w, (lo, hi) in enumerate(segs):
            acc += mm(
                jnp.concatenate([gg_ref[j, :, lo:hi] for j in range(groups)], axis=1),
                jnp.concatenate([w_ref[j, lo:hi, cols] for j in range(groups)], axis=0),
            )
            out_ref[w, :, cols] = (tok + recips[w] * acc).astype(BF16)
            new.append(dots[w] + jnp.sum(cot_ref[w, :, cols].astype(F32) * acc, axis=1, keepdims=True))
        combined = jnp.zeros((rows_num, tile), F32)
        for w in reversed(range(4)):
            combined += recips[w] * cot_ref[w, :, cols].astype(F32)
            dy_ref[w, :, cols] = combined.astype(BF16)
        return tuple(new)

    dots = lax.fori_loop(
        0, model // tile, forward, tuple(jnp.zeros((rows_num, 1), F32) for _ in segs)
    )
    scales = [None] * 4
    scale = jnp.zeros((rows_num, 1), F32)
    for w in reversed(range(4)):
        scale = scale + recips[w] ** 3 * dots[w] / (segs[w][1] * groups)
        scales[w] = scale

    def back(j, carry):
        for w, (lo, hi) in enumerate(segs):
            dn = mm_nt(dy_ref[w], w_ref[j, lo:hi, :])
            g = g_ref[j, :, lo:hi].astype(F32)
            ggrad_ref[j, :, lo:hi] = jnp.sum(g * dn, axis=0, keepdims=True)
            dg_ref[j, :, lo:hi] = (gain_ref[j, :, lo:hi] * dn - g * scales[w]).astype(BF16)
        return carry

    lax.fori_loop(0, groups, back, 0)


def middle_call(g, w_all, gain, tok, cot):
    groups, rows_num, channels = g.shape
    model = tok.shape[1]
    return pl.pallas_call(
        middle_kernel,
        out_shape=[
            jax.ShapeDtypeStruct((4, rows_num, model), BF16),
            jax.ShapeDtypeStruct(g.shape, BF16),
            jax.ShapeDtypeStruct((4, rows_num, model), BF16),
            jax.ShapeDtypeStruct(g.shape, BF16),
            jax.ShapeDtypeStruct((groups, 1, channels), F32),
        ],
        compiler_params=pltpu.CompilerParams(vmem_limit_bytes=VMEM_BYTES),
        cost_estimate=pl.CostEstimate(
            flops=4 * groups * rows_num * channels * model, bytes_accessed=36 * 2**20, transcendentals=0
        ),
        name="nested_norm",
    )(g, w_all, gain, tok, cot)


def partner(axis, bit):
    me = lax.axis_index(axis)
    return me + (1 - 2 * ((me // 2**bit) % 2)) * 2**bit


def bits_of(axis, count):
    me = lax.axis_index(axis)
    return [(me // 2**b) % 2 for b in range(count)]


def log2(value):
    return value.bit_length() - 1


def place(count, fixed):
    return tuple(fixed[b] if b in fixed else slice(None) for b in reversed(range(count)))


class Links:
    def __init__(self, send, recv):
        self.send, self.recv, self.used = send, recv, 0

    def copy(self, src, dst, axis, to):
        at = self.used
        self.used += 1
        return pltpu.make_async_remote_copy(
            src_ref=src, dst_ref=dst, send_sem=self.send.at[at], recv_sem=self.recv.at[at],
            device_id={axis: to}, device_id_type=pl.DeviceIdType.MESH,
        )


def meet(peers):
    barrier = pltpu.get_barrier_semaphore()
    for axis, to in peers:
        pl.semaphore_signal(barrier, inc=1, device_id={axis: to}, device_id_type=pl.DeviceIdType.MESH)
    pl.semaphore_wait(barrier, len(peers))


def add_block(buf, index, slot, at):
    rows = slot.shape[-2]
    step = min(rows, 32)
    index = index + (slice(None),) * (len(buf.shape) - len(index))
    free = [i for i, v in enumerate(index[:-2]) if isinstance(v, slice)]
    full = list(index[:-2])
    for i, v in zip(free, at):
        full[i] = v
    full = tuple(full)

    def piece(r, carry):
        rs = pl.ds(pl.multiple_of(r * step, step), step)
        total = buf[full + (rs, index[-1])].astype(F32) + slot[tuple(at) + (rs, slice(None))].astype(F32)
        buf[full + (rs, index[-1])] = total.astype(buf.dtype)
        return carry

    lax.fori_loop(0, rows // step, piece, 0)


def scatter(links, buf, slots, order, lead=()):
    count = len(order)
    mine = bits_of("batch", count)
    fixed = {}
    for i, b in enumerate(order):
        keep = {**fixed, b: mine[b]}
        copy = links.copy(buf.at[place(count, {**fixed, b: 1 - mine[b]})], slots[i], "batch", partner("batch", b))
        copy.start()
        yield
        copy.wait()
        dims = slots[i].shape[:-2]
        for at in itertools.product(*(range(d) for d in dims)):
            add_block(buf, place(count, keep), slots[i], at)
        fixed = keep


def gather(links, buf, order):
    count = len(order)
    fixed = dict(enumerate(bits_of("batch", count)))
    for b in order:
        at = buf.at[place(count, fixed)]
        copy = links.copy(at, at, "batch", partner("batch", b))
        copy.start()
        yield
        copy.wait()
        fixed = {k: v for k, v in fixed.items() if k != b}


def doubling(links, buf, slots, axis, bits):
    for i, b in enumerate(bits):
        copy = links.copy(buf, slots[i], axis, partner(axis, b))
        copy.start()
        yield
        copy.wait()
        buf[...] = (buf[...].astype(F32) + slots[i][...].astype(F32)).astype(buf.dtype)


def chain(*parts):
    for part in parts:
        yield from part


def run_streams(streams):
    live = list(streams)
    while live:
        live = [s for s in live if next(s, live) is not live]


def halving_slots(count, block, dtype):
    return [pltpu.VMEM((2,) * (count - 1 - i) + tuple(block), dtype) for i in range(count)]


def weights_kernel(w_ref, gain_ref, all_ref, gains_ref, local, send, recv):
    groups = all_ref.shape[0]
    count = len(all_ref.shape) - 3
    part, model = all_ref.shape[-2:]
    half = model // 2
    group_bits = log2(groups)
    me = lax.axis_index("head")
    mine = bits_of("batch", count)
    others = [me + sum((1 - 2 * ((me // 2**b) % 2)) * 2**b for b in range(group_bits) if k & 2**b) for k in range(1, groups)]
    links = Links(send, recv)
    meet([("head", z) for z in others] + [("batch", partner("batch", b)) for b in range(count)])
    own = place(count, dict(enumerate(mine)))
    own_copy = pltpu.make_async_copy(w_ref, all_ref.at[me], local.at[0])
    own_copy.start()
    gain_copy = pltpu.make_async_copy(gain_ref, gains_ref.at[me], local.at[1])
    gain_copy.start()
    gain_sends = []
    for z in others:
        gain_sends.append(links.copy(gain_ref, gains_ref.at[me], "head", z))
        gain_sends[-1].start()
    up = list(range(1, count))

    def stream(z, cols, order):
        copy = links.copy(
            w_ref.at[own + (slice(None), cols)], all_ref.at[(me,) + own + (slice(None), cols)], "head", z
        )
        copy.start()
        yield
        copy.wait()
        fixed = dict(enumerate(mine))
        for b in order:
            at = all_ref.at[(z,) + place(count, fixed) + (slice(None), cols)]
            step = links.copy(at, at, "batch", partner("batch", b))
            step.start()
            yield
            step.wait()
            fixed = {k: v for k, v in fixed.items() if k != b}

    streams = []
    for z in others:
        streams.append(stream(z, pl.ds(0, half), up + [0]))
        streams.append(stream(z, pl.ds(half, half), up[::-1] + [0]))
    run_streams(streams)
    for c in gain_sends:
        c.wait()
    own_copy.wait()
    gain_copy.wait()


def weights_call(out_weight, norm_gain, groups, batches):
    channels, model = out_weight.shape
    count = log2(batches)
    part = channels // batches
    copies = (groups - 1) * (1 + 2 * (1 + count))
    hbm = pl.BlockSpec(memory_space=pl.ANY)
    w_all, gains = pl.pallas_call(
        weights_kernel,
        in_specs=[hbm, hbm],
        out_specs=[hbm, hbm],
        out_shape=[
            jax.ShapeDtypeStruct((groups,) + (2,) * count + (part, model), BF16),
            jax.ShapeDtypeStruct((groups, 8, channels), F32),
        ],
        scratch_shapes=[
            pltpu.SemaphoreType.DMA((2,)), pltpu.SemaphoreType.DMA((copies,)), pltpu.SemaphoreType.DMA((copies,)),
        ],
        compiler_params=pltpu.CompilerParams(
            collective_id=1, has_side_effects=True, vmem_limit_bytes=VMEM_BYTES
        ),
        cost_estimate=pl.CostEstimate(flops=0, bytes_accessed=300 * 2**20, transcendentals=0),
        name="gather_weights",
    )(out_weight.reshape((2,) * count + (part, model)), jnp.broadcast_to(norm_gain[None], (8, channels)))
    return w_all.reshape(groups, channels, model), gains[:, :1]


def outgrad_scatter_kernel(count, gg_ref, dy_ref, out_ref, *refs):
    buf, send, recv = refs[0], refs[-2], refs[-1]
    streams_num = 4
    slots = [refs[1 + s * count : 1 + (s + 1) * count] for s in range(streams_num)]
    groups, _, channels = gg_ref.shape
    part, cols = buf.shape[-2:]
    model = dy_ref.shape[2]
    links = Links(send, recv)
    meet([("batch", partner("batch", b)) for b in range(count)])
    up = list(range(1, count))

    def stream(s):
        g0, c0 = (s // 2) * (groups // 2), (s % 2) * cols
        for j in range(groups // 2):
            for w, (lo, hi) in enumerate(segments(channels)):
                term = mm_tn(gg_ref[g0 + j, :, lo:hi], dy_ref[w, :, c0 : c0 + cols]).astype(BF16)
                for p in range(lo // part, hi // part):
                    index = tuple((p >> b) & 1 for b in reversed(range(count)))
                    buf[(s,) + index + (j,)] = term[p * part - lo : (p + 1) * part - lo]
        order = [0] + (up if s % 2 == 0 else up[::-1])
        yield from scatter(links, buf.at[s], slots[s], order)
        mine = place(count, dict(enumerate(bits_of("batch", count))))
        for j in range(groups // 2):
            out_ref[g0 + j, :, c0 : c0 + cols] = buf[(s,) + mine + (j,)]

    run_streams([stream(s) for s in range(streams_num)])


def outgrad_scatter_call(gg, dy, batches):
    groups, _, channels = gg.shape
    model = dy.shape[2]
    count = log2(batches)
    part = channels // batches
    block = (groups // 2, part, model // 2)
    vmem = pl.BlockSpec(memory_space=pltpu.VMEM)
    return pl.pallas_call(
        functools.partial(outgrad_scatter_kernel, count),
        in_specs=[vmem, vmem],
        out_specs=vmem,
        out_shape=jax.ShapeDtypeStruct((groups, part, model), BF16),
        scratch_shapes=[pltpu.VMEM((4,) + (2,) * count + block, BF16)]
        + [s for _ in range(4) for s in halving_slots(count, block, BF16)]
        + [pltpu.SemaphoreType.DMA((4 * count,)), pltpu.SemaphoreType.DMA((4 * count,))],
        compiler_params=pltpu.CompilerParams(
            collective_id=2, has_side_effects=True, vmem_limit_bytes=VMEM_BYTES
        ),
        cost_estimate=pl.CostEstimate(
            flops=2 * groups * gg.shape[1] * channels * model, bytes_accessed=200 * 2**20, transcendentals=0
        ),
        name="out_weight_grad",
    )(gg, dy)


def tail_kernel(
    count, group_bits,
    z_ref, x_ref, o_ref, bc_ref, small_ref,
    zo_ref, xo_ref, oo_ref, bco_ref, smallo_ref, *refs
):
    zx, zx_full, obuf, bcbuf, bc_full, small = refs[:6]
    refs = refs[6:]
    zx_slots = [refs[s * count : (s + 1) * count] for s in range(4)]
    refs = refs[4 * count :]
    bc_slots, refs = refs[:count], refs[count:]
    bc_head, refs = refs[:group_bits], refs[group_bits:]
    small_slots, refs = refs[:count], refs[count:]
    small_head, refs = refs[:group_bits], refs[group_bits:]
    local, send, recv = refs
    cols = zx.shape[-1]
    ocols = obuf.shape[-1]
    shared = small_head[0].shape[0]
    links = Links(send, recv)
    mine = place(count, dict(enumerate(bits_of("batch", count))))
    loads = []
    for s in range(4):
        src = (z_ref, x_ref)[s // 2]
        index = (slice(None),) * (count + 1) + (pl.ds((s % 2) * cols, cols),)
        loads.append(pltpu.make_async_copy(src.at[index], zx.at[s], local.at[s]))
    loads.append(pltpu.make_async_copy(bc_ref, bcbuf, local.at[4]))
    loads.append(pltpu.make_async_copy(small_ref, small, local.at[5]))
    for s in range(2):
        loads.append(
            pltpu.make_async_copy(o_ref.at[:, pl.ds(s * ocols, ocols)], obuf.at[(s,) + mine], local.at[6 + s])
        )
    for load in loads:
        load.start()
    meet(
        [("batch", partner("batch", b)) for b in range(count)]
        + [("head", partner("head", b)) for b in range(group_bits)]
    )
    up = list(range(1, count))
    orders = [up, up[::-1]]
    stores = []

    def store(src, dst, at):
        stores.append(pltpu.make_async_copy(src, dst, local.at[at]))
        stores[-1].start()

    def grads(s):
        loads[s].wait()
        yield from scatter(links, zx.at[s], zx_slots[s], [0] + orders[s // 2])
        zx_full[(s,) + mine] = zx[(s,) + mine]
        yield from gather(links, zx_full.at[s], orders[s // 2][::-1] + [0])
        index = (slice(None),) * (count + 1) + (pl.ds((s % 2) * cols, cols),)
        store(zx_full.at[s], (zo_ref, xo_ref)[s // 2].at[index], 8 + s)

    def state(order):
        loads[4].wait()
        yield from scatter(links, bcbuf, bc_slots, [0] + order)
        yield from doubling(links, bcbuf.at[mine], bc_head, "head", range(group_bits))
        bc_full[mine] = bcbuf[mine]
        yield from gather(links, bc_full, order[::-1] + [0])
        store(bc_full, bco_ref, 12)

    def vectors():
        loads[5].wait()
        yield from doubling(links, small, small_slots, "batch", range(count))
        yield from doubling(links, small.at[pl.ds(0, shared)], small_head, "head", range(group_bits))
        smallo_ref[...] = small[...]

    def outs(s):
        loads[6 + s].wait()
        yield from gather(links, obuf.at[s], orders[s] + [0])
        index = (slice(None),) * (count + 1) + (pl.ds(s * ocols, ocols),)
        store(obuf.at[s], oo_ref.at[index], 13 + s)

    run_streams([grads(0), grads(2), grads(1), grads(3), vectors(), state(orders[0]), outs(0), outs(1)])
    for item in stores:
        item.wait()


def tail_call(z_grad, x_grad, out_own, bc_grad, small, shared, groups, batches):
    model, channels = z_grad.shape
    count = log2(batches)
    group_bits = log2(groups)
    rows = model // batches
    part, width = out_own.shape
    n2 = bc_grad.shape[1]
    lead = (2,) * count
    hbm = pl.BlockSpec(memory_space=pl.ANY)
    vmem = pl.BlockSpec(memory_space=pltpu.VMEM)
    block = (rows, channels // 2)
    copies = 4 * 2 * count + 2 * count + group_bits + count + group_bits + 2 * count
    zo, xo, oo, bco, smallo = pl.pallas_call(
        functools.partial(tail_kernel, count, group_bits),
        in_specs=[hbm] * 5,
        out_specs=[hbm] * 4 + [vmem],
        out_shape=[
            jax.ShapeDtypeStruct(lead + (rows, channels), BF16),
            jax.ShapeDtypeStruct(lead + (rows, channels), BF16),
            jax.ShapeDtypeStruct(lead + (part, width), BF16),
            jax.ShapeDtypeStruct(lead + (rows, n2), BF16),
            jax.ShapeDtypeStruct(small.shape, F32),
        ],
        scratch_shapes=[
            pltpu.VMEM((4,) + lead + block, BF16),
            pltpu.VMEM((4,) + lead + block, BF16),
            pltpu.VMEM((2,) + lead + (part, width // 2), BF16),
            pltpu.VMEM(lead + (rows, n2), BF16),
            pltpu.VMEM(lead + (rows, n2), BF16),
            pltpu.VMEM(small.shape, F32),
        ]
        + [s for _ in range(4) for s in halving_slots(count, block, BF16)]
        + halving_slots(count, (rows, n2), BF16)
        + [pltpu.VMEM((rows, n2), BF16)] * group_bits
        + [pltpu.VMEM(small.shape, F32)] * count
        + [pltpu.VMEM((shared, small.shape[1]), F32)] * group_bits
        + [
            pltpu.SemaphoreType.DMA((15,)), pltpu.SemaphoreType.DMA((copies,)), pltpu.SemaphoreType.DMA((copies,)),
        ],
        compiler_params=pltpu.CompilerParams(
            collective_id=3, has_side_effects=True, vmem_limit_bytes=VMEM_BYTES
        ),
        cost_estimate=pl.CostEstimate(flops=0, bytes_accessed=300 * 2**20, transcendentals=0),
        name="sum_grads",
    )(
        z_grad.reshape(lead + (rows, channels)), x_grad.reshape(lead + (rows, channels)), out_own,
        bc_grad.reshape(lead + (rows, n2)), small,
    )
    return (
        zo.reshape(model, channels), xo.reshape(model, channels), oo.reshape(part * batches, width),
        bco.reshape(model, n2), smallo,
    )


def per_device(
    tokens, z_weight, x_weight, bc_weight, dt_weight, conv_weight, conv_bias, dt_bias,
    a_log, skip, norm_gain, pre_gain, out_weight, cotangent,
):
    groups = lax.axis_size("head")
    batches = lax.axis_size("batch")
    head_at = lax.axis_index("head")
    _, own_len, model = tokens.shape
    tokens = tokens[0]
    cot = cotangent[:, 0]
    channels = z_weight.shape[1]
    heads = dt_weight.shape[1]
    tokens_f = tokens.astype(F32)
    recip_in = lax.rsqrt(jnp.mean(tokens_f * tokens_f, axis=-1, keepdims=True) + EPSILON)
    normed = (tokens_f * recip_in * pre_gain).astype(BF16)
    x = lax.all_gather(normed, "head", axis=0, tiled=True)
    w_all, gain_all = weights_call(out_weight, norm_gain, groups, batches)
    x, w_all = lax.optimization_barrier((x, w_all))

    pad = lambda v: jnp.pad(v, ((0, 0), (0, 128 - heads)))
    dtb = pad(dt_bias[None])
    alog = pad(a_log[None])
    skip_r = skip[None]
    gated, gate, scan, conv, inner, bc, step, prev = forward_call(
        x, z_weight, x_weight, bc_weight, pad(dt_weight), conv_weight, conv_bias[None], dtb, alog, skip_r
    )
    gated = lax.all_to_all(gated.reshape(groups, own_len, channels), "head", 0, 0, tiled=True)
    outputs, d_gated, dy, gg, gain_grad = middle_call(gated, w_all, gain_all, tokens, cot)
    d_gated = lax.all_to_all(d_gated, "head", 0, 0, tiled=True).reshape(groups * own_len, channels)
    out_part = outgrad_scatter_call(gg, dy, batches)
    d_gated, out_part = lax.optimization_barrier((d_gated, out_part))
    out_part = lax.psum_scatter(out_part.reshape(-1, model), "head", scatter_dimension=0, tiled=True)
    hot = (jnp.arange(channels)[None] // (channels // heads) == jnp.arange(heads)[:, None]).astype(BF16)
    d_gate, d_inner, d_bc, d_step, vec, per_head = backward_call(
        d_gated, gate, scan, conv, inner, bc, step, prev, conv_weight, dtb, alog, skip_r, hot
    )
    d_step = d_step.astype(BF16)
    d_bc = d_bc.astype(BF16)
    d_rows = (
        mm_nt(d_gate, z_weight)
        + mm_nt(d_inner, x_weight)
        + lax.dot_general(d_step, dt_weight, (((0,), (1,)), ((), ())), preferred_element_type=F32)
        + mm_nt(d_bc, bc_weight)
    )
    d_rows = d_rows.astype(BF16)
    d_own = lax.psum_scatter(d_rows, "head", scatter_dimension=0, tiled=True).astype(F32)
    z_grad = mm_tn(x, d_gate).astype(BF16)
    x_grad = mm_tn(x, d_inner).astype(BF16)
    dt_grad = lax.dot_general(x, d_step, (((0,), (1,)), ((), ())), preferred_element_type=F32)
    bc_grad = mm_tn(x, d_bc).astype(BF16)
    pre_grad = jnp.sum(x.astype(F32) * d_rows.astype(F32), axis=0) / pre_gain

    width = 1024
    all_part = jnp.concatenate([jnp.zeros((groups, channels), F32) + gain_grad[:, 0], pre_grad.reshape(-1, width)])
    shared = -(-all_part.shape[0] // 8) * 8
    own_part = jnp.concatenate([vec[:6].reshape(-1), jnp.sum(per_head, axis=1), dt_grad.reshape(-1)])
    own_rows = -(-own_part.shape[0] // (8 * width)) * 8
    small = jnp.concatenate([
        jnp.pad(all_part, ((0, shared - all_part.shape[0]), (0, 0))),
        jnp.pad(own_part, (0, own_rows * width - own_part.shape[0])).reshape(own_rows, width),
    ])
    z_grad, x_grad, out_grad, bc_grad, small = tail_call(
        z_grad, x_grad, out_part, bc_grad, small, shared, groups, batches
    )
    z_grad, x_grad, out_grad, bc_grad = (v.astype(F32) for v in (z_grad, x_grad, out_grad, bc_grad))
    gain_grad = lax.dynamic_slice_in_dim(small, head_at, 1, 0)[0]
    pre_grad = small[groups : groups + model // width].reshape(-1)
    own = small[shared:].reshape(-1)

    inner_sum = jnp.mean(tokens_f * pre_gain * d_own, axis=-1, keepdims=True)
    tokens_grad = jnp.sum(cot.astype(F32), axis=0) + pre_gain * recip_in * d_own
    tokens_grad = (tokens_grad - tokens_f * recip_in**3 * inner_sum).astype(BF16)
    c = channels
    return (
        outputs[:, None],
        tokens_grad[None],
        z_grad,
        x_grad,
        bc_grad,
        own[6 * c + 2 * heads : 6 * c + 2 * heads + model * heads].reshape(model, heads),
        own[: 4 * c].reshape(4, c),
        own[4 * c : 5 * c],
        own[6 * c : 6 * c + heads],
        own[6 * c + heads : 6 * c + 2 * heads],
        own[5 * c : 6 * c],
        gain_grad,
        pre_grad,
        out_grad,
    )


def solution(mesh):
    head_cols = P(None, "head")
    rows4 = P(None, "batch", "head", None)
    return jax.shard_map(
        per_device,
        mesh=mesh,
        in_specs=(
            P("batch", "head", None), head_cols, head_cols, P(), head_cols, head_cols, P("head"),
            P("head"), P("head"), P("head"), P("head"), P(), P("head", None), rows4,
        ),
        out_specs=(
            rows4, P("batch", "head", None), head_cols, head_cols, P(), head_cols, head_cols,
            P("head"), P("head"), P("head"), P("head"), P("head"), P(), P("head", None),
        ),
        check_vma=False,
    )
```

```python
import functools
import itertools

import jax
import jax.numpy as jnp
from jax import lax
from jax.experimental import pallas as pl
from jax.experimental.pallas import tpu as pltpu
from jax.sharding import PartitionSpec as P

SPAN = 128
ROWS = 256
EPSILON = 1e-05
BF16 = jnp.bfloat16
F32 = jnp.float32
HIGHEST = lax.Precision.HIGHEST
VMEM_BYTES = 60 * 1024 * 1024


def mm(a, b):
    return lax.dot_general(a, b, (((1,), (0,)), ((), ())), preferred_element_type=F32)


def mm_nt(a, b):
    return lax.dot_general(a, b, (((1,), (1,)), ((), ())), preferred_element_type=F32)


def mm_tn(a, b):
    return lax.dot_general(a, b, (((0,), (0,)), ((), ())), preferred_element_type=F32)


def mm_exact(a, b):
    return lax.dot_general(
        a, b, (((1,), (0,)), ((), ())), preferred_element_type=F32, precision=HIGHEST
    )


def lower_mask(shape):
    return lax.broadcasted_iota(jnp.int32, shape, 0) >= lax.broadcasted_iota(jnp.int32, shape, 1)


def softplus(v):
    return jnp.maximum(v, 0.0) + jnp.log1p(jnp.exp(-jnp.abs(v)))


def sigmoid(v):
    return 1.0 / (1.0 + jnp.exp(-v))


def pair_columns(values, pair, left):
    shape = (SPAN, 128)
    one = jnp.broadcast_to(values[:, 2 * pair : 2 * pair + 1], shape)
    two = jnp.broadcast_to(values[:, 2 * pair + 1 : 2 * pair + 2], shape)
    return one, two, jnp.where(left, one, two)


def backward_kernel(
    dg_ref, gate_ref, scan_ref, conv_ref, inner_ref, bc_ref, step_ref, prev_ref,
    convw_ref, dtb_ref, alog_ref, skip_ref, hot_ref,
    dgate_ref, dinner_ref, dbc_ref, dstep_ref, vec_ref, head_ref,
    lam, dconv, dyc_s, vt_s, q_s, v_s, w_s, da_s, etot_s,
):
    rows_num, channels = gate_ref.shape
    n = lam.shape[0]
    heads = hot_ref.shape[0]

    @pl.when(pl.program_id(0) == 0)
    def _():
        lam[...] = jnp.zeros_like(lam)
        dconv[rows_num:, :] = jnp.zeros((8, channels), F32)
        vec_ref[...] = jnp.zeros_like(vec_ref)
        head_ref[...] = jnp.zeros_like(head_ref)

    rate = -jnp.exp(alog_ref[...])
    lower = lower_mask((SPAN, SPAN))
    lower_f = lower.astype(F32)
    lower_b = lower.astype(BF16)
    row_at = lax.broadcasted_iota(jnp.int32, (SPAN, SPAN), 0)
    col_at = lax.broadcasted_iota(jnp.int32, (SPAN, SPAN), 1)
    upper = row_at <= col_at
    strict = row_at < col_at
    strict_f = strict.astype(F32)
    left = lax.broadcasted_iota(jnp.int32, (SPAN, 128), 1) < 64

    def block(back, carry):
        at = rows_num // SPAN - 1 - back
        rows = pl.ds(pl.multiple_of(at * SPAN, SPAN), SPAN)
        raw = step_ref[rows, :] + dtb_ref[...]
        delta = softplus(raw)
        cum = mm_exact(lower_f, delta * rate)
        cum_t = cum.T
        delta_t = delta.T
        slope_t = sigmoid(raw).T
        rate_t = jnp.broadcast_to(rate, (SPAN, 128)).T
        b_val = bc_ref[rows, :n].astype(BF16)
        c_val = bc_ref[rows, n:].astype(BF16)
        inner = jnp.where(upper, mm_nt(b_val, c_val), 0.0)
        before = prev_ref[at]
        lam_b = lam[...].astype(BF16)
        across = mm(c_val, before)
        dtail = mm(b_val, lam_b)
        d_inner_prod = jnp.zeros((SPAN, SPAN), F32)
        for pair in range(channels // 128):
            cols = slice(pair * 128, pair * 128 + 128)
            c0, c1, ce = pair_columns(cum, pair, left)
            _, _, de = pair_columns(delta, pair, left)
            tot = ce[SPAN - 1 : SPAN, :]
            e_cum = jnp.exp(ce)
            e_tail = jnp.exp(tot - ce)
            dg = dg_ref[rows, cols].astype(F32)
            gate = gate_ref[rows, cols]
            sg = sigmoid(gate)
            sl = gate * sg
            dgate_ref[rows, cols] = (dg * scan_ref[rows, cols] * (sg + sl * (1.0 - sg))).astype(BF16)
            dy = dg * sl
            conv_p = conv_ref[rows, cols]
            sc = sigmoid(conv_p)
            act = conv_p * sc
            vec_ref[5:6, cols] += jnp.sum(dy * act, axis=0, keepdims=True)
            u = act * de
            u_b = u.astype(BF16)
            dy0 = jnp.where(left, dy, 0.0).astype(BF16)
            dy1 = jnp.where(left, 0.0, dy).astype(BF16)
            dy01 = jnp.concatenate([dy0, dy1], axis=0)
            m0 = jnp.exp(jnp.minimum(cum_t[2 * pair : 2 * pair + 1, :] - c0, 0.0))
            m1 = jnp.exp(jnp.minimum(cum_t[2 * pair + 1 : 2 * pair + 2, :] - c1, 0.0))
            p0 = m0 * inner
            p1 = m1 * inner
            du = mm(jnp.concatenate([p0.astype(BF16), p1.astype(BF16)], axis=1), dy01)
            dp = mm_nt(u_b, dy01)
            dp0, dp1 = dp[:, :SPAN], dp[:, SPAN:]
            d_inner_prod += dp0 * m0 + dp1 * m1
            e01 = jnp.concatenate([(dp0 * p0).astype(BF16), (dp1 * p1).astype(BF16)], axis=0)
            spans = mm(e01, lower_b)
            da_s[2 * pair : 2 * pair + 1, :] = jnp.sum(
                jnp.where(strict, spans[:SPAN], 0.0), axis=0, keepdims=True
            )
            da_s[2 * pair + 1 : 2 * pair + 2, :] = jnp.sum(
                jnp.where(strict, spans[SPAN:], 0.0), axis=0, keepdims=True
            )
            dut = dtail[:, cols] * e_tail
            du = du + dut
            dye = dy * e_cum
            dyc_s[:, cols] = dye.astype(BF16)
            vt_s[:, cols] = (u * e_tail).astype(BF16)
            q_s[:, cols] = (dye * across[:, cols]).astype(BF16)
            v_s[:, cols] = (u * dut).astype(BF16)
            w_s[:, cols] = (act * du).astype(BF16)
            etot_s[:, cols] = jnp.exp(tot)
            d_act = de * du + skip_ref[:, cols] * dy
            dconv[rows, cols] = d_act * (sc * (1.0 + conv_p * (1.0 - sc)))
        hot = hot_ref[...]
        over = jnp.sum(lam[...] * before.astype(F32), axis=0, keepdims=True) * etot_s[...]
        over = jnp.broadcast_to(over, (128, channels))
        over = lax.dot_general(
            hot.astype(F32), over, (((1,), (1,)), ((), ())), preferred_element_type=F32, precision=HIGHEST
        )
        da = (
            da_s[...]
            + mm_exact(mm_nt(hot, q_s[...]), lower_f)
            + mm_exact(mm_nt(hot, v_s[...]), strict_f)
            + over
        )
        d_step = mm_nt(hot, w_s[...]) + rate_t[:heads] * da
        d_raw = d_step * slope_t[:heads]
        head_ref[0:heads, :] += d_raw
        head_ref[heads : 2 * heads, :] += delta_t[:heads] * da * rate_t[:heads]
        dstep_ref[:, rows] = d_raw
        dg_b = jnp.where(upper, d_inner_prod, 0.0)
        dbc_ref[rows, :n] = mm(dg_b.astype(BF16), c_val) + mm_nt(vt_s[...], lam_b)
        dbc_ref[rows, n:] = mm(dg_b.T.astype(BF16), b_val) + mm_nt(dyc_s[...], before)
        lam[...] = lam[...] * etot_s[...] + mm(bc_ref[rows, n:].T.astype(BF16), dyc_s[...])
        return carry

    lax.fori_loop(0, rows_num // SPAN, block, 0)
    inner_v = inner_ref[...]
    d_in = jnp.zeros((rows_num, channels), F32)
    for k in range(4):
        shifted = dconv[3 - k : 3 - k + rows_num, :]
        d_in += convw_ref[k : k + 1, :] * shifted
        vec_ref[k : k + 1, :] += jnp.sum(inner_v * shifted, axis=0, keepdims=True)
    vec_ref[4:5, :] += jnp.sum(dconv[0:rows_num, :], axis=0, keepdims=True)
    dinner_ref[...] = d_in.astype(BF16)
    dconv[rows_num:, :] = dconv[0:8, :]


def backward_call(dg, gate, scan, conv, inner, bc, step, prev, convw, dtb, alog, skip, hot):
    length, channels = gate.shape
    n = bc.shape[1] // 2
    heads = hot.shape[0]
    steps = length // ROWS
    fixed = lambda a: pl.BlockSpec(a.shape, lambda i: (0,) * a.ndim)
    rows = lambda w: pl.BlockSpec((ROWS, w), lambda i: (steps - 1 - i, 0))
    sub = ROWS // SPAN
    return pl.pallas_call(
        backward_kernel,
        grid=(steps,),
        in_specs=[rows(a.shape[1]) for a in (dg, gate, scan, conv, inner, bc, step)]
        + [pl.BlockSpec((sub, n, channels), lambda i: (steps - 1 - i, 0, 0))]
        + [fixed(a) for a in (convw, dtb, alog, skip, hot)],
        out_specs=[
            rows(channels), rows(channels), rows(2 * n),
            pl.BlockSpec((heads, ROWS), lambda i: (0, steps - 1 - i)),
            pl.BlockSpec((8, channels), lambda i: (0, 0)),
            pl.BlockSpec((2 * heads, SPAN), lambda i: (0, 0)),
        ],
        out_shape=[
            jax.ShapeDtypeStruct((length, channels), BF16),
            jax.ShapeDtypeStruct((length, channels), BF16),
            jax.ShapeDtypeStruct((length, 2 * n), F32),
            jax.ShapeDtypeStruct((heads, length), F32),
            jax.ShapeDtypeStruct((8, channels), F32),
            jax.ShapeDtypeStruct((2 * heads, SPAN), F32),
        ],
        scratch_shapes=[
            pltpu.VMEM((n, channels), F32),
            pltpu.VMEM((ROWS + 8, channels), F32),
        ]
        + [pltpu.VMEM((SPAN, channels), BF16)] * 5
        + [pltpu.VMEM((heads, SPAN), F32), pltpu.VMEM((1, channels), F32)],
        compiler_params=pltpu.CompilerParams(vmem_limit_bytes=VMEM_BYTES),
        cost_estimate=pl.CostEstimate(
            flops=2**31, bytes_accessed=30 * 2**20, transcendentals=length * channels * 16
        ),
        name="scan_backward",
    )(dg, gate, scan, conv, inner, bc, step, prev, convw, dtb, alog, skip, hot)


def segments(channels):
    ends = [channels * 2**w // 8 for w in range(4)]
    return list(zip([0] + ends[:-1], ends))


def middle_kernel(g_ref, w_ref, gain_ref, tok_ref, cot_ref, out_ref, dg_ref, dy_ref, gg_ref, ggrad_ref):
    groups, rows_num, channels = g_ref.shape
    model = tok_ref.shape[1]
    segs = segments(channels)
    sums = [jnp.zeros((rows_num, 1), F32) for _ in segs]
    for j in range(groups):
        g = g_ref[j].astype(F32)
        gg_ref[j] = (g * gain_ref[j]).astype(BF16)
        for w, (lo, hi) in enumerate(segs):
            sums[w] += jnp.sum(g[:, lo:hi] * g[:, lo:hi], axis=1, keepdims=True)
    recips = []
    total = jnp.zeros((rows_num, 1), F32)
    for w, (lo, hi) in enumerate(segs):
        total = total + sums[w]
        recips.append(lax.rsqrt(total / (hi * groups) + EPSILON))
    tile = 512

    def forward(at, dots):
        cols = pl.ds(pl.multiple_of(at * tile, tile), tile)
        acc = jnp.zeros((rows_num, tile), F32)
        tok = tok_ref[:, cols].astype(F32)
        new = []
        for w, (lo, hi) in enumerate(segs):
            acc += mm(
                jnp.concatenate([gg_ref[j, :, lo:hi] for j in range(groups)], axis=1),
                jnp.concatenate([w_ref[j, lo:hi, cols] for j in range(groups)], axis=0),
            )
            out_ref[w, :, cols] = (tok + recips[w] * acc).astype(BF16)
            new.append(dots[w] + jnp.sum(cot_ref[w, :, cols].astype(F32) * acc, axis=1, keepdims=True))
        combined = jnp.zeros((rows_num, tile), F32)
        for w in reversed(range(4)):
            combined += recips[w] * cot_ref[w, :, cols].astype(F32)
            dy_ref[w, :, cols] = combined.astype(BF16)
        return tuple(new)

    dots = lax.fori_loop(
        0, model // tile, forward, tuple(jnp.zeros((rows_num, 1), F32) for _ in segs)
    )
    scales = [None] * 4
    scale = jnp.zeros((rows_num, 1), F32)
    for w in reversed(range(4)):
        scale = scale + recips[w] ** 3 * dots[w] / (segs[w][1] * groups)
        scales[w] = scale

    def back(j, carry):
        for w, (lo, hi) in enumerate(segs):
            dn = mm_nt(dy_ref[w], w_ref[j, lo:hi, :])
            g = g_ref[j, :, lo:hi].astype(F32)
            ggrad_ref[j, :, lo:hi] = jnp.sum(g * dn, axis=0, keepdims=True)
            dg_ref[j, :, lo:hi] = (gain_ref[j, :, lo:hi] * dn - g * scales[w]).astype(BF16)
        return carry

    lax.fori_loop(0, groups, back, 0)


def middle_call(g, w_all, gain, tok, cot):
    groups, rows_num, channels = g.shape
    model = tok.shape[1]
    return pl.pallas_call(
        middle_kernel,
        out_shape=[
            jax.ShapeDtypeStruct((4, rows_num, model), BF16),
            jax.ShapeDtypeStruct(g.shape, BF16),
            jax.ShapeDtypeStruct((4, rows_num, model), BF16),
            jax.ShapeDtypeStruct(g.shape, BF16),
            jax.ShapeDtypeStruct((groups, 1, channels), F32),
        ],
        compiler_params=pltpu.CompilerParams(vmem_limit_bytes=VMEM_BYTES),
        cost_estimate=pl.CostEstimate(
            flops=4 * groups * rows_num * channels * model, bytes_accessed=36 * 2**20, transcendentals=0
        ),
        name="nested_norm",
    )(g, w_all, gain, tok, cot)


def partner(axis, bit):
    me = lax.axis_index(axis)
    return me + (1 - 2 * ((me // 2**bit) % 2)) * 2**bit


def bits_of(axis, count):
    me = lax.axis_index(axis)
    return [(me // 2**b) % 2 for b in range(count)]


def log2(value):
    return value.bit_length() - 1


def place(count, fixed):
    return tuple(fixed[b] if b in fixed else slice(None) for b in reversed(range(count)))


class Links:
    def __init__(self, send, recv):
        self.send, self.recv, self.used = send, recv, 0

    def copy(self, src, dst, axis, to):
        at = self.used
        self.used += 1
        return pltpu.make_async_remote_copy(
            src_ref=src, dst_ref=dst, send_sem=self.send.at[at], recv_sem=self.recv.at[at],
            device_id={axis: to}, device_id_type=pl.DeviceIdType.MESH,
        )


def meet(peers):
    barrier = pltpu.get_barrier_semaphore()
    for axis, to in peers:
        pl.semaphore_signal(barrier, inc=1, device_id={axis: to}, device_id_type=pl.DeviceIdType.MESH)
    pl.semaphore_wait(barrier, len(peers))


def add_block(buf, index, slot, at):
    rows = slot.shape[-2]
    step = min(rows, 32)
    index = index + (slice(None),) * (len(buf.shape) - len(index))
    free = [i for i, v in enumerate(index[:-2]) if isinstance(v, slice)]
    full = list(index[:-2])
    for i, v in zip(free, at):
        full[i] = v
    full = tuple(full)

    def piece(r, carry):
        rs = pl.ds(pl.multiple_of(r * step, step), step)
        total = buf[full + (rs, index[-1])].astype(F32) + slot[tuple(at) + (rs, slice(None))].astype(F32)
        buf[full + (rs, index[-1])] = total.astype(buf.dtype)
        return carry

    lax.fori_loop(0, rows // step, piece, 0)


def scatter(links, buf, slots, order, lead=()):
    count = len(order)
    mine = bits_of("batch", count)
    fixed = {}
    for i, b in enumerate(order):
        keep = {**fixed, b: mine[b]}
        copy = links.copy(buf.at[place(count, {**fixed, b: 1 - mine[b]})], slots[i], "batch", partner("batch", b))
        copy.start()
        yield
        copy.wait()
        dims = slots[i].shape[:-2]
        for at in itertools.product(*(range(d) for d in dims)):
            add_block(buf, place(count, keep), slots[i], at)
        fixed = keep


def gather(links, buf, order):
    count = len(order)
    fixed = dict(enumerate(bits_of("batch", count)))
    for b in order:
        at = buf.at[place(count, fixed)]
        copy = links.copy(at, at, "batch", partner("batch", b))
        copy.start()
        yield
        copy.wait()
        fixed = {k: v for k, v in fixed.items() if k != b}


def doubling(links, buf, slots, axis, bits):
    for i, b in enumerate(bits):
        copy = links.copy(buf, slots[i], axis, partner(axis, b))
        copy.start()
        yield
        copy.wait()
        buf[...] = (buf[...].astype(F32) + slots[i][...].astype(F32)).astype(buf.dtype)


def chain(*parts):
    for part in parts:
        yield from part


def run_streams(streams):
    live = list(streams)
    while live:
        live = [s for s in live if next(s, live) is not live]


def halving_slots(count, block, dtype):
    return [pltpu.VMEM((2,) * (count - 1 - i) + tuple(block), dtype) for i in range(count)]


def front_kernel(
    count, tok_ref, pre_ref, zw_hbm, xw_hbm, bcw_hbm, dtw_hbm, w_hbm, gain_hbm,
    convw_ref, convb_ref, dtb_ref, alog_ref, skip_ref,
    x_out, gate_out, scan_out, conv_out, inner_out, bc_out, step_out, prev_out, gated_out, all_ref, gains_ref,
    xs, zw, xw, bcw, dtw, gate_s, scan_s, conv_s, inner_s, bc_s, step_s, prev_s, gated_s, state, tails,
    load_sem, local_sem, store_sem, away_sem, here_sem, send, recv,
):
    rows_num, channels = gated_s.shape[1:]
    groups = gated_s.shape[0]
    length = groups * rows_num
    n = state.shape[0]
    model = tok_ref.shape[1]
    chunks = 2
    chunk = rows_num // chunks
    me = lax.axis_index("head")
    hi, lo = me // 2, me % 2
    near = partner("head", 0)
    far = partner("head", 1)
    others = [near, far, near + far - me]
    links = Links(send, recv)

    loads = [
        pltpu.make_async_copy(src, dst, load_sem.at[i])
        for i, (src, dst) in enumerate(((zw_hbm, zw), (xw_hbm, xw), (bcw_hbm, bcw), (dtw_hbm, dtw)))
    ]
    for load in loads:
        load.start()
    tok = tok_ref[...].astype(F32)
    recip = lax.rsqrt(jnp.mean(tok * tok, axis=-1, keepdims=True) + EPSILON)
    xs[hi, lo] = (tok * recip * pre_ref[...]).astype(BF16)
    meet([("head", z) for z in others] + [("batch", partner("batch", b)) for b in range(count)])

    own_rows = xs.at[hi, lo]
    to_far = []
    for c in range(chunks):
        part = xs.at[hi, lo, pl.ds(c * chunk, chunk)]
        to_far.append(links.copy(part, part, "head", far))
        to_far[-1].start()
    to_near = links.copy(own_rows, own_rows, "head", near)
    to_near.start()
    mine = bits_of("batch", count)
    own = place(count, dict(enumerate(mine)))
    keep = [pltpu.make_async_copy(w_hbm, all_ref.at[me], local_sem.at[0])]
    keep.append(pltpu.make_async_copy(gain_hbm, gains_ref.at[me], local_sem.at[1]))
    for item in keep:
        item.start()
    inner_s[0:8, :] = jnp.zeros((8, channels), F32)
    state[...] = jnp.zeros_like(state)
    for load in loads:
        load.wait()

    def project(at_hi, at_lo):
        first = pl.multiple_of((2 * at_hi + at_lo) * rows_num, rows_num)
        rows = pl.ds(first, rows_num)
        inner_rows = pl.ds(pl.multiple_of(first + 8, 8), rows_num)
        tile = 256

        def columns(t, carry):
            cols = pl.ds(pl.multiple_of(t * tile, tile), tile)
            x = xs[at_hi, at_lo]
            gate_s[rows, cols] = mm(x, zw[:, cols])
            inner_s[inner_rows, cols] = mm(x, xw[:, cols])
            return carry

        lax.fori_loop(0, channels // tile, columns, 0)
        x = xs[at_hi, at_lo]
        bc_s[rows, :] = mm(x, bcw[...])
        step_s[rows, :] = mm(x, dtw[...])

    project(hi, lo)
    to_near.wait()
    project(hi, 1 - lo)
    onward = []
    for c in range(chunks):
        to_far[c].wait()
        part = xs.at[1 - hi, lo, pl.ds(c * chunk, chunk)]
        onward.append(links.copy(part, part, "head", near))
        onward[-1].start()

    half = w_hbm.shape[-1] // 2

    def pieces(z, cols, order):
        copy = links.copy(
            w_hbm.at[own + (slice(None), cols)], all_ref.at[(me,) + own + (slice(None), cols)], "head", z
        )
        copy.start()
        yield
        copy.wait()
        fixed = dict(enumerate(mine))
        for b in order:
            at = all_ref.at[(z,) + place(count, fixed) + (slice(None), cols)]
            step = links.copy(at, at, "batch", partner("batch", b))
            step.start()
            yield
            step.wait()
            fixed = {k: v for k, v in fixed.items() if k != b}

    up = list(range(1, count))
    streams = []
    for z in others:
        streams.append(pieces(z, pl.ds(0, half), up + [0]))
        streams.append(pieces(z, pl.ds(half, half), up[::-1] + [0]))
    for s in streams:
        next(s)
    gain_sends = [links.copy(gain_hbm, gains_ref.at[me], "head", z) for z in others]
    for item in gain_sends:
        item.start()

    project(1 - hi, lo)
    for item in onward:
        item.wait()
    project(1 - hi, 1 - lo)

    rate = -jnp.exp(alog_ref[...])
    lower = lower_mask((SPAN, SPAN))
    lower_f = lower.astype(F32)
    left = lax.broadcasted_iota(jnp.int32, (SPAN, 128), 1) < 64

    def block(at, carry):
        first = pl.multiple_of(at * SPAN, SPAN)
        rows = pl.ds(first, SPAN)
        delta = softplus(step_s[rows, :] + dtb_ref[...])
        cum = mm_exact(lower_f, delta * rate)
        cum_t = cum.T
        b_val = bc_s[rows, :n].astype(BF16)
        c_val = bc_s[rows, n:].astype(BF16)
        inner = jnp.where(lower, mm_nt(c_val, b_val), 0.0)
        before = state[...].astype(BF16)
        prev_s[at] = before
        across = mm(c_val, before)
        quarter = at // (rows_num // SPAN)
        sub = pl.ds(pl.multiple_of((at % (rows_num // SPAN)) * SPAN, SPAN), SPAN)
        for pair in range(channels // 128):
            cols = slice(pair * 128, pair * 128 + 128)
            c0, c1, ce = pair_columns(cum, pair, left)
            _, _, de = pair_columns(delta, pair, left)
            tot = ce[SPAN - 1 : SPAN, :]
            window = inner_s[pl.ds(first, SPAN + 8), cols]
            conv_p = convb_ref[:, cols] + sum(
                convw_ref[k : k + 1, cols] * window[5 + k : 5 + k + SPAN] for k in range(4)
            )
            conv_s[rows, cols] = conv_p
            act = conv_p * sigmoid(conv_p)
            u = act * de
            tails[:, cols] = (u * jnp.exp(tot - ce)).astype(BF16)
            u0 = jnp.where(left, u, 0.0).astype(BF16)
            u1 = jnp.where(left, 0.0, u).astype(BF16)
            p0 = (jnp.exp(jnp.minimum(c0 - cum_t[2 * pair : 2 * pair + 1, :], 0.0)) * inner).astype(BF16)
            p1 = (jnp.exp(jnp.minimum(c1 - cum_t[2 * pair + 1 : 2 * pair + 2, :], 0.0)) * inner).astype(BF16)
            within = mm(jnp.concatenate([p0, p1], axis=1), jnp.concatenate([u0, u1], axis=0))
            y = within + across[:, cols] * jnp.exp(ce) + skip_ref[:, cols] * act
            scan_s[rows, cols] = y
            gate = gate_s[rows, cols]
            gated_s[quarter, sub, cols] = (y * gate * sigmoid(gate)).astype(BF16)
            state[:, cols] = state[:, cols] * jnp.exp(tot)
        state[...] += mm(bc_s[rows, :n].T.astype(BF16), tails[...])
        return carry

    def leave(q):
        return pltpu.make_async_remote_copy(
            src_ref=gated_s.at[q], dst_ref=gated_out.at[me], send_sem=away_sem.at[q], recv_sem=here_sem.at[me],
            device_id={"head": q}, device_id_type=pl.DeviceIdType.MESH,
        )

    def arrive(q):
        return pltpu.make_async_remote_copy(
            src_ref=gated_s.at[q], dst_ref=gated_out.at[q], send_sem=away_sem.at[q], recv_sem=here_sem.at[q],
            device_id={"head": q}, device_id_type=pl.DeviceIdType.MESH,
        )

    subs = rows_num // SPAN

    def stores(q):
        rows = pl.ds(pl.multiple_of(q * rows_num, rows_num), rows_num)
        inner_rows = pl.ds(pl.multiple_of(q * rows_num + 8, 8), rows_num)
        pairs = (
            (xs.at[q // 2, q % 2], x_out.at[rows]),
            (gate_s.at[rows], gate_out.at[rows]),
            (scan_s.at[rows], scan_out.at[rows]),
            (conv_s.at[rows], conv_out.at[rows]),
            (inner_s.at[inner_rows], inner_out.at[rows]),
            (bc_s.at[rows], bc_out.at[rows]),
            (step_s.at[rows], step_out.at[rows]),
            (prev_s.at[pl.ds(q * subs, subs)], prev_out.at[pl.ds(q * subs, subs)]),
        )
        return [pltpu.make_async_copy(src, dst, store_sem.at[i, q]) for i, (src, dst) in enumerate(pairs)]

    def quarter_step(q, carry):
        lax.fori_loop(q * subs, (q + 1) * subs, block, 0)

        @pl.when(q != me)
        def _():
            leave(q).start()

        for item in stores(q):
            item.start()
        return carry

    lax.fori_loop(0, groups, quarter_step, 0)
    stay = pltpu.make_async_copy(gated_s.at[me], gated_out.at[me], local_sem.at[2])
    stay.start()
    run_streams(streams)
    for item in gain_sends:
        item.wait()
    for item in keep:
        item.wait()
    stay.wait()

    def finish(q, carry):
        @pl.when(q != me)
        def _():
            leave(q).wait_send()
            arrive(q).wait_recv()

        for item in stores(q):
            item.wait()
        return carry

    lax.fori_loop(0, groups, finish, 0)


def front_call(tokens, pre_gain, zw, xw, bcw, dtw, out_weight, norm_gain, convw, convb, dtb, alog, skip, groups, batches):
    rows_num, model = tokens.shape
    channels = zw.shape[1]
    n = bcw.shape[1] // 2
    length = rows_num * groups
    count = log2(batches)
    part = channels // batches
    copies = 3 + 2 + (groups - 1) * (1 + 2 * (1 + count))
    hbm = pl.BlockSpec(memory_space=pl.ANY)
    vmem = pl.BlockSpec(memory_space=pltpu.VMEM)
    wide = jax.ShapeDtypeStruct((length, channels), F32)
    outs = [
        jax.ShapeDtypeStruct((length, model), BF16), wide, wide, wide, wide,
        jax.ShapeDtypeStruct((length, 2 * n), F32),
        jax.ShapeDtypeStruct((length, dtw.shape[1]), F32),
        jax.ShapeDtypeStruct((length // SPAN, n, channels), BF16),
        jax.ShapeDtypeStruct((groups, rows_num, channels), BF16),
        jax.ShapeDtypeStruct((groups,) + (2,) * count + (part, model), BF16),
        jax.ShapeDtypeStruct((groups, 8, channels), F32),
    ]
    dma = pltpu.SemaphoreType.DMA
    result = pl.pallas_call(
        functools.partial(front_kernel, count),
        in_specs=[vmem, vmem] + [hbm] * 6 + [vmem] * 5,
        out_specs=[hbm] * len(outs),
        out_shape=outs,
        scratch_shapes=[
            pltpu.VMEM((2, 2, rows_num, model), BF16),
            pltpu.VMEM(zw.shape, BF16), pltpu.VMEM(xw.shape, BF16),
            pltpu.VMEM(bcw.shape, BF16), pltpu.VMEM(dtw.shape, BF16),
            pltpu.VMEM((length, channels), F32), pltpu.VMEM((length, channels), F32),
            pltpu.VMEM((length, channels), F32), pltpu.VMEM((length + 8, channels), F32),
            pltpu.VMEM((length, 2 * n), F32), pltpu.VMEM((length, dtw.shape[1]), F32),
            pltpu.VMEM((length // SPAN, n, channels), BF16),
            pltpu.VMEM((groups, rows_num, channels), BF16),
            pltpu.VMEM((n, channels), F32), pltpu.VMEM((SPAN, channels), BF16),
            dma((4,)), dma((3,)), dma((8, groups)), dma((groups,)), dma((groups,)), dma((copies,)), dma((copies,)),
        ],
        compiler_params=pltpu.CompilerParams(
            collective_id=1, has_side_effects=True, vmem_limit_bytes=VMEM_BYTES
        ),
        cost_estimate=pl.CostEstimate(
            flops=4 * length * model * channels, bytes_accessed=400 * 2**20, transcendentals=0
        ),
        name="front",
    )(
        tokens, pre_gain[None], zw, xw, bcw, dtw, out_weight.reshape((2,) * count + (part, model)),
        jnp.broadcast_to(norm_gain[None], (8, channels)), convw, convb, dtb, alog, skip,
    )
    x, gate, scan, conv, inner, bc, step, prev, gated, w_all, gains = result
    return x, gate, scan, conv, inner, bc, step, prev, gated, w_all.reshape(groups, channels, model), gains[:, :1]


def outgrad_scatter_kernel(count, gg_ref, dy_ref, out_ref, *refs):
    buf, send, recv = refs[0], refs[-2], refs[-1]
    streams_num = 4
    slots = [refs[1 + s * count : 1 + (s + 1) * count] for s in range(streams_num)]
    groups, _, channels = gg_ref.shape
    part, cols = buf.shape[-2:]
    model = dy_ref.shape[2]
    links = Links(send, recv)
    meet([("batch", partner("batch", b)) for b in range(count)])
    up = list(range(1, count))

    def stream(s):
        g0, c0 = (s // 2) * (groups // 2), (s % 2) * cols
        for j in range(groups // 2):
            for w, (lo, hi) in enumerate(segments(channels)):
                term = mm_tn(gg_ref[g0 + j, :, lo:hi], dy_ref[w, :, c0 : c0 + cols]).astype(BF16)
                for p in range(lo // part, hi // part):
                    index = tuple((p >> b) & 1 for b in reversed(range(count)))
                    buf[(s,) + index + (j,)] = term[p * part - lo : (p + 1) * part - lo]
        order = [0] + (up if s % 2 == 0 else up[::-1])
        yield from scatter(links, buf.at[s], slots[s], order)
        mine = place(count, dict(enumerate(bits_of("batch", count))))
        for j in range(groups // 2):
            out_ref[g0 + j, :, c0 : c0 + cols] = buf[(s,) + mine + (j,)]

    run_streams([stream(s) for s in range(streams_num)])


def outgrad_scatter_call(gg, dy, batches):
    groups, _, channels = gg.shape
    model = dy.shape[2]
    count = log2(batches)
    part = channels // batches
    block = (groups // 2, part, model // 2)
    vmem = pl.BlockSpec(memory_space=pltpu.VMEM)
    return pl.pallas_call(
        functools.partial(outgrad_scatter_kernel, count),
        in_specs=[vmem, vmem],
        out_specs=vmem,
        out_shape=jax.ShapeDtypeStruct((groups, part, model), BF16),
        scratch_shapes=[pltpu.VMEM((4,) + (2,) * count + block, BF16)]
        + [s for _ in range(4) for s in halving_slots(count, block, BF16)]
        + [pltpu.SemaphoreType.DMA((4 * count,)), pltpu.SemaphoreType.DMA((4 * count,))],
        compiler_params=pltpu.CompilerParams(
            collective_id=2, has_side_effects=True, vmem_limit_bytes=VMEM_BYTES
        ),
        cost_estimate=pl.CostEstimate(
            flops=2 * groups * gg.shape[1] * channels * model, bytes_accessed=200 * 2**20, transcendentals=0
        ),
        name="out_weight_grad",
    )(gg, dy)


def tail_kernel(
    count, group_bits,
    z_ref, x_ref, o_ref, bc_ref, small_ref,
    zo_ref, xo_ref, oo_ref, bco_ref, smallo_ref, *refs
):
    zx, zx_full, obuf, bcbuf, bc_full, small = refs[:6]
    refs = refs[6:]
    zx_slots = [refs[s * count : (s + 1) * count] for s in range(4)]
    refs = refs[4 * count :]
    bc_slots, refs = refs[:count], refs[count:]
    bc_head, refs = refs[:group_bits], refs[group_bits:]
    small_slots, refs = refs[:count], refs[count:]
    small_head, refs = refs[:group_bits], refs[group_bits:]
    local, send, recv = refs
    cols = zx.shape[-1]
    ocols = obuf.shape[-1]
    shared = small_head[0].shape[0]
    links = Links(send, recv)
    mine = place(count, dict(enumerate(bits_of("batch", count))))
    loads = []
    for s in range(4):
        src = (z_ref, x_ref)[s // 2]
        index = (slice(None),) * (count + 1) + (pl.ds((s % 2) * cols, cols),)
        loads.append(pltpu.make_async_copy(src.at[index], zx.at[s], local.at[s]))
    loads.append(pltpu.make_async_copy(bc_ref, bcbuf, local.at[4]))
    loads.append(pltpu.make_async_copy(small_ref, small, local.at[5]))
    for s in range(2):
        loads.append(
            pltpu.make_async_copy(o_ref.at[:, pl.ds(s * ocols, ocols)], obuf.at[(s,) + mine], local.at[6 + s])
        )
    for load in loads:
        load.start()
    meet(
        [("batch", partner("batch", b)) for b in range(count)]
        + [("head", partner("head", b)) for b in range(group_bits)]
    )
    up = list(range(1, count))
    orders = [up, up[::-1]]
    stores = []

    def store(src, dst, at):
        stores.append(pltpu.make_async_copy(src, dst, local.at[at]))
        stores[-1].start()

    def grads(s):
        loads[s].wait()
        yield from scatter(links, zx.at[s], zx_slots[s], [0] + orders[s // 2])
        zx_full[(s,) + mine] = zx[(s,) + mine]
        yield from gather(links, zx_full.at[s], orders[s // 2][::-1] + [0])
        index = (slice(None),) * (count + 1) + (pl.ds((s % 2) * cols, cols),)
        store(zx_full.at[s], (zo_ref, xo_ref)[s // 2].at[index], 8 + s)

    def state(order):
        loads[4].wait()
        yield from scatter(links, bcbuf, bc_slots, [0] + order)
        yield from doubling(links, bcbuf.at[mine], bc_head, "head", range(group_bits))
        bc_full[mine] = bcbuf[mine]
        yield from gather(links, bc_full, order[::-1] + [0])
        store(bc_full, bco_ref, 12)

    def vectors():
        loads[5].wait()
        yield from doubling(links, small, small_slots, "batch", range(count))
        yield from doubling(links, small.at[pl.ds(0, shared)], small_head, "head", range(group_bits))
        smallo_ref[...] = small[...]

    def outs(s):
        loads[6 + s].wait()
        yield from gather(links, obuf.at[s], orders[s] + [0])
        index = (slice(None),) * (count + 1) + (pl.ds(s * ocols, ocols),)
        store(obuf.at[s], oo_ref.at[index], 13 + s)

    run_streams([grads(0), grads(2), grads(1), grads(3), vectors(), state(orders[0]), outs(0), outs(1)])
    for item in stores:
        item.wait()


def tail_call(z_grad, x_grad, out_own, bc_grad, small, shared, groups, batches):
    model, channels = z_grad.shape
    count = log2(batches)
    group_bits = log2(groups)
    rows = model // batches
    part, width = out_own.shape
    n2 = bc_grad.shape[1]
    lead = (2,) * count
    hbm = pl.BlockSpec(memory_space=pl.ANY)
    vmem = pl.BlockSpec(memory_space=pltpu.VMEM)
    block = (rows, channels // 2)
    copies = 4 * 2 * count + 2 * count + group_bits + count + group_bits + 2 * count
    zo, xo, oo, bco, smallo = pl.pallas_call(
        functools.partial(tail_kernel, count, group_bits),
        in_specs=[hbm] * 5,
        out_specs=[hbm] * 4 + [vmem],
        out_shape=[
            jax.ShapeDtypeStruct(lead + (rows, channels), BF16),
            jax.ShapeDtypeStruct(lead + (rows, channels), BF16),
            jax.ShapeDtypeStruct(lead + (part, width), BF16),
            jax.ShapeDtypeStruct(lead + (rows, n2), BF16),
            jax.ShapeDtypeStruct(small.shape, F32),
        ],
        scratch_shapes=[
            pltpu.VMEM((4,) + lead + block, BF16),
            pltpu.VMEM((4,) + lead + block, BF16),
            pltpu.VMEM((2,) + lead + (part, width // 2), BF16),
            pltpu.VMEM(lead + (rows, n2), BF16),
            pltpu.VMEM(lead + (rows, n2), BF16),
            pltpu.VMEM(small.shape, F32),
        ]
        + [s for _ in range(4) for s in halving_slots(count, block, BF16)]
        + halving_slots(count, (rows, n2), BF16)
        + [pltpu.VMEM((rows, n2), BF16)] * group_bits
        + [pltpu.VMEM(small.shape, F32)] * count
        + [pltpu.VMEM((shared, small.shape[1]), F32)] * group_bits
        + [
            pltpu.SemaphoreType.DMA((15,)), pltpu.SemaphoreType.DMA((copies,)), pltpu.SemaphoreType.DMA((copies,)),
        ],
        compiler_params=pltpu.CompilerParams(
            collective_id=3, has_side_effects=True, vmem_limit_bytes=VMEM_BYTES
        ),
        cost_estimate=pl.CostEstimate(flops=0, bytes_accessed=300 * 2**20, transcendentals=0),
        name="sum_grads",
    )(
        z_grad.reshape(lead + (rows, channels)), x_grad.reshape(lead + (rows, channels)), out_own,
        bc_grad.reshape(lead + (rows, n2)), small,
    )
    return (
        zo.reshape(model, channels), xo.reshape(model, channels), oo.reshape(part * batches, width),
        bco.reshape(model, n2), smallo,
    )


def per_device(
    tokens, z_weight, x_weight, bc_weight, dt_weight, conv_weight, conv_bias, dt_bias,
    a_log, skip, norm_gain, pre_gain, out_weight, cotangent,
):
    groups = lax.axis_size("head")
    batches = lax.axis_size("batch")
    head_at = lax.axis_index("head")
    _, own_len, model = tokens.shape
    tokens = tokens[0]
    cot = cotangent[:, 0]
    channels = z_weight.shape[1]
    heads = dt_weight.shape[1]
    tokens_f = tokens.astype(F32)
    recip_in = lax.rsqrt(jnp.mean(tokens_f * tokens_f, axis=-1, keepdims=True) + EPSILON)
    pad = lambda v: jnp.pad(v, ((0, 0), (0, 128 - heads)))
    dtb = pad(dt_bias[None])
    alog = pad(a_log[None])
    skip_r = skip[None]
    x, gate, scan, conv, inner, bc, step, prev, gated, w_all, gain_all = front_call(
        tokens, pre_gain, z_weight, x_weight, bc_weight, pad(dt_weight), out_weight, norm_gain,
        conv_weight, conv_bias[None], dtb, alog, skip_r, groups, batches,
    )
    outputs, d_gated, dy, gg, gain_grad = middle_call(gated, w_all, gain_all, tokens, cot)
    d_gated = lax.all_to_all(d_gated, "head", 0, 0, tiled=True).reshape(groups * own_len, channels)
    out_part = outgrad_scatter_call(gg, dy, batches)
    d_gated, out_part = lax.optimization_barrier((d_gated, out_part))
    out_part = lax.psum_scatter(out_part.reshape(-1, model), "head", scatter_dimension=0, tiled=True)
    hot = (jnp.arange(channels)[None] // (channels // heads) == jnp.arange(heads)[:, None]).astype(BF16)
    d_gate, d_inner, d_bc, d_step, vec, per_head = backward_call(
        d_gated, gate, scan, conv, inner, bc, step, prev, conv_weight, dtb, alog, skip_r, hot
    )
    d_step = d_step.astype(BF16)
    d_bc = d_bc.astype(BF16)
    d_rows = (
        mm_nt(d_gate, z_weight)
        + mm_nt(d_inner, x_weight)
        + lax.dot_general(d_step, dt_weight, (((0,), (1,)), ((), ())), preferred_element_type=F32)
        + mm_nt(d_bc, bc_weight)
    )
    d_rows = d_rows.astype(BF16)
    d_own = lax.psum_scatter(d_rows, "head", scatter_dimension=0, tiled=True).astype(F32)
    z_grad = mm_tn(x, d_gate).astype(BF16)
    x_grad = mm_tn(x, d_inner).astype(BF16)
    dt_grad = lax.dot_general(x, d_step, (((0,), (1,)), ((), ())), preferred_element_type=F32)
    bc_grad = mm_tn(x, d_bc).astype(BF16)
    pre_grad = jnp.sum(x.astype(F32) * d_rows.astype(F32), axis=0) / pre_gain

    width = 1024
    all_part = jnp.concatenate([jnp.zeros((groups, channels), F32) + gain_grad[:, 0], pre_grad.reshape(-1, width)])
    shared = -(-all_part.shape[0] // 8) * 8
    own_part = jnp.concatenate([vec[:6].reshape(-1), jnp.sum(per_head, axis=1), dt_grad.reshape(-1)])
    own_rows = -(-own_part.shape[0] // (8 * width)) * 8
    small = jnp.concatenate([
        jnp.pad(all_part, ((0, shared - all_part.shape[0]), (0, 0))),
        jnp.pad(own_part, (0, own_rows * width - own_part.shape[0])).reshape(own_rows, width),
    ])
    z_grad, x_grad, out_grad, bc_grad, small = tail_call(
        z_grad, x_grad, out_part, bc_grad, small, shared, groups, batches
    )
    z_grad, x_grad, out_grad, bc_grad = (v.astype(F32) for v in (z_grad, x_grad, out_grad, bc_grad))
    gain_grad = lax.dynamic_slice_in_dim(small, head_at, 1, 0)[0]
    pre_grad = small[groups : groups + model // width].reshape(-1)
    own = small[shared:].reshape(-1)

    inner_sum = jnp.mean(tokens_f * pre_gain * d_own, axis=-1, keepdims=True)
    tokens_grad = jnp.sum(cot.astype(F32), axis=0) + pre_gain * recip_in * d_own
    tokens_grad = (tokens_grad - tokens_f * recip_in**3 * inner_sum).astype(BF16)
    c = channels
    return (
        outputs[:, None],
        tokens_grad[None],
        z_grad,
        x_grad,
        bc_grad,
        own[6 * c + 2 * heads : 6 * c + 2 * heads + model * heads].reshape(model, heads),
        own[: 4 * c].reshape(4, c),
        own[4 * c : 5 * c],
        own[6 * c : 6 * c + heads],
        own[6 * c + heads : 6 * c + 2 * heads],
        own[5 * c : 6 * c],
        gain_grad,
        pre_grad,
        out_grad,
    )


def solution(mesh):
    head_cols = P(None, "head")
    rows4 = P(None, "batch", "head", None)
    return jax.shard_map(
        per_device,
        mesh=mesh,
        in_specs=(
            P("batch", "head", None), head_cols, head_cols, P(), head_cols, head_cols, P("head"),
            P("head"), P("head"), P("head"), P("head"), P(), P("head", None), rows4,
        ),
        out_specs=(
            rows4, P("batch", "head", None), head_cols, head_cols, P(), head_cols, head_cols,
            P("head"), P("head"), P("head"), P("head"), P("head"), P(), P("head", None),
        ),
        check_vma=False,
    )
```

```python
import functools
import itertools

import jax
import jax.numpy as jnp
from jax import lax
from jax.experimental import pallas as pl
from jax.experimental.pallas import tpu as pltpu
from jax.sharding import PartitionSpec as P

SPAN = 128
ROWS = 256
EPSILON = 1e-05
BF16 = jnp.bfloat16
F32 = jnp.float32
HIGHEST = lax.Precision.HIGHEST
VMEM_BYTES = 60 * 1024 * 1024
BACK_VMEM_BYTES = 63 * 1024 * 1024


def mm(a, b):
    return lax.dot_general(a, b, (((1,), (0,)), ((), ())), preferred_element_type=F32)


def mm_nt(a, b):
    return lax.dot_general(a, b, (((1,), (1,)), ((), ())), preferred_element_type=F32)


def mm_tn(a, b):
    return lax.dot_general(a, b, (((0,), (0,)), ((), ())), preferred_element_type=F32)


def mm_exact(a, b):
    return lax.dot_general(
        a, b, (((1,), (0,)), ((), ())), preferred_element_type=F32, precision=HIGHEST
    )


def lower_mask(shape):
    return lax.broadcasted_iota(jnp.int32, shape, 0) >= lax.broadcasted_iota(jnp.int32, shape, 1)


def softplus(v):
    return jnp.maximum(v, 0.0) + jnp.log1p(jnp.exp(-jnp.abs(v)))


def sigmoid(v):
    return 1.0 / (1.0 + jnp.exp(-v))


def pair_columns(values, pair, left):
    shape = (SPAN, 128)
    one = jnp.broadcast_to(values[:, 2 * pair : 2 * pair + 1], shape)
    two = jnp.broadcast_to(values[:, 2 * pair + 1 : 2 * pair + 2], shape)
    return one, two, jnp.where(left, one, two)


def segments(channels):
    ends = [channels * 2**w // 8 for w in range(4)]
    return list(zip([0] + ends[:-1], ends))


def middle_kernel(g_ref, w_ref, gain_ref, tok_ref, cot_ref, out_ref, dg_ref, dy_ref, gg_ref, ggrad_ref):
    groups, rows_num, channels = g_ref.shape
    model = tok_ref.shape[1]
    segs = segments(channels)
    sums = [jnp.zeros((rows_num, 1), F32) for _ in segs]
    for j in range(groups):
        g = g_ref[j].astype(F32)
        gg_ref[j] = (g * gain_ref[j]).astype(BF16)
        for w, (lo, hi) in enumerate(segs):
            sums[w] += jnp.sum(g[:, lo:hi] * g[:, lo:hi], axis=1, keepdims=True)
    recips = []
    total = jnp.zeros((rows_num, 1), F32)
    for w, (lo, hi) in enumerate(segs):
        total = total + sums[w]
        recips.append(lax.rsqrt(total / (hi * groups) + EPSILON))
    tile = 512

    def forward(at, dots):
        cols = pl.ds(pl.multiple_of(at * tile, tile), tile)
        acc = jnp.zeros((rows_num, tile), F32)
        tok = tok_ref[:, cols].astype(F32)
        new = []
        for w, (lo, hi) in enumerate(segs):
            acc += mm(
                jnp.concatenate([gg_ref[j, :, lo:hi] for j in range(groups)], axis=1),
                jnp.concatenate([w_ref[j, lo:hi, cols] for j in range(groups)], axis=0),
            )
            out_ref[w, :, cols] = (tok + recips[w] * acc).astype(BF16)
            new.append(dots[w] + jnp.sum(cot_ref[w, :, cols].astype(F32) * acc, axis=1, keepdims=True))
        combined = jnp.zeros((rows_num, tile), F32)
        for w in reversed(range(4)):
            combined += recips[w] * cot_ref[w, :, cols].astype(F32)
            dy_ref[w, :, cols] = combined.astype(BF16)
        return tuple(new)

    dots = lax.fori_loop(
        0, model // tile, forward, tuple(jnp.zeros((rows_num, 1), F32) for _ in segs)
    )
    scales = [None] * 4
    scale = jnp.zeros((rows_num, 1), F32)
    for w in reversed(range(4)):
        scale = scale + recips[w] ** 3 * dots[w] / (segs[w][1] * groups)
        scales[w] = scale

    def back(j, carry):
        for w, (lo, hi) in enumerate(segs):
            dn = mm_nt(dy_ref[w], w_ref[j, lo:hi, :])
            g = g_ref[j, :, lo:hi].astype(F32)
            ggrad_ref[j, :, lo:hi] = jnp.sum(g * dn, axis=0, keepdims=True)
            dg_ref[j, :, lo:hi] = (gain_ref[j, :, lo:hi] * dn - g * scales[w]).astype(BF16)
        return carry

    lax.fori_loop(0, groups, back, 0)


def middle_call(g, w_all, gain, tok, cot):
    groups, rows_num, channels = g.shape
    model = tok.shape[1]
    return pl.pallas_call(
        middle_kernel,
        out_shape=[
            jax.ShapeDtypeStruct((4, rows_num, model), BF16),
            jax.ShapeDtypeStruct(g.shape, BF16),
            jax.ShapeDtypeStruct((4, rows_num, model), BF16),
            jax.ShapeDtypeStruct(g.shape, BF16),
            jax.ShapeDtypeStruct((groups, 1, channels), F32),
        ],
        compiler_params=pltpu.CompilerParams(vmem_limit_bytes=VMEM_BYTES),
        cost_estimate=pl.CostEstimate(
            flops=4 * groups * rows_num * channels * model, bytes_accessed=36 * 2**20, transcendentals=0
        ),
        name="nested_norm",
    )(g, w_all, gain, tok, cot)


def partner(axis, bit):
    me = lax.axis_index(axis)
    return me + (1 - 2 * ((me // 2**bit) % 2)) * 2**bit


def bits_of(axis, count):
    me = lax.axis_index(axis)
    return [(me // 2**b) % 2 for b in range(count)]


def log2(value):
    return value.bit_length() - 1


def place(count, fixed):
    return tuple(fixed[b] if b in fixed else slice(None) for b in reversed(range(count)))


class Links:
    def __init__(self, send, recv):
        self.send, self.recv, self.used = send, recv, 0

    def copy(self, src, dst, axis, to):
        at = self.used
        self.used += 1
        return pltpu.make_async_remote_copy(
            src_ref=src, dst_ref=dst, send_sem=self.send.at[at], recv_sem=self.recv.at[at],
            device_id={axis: to}, device_id_type=pl.DeviceIdType.MESH,
        )


def meet(peers):
    barrier = pltpu.get_barrier_semaphore()
    for axis, to in peers:
        pl.semaphore_signal(barrier, inc=1, device_id={axis: to}, device_id_type=pl.DeviceIdType.MESH)
    pl.semaphore_wait(barrier, len(peers))


def add_block(buf, index, slot, at):
    rows = slot.shape[-2]
    step = min(rows, 32)
    index = index + (slice(None),) * (len(buf.shape) - len(index))
    free = [i for i, v in enumerate(index[:-2]) if isinstance(v, slice)]
    full = list(index[:-2])
    for i, v in zip(free, at):
        full[i] = v
    full = tuple(full)

    def piece(r, carry):
        rs = pl.ds(pl.multiple_of(r * step, step), step)
        total = buf[full + (rs, index[-1])].astype(F32) + slot[tuple(at) + (rs, slice(None))].astype(F32)
        buf[full + (rs, index[-1])] = total.astype(buf.dtype)
        return carry

    lax.fori_loop(0, rows // step, piece, 0)


def scatter(links, buf, slots, order, lead=()):
    count = len(order)
    mine = bits_of("batch", count)
    fixed = {}
    for i, b in enumerate(order):
        keep = {**fixed, b: mine[b]}
        copy = links.copy(buf.at[place(count, {**fixed, b: 1 - mine[b]})], slots[i], "batch", partner("batch", b))
        copy.start()
        yield
        copy.wait()
        dims = slots[i].shape[:-2]
        for at in itertools.product(*(range(d) for d in dims)):
            add_block(buf, place(count, keep), slots[i], at)
        fixed = keep


def gather(links, buf, order):
    count = len(order)
    fixed = dict(enumerate(bits_of("batch", count)))
    for b in order:
        at = buf.at[place(count, fixed)]
        copy = links.copy(at, at, "batch", partner("batch", b))
        copy.start()
        yield
        copy.wait()
        fixed = {k: v for k, v in fixed.items() if k != b}


def doubling(links, buf, slots, axis, bits):
    for i, b in enumerate(bits):
        copy = links.copy(buf, slots[i], axis, partner(axis, b))
        copy.start()
        yield
        copy.wait()
        buf[...] = (buf[...].astype(F32) + slots[i][...].astype(F32)).astype(buf.dtype)


def chain(*parts):
    for part in parts:
        yield from part


def run_streams(streams):
    live = list(streams)
    while live:
        live = [s for s in live if next(s, live) is not live]


def halving_slots(count, block, dtype):
    return [pltpu.VMEM((2,) * (count - 1 - i) + tuple(block), dtype) for i in range(count)]


def front_kernel(
    count, tok_ref, pre_ref, zw_hbm, xw_hbm, bcw_hbm, dtw_hbm, w_hbm, gain_hbm,
    convw_ref, convb_ref, dtb_ref, alog_ref, skip_ref,
    x_out, a_out, s_out, act_out, dsc_out, inn_out, bc_out, step_out, prev_out, gated_out, all_ref, gains_ref,
    xs, zw, xw, bcw, dtw, gate_s, a_s, s_s, act_s, dsc_s, inn_s, inner_s, bc_s, bcb_s, step_s, prev_s, gated_s, state, tails,
    load_sem, local_sem, store_sem, away_sem, here_sem, send, recv,
):
    rows_num, channels = gated_s.shape[1:]
    groups = gated_s.shape[0]
    length = groups * rows_num
    n = state.shape[0]
    model = tok_ref.shape[1]
    chunks = 2
    chunk = rows_num // chunks
    me = lax.axis_index("head")
    hi, lo = me // 2, me % 2
    near = partner("head", 0)
    far = partner("head", 1)
    others = [near, far, near + far - me]
    links = Links(send, recv)

    loads = [
        pltpu.make_async_copy(src, dst, load_sem.at[i])
        for i, (src, dst) in enumerate(((zw_hbm, zw), (xw_hbm, xw), (bcw_hbm, bcw), (dtw_hbm, dtw)))
    ]
    for load in loads:
        load.start()
    tok = tok_ref[...].astype(F32)
    recip = lax.rsqrt(jnp.mean(tok * tok, axis=-1, keepdims=True) + EPSILON)
    xs[hi, lo] = (tok * recip * pre_ref[...]).astype(BF16)
    meet([("head", z) for z in others] + [("batch", partner("batch", b)) for b in range(count)])

    own_rows = xs.at[hi, lo]
    to_far = []
    for c in range(chunks):
        part = xs.at[hi, lo, pl.ds(c * chunk, chunk)]
        to_far.append(links.copy(part, part, "head", far))
        to_far[-1].start()
    to_near = links.copy(own_rows, own_rows, "head", near)
    to_near.start()
    mine = bits_of("batch", count)
    own = place(count, dict(enumerate(mine)))
    keep = [pltpu.make_async_copy(w_hbm, all_ref.at[me], local_sem.at[0])]
    keep.append(pltpu.make_async_copy(gain_hbm, gains_ref.at[me], local_sem.at[1]))
    for item in keep:
        item.start()
    inner_s[0:8, :] = jnp.zeros((8, channels), F32)
    state[...] = jnp.zeros_like(state)
    for load in loads:
        load.wait()

    def project(at_hi, at_lo):
        first = pl.multiple_of((2 * at_hi + at_lo) * rows_num, rows_num)
        rows = pl.ds(first, rows_num)
        inner_rows = pl.ds(pl.multiple_of(first + 8, 8), rows_num)
        tile = 256

        def columns(t, carry):
            cols = pl.ds(pl.multiple_of(t * tile, tile), tile)
            x = xs[at_hi, at_lo]
            gate_s[rows, cols] = mm(x, zw[:, cols])
            inner_s[inner_rows, cols] = mm(x, xw[:, cols])
            return carry

        lax.fori_loop(0, channels // tile, columns, 0)
        x = xs[at_hi, at_lo]
        bc_s[rows, :] = mm(x, bcw[...])
        step_s[rows, :] = mm(x, dtw[...])

    project(hi, lo)
    to_near.wait()
    project(hi, 1 - lo)
    onward = []
    for c in range(chunks):
        to_far[c].wait()
        part = xs.at[1 - hi, lo, pl.ds(c * chunk, chunk)]
        onward.append(links.copy(part, part, "head", near))
        onward[-1].start()

    half = w_hbm.shape[-1] // 2

    def pieces(z, cols, order):
        copy = links.copy(
            w_hbm.at[own + (slice(None), cols)], all_ref.at[(me,) + own + (slice(None), cols)], "head", z
        )
        copy.start()
        yield
        copy.wait()
        fixed = dict(enumerate(mine))
        for b in order:
            at = all_ref.at[(z,) + place(count, fixed) + (slice(None), cols)]
            step = links.copy(at, at, "batch", partner("batch", b))
            step.start()
            yield
            step.wait()
            fixed = {k: v for k, v in fixed.items() if k != b}

    up = list(range(1, count))
    streams = []
    for z in others:
        streams.append(pieces(z, pl.ds(0, half), up + [0]))
        streams.append(pieces(z, pl.ds(half, half), up[::-1] + [0]))
    for s in streams:
        next(s)
    gain_sends = [links.copy(gain_hbm, gains_ref.at[me], "head", z) for z in others]
    for item in gain_sends:
        item.start()

    project(1 - hi, lo)
    for item in onward:
        item.wait()
    project(1 - hi, 1 - lo)

    rate = -jnp.exp(alog_ref[...])
    lower = lower_mask((SPAN, SPAN))
    lower_f = lower.astype(F32)
    left = lax.broadcasted_iota(jnp.int32, (SPAN, 128), 1) < 64

    def block(at, carry):
        first = pl.multiple_of(at * SPAN, SPAN)
        rows = pl.ds(first, SPAN)
        delta = softplus(step_s[rows, :] + dtb_ref[...])
        cum = mm_exact(lower_f, delta * rate)
        cum_t = cum.T
        bcb_s[rows, :] = bc_s[rows, :].astype(BF16)
        b_val = bcb_s[rows, :n]
        c_val = bcb_s[rows, n:]
        inner = jnp.where(lower, mm_nt(c_val, b_val), 0.0)
        before = state[...].astype(BF16)
        prev_s[at] = before
        across = mm(c_val, before)
        quarter = at // (rows_num // SPAN)
        sub = pl.ds(pl.multiple_of((at % (rows_num // SPAN)) * SPAN, SPAN), SPAN)
        for pair in range(channels // 128):
            cols = slice(pair * 128, pair * 128 + 128)
            c0, c1, ce = pair_columns(cum, pair, left)
            _, _, de = pair_columns(delta, pair, left)
            tot = ce[SPAN - 1 : SPAN, :]
            window = inner_s[pl.ds(first, SPAN + 8), cols]
            conv_p = convb_ref[:, cols] + sum(
                convw_ref[k : k + 1, cols] * window[5 + k : 5 + k + SPAN] for k in range(4)
            )
            inn_s[rows, cols] = window[8:].astype(BF16)
            sc = sigmoid(conv_p)
            act = conv_p * sc
            act_s[rows, cols] = act.astype(BF16)
            dsc_s[rows, cols] = (sc + act * (1.0 - sc)).astype(BF16)
            u = act * de
            tails[:, cols] = (u * jnp.exp(tot - ce)).astype(BF16)
            u0 = jnp.where(left, u, 0.0).astype(BF16)
            u1 = jnp.where(left, 0.0, u).astype(BF16)
            p0 = (jnp.exp(jnp.minimum(c0 - cum_t[2 * pair : 2 * pair + 1, :], 0.0)) * inner).astype(BF16)
            p1 = (jnp.exp(jnp.minimum(c1 - cum_t[2 * pair + 1 : 2 * pair + 2, :], 0.0)) * inner).astype(BF16)
            within = mm(jnp.concatenate([p0, p1], axis=1), jnp.concatenate([u0, u1], axis=0))
            y = within + across[:, cols] * jnp.exp(ce) + skip_ref[:, cols] * act
            gate = gate_s[rows, cols]
            sg = sigmoid(gate)
            sl = gate * sg
            s_s[rows, cols] = sl.astype(BF16)
            a_s[rows, cols] = (y * (sg + sl * (1.0 - sg))).astype(BF16)
            gated_s[quarter, sub, cols] = (y * sl).astype(BF16)
            state[:, cols] = state[:, cols] * jnp.exp(tot)
        state[...] += mm(bc_s[rows, :n].T.astype(BF16), tails[...])
        return carry

    def leave(q):
        return pltpu.make_async_remote_copy(
            src_ref=gated_s.at[q], dst_ref=gated_out.at[me], send_sem=away_sem.at[q], recv_sem=here_sem.at[me],
            device_id={"head": q}, device_id_type=pl.DeviceIdType.MESH,
        )

    def arrive(q):
        return pltpu.make_async_remote_copy(
            src_ref=gated_s.at[q], dst_ref=gated_out.at[q], send_sem=away_sem.at[q], recv_sem=here_sem.at[q],
            device_id={"head": q}, device_id_type=pl.DeviceIdType.MESH,
        )

    subs = rows_num // SPAN

    def stores(q):
        rows = pl.ds(pl.multiple_of(q * rows_num, rows_num), rows_num)
        pairs = (
            (xs.at[q // 2, q % 2], x_out.at[rows]),
            (a_s.at[rows], a_out.at[rows]),
            (s_s.at[rows], s_out.at[rows]),
            (act_s.at[rows], act_out.at[rows]),
            (dsc_s.at[rows], dsc_out.at[rows]),
            (inn_s.at[rows], inn_out.at[rows]),
            (bcb_s.at[rows], bc_out.at[rows]),
            (step_s.at[rows], step_out.at[rows]),
            (prev_s.at[pl.ds(q * subs, subs)], prev_out.at[pl.ds(q * subs, subs)]),
        )
        return [pltpu.make_async_copy(src, dst, store_sem.at[i, q]) for i, (src, dst) in enumerate(pairs)]

    def quarter_step(q, carry):
        lax.fori_loop(q * subs, (q + 1) * subs, block, 0)

        @pl.when(q != me)
        def _():
            leave(q).start()

        for item in stores(q):
            item.start()
        return carry

    lax.fori_loop(0, groups, quarter_step, 0)
    stay = pltpu.make_async_copy(gated_s.at[me], gated_out.at[me], local_sem.at[2])
    stay.start()
    run_streams(streams)
    for item in gain_sends:
        item.wait()
    for item in keep:
        item.wait()
    stay.wait()

    def finish(q, carry):
        @pl.when(q != me)
        def _():
            leave(q).wait_send()
            arrive(q).wait_recv()

        for item in stores(q):
            item.wait()
        return carry

    lax.fori_loop(0, groups, finish, 0)


def front_call(tokens, pre_gain, zw, xw, bcw, dtw, out_weight, norm_gain, convw, convb, dtb, alog, skip, groups, batches):
    rows_num, model = tokens.shape
    channels = zw.shape[1]
    n = bcw.shape[1] // 2
    length = rows_num * groups
    count = log2(batches)
    part = channels // batches
    copies = 3 + 2 + (groups - 1) * (1 + 2 * (1 + count))
    hbm = pl.BlockSpec(memory_space=pl.ANY)
    vmem = pl.BlockSpec(memory_space=pltpu.VMEM)
    wide = jax.ShapeDtypeStruct((length, channels), BF16)
    outs = [
        jax.ShapeDtypeStruct((length, model), BF16), wide, wide, wide, wide, wide,
        jax.ShapeDtypeStruct((length, 2 * n), BF16),
        jax.ShapeDtypeStruct((length, dtw.shape[1]), F32),
        jax.ShapeDtypeStruct((length // SPAN, n, channels), BF16),
        jax.ShapeDtypeStruct((groups, rows_num, channels), BF16),
        jax.ShapeDtypeStruct((groups,) + (2,) * count + (part, model), BF16),
        jax.ShapeDtypeStruct((groups, 8, channels), F32),
    ]
    dma = pltpu.SemaphoreType.DMA
    result = pl.pallas_call(
        functools.partial(front_kernel, count),
        in_specs=[vmem, vmem] + [hbm] * 6 + [vmem] * 5,
        out_specs=[hbm] * len(outs),
        out_shape=outs,
        scratch_shapes=[
            pltpu.VMEM((2, 2, rows_num, model), BF16),
            pltpu.VMEM(zw.shape, BF16), pltpu.VMEM(xw.shape, BF16),
            pltpu.VMEM(bcw.shape, BF16), pltpu.VMEM(dtw.shape, BF16),
            pltpu.VMEM((length, channels), F32),
            pltpu.VMEM((length, channels), BF16), pltpu.VMEM((length, channels), BF16),
            pltpu.VMEM((length, channels), BF16), pltpu.VMEM((length, channels), BF16),
            pltpu.VMEM((length, channels), BF16), pltpu.VMEM((length + 8, channels), F32),
            pltpu.VMEM((length, 2 * n), F32), pltpu.VMEM((length, 2 * n), BF16),
            pltpu.VMEM((length, dtw.shape[1]), F32), pltpu.VMEM((length // SPAN, n, channels), BF16),
            pltpu.VMEM((groups, rows_num, channels), BF16),
            pltpu.VMEM((n, channels), F32), pltpu.VMEM((SPAN, channels), BF16),
            dma((4,)), dma((3,)), dma((9, groups)), dma((groups,)), dma((groups,)), dma((copies,)), dma((copies,)),
        ],
        compiler_params=pltpu.CompilerParams(
            collective_id=1, has_side_effects=True, vmem_limit_bytes=VMEM_BYTES
        ),
        cost_estimate=pl.CostEstimate(
            flops=4 * length * model * channels, bytes_accessed=400 * 2**20, transcendentals=0
        ),
        name="front",
    )(
        tokens, pre_gain[None], zw, xw, bcw, dtw, out_weight.reshape((2,) * count + (part, model)),
        jnp.broadcast_to(norm_gain[None], (8, channels)), convw, convb, dtb, alog, skip,
    )
    x, a, s, act, dsc, inn, bc, step, prev, gated, w_all, gains = result
    return x, (a, s, act, dsc, inn), bc, step, prev, gated, w_all.reshape(groups, channels, model), gains[:, :1]


def outgrad_scatter_kernel(count, gg_ref, dy_ref, out_ref, *refs):
    buf, send, recv = refs[0], refs[-2], refs[-1]
    streams_num = 4
    slots = [refs[1 + s * count : 1 + (s + 1) * count] for s in range(streams_num)]
    groups, _, channels = gg_ref.shape
    part, cols = buf.shape[-2:]
    model = dy_ref.shape[2]
    links = Links(send, recv)
    meet([("batch", partner("batch", b)) for b in range(count)])
    up = list(range(1, count))

    def stream(s):
        g0, c0 = (s // 2) * (groups // 2), (s % 2) * cols
        for j in range(groups // 2):
            for w, (lo, hi) in enumerate(segments(channels)):
                term = mm_tn(gg_ref[g0 + j, :, lo:hi], dy_ref[w, :, c0 : c0 + cols]).astype(BF16)
                for p in range(lo // part, hi // part):
                    index = tuple((p >> b) & 1 for b in reversed(range(count)))
                    buf[(s,) + index + (j,)] = term[p * part - lo : (p + 1) * part - lo]
        order = [0] + (up if s % 2 == 0 else up[::-1])
        yield from scatter(links, buf.at[s], slots[s], order)
        mine = place(count, dict(enumerate(bits_of("batch", count))))
        for j in range(groups // 2):
            out_ref[g0 + j, :, c0 : c0 + cols] = buf[(s,) + mine + (j,)]

    run_streams([stream(s) for s in range(streams_num)])


def outgrad_scatter_call(gg, dy, batches):
    groups, _, channels = gg.shape
    model = dy.shape[2]
    count = log2(batches)
    part = channels // batches
    block = (groups // 2, part, model // 2)
    vmem = pl.BlockSpec(memory_space=pltpu.VMEM)
    return pl.pallas_call(
        functools.partial(outgrad_scatter_kernel, count),
        in_specs=[vmem, vmem],
        out_specs=vmem,
        out_shape=jax.ShapeDtypeStruct((groups, part, model), BF16),
        scratch_shapes=[pltpu.VMEM((4,) + (2,) * count + block, BF16)]
        + [s for _ in range(4) for s in halving_slots(count, block, BF16)]
        + [pltpu.SemaphoreType.DMA((4 * count,)), pltpu.SemaphoreType.DMA((4 * count,))],
        compiler_params=pltpu.CompilerParams(
            collective_id=2, has_side_effects=True, vmem_limit_bytes=VMEM_BYTES
        ),
        cost_estimate=pl.CostEstimate(
            flops=2 * groups * gg.shape[1] * channels * model, bytes_accessed=200 * 2**20, transcendentals=0
        ),
        name="out_weight_grad",
    )(gg, dy)


class Stream:
    def __init__(self, *parts):
        self.steps = []
        for part in parts:
            if self.steps and part:
                last, first = self.steps.pop(), part[0]
                self.steps.append(lambda last=last, first=first: (last(), first()))
                part = part[1:]
            self.steps.extend(part)

    def advance(self):
        if self.steps:
            self.steps.pop(0)()


def advance_all(streams):
    for s in streams:
        s.advance()


def drain(streams):
    while any(s.steps for s in streams):
        advance_all(streams)


class Ports:
    def __init__(self, send, recv):
        self.send, self.recv, self.used = send, recv, 0

    def make(self, src, dst, axis, to):
        at = self.used
        self.used += 1

        def describe():
            return pltpu.make_async_remote_copy(
                src_ref=src(), dst_ref=dst(), send_sem=self.send.at[at], recv_sem=self.recv.at[at],
                device_id={axis: to()}, device_id_type=pl.DeviceIdType.MESH,
            )

        return describe


def linked(copies, work):
    steps = []
    for i in range(len(copies) + 1):
        def step(i=i):
            if i:
                copies[i - 1]().wait()
                work(i - 1)
            if i < len(copies):
                copies[i]().start()

        steps.append(step)
    return steps


def halving(ports, axis, buf, slots, order):
    count = len(order)

    def fixed(i, give):
        mine = bits_of(axis, count)
        out = {b: mine[b] for b in order[: i + 1]}
        if give:
            out[order[i]] = 1 - out[order[i]]
        return out

    copies = [
        ports.make(
            lambda i=i: buf().at[place(count, fixed(i, True))], lambda i=i: slots[i],
            axis, lambda i=i: partner(axis, order[i]),
        )
        for i in range(count)
    ]

    def work(i):
        for at in itertools.product(*(range(d) for d in slots[i].shape[:-2])):
            add_block(buf(), place(count, fixed(i, False)), slots[i], at)

    return linked(copies, work)


def spreading(ports, axis, buf, order):
    count = len(order)

    def at(i):
        mine = bits_of(axis, count)
        return buf().at[place(count, {b: mine[b] for b in order[i:]})]

    copies = [
        ports.make(lambda i=i: at(i), lambda i=i: at(i), axis, lambda i=i: partner(axis, order[i]))
        for i in range(count)
    ]
    return linked(copies, lambda i: None)


def exchanging(ports, axis, buf, slots, order):
    copies = [
        ports.make(buf, lambda i=i: slots[i], axis, lambda i=i: partner(axis, order[i])) for i in range(len(order))
    ]

    def work(i):
        ref = buf()
        ref[...] = (ref[...].astype(F32) + slots[i][...].astype(F32)).astype(ref.dtype)

    return linked(copies, work)


def back_kernel(
    count, group_bits,
    dg_hbm, a_hbm, s_hbm, act_hbm, dsc_hbm, inn_hbm, x_hbm, bc_hbm, step_hbm, prev_hbm,
    zw_hbm, xw_hbm, bcw_hbm, dtw_hbm, o_hbm, gain_ref, convw_ref, dtb_ref, alog_ref, skip_ref, hot_ref,
    z_out, x_out, o_out, bc_out, small_out, own_out,
    dg, a, s, act, dsc, inn, x, bc, step, prev, zw, xw, bdw, obuf,
    lam, dconv, dyc_s, vt_s, q_s, v_s, w_s, da_s, etot_s, draw_s, head_s, vec_s, pre_s, dbs,
    rows_s, far_s, zg, bcbuf, small, *refs,
):
    zx_slots = [refs[i * count : (i + 1) * count] for i in range(4)]
    refs = refs[4 * count :]
    bc_slots, refs = (refs[:count], refs[count : 2 * count]), refs[2 * count :]
    bc_head, refs = (refs[:group_bits], refs[group_bits : 2 * group_bits]), refs[2 * group_bits :]
    small_slots, refs = refs[:count], refs[count:]
    small_head, refs = refs[:group_bits], refs[group_bits:]
    o_slots, refs = refs[:group_bits], refs[group_bits:]
    load_sem, store_sem, rsend, rrecv, send, recv = refs
    length, channels = a.shape
    model = x.shape[1]
    n = lam.shape[0]
    heads = hot_ref.shape[0]
    groups = rows_s.shape[0] * rows_s.shape[1]
    rows_num = length // groups
    subs = rows_num // SPAN
    wide = bcbuf.shape[-1]
    me = lax.axis_index("head")
    my_hi, my_lo = me // 2, me % 2

    pairs = [
        (dg_hbm, dg), (a_hbm, a), (s_hbm, s), (x_hbm, x), (o_hbm, obuf), (step_hbm, step), (bc_hbm, bc),
        (prev_hbm, prev), (act_hbm, act), (dsc_hbm, dsc), (inn_hbm, inn), (zw_hbm, zw), (xw_hbm, xw),
        (bcw_hbm, bdw.at[:, pl.ds(0, 2 * n)]), (dtw_hbm, bdw.at[:, pl.ds(2 * n, 128)]),
    ]
    loads = [pltpu.make_async_copy(src, dst, load_sem.at[i]) for i, (src, dst) in enumerate(pairs)]
    for load in loads:
        load.start()
    for load in loads[:3]:
        load.wait()

    def gates(i, carry):
        per = rows_num // 64
        rows = pl.ds(pl.multiple_of(i * 64, 64), 64)
        d = dg[i // per, pl.ds(pl.multiple_of((i % per) * 64, 64), 64), :].astype(F32)
        a[rows, :] = (d * a[rows, :].astype(F32)).astype(BF16)
        s[rows, :] = (d * s[rows, :].astype(F32)).astype(BF16)
        return carry

    lax.fori_loop(0, length // 64, gates, 0)
    meet(
        [("batch", partner("batch", b)) for b in range(count)]
        + [("head", partner("head", b)) for b in range(group_bits)]
    )

    ports = Ports(send, recv)
    up = list(range(1, count))
    orders = [up, up[::-1]]
    cols_num = channels // 2

    def own_at():
        return place(count, dict(enumerate(bits_of("batch", count))))

    def keep(src, dst, sem):
        def step():
            copy = pltpu.make_async_copy(src(), dst(), store_sem.at[sem])
            copy.start()
            copy.wait()

        return [step]

    def grads(i):
        part = (slice(None),) * (count + 1) + (pl.ds((i % 2) * cols_num, cols_num),)
        view = lambda: (z_out, x_out)[i // 2].at[part]
        buf = lambda: (zg, zw)[i // 2].at[part]
        order = orders[i % 2]
        return Stream(
            halving(ports, "batch", buf, zx_slots[i], [0] + order),
            keep(lambda: buf().at[own_at()], lambda: view().at[own_at()], i),
            spreading(ports, "batch", view, order[::-1] + [0]),
        )

    streams = [grads(i) for i in range(4)]
    def state_part(i):
        part = (slice(None),) * (count + 1) + ((pl.ds(n, n + 128), pl.ds(0, n))[i],)
        buf = lambda: bcbuf.at[part]
        view = lambda: bc_out.at[part]
        return Stream(
            halving(ports, "batch", buf, bc_slots[i], [0] + orders[i]),
            exchanging(
                ports, "head", lambda: bcbuf.at[own_at() + (slice(None), pl.ds((n, 0)[i], n))], bc_head[i],
                range(group_bits),
            ),
            keep(lambda: buf().at[own_at()], lambda: view().at[own_at()], (4, 6)[i]),
            spreading(ports, "batch", view, orders[i][::-1] + [0]),
        )

    state = [state_part(i) for i in range(2)]
    vectors = Stream(
        exchanging(ports, "batch", lambda: small, small_slots, range(count)),
        exchanging(ports, "head", lambda: small.at[pl.ds(0, 8)], small_head, range(group_bits)),
    )
    half = model // 2

    def head_own():
        return place(group_bits, dict(enumerate(bits_of("head", group_bits))))

    def o_view(i):
        return o_out.at[(slice(None),) * (count + 1) + (pl.ds(i * half, half),)]

    outs = Stream(
        halving(ports, "head", lambda: obuf, o_slots, list(range(group_bits))),
        keep(lambda: obuf.at[head_own()], lambda: o_out.at[own_at()], 5),
    )
    spread = [Stream(spreading(ports, "batch", lambda i=i: o_view(i), orders[i] + [0])) for i in range(2)]

    for load in loads[3:5]:
        load.wait()
    outs.advance()
    tile = 256
    block_rows = model >> count

    def put(target, t, value):
        for k in range(tile // min(block_rows, tile)):
            p = (t * tile) // block_rows + k
            index = tuple((p // 2**b) % 2 for b in reversed(range(count)))
            if block_rows <= tile:
                target[index] = value[k * block_rows : (k + 1) * block_rows].astype(BF16)
            else:
                first = pl.multiple_of((t * tile) % block_rows, tile)
                target[index + (pl.ds(first, tile), slice(None))] = value.astype(BF16)

    def take(source, t):
        if block_rows >= tile:
            p = (t * tile) // block_rows
            index = tuple((p // 2**b) % 2 for b in reversed(range(count)))
            return source[index + (pl.ds(pl.multiple_of((t * tile) % block_rows, tile), tile), slice(None))]
        found = []
        for k in range(tile // block_rows):
            p = (t * tile) // block_rows + k
            found.append(source[tuple((p // 2**b) % 2 for b in reversed(range(count)))])
        return jnp.concatenate(found, axis=0)

    def weight_grad(right, target):
        def one(t, carry):
            put(target, t, mm_tn(x[:, pl.ds(pl.multiple_of(t * tile, tile), tile)], right[...]))
            return carry

        lax.fori_loop(0, model // tile, one, 0)

    weight_grad(a, zg)
    advance_all(streams[:2])
    for load in loads[5:]:
        load.wait()

    lam[...] = jnp.zeros_like(lam)
    dconv[rows_num:, :] = jnp.zeros((8, channels), F32)
    vec_s[...] = jnp.zeros_like(vec_s)
    head_s[...] = jnp.zeros_like(head_s)
    draw_s[...] = jnp.zeros_like(draw_s)
    pre_s[...] = jnp.zeros_like(pre_s)
    rate = -jnp.exp(alog_ref[...])
    lower = lower_mask((SPAN, SPAN))
    lower_f = lower.astype(F32)
    lower_b = lower.astype(BF16)
    row_at = lax.broadcasted_iota(jnp.int32, (SPAN, SPAN), 0)
    col_at = lax.broadcasted_iota(jnp.int32, (SPAN, SPAN), 1)
    upper = row_at <= col_at
    strict = row_at < col_at
    strict_f = strict.astype(F32)
    left = lax.broadcasted_iota(jnp.int32, (SPAN, 128), 1) < 64

    def block(at, local):
        rows = pl.ds(pl.multiple_of(at * SPAN, SPAN), SPAN)
        local_rows = pl.ds(pl.multiple_of(local * SPAN, SPAN), SPAN)
        raw = step[rows, :] + dtb_ref[...]
        delta = softplus(raw)
        cum = mm_exact(lower_f, delta * rate)
        cum_t = cum.T
        delta_t = delta.T
        slope_t = sigmoid(raw).T
        rate_t = jnp.broadcast_to(rate, (SPAN, 128)).T
        b_val = bc[rows, :n]
        c_val = bc[rows, n:]
        inner = jnp.where(upper, mm_nt(b_val, c_val), 0.0)
        before = prev[at]
        lam_b = lam[...].astype(BF16)
        across = mm(c_val, before)
        dtail = mm(b_val, lam_b)
        d_inner_prod = jnp.zeros((SPAN, SPAN), F32)
        for pair in range(channels // 128):
            cols = slice(pair * 128, pair * 128 + 128)
            c0, c1, ce = pair_columns(cum, pair, left)
            _, _, de = pair_columns(delta, pair, left)
            tot = ce[SPAN - 1 : SPAN, :]
            e_cum = jnp.exp(ce)
            e_tail = jnp.exp(tot - ce)
            dy_b = s[rows, cols]
            dy = dy_b.astype(F32)
            act_p = act[rows, cols].astype(F32)
            vec_s[5:6, cols] += jnp.sum(dy * act_p, axis=0, keepdims=True)
            u = act_p * de
            u_b = u.astype(BF16)
            zero = jnp.zeros_like(dy_b)
            dy01 = jnp.concatenate([jnp.where(left, dy_b, zero), jnp.where(left, zero, dy_b)], axis=0)
            m0 = jnp.exp(jnp.minimum(cum_t[2 * pair : 2 * pair + 1, :] - c0, 0.0))
            m1 = jnp.exp(jnp.minimum(cum_t[2 * pair + 1 : 2 * pair + 2, :] - c1, 0.0))
            p0 = m0 * inner
            p1 = m1 * inner
            du = mm(jnp.concatenate([p0.astype(BF16), p1.astype(BF16)], axis=1), dy01)
            dp = mm_nt(u_b, dy01)
            dp0, dp1 = dp[:, :SPAN], dp[:, SPAN:]
            d_inner_prod += dp0 * m0 + dp1 * m1
            e01 = jnp.concatenate([(dp0 * p0).astype(BF16), (dp1 * p1).astype(BF16)], axis=0)
            spans = mm(e01, lower_b)
            da_s[2 * pair : 2 * pair + 1, :] = jnp.sum(
                jnp.where(strict, spans[:SPAN], 0.0), axis=0, keepdims=True
            )
            da_s[2 * pair + 1 : 2 * pair + 2, :] = jnp.sum(
                jnp.where(strict, spans[SPAN:], 0.0), axis=0, keepdims=True
            )
            dut = dtail[:, cols] * e_tail
            du = du + dut
            dye = dy * e_cum
            dyc_s[:, cols] = dye.astype(BF16)
            vt_s[:, cols] = (u * e_tail).astype(BF16)
            q_s[:, cols] = (dye * across[:, cols]).astype(BF16)
            v_s[:, cols] = (u * dut).astype(BF16)
            w_s[:, cols] = (act_p * du).astype(BF16)
            etot_s[:, cols] = jnp.exp(tot)
            d_act = de * du + skip_ref[:, cols] * dy
            dconv[local_rows, cols] = d_act * dsc[rows, cols].astype(F32)
        hot = hot_ref[...]
        over = jnp.sum(lam[...] * before.astype(F32), axis=0, keepdims=True) * etot_s[...]
        over = jnp.broadcast_to(over, (128, channels))
        over = lax.dot_general(
            hot.astype(F32), over, (((1,), (1,)), ((), ())), preferred_element_type=F32, precision=HIGHEST
        )
        da = (
            da_s[...]
            + mm_exact(mm_nt(hot, q_s[...]), lower_f)
            + mm_exact(mm_nt(hot, v_s[...]), strict_f)
            + over
        )
        d_step = mm_nt(hot, w_s[...]) + rate_t[:heads] * da
        d_raw = d_step * slope_t[:heads]
        head_s[0:heads, :] += d_raw
        head_s[heads : 2 * heads, :] += delta_t[:heads] * da * rate_t[:heads]
        draw_s[0:heads, :] = d_raw
        dg_b = jnp.where(upper, d_inner_prod, 0.0)
        dbs[rows, :n] = (mm(dg_b.astype(BF16), c_val) + mm_nt(vt_s[...], lam_b)).astype(BF16)
        dbs[rows, n : 2 * n] = (mm(dg_b.T.astype(BF16), b_val) + mm_nt(dyc_s[...], before)).astype(BF16)
        dbs[rows, 2 * n :] = draw_s[...].T.astype(BF16)
        lam[...] = lam[...] * etot_s[...] + mm(bc[rows, n:].astype(F32).T.astype(BF16), dyc_s[...])

    def near_copy(hi, h):
        at = 2 * hi + h
        return pltpu.make_async_remote_copy(
            src_ref=rows_s.at[hi, 1 - my_lo, h], dst_ref=dg.at[at], send_sem=rsend.at[at], recv_sem=rrecv.at[at],
            device_id={"head": partner("head", 0)}, device_id_type=pl.DeviceIdType.MESH,
        )

    def far_copy(h):
        return pltpu.make_async_remote_copy(
            src_ref=rows_s.at[1 - my_hi, my_lo, h], dst_ref=far_s.at[h], send_sem=rsend.at[4 + h],
            recv_sem=rrecv.at[4 + h],
            device_id={"head": partner("head", 1)}, device_id_type=pl.DeviceIdType.MESH,
        )

    def join_near(hi, h):
        near_copy(hi, h).wait()
        add_block(rows_s, (hi, my_lo, h), dg.at[2 * hi + h], ())

        @pl.when(my_hi != hi)
        def _():
            far_copy(h).start()

    def quarter_step(i, carry):
        q = groups - 1 - i
        rows = pl.ds(pl.multiple_of(q * rows_num, rows_num), rows_num)

        def one(j, inner_carry):
            block(q * subs + subs - 1 - j, subs - 1 - j)
            return inner_carry

        lax.fori_loop(0, subs, one, 0)
        for k in range(groups):
            @pl.when(i == k)
            def _():
                for action in plan[k, "a"]:
                    action()

        for c in range(0, channels, 128):
            cols = slice(c, c + 128)
            inner_v = inn[rows, cols].astype(F32)
            d_in = jnp.zeros((rows_num, 128), F32)
            for k in range(4):
                shifted = dconv[3 - k : 3 - k + rows_num, cols]
                d_in += convw_ref[k : k + 1, cols] * shifted
                vec_s[k : k + 1, cols] += jnp.sum(inner_v * shifted, axis=0, keepdims=True)
            vec_s[4:5, cols] += jnp.sum(dconv[0:rows_num, cols], axis=0, keepdims=True)
            inn[rows, cols] = d_in.astype(BF16)
        dconv[rows_num:, :] = dconv[0:8, :]

        def columns(t, inner_carry):
            cols = pl.ds(pl.multiple_of(t * tile, tile), tile)
            value = mm_nt(a[rows, :], take(zw, t)) + mm_nt(inn[rows, :], xw[cols, :]) + mm_nt(dbs[rows, :], bdw[cols, :])
            pre_s[:, cols] += jnp.sum(value * x[rows, cols].astype(F32), axis=0, keepdims=True)
            per = model // 2 // tile
            rows_s[q // 2, q % 2, t // per, :, pl.ds(pl.multiple_of((t % per) * tile, tile), tile)] = value.astype(BF16)
            return inner_carry

        lax.fori_loop(0, model // tile, columns, 0)

        @pl.when(q % 2 != my_lo)
        def _():
            for h in range(2):
                near_copy(q // 2, h).start()

        for k in range(groups):
            @pl.when(i == k)
            def _():
                for action in plan[k, "b"]:
                    action()

        return carry

    plan = {(k, half_at): [] for k in range(groups) for half_at in "ab"}

    def book(stream, slots):
        for slot in slots:
            if stream.steps:
                plan[slot].append(stream.steps.pop(0))

    for st in streams[:2]:
        book(st, [(0, "a"), (1, "a"), (2, "a"), (2, "b"), (3, "b")])
    book(outs, [(1, "a"), (2, "b")])
    for st in spread:
        book(st, [(2, "b"), (3, "a"), (3, "b")])
    plan[3, "b"] += [lambda h=h: join_near(1, h) for h in range(2)]
    lax.fori_loop(0, groups, quarter_step, 0)

    weight_grad(inn, zw)
    advance_all(streams[2:])

    def state_grad(t, carry):
        put(bcbuf, t, mm_tn(x[:, pl.ds(pl.multiple_of(t * tile, tile), tile)], dbs[...]))
        return carry

    lax.fori_loop(0, model // tile, state_grad, 0)
    advance_all(state)
    small[...] = jnp.zeros_like(small)
    for j in range(groups):
        small[j : j + 1, :] = gain_ref[j]
    for j in range(model // channels):
        small[groups + j : groups + j + 1, :] = pre_s[:, j * channels : (j + 1) * channels]
    small[8:14, :] = vec_s[0:6, :]
    totals = lax.dot_general(
        jnp.ones((8, SPAN), F32), head_s[...], (((1,), (1,)), ((), ())),
        preferred_element_type=F32, precision=HIGHEST,
    )
    small[14:15, 0:128] = totals[0:1]
    vectors.advance()
    advance_all(streams)
    advance_all(spread)
    join_near(0, 0)
    advance_all(state + [vectors])
    join_near(0, 1)
    drain(streams + spread + state + [vectors, outs])
    for h in range(2):
        far_copy(h).wait()
    small_out[...] = small[...]

    def total(r, carry):
        rs = pl.ds(pl.multiple_of(r * 32, 32), 32)
        for h in range(2):
            own_out[rs, h * half : (h + 1) * half] = rows_s[my_hi, my_lo, h, rs, :].astype(F32) + far_s[h, rs, :].astype(F32)
        return carry

    lax.fori_loop(0, rows_num // 32, total, 0)


def back_call(dg, res, x, bc, step, prev, zw, xw, bcw, dtw, out_part, gain_grad, convw, dtb, alog, skip, hot, groups, batches):
    length, model = x.shape
    channels = xw.shape[1]
    n = bc.shape[1] // 2
    heads = hot.shape[0]
    rows_num = length // groups
    count = log2(batches)
    group_bits = log2(groups)
    lead = (2,) * count
    part = channels // batches
    rows = model // batches
    wide = 2 * n + 128
    block = (rows, channels // 2)
    hbm = pl.BlockSpec(memory_space=pl.ANY)
    vmem = pl.BlockSpec(memory_space=pltpu.VMEM)
    dma = pltpu.SemaphoreType.DMA
    copies = 4 * 2 * count + 2 * (2 * count + group_bits) + (count + group_bits) + group_bits + 2 * count
    tall = lambda w, t: pltpu.VMEM((length, w), t)
    span = pltpu.VMEM((SPAN, channels), BF16)
    z, xg, o, bcg, small, own = pl.pallas_call(
        functools.partial(back_kernel, count, group_bits),
        in_specs=[hbm] * 15 + [vmem] * 6,
        out_specs=[hbm] * 4 + [vmem] * 2,
        out_shape=[
            jax.ShapeDtypeStruct(lead + (rows, channels), BF16),
            jax.ShapeDtypeStruct(lead + (rows, channels), BF16),
            jax.ShapeDtypeStruct(lead + (part, model), BF16),
            jax.ShapeDtypeStruct(lead + (rows, wide), BF16),
            jax.ShapeDtypeStruct((16, channels), F32),
            jax.ShapeDtypeStruct((rows_num, model), F32),
        ],
        scratch_shapes=[pltpu.VMEM((groups, rows_num, model // 2), BF16)] + [tall(channels, BF16)] * 5
        + [
            tall(model, BF16), tall(2 * n, BF16), tall(128, F32), pltpu.VMEM(prev.shape, BF16),
            pltpu.VMEM(lead + (rows, channels), BF16), pltpu.VMEM(xw.shape, BF16), pltpu.VMEM((model, wide), BF16),
            pltpu.VMEM((2,) * group_bits + (part, model), BF16),
            pltpu.VMEM((n, channels), F32), pltpu.VMEM((rows_num + 8, channels), F32),
        ]
        + [span] * 5
        + [
            pltpu.VMEM((heads, SPAN), F32), pltpu.VMEM((1, channels), F32), pltpu.VMEM((128, SPAN), F32),
            pltpu.VMEM((128, SPAN), F32), pltpu.VMEM((8, channels), F32), pltpu.VMEM((1, model), F32),
            tall(wide, BF16),
            pltpu.VMEM((2, 2, 2, rows_num, model // 2), BF16), pltpu.VMEM((2, rows_num, model // 2), BF16),
            pltpu.VMEM(lead + (rows, channels), BF16), pltpu.VMEM(lead + (rows, wide), BF16),
            pltpu.VMEM((16, channels), F32),
        ]
        + [s for _ in range(4) for s in halving_slots(count, block, BF16)]
        + halving_slots(count, (rows, n + 128), BF16)
        + halving_slots(count, (rows, n), BF16)
        + [pltpu.VMEM((rows, n), BF16)] * (2 * group_bits)
        + [pltpu.VMEM((16, channels), F32)] * count
        + [pltpu.VMEM((8, channels), F32)] * group_bits
        + halving_slots(group_bits, (part, model), BF16)
        + [dma((15,)), dma((7,)), dma((6,)), dma((6,)), dma((copies,)), dma((copies,))],
        compiler_params=pltpu.CompilerParams(
            collective_id=3, has_side_effects=True, vmem_limit_bytes=BACK_VMEM_BYTES
        ),
        cost_estimate=pl.CostEstimate(
            flops=10 * length * model * channels, bytes_accessed=300 * 2**20, transcendentals=0
        ),
        name="back",
    )(
        dg, *res, x, bc, step, prev, zw.reshape(lead + (rows, channels)), xw, bcw, dtw, out_part.reshape((2,) * group_bits + (part, model)),
        gain_grad, convw, dtb, alog, skip, hot,
    )
    return (
        z.reshape(model, channels), xg.reshape(model, channels), o.reshape(channels, model),
        bcg.reshape(model, wide), small, own,
    )


def finish_kernel(
    z_ref, x_ref, o_ref, bc_ref, small_ref, own_ref, tok_ref, cot_ref, pre_ref,
    zf_ref, xf_ref, of_ref, bcf_ref, dt_ref, grad_ref, convw_ref, convb_ref, skip_ref, gain_ref, pre_out, dtb_ref, alog_ref,
):
    zf_ref[...] = z_ref[...].astype(F32)
    xf_ref[...] = x_ref[...].astype(F32)
    of_ref[...] = o_ref[...].astype(F32)
    width = bcf_ref.shape[1]
    heads = dt_ref.shape[1]
    bcf_ref[...] = bc_ref[:, :width].astype(F32)
    dt_ref[...] = bc_ref[:, width : width + 128].astype(F32)[:, :heads]
    tok = tok_ref[...].astype(F32)
    recip = lax.rsqrt(jnp.mean(tok * tok, axis=-1, keepdims=True) + EPSILON)
    scaled = pre_ref[...] * own_ref[...]
    mean = jnp.mean(tok * scaled, axis=-1, keepdims=True)
    passed = sum(cot_ref[w].astype(F32) for w in range(4))
    grad_ref[...] = (passed + recip * scaled - tok * recip**3 * mean).astype(BF16)

    @pl.when(pl.program_id(0) == 0)
    def _():
        groups = small_ref.shape[0] // 4
        channels = small_ref.shape[1]
        convw_ref[...] = small_ref[8:12, :]
        convb_ref[...] = small_ref[12:13, :]
        skip_ref[...] = small_ref[13:14, :]
        me = lax.axis_index("head")
        gain = small_ref[0:1, :]
        for j in range(1, groups):
            gain = jnp.where(me == j, small_ref[j : j + 1, :], gain)
        gain_ref[...] = gain
        for j in range(pre_out.shape[1] // channels):
            cols = slice(j * channels, (j + 1) * channels)
            pre_out[:, cols] = small_ref[groups + j : groups + j + 1, :] / pre_ref[:, cols]
        dtb_ref[...] = small_ref[14:15, 0:heads]
        alog_ref[...] = small_ref[14:15, heads : 2 * heads]


def finish_call(z, x, o, bc, small, own, tok, cot, pre_gain, heads):
    model, channels = z.shape
    rows_num = tok.shape[0]
    steps = 8
    wide = bc.shape[1]
    rows = lambda r, w: pl.BlockSpec((r // steps, w), lambda i: (i, 0))
    fixed = lambda shape: pl.BlockSpec(shape, lambda i: (0, 0))
    shapes = [
        ((model, channels), F32), ((model, channels), F32), ((channels, model), F32), ((model, wide - 128), F32),
        ((model, heads), F32), ((rows_num, model), BF16),
    ]
    flat = [(4, channels), (1, channels), (1, channels), (1, channels), (1, model), (1, heads), (1, heads)]
    return pl.pallas_call(
        finish_kernel,
        grid=(steps,),
        in_specs=[
            rows(model, channels), rows(model, channels), rows(channels, model), rows(model, wide),
            fixed(small.shape), rows(rows_num, model), rows(rows_num, model),
            pl.BlockSpec((4, rows_num // steps, model), lambda i: (0, i, 0)), fixed((1, model)),
        ],
        out_specs=[rows(*shape) for shape, _ in shapes] + [fixed(shape) for shape in flat],
        out_shape=[jax.ShapeDtypeStruct(shape, t) for shape, t in shapes]
        + [jax.ShapeDtypeStruct(shape, F32) for shape in flat],
        compiler_params=pltpu.CompilerParams(vmem_limit_bytes=VMEM_BYTES),
        cost_estimate=pl.CostEstimate(flops=0, bytes_accessed=46 * 2**20, transcendentals=0),
        name="finish",
    )(z, x, o, bc, small, own, tok, cot, pre_gain[None])


def per_device(
    tokens, z_weight, x_weight, bc_weight, dt_weight, conv_weight, conv_bias, dt_bias,
    a_log, skip, norm_gain, pre_gain, out_weight, cotangent,
):
    groups = lax.axis_size("head")
    batches = lax.axis_size("batch")
    _, own_len, model = tokens.shape
    tokens = tokens[0]
    cot = cotangent[:, 0]
    channels = z_weight.shape[1]
    heads = dt_weight.shape[1]
    pad = lambda v: jnp.pad(v, ((0, 0), (0, 128 - heads)))
    dtb = pad(dt_bias[None])
    alog = pad(a_log[None])
    skip_r = skip[None]
    dtw = pad(dt_weight)
    x, res, bc, step, prev, gated, w_all, gain_all = front_call(
        tokens, pre_gain, z_weight, x_weight, bc_weight, dtw, out_weight, norm_gain,
        conv_weight, conv_bias[None], dtb, alog, skip_r, groups, batches,
    )
    outputs, d_gated, dy, gg, gain_grad = middle_call(gated, w_all, gain_all, tokens, cot)
    d_gated = lax.all_to_all(d_gated, "head", 0, 0, tiled=True)
    out_part = outgrad_scatter_call(gg, dy, batches)
    hot = (jnp.arange(channels)[None] // (channels // heads) == jnp.arange(heads)[:, None]).astype(BF16)
    z_grad, x_grad, out_grad, bcdt_grad, small, d_own = back_call(
        d_gated, res, x, bc, step, prev, z_weight, x_weight, bc_weight, dtw, out_part, gain_grad,
        conv_weight, dtb, alog, skip_r, hot, groups, batches,
    )
    z_grad, x_grad, out_grad, bc_grad, dt_grad, tokens_grad, convw, convb, skip_g, gain_g, pre_g, dtb_g, alog_g = finish_call(
        z_grad, x_grad, out_grad, bcdt_grad, small, d_own, tokens, cot, pre_gain, heads
    )
    flat = lambda v: v.reshape(-1)
    return (
        outputs[:, None], tokens_grad[None], z_grad, x_grad, bc_grad, dt_grad, convw, flat(convb), flat(dtb_g),
        flat(alog_g), flat(skip_g), flat(gain_g), flat(pre_g), out_grad,
    )


def solution(mesh):
    head_cols = P(None, "head")
    rows4 = P(None, "batch", "head", None)
    return jax.shard_map(
        per_device,
        mesh=mesh,
        in_specs=(
            P("batch", "head", None), head_cols, head_cols, P(), head_cols, head_cols, P("head"),
            P("head"), P("head"), P("head"), P("head"), P(), P("head", None), rows4,
        ),
        out_specs=(
            rows4, P("batch", "head", None), head_cols, head_cols, P(), head_cols, head_cols,
            P("head"), P("head"), P("head"), P("head"), P("head"), P(), P("head", None),
        ),
        check_vma=False,
    )
```

```python
import functools
import itertools

import jax
import jax.numpy as jnp
from jax import lax
from jax.experimental import pallas as pl
from jax.experimental.pallas import tpu as pltpu
from jax.sharding import PartitionSpec as P

SPAN = 128
ROWS = 256
EPSILON = 1e-05
BF16 = jnp.bfloat16
F32 = jnp.float32
HIGHEST = lax.Precision.HIGHEST
VMEM_BYTES = 60 * 1024 * 1024
BACK_VMEM_BYTES = 63 * 1024 * 1024


def mm(a, b):
    return lax.dot_general(a, b, (((1,), (0,)), ((), ())), preferred_element_type=F32)


def mm_nt(a, b):
    return lax.dot_general(a, b, (((1,), (1,)), ((), ())), preferred_element_type=F32)


def mm_tn(a, b):
    return lax.dot_general(a, b, (((0,), (0,)), ((), ())), preferred_element_type=F32)


def mm_exact(a, b):
    return lax.dot_general(
        a, b, (((1,), (0,)), ((), ())), preferred_element_type=F32, precision=HIGHEST
    )


def lower_mask(shape):
    return lax.broadcasted_iota(jnp.int32, shape, 0) >= lax.broadcasted_iota(jnp.int32, shape, 1)


def softplus(v):
    return jnp.maximum(v, 0.0) + jnp.log1p(jnp.exp(-jnp.abs(v)))


def sigmoid(v):
    return 1.0 / (1.0 + jnp.exp(-v))


def pair_columns(values, pair, left):
    shape = (SPAN, 128)
    one = jnp.broadcast_to(values[:, 2 * pair : 2 * pair + 1], shape)
    two = jnp.broadcast_to(values[:, 2 * pair + 1 : 2 * pair + 2], shape)
    return one, two, jnp.where(left, one, two)


def segments(channels):
    ends = [channels * 2**w // 8 for w in range(4)]
    return list(zip([0] + ends[:-1], ends))


def partner(axis, bit):
    me = lax.axis_index(axis)
    return me + (1 - 2 * ((me // 2**bit) % 2)) * 2**bit


def bits_of(axis, count):
    me = lax.axis_index(axis)
    return [(me // 2**b) % 2 for b in range(count)]


def log2(value):
    return value.bit_length() - 1


def place(bits, fixed):
    bits = range(bits) if isinstance(bits, int) else sorted(bits)
    return tuple(fixed[b] if b in fixed else slice(None) for b in reversed(bits))


class Links:
    def __init__(self, send, recv):
        self.send, self.recv, self.used = send, recv, 0

    def copy(self, src, dst, axis, to):
        at = self.used
        self.used += 1
        return pltpu.make_async_remote_copy(
            src_ref=src, dst_ref=dst, send_sem=self.send.at[at], recv_sem=self.recv.at[at],
            device_id={axis: to}, device_id_type=pl.DeviceIdType.MESH,
        )


def meet(peers):
    barrier = pltpu.get_barrier_semaphore()
    for axis, to in peers:
        pl.semaphore_signal(barrier, inc=1, device_id={axis: to}, device_id_type=pl.DeviceIdType.MESH)
    pl.semaphore_wait(barrier, len(peers))


def add_block(buf, index, slot, at):
    rows = slot.shape[-2]
    step = min(rows, 32)
    index = index + (slice(None),) * (len(buf.shape) - len(index))
    free = [i for i, v in enumerate(index[:-2]) if isinstance(v, slice)]
    full = list(index[:-2])
    for i, v in zip(free, at):
        full[i] = v
    full = tuple(full)

    def piece(r, carry):
        rs = pl.ds(pl.multiple_of(r * step, step), step)
        total = buf[full + (rs, index[-1])].astype(F32) + slot[tuple(at) + (rs, slice(None))].astype(F32)
        buf[full + (rs, index[-1])] = total.astype(buf.dtype)
        return carry

    lax.fori_loop(0, rows // step, piece, 0)


def halving_slots(count, block, dtype):
    return [pltpu.VMEM((2,) * (count - 1 - i) + tuple(block), dtype) for i in range(count)]


class Stream:
    def __init__(self, *parts):
        self.steps = []
        for part in parts:
            if self.steps and part:
                last, first = self.steps.pop(), part[0]
                self.steps.append(lambda last=last, first=first: (last(), first()))
                part = part[1:]
            self.steps.extend(part)

    def advance(self):
        if self.steps:
            self.steps.pop(0)()


def advance_all(streams):
    for s in streams:
        s.advance()


def drain(streams):
    while any(s.steps for s in streams):
        advance_all(streams)


class Ports:
    def __init__(self, send, recv):
        self.send, self.recv, self.used = send, recv, 0

    def make(self, src, dst, axis, to):
        at = self.used
        self.used += 1

        def describe():
            return pltpu.make_async_remote_copy(
                src_ref=src(), dst_ref=dst(), send_sem=self.send.at[at], recv_sem=self.recv.at[at],
                device_id={axis: to()}, device_id_type=pl.DeviceIdType.MESH,
            )

        return describe


def linked(copies, work):
    steps = []
    for i in range(len(copies) + 1):
        def step(i=i):
            if i:
                copies[i - 1]().wait()
                work(i - 1)
            if i < len(copies):
                copies[i]().start()

        steps.append(step)
    return steps


def halving(ports, axis, buf, slots, order):
    count = len(order)

    def fixed(i, give):
        mine = bits_of(axis, max(order) + 1)
        out = {b: mine[b] for b in order[: i + 1]}
        if give:
            out[order[i]] = 1 - out[order[i]]
        return out

    copies = [
        ports.make(
            lambda i=i: buf().at[place(order, fixed(i, True))], lambda i=i: slots[i],
            axis, lambda i=i: partner(axis, order[i]),
        )
        for i in range(count)
    ]

    def work(i):
        for at in itertools.product(*(range(d) for d in slots[i].shape[:-2])):
            add_block(buf(), place(order, fixed(i, False)), slots[i], at)

    return linked(copies, work)


def spreading(ports, axis, buf, order):
    count = len(order)

    def at(i):
        mine = bits_of(axis, count)
        return buf().at[place(count, {b: mine[b] for b in order[i:]})]

    copies = [
        ports.make(lambda i=i: at(i), lambda i=i: at(i), axis, lambda i=i: partner(axis, order[i]))
        for i in range(count)
    ]
    return linked(copies, lambda i: None)


def exchanging(ports, axis, buf, slots, order):
    copies = [
        ports.make(buf, lambda i=i: slots[i], axis, lambda i=i: partner(axis, order[i])) for i in range(len(order))
    ]

    def work(i):
        ref = buf()
        ref[...] = (ref[...].astype(F32) + slots[i][...].astype(F32)).astype(ref.dtype)

    return linked(copies, work)


PIECE_POLLS = (
    ("a", 0), ("a", 1), ("a", 2), ("c", 0), ("d", 1), ("e", 2), ("e", 0), (0, 1), (1, 2), (1, 0), (2, 1), (3, 2),
)


def front_kernel(
    count, tok_ref, pre_ref, zw_hbm, xw_hbm, bcw_hbm, dtw_hbm, w_hbm, gain_hbm,
    convw_ref, convb_ref, dtb_ref, alog_ref, skip_ref,
    x_out, a_out, s_out, act_out, dsc_out, inn_out, bc_out, step_out, prev_out, gated_out, all_ref, gains_ref,
    xs, zw, xw, bcw, dtw, wv, gate_s, a_s, s_s, act_s, dsc_s, inn_s, inner_s, bc_s, bcb_s, step_s, prev_s, gated_s, state, tails,
    load_sem, local_sem, store_sem, away_sem, here_sem, send, recv, send2, recv2,
):
    rows_num, channels = gated_s.shape[1:]
    groups = gated_s.shape[0]
    length = groups * rows_num
    n = state.shape[0]
    model = tok_ref.shape[1]
    chunks = 2
    chunk = rows_num // chunks
    me = lax.axis_index("head")
    hi, lo = me // 2, me % 2
    near = partner("head", 0)
    far = partner("head", 1)
    others = [near, far, near + far - me]
    links = Links(send, recv)

    loads = [
        pltpu.make_async_copy(src, dst, load_sem.at[i])
        for i, (src, dst) in enumerate(((zw_hbm, zw), (xw_hbm, xw), (bcw_hbm, bcw), (dtw_hbm, dtw), (w_hbm, wv)))
    ]
    for load in loads:
        load.start()
    tok = tok_ref[...].astype(F32)
    recip = lax.rsqrt(jnp.mean(tok * tok, axis=-1, keepdims=True) + EPSILON)
    xs[hi, lo] = (tok * recip * pre_ref[...]).astype(BF16)
    meet([("head", z) for z in others] + [("batch", partner("batch", b)) for b in range(count)])

    own_rows = xs.at[hi, lo]
    to_far = []
    for c in range(chunks):
        part = xs.at[hi, lo, pl.ds(c * chunk, chunk)]
        to_far.append(links.copy(part, part, "head", far))
        to_far[-1].start()
    to_near = links.copy(own_rows, own_rows, "head", near)
    to_near.start()
    half = w_hbm.shape[-1] // 2

    def pieces(z, cols, order):
        def own_piece(ref):
            return ref.at[place(count, dict(enumerate(bits_of("batch", count)))) + (slice(None), cols)]

        first = ports.make(
            lambda: own_piece(w_hbm), lambda: own_piece(all_ref.at[lax.axis_index("head")]), "head", z
        )

        def at(i):
            bits = bits_of("batch", count)
            return all_ref.at[(z(),) + place(count, {b: bits[b] for b in order[i:]}) + (slice(None), cols)]

        rest = [
            ports.make(lambda i=i: at(i), lambda i=i: at(i), "batch", lambda i=i: partner("batch", order[i]))
            for i in range(count)
        ]
        return Stream(linked([first] + rest, lambda i: None))

    up = list(range(1, count))
    ports = Ports(send2, recv2)
    near_at = lambda: partner("head", 0)
    far_at = lambda: partner("head", 1)
    streams = []
    for z in (near_at, far_at, lambda: near_at() + far_at() - lax.axis_index("head")):
        streams.append(pieces(z, pl.ds(0, half), up + [0]))
        streams.append(pieces(z, pl.ds(half, half), up[::-1] + [0]))
    plan = [[] for _ in range(groups)]
    early = {spot: [] for spot in "abcde"}
    for spot, group in PIECE_POLLS:
        for st in streams[2 * group : 2 * group + 2]:
            if st.steps:
                (early[spot] if spot in early else plan[spot]).append(st.steps.pop(0))

    def poll(spot):
        for action in early[spot]:
            action()

    poll("a")
    keep = [pltpu.make_async_copy(gain_hbm, gains_ref.at[me], local_sem.at[1])]
    keep[0].start()
    inner_s[0:8, :] = jnp.zeros((8, channels), F32)
    state[...] = jnp.zeros_like(state)
    for load in loads:
        load.wait()
    keep.append(pltpu.make_async_copy(wv, all_ref.at[me], local_sem.at[0]))
    keep[-1].start()

    def project(at_hi, at_lo):
        first = pl.multiple_of((2 * at_hi + at_lo) * rows_num, rows_num)
        rows = pl.ds(first, rows_num)
        inner_rows = pl.ds(pl.multiple_of(first + 8, 8), rows_num)
        tile = 256

        def columns(t, carry):
            cols = pl.ds(pl.multiple_of(t * tile, tile), tile)
            x = xs[at_hi, at_lo]
            gate_s[rows, cols] = mm(x, zw[:, cols])
            inner_s[inner_rows, cols] = mm(x, xw[:, cols])
            return carry

        lax.fori_loop(0, channels // tile, columns, 0)
        x = xs[at_hi, at_lo]
        bc_s[rows, :] = mm(x, bcw[...])
        step_s[rows, :] = mm(x, dtw[...])

    project(hi, lo)
    to_near.wait()
    project(hi, 1 - lo)
    poll("b")
    onward = []
    for c in range(chunks):
        to_far[c].wait()
        part = xs.at[1 - hi, lo, pl.ds(c * chunk, chunk)]
        onward.append(links.copy(part, part, "head", near))
        onward[-1].start()

    poll("c")
    gain_sends = [links.copy(gain_hbm, gains_ref.at[me], "head", z) for z in others]
    for item in gain_sends:
        item.start()

    project(1 - hi, lo)
    poll("d")
    for item in onward:
        item.wait()
    project(1 - hi, 1 - lo)
    poll("e")

    rate = -jnp.exp(alog_ref[...])
    lower = lower_mask((SPAN, SPAN))
    lower_f = lower.astype(F32)
    left = lax.broadcasted_iota(jnp.int32, (SPAN, 128), 1) < 64

    def block(at, carry):
        first = pl.multiple_of(at * SPAN, SPAN)
        rows = pl.ds(first, SPAN)
        delta = softplus(step_s[rows, :] + dtb_ref[...])
        cum = mm_exact(lower_f, delta * rate)
        cum_t = cum.T
        bcb_s[rows, :] = bc_s[rows, :].astype(BF16)
        b_val = bcb_s[rows, :n]
        c_val = bcb_s[rows, n:]
        inner = jnp.where(lower, mm_nt(c_val, b_val), 0.0)
        before = state[...].astype(BF16)
        prev_s[at] = before
        across = mm(c_val, before)
        quarter = at // (rows_num // SPAN)
        sub = pl.ds(pl.multiple_of((at % (rows_num // SPAN)) * SPAN, SPAN), SPAN)
        for pair in range(channels // 128):
            cols = slice(pair * 128, pair * 128 + 128)
            c0, c1, ce = pair_columns(cum, pair, left)
            _, _, de = pair_columns(delta, pair, left)
            tot = ce[SPAN - 1 : SPAN, :]
            window = inner_s[pl.ds(first, SPAN + 8), cols]
            conv_p = convb_ref[:, cols] + sum(
                convw_ref[k : k + 1, cols] * window[5 + k : 5 + k + SPAN] for k in range(4)
            )
            inn_s[rows, cols] = window[8:].astype(BF16)
            sc = sigmoid(conv_p)
            act = conv_p * sc
            act_s[rows, cols] = act.astype(BF16)
            dsc_s[rows, cols] = (sc + act * (1.0 - sc)).astype(BF16)
            u = act * de
            tails[:, cols] = (u * jnp.exp(tot - ce)).astype(BF16)
            u0 = jnp.where(left, u, 0.0).astype(BF16)
            u1 = jnp.where(left, 0.0, u).astype(BF16)
            p0 = (jnp.exp(jnp.minimum(c0 - cum_t[2 * pair : 2 * pair + 1, :], 0.0)) * inner).astype(BF16)
            p1 = (jnp.exp(jnp.minimum(c1 - cum_t[2 * pair + 1 : 2 * pair + 2, :], 0.0)) * inner).astype(BF16)
            within = mm(jnp.concatenate([p0, p1], axis=1), jnp.concatenate([u0, u1], axis=0))
            y = within + across[:, cols] * jnp.exp(ce) + skip_ref[:, cols] * act
            gate = gate_s[rows, cols]
            sg = sigmoid(gate)
            sl = gate * sg
            s_s[rows, cols] = sl.astype(BF16)
            a_s[rows, cols] = (y * (sg + sl * (1.0 - sg))).astype(BF16)
            gated_s[quarter, sub, cols] = (y * sl).astype(BF16)
            state[:, cols] = state[:, cols] * jnp.exp(tot)
        state[...] += mm(bc_s[rows, :n].T.astype(BF16), tails[...])
        return carry

    def leave(q):
        return pltpu.make_async_remote_copy(
            src_ref=gated_s.at[q], dst_ref=gated_out.at[me], send_sem=away_sem.at[q], recv_sem=here_sem.at[me],
            device_id={"head": q}, device_id_type=pl.DeviceIdType.MESH,
        )

    def arrive(q):
        return pltpu.make_async_remote_copy(
            src_ref=gated_s.at[q], dst_ref=gated_out.at[q], send_sem=away_sem.at[q], recv_sem=here_sem.at[q],
            device_id={"head": q}, device_id_type=pl.DeviceIdType.MESH,
        )

    subs = rows_num // SPAN

    def stores(q):
        rows = pl.ds(pl.multiple_of(q * rows_num, rows_num), rows_num)
        pairs = (
            (xs.at[q // 2, q % 2], x_out.at[rows]),
            (a_s.at[rows], a_out.at[rows]),
            (s_s.at[rows], s_out.at[rows]),
            (act_s.at[rows], act_out.at[rows]),
            (dsc_s.at[rows], dsc_out.at[rows]),
            (inn_s.at[rows], inn_out.at[rows]),
            (bcb_s.at[rows], bc_out.at[rows]),
            (step_s.at[rows], step_out.at[rows]),
            (prev_s.at[pl.ds(q * subs, subs)], prev_out.at[pl.ds(q * subs, subs)]),
        )
        return [pltpu.make_async_copy(src, dst, store_sem.at[i, q]) for i, (src, dst) in enumerate(pairs)]

    def quarter_step(q, carry):
        lax.fori_loop(q * subs, (q + 1) * subs, block, 0)

        @pl.when(q != me)
        def _():
            leave(q).start()

        for item in stores(q):
            item.start()
        for k in range(groups):
            @pl.when(q == k)
            def _():
                for action in plan[k]:
                    action()
        return carry

    lax.fori_loop(0, groups, quarter_step, 0)
    stay = pltpu.make_async_copy(gated_s.at[me], gated_out.at[me], local_sem.at[2])
    stay.start()
    drain(streams)
    for item in gain_sends:
        item.wait()
    for item in keep:
        item.wait()
    stay.wait()

    def finish(q, carry):
        @pl.when(q != me)
        def _():
            leave(q).wait_send()
            arrive(q).wait_recv()

        for item in stores(q):
            item.wait()
        return carry

    lax.fori_loop(0, groups, finish, 0)


def front_call(tokens, pre_gain, zw, xw, bcw, dtw, out_weight, norm_gain, convw, convb, dtb, alog, skip, groups, batches):
    rows_num, model = tokens.shape
    channels = zw.shape[1]
    n = bcw.shape[1] // 2
    length = rows_num * groups
    count = log2(batches)
    part = channels // batches
    copies = 5 + groups - 1
    piece_copies = 2 * (groups - 1) * (1 + count)
    hbm = pl.BlockSpec(memory_space=pl.ANY)
    vmem = pl.BlockSpec(memory_space=pltpu.VMEM)
    wide = jax.ShapeDtypeStruct((length, channels), BF16)
    outs = [
        jax.ShapeDtypeStruct((length, model), BF16), wide, wide, wide, wide, wide,
        jax.ShapeDtypeStruct((length, 2 * n), BF16),
        jax.ShapeDtypeStruct((length, dtw.shape[1]), F32),
        jax.ShapeDtypeStruct((length // SPAN, n, channels), BF16),
        jax.ShapeDtypeStruct((groups, rows_num, channels), BF16),
        jax.ShapeDtypeStruct((groups,) + (2,) * count + (part, model), BF16),
        jax.ShapeDtypeStruct((groups, 8, channels), F32),
    ]
    dma = pltpu.SemaphoreType.DMA
    result = pl.pallas_call(
        functools.partial(front_kernel, count),
        in_specs=[vmem, vmem] + [hbm] * 6 + [vmem] * 5,
        out_specs=[hbm] * len(outs),
        out_shape=outs,
        scratch_shapes=[
            pltpu.VMEM((2, 2, rows_num, model), BF16),
            pltpu.VMEM(zw.shape, BF16), pltpu.VMEM(xw.shape, BF16),
            pltpu.VMEM(bcw.shape, BF16), pltpu.VMEM(dtw.shape, BF16),
            pltpu.VMEM((2,) * count + (part, model), BF16),
            pltpu.VMEM((length, channels), F32),
            pltpu.VMEM((length, channels), BF16), pltpu.VMEM((length, channels), BF16),
            pltpu.VMEM((length, channels), BF16), pltpu.VMEM((length, channels), BF16),
            pltpu.VMEM((length, channels), BF16), pltpu.VMEM((length + 8, channels), F32),
            pltpu.VMEM((length, 2 * n), F32), pltpu.VMEM((length, 2 * n), BF16),
            pltpu.VMEM((length, dtw.shape[1]), F32), pltpu.VMEM((length // SPAN, n, channels), BF16),
            pltpu.VMEM((groups, rows_num, channels), BF16),
            pltpu.VMEM((n, channels), F32), pltpu.VMEM((SPAN, channels), BF16),
            dma((5,)), dma((3,)), dma((9, groups)), dma((groups,)), dma((groups,)), dma((copies,)), dma((copies,)),
            dma((piece_copies,)), dma((piece_copies,)),
        ],
        compiler_params=pltpu.CompilerParams(
            collective_id=1, has_side_effects=True, vmem_limit_bytes=VMEM_BYTES
        ),
        cost_estimate=pl.CostEstimate(
            flops=4 * length * model * channels, bytes_accessed=400 * 2**20, transcendentals=0
        ),
        name="front",
    )(
        tokens, pre_gain[None], zw, xw, bcw, dtw, out_weight.reshape((2,) * count + (part, model)),
        jnp.broadcast_to(norm_gain[None], (8, channels)), convw, convb, dtb, alog, skip,
    )
    x, a, s, act, dsc, inn, bc, step, prev, gated, w_all, gains = result
    return x, (a, s, act, dsc, inn), bc, step, prev, gated, w_all.reshape(groups, channels, model), gains


def middle_kernel(
    count, g_hbm, w_hbm, cot_hbm, gain_ref, tok_ref,
    out_hbm, dg_out, part_ref, ggrad_ref,
    g_s, w_s, cot_s, gg_s, out_s, dg_s, give_s, kept_s, *refs,
):
    slots = [refs[i * (count - 1) : (i + 1) * (count - 1)] for i in range(4)]
    load_sem, store_sem, away_sem, here_sem, send, recv = refs[4 * (count - 1) :]
    groups, rows_num, channels = g_s.shape
    model = tok_ref.shape[1]
    part, half = kept_s.shape[-2:]
    pairs_num = groups // 2
    segs = segments(channels)
    tile = 512
    tiles = model // tile
    me = lax.axis_index("head")

    def w_load(t):
        cols = pl.ds(pl.multiple_of(t * tile, tile), tile)
        return pltpu.make_async_copy(w_hbm.at[:, :, cols], w_s.at[:, :, cols], load_sem.at[2 + t])

    loads = [
        pltpu.make_async_copy(g_hbm, g_s, load_sem.at[0]), pltpu.make_async_copy(cot_hbm, cot_s, load_sem.at[1]),
    ]
    loads[0].start()
    w_load(0).start()
    loads[1].start()
    for t in range(1, tiles):
        w_load(t).start()
    loads[0].wait()
    sums = [jnp.zeros((rows_num, 1), F32) for _ in segs]
    for j in range(groups):
        for w, (lo, hi) in enumerate(segs):
            g = g_s[j, :, lo:hi].astype(F32)
            gg_s[j, :, lo:hi] = (g * gain_ref[j, 0:1, lo:hi]).astype(BF16)
            sums[w] += jnp.sum(g * g, axis=1, keepdims=True)
    recips = []
    total = jnp.zeros((rows_num, 1), F32)
    for w, (lo, hi) in enumerate(segs):
        total = total + sums[w]
        recips.append(lax.rsqrt(total / (hi * groups) + EPSILON))
    meet(
        [("batch", partner("batch", b)) for b in range(count)]
        + [("head", z) for z in (partner("head", 0), partner("head", 1), partner("head", 0) + partner("head", 1) - me)]
    )
    loads[1].wait()

    def out_store(t):
        cols = pl.ds(pl.multiple_of(t * tile, tile), tile)
        return pltpu.make_async_copy(out_s.at[:, :, cols], out_hbm.at[:, :, cols], store_sem.at[t])

    def forward(t, dots):
        cols = pl.ds(pl.multiple_of(t * tile, tile), tile)
        w_load(t).wait()
        acc = jnp.zeros((rows_num, tile), F32)
        tok = tok_ref[:, cols].astype(F32)
        new = []
        for w, (lo, hi) in enumerate(segs):
            acc += mm(
                jnp.concatenate([gg_s[j, :, lo:hi] for j in range(groups)], axis=1),
                jnp.concatenate([w_s[j, lo:hi, cols] for j in range(groups)], axis=0),
            )
            out_s[w, :, cols] = (tok + recips[w] * acc).astype(BF16)
            new.append(dots[w] + jnp.sum(cot_s[w, :, cols].astype(F32) * acc, axis=1, keepdims=True))
        out_store(t).start()
        combined = jnp.zeros((rows_num, tile), F32)
        for w in reversed(range(4)):
            combined += recips[w] * cot_s[w, :, cols].astype(F32)
            cot_s[w, :, cols] = combined.astype(BF16)
        return tuple(new)

    dots = lax.fori_loop(0, tiles, forward, tuple(jnp.zeros((rows_num, 1), F32) for _ in segs))
    dy_s = cot_s
    scales = [None] * 4
    scale = jnp.zeros((rows_num, 1), F32)
    for w in reversed(range(4)):
        scale = scale + recips[w] ** 3 * dots[w] / (segs[w][1] * groups)
        scales[w] = scale

    def leave(j):
        return pltpu.make_async_remote_copy(
            src_ref=dg_s.at[j], dst_ref=dg_out.at[me], send_sem=away_sem.at[j], recv_sem=here_sem.at[me],
            device_id={"head": j}, device_id_type=pl.DeviceIdType.MESH,
        )

    def arrive(j):
        return pltpu.make_async_remote_copy(
            src_ref=dg_s.at[j], dst_ref=dg_out.at[j], send_sem=away_sem.at[j], recv_sem=here_sem.at[j],
            device_id={"head": j}, device_id_type=pl.DeviceIdType.MESH,
        )

    def back(k, carry):
        j = (me + 1 + k) % groups
        for w, (lo, hi) in enumerate(segs):
            dn = mm_nt(dy_s[w], w_s[j, lo:hi, :])
            g = g_s[j, :, lo:hi].astype(F32)
            ggrad_ref[j, :, lo:hi] = jnp.sum(g * dn, axis=0, keepdims=True)
            dg_s[j, :, lo:hi] = (gain_ref[j, 0:1, lo:hi] * dn - g * scales[w]).astype(BF16)

        @pl.when(j != me)
        def _():
            leave(j).start()

        return carry

    ports = Ports(send, recv)
    up = list(range(1, count))
    core = bits_of("batch", 1)[0]

    def upper_index(p):
        return tuple((p >> b) & 1 for b in reversed(range(1, count)))

    def terms(s, bit, use):
        g0, c0 = (s // 2) * pairs_num, (s % 2) * half
        if part % 128 == 0:
            for q in range(2 ** (count - 1)):
                at = pl.ds(pl.multiple_of((2 * q + bit) * part, part), part)
                left = jnp.concatenate([gg_s[g0 + j, :, at] for j in range(pairs_num)], axis=1)
                owners = [[w for w, (lo, hi) in enumerate(segs) if lo <= (2 * q + c) * part < hi][0] for c in range(2)]
                w = owners[0] + (owners[1] - owners[0]) * bit
                term = mm_tn(left, dy_s[w, :, c0 : c0 + half])
                for j in range(pairs_num):
                    use(upper_index(2 * q), j, term[j * part : (j + 1) * part])
            return
        for j in range(pairs_num):
            for w, (lo, hi) in enumerate(segs):
                term = mm_tn(gg_s[g0 + j, :, lo:hi], dy_s[w, :, c0 : c0 + half])
                for p in range(lo // part, hi // part):
                    @pl.when(bit == p % 2)
                    def _():
                        use(upper_index(p), j, term[p * part - lo : (p + 1) * part - lo])

    def to_core(s):
        return pltpu.make_async_remote_copy(
            src_ref=give_s.at[s], dst_ref=kept_s.at[s], send_sem=send.at[s], recv_sem=recv.at[s],
            device_id={"batch": partner("batch", 0)}, device_id_type=pl.DeviceIdType.MESH,
        )

    def give(s):
        def use(index, j, rows):
            give_s[(s,) + index + (j,)] = rows.astype(BF16)

        terms(s, 1 - core, use)
        to_core(s).start()

    def keep(s):
        to_core(s).wait()

        def use(index, j, rows):
            at = (s,) + index + (j,)
            kept_s[at] = (kept_s[at].astype(F32) + rows).astype(BF16)

        terms(s, core, use)

    ports.used = 4
    streams = [
        Stream(halving(ports, "batch", lambda s=s: kept_s.at[s], slots[s], up if s % 2 == 0 else up[::-1]))
        for s in range(4)
    ]
    for s in range(2):
        give(s)
    for s in range(2):
        keep(s)
        streams[s].advance()
    lax.fori_loop(0, groups, back, 0)
    stay = pltpu.make_async_copy(dg_s.at[me], dg_out.at[me], load_sem.at[0])
    stay.start()
    for s in range(2, 4):
        give(s)
    advance_all(streams[:2])
    for s in range(2, 4):
        keep(s)
        streams[s].advance()
    drain(streams)
    mine = bits_of("batch", count)
    own = place(up, {b: mine[b] for b in up})
    for s in range(4):
        for j in range(pairs_num):
            part_ref[(s // 2) * pairs_num + j, :, (s % 2) * half : (s % 2 + 1) * half] = kept_s[(s,) + own + (j,)]
    stay.wait()

    def finish(j, carry):
        @pl.when(j != me)
        def _():
            leave(j).wait_send()
            arrive(j).wait_recv()

        return carry

    lax.fori_loop(0, groups, finish, 0)

    def stored(t, carry):
        out_store(t).wait()
        return carry

    lax.fori_loop(0, tiles, stored, 0)


def middle_call(g, w_all, gain, tok, cot, batches):
    groups, rows_num, channels = g.shape
    model = tok.shape[1]
    count = log2(batches)
    part = channels // batches
    half = model // 2
    block = (groups // 2, part, half)
    hbm = pl.BlockSpec(memory_space=pl.ANY)
    vmem = pl.BlockSpec(memory_space=pltpu.VMEM)
    dma = pltpu.SemaphoreType.DMA
    wide = pltpu.VMEM((groups, rows_num, channels), BF16)
    tall = pltpu.VMEM((4, rows_num, model), BF16)
    halves = pltpu.VMEM((4,) + (2,) * (count - 1) + block, BF16)
    return pl.pallas_call(
        functools.partial(middle_kernel, count),
        in_specs=[hbm] * 3 + [vmem] * 2,
        out_specs=[hbm, hbm, vmem, vmem],
        out_shape=[
            jax.ShapeDtypeStruct((4, rows_num, model), BF16),
            jax.ShapeDtypeStruct(g.shape, BF16),
            jax.ShapeDtypeStruct((groups, part, model), BF16),
            jax.ShapeDtypeStruct((groups, 1, channels), F32),
        ],
        scratch_shapes=[
            wide, pltpu.VMEM((groups, channels, model), BF16), tall, wide, tall, wide, halves, halves,
        ]
        + [s for _ in range(4) for s in halving_slots(count - 1, block, BF16)]
        + [
            dma((2 + model // 512,)), dma((model // 512,)), dma((groups,)), dma((groups,)),
            dma((4 * count,)), dma((4 * count,)),
        ],
        compiler_params=pltpu.CompilerParams(
            collective_id=2, has_side_effects=True, vmem_limit_bytes=VMEM_BYTES
        ),
        cost_estimate=pl.CostEstimate(
            flops=6 * groups * rows_num * channels * model, bytes_accessed=200 * 2**20, transcendentals=0
        ),
        name="nested_norm",
    )(g, w_all, cot, gain, tok)


def back_kernel(
    count, group_bits,
    dg_hbm, a_hbm, s_hbm, act_hbm, dsc_hbm, inn_hbm, x_hbm, bc_hbm, step_hbm, prev_hbm,
    zw_hbm, xw_hbm, bcw_hbm, dtw_hbm, o_hbm, gain_ref, convw_ref, dtb_ref, alog_ref, skip_ref, hot_ref,
    z_out, x_out, o_out, bc_out, small_out, own_out,
    dg, a, s, act, dsc, inn, x, bc, step, prev, zw, xw, bdw, obuf,
    lam, dconv, dyc_s, vt_s, q_s, v_s, w_s, da_s, etot_s, draw_s, head_s, vec_s, pre_s, dbs,
    rows_s, far_s, zg, bcbuf, small, *refs,
):
    zx_slots = [refs[i * count : (i + 1) * count] for i in range(4)]
    refs = refs[4 * count :]
    bc_slots, refs = (refs[:count], refs[count : 2 * count]), refs[2 * count :]
    bc_head, refs = (refs[:group_bits], refs[group_bits : 2 * group_bits]), refs[2 * group_bits :]
    small_slots, refs = refs[:count], refs[count:]
    small_head, refs = refs[:group_bits], refs[group_bits:]
    o_slots, refs = refs[:group_bits], refs[group_bits:]
    load_sem, store_sem, rsend, rrecv, send, recv = refs
    length, channels = a.shape
    model = x.shape[1]
    n = lam.shape[0]
    heads = hot_ref.shape[0]
    groups = rows_s.shape[0] * rows_s.shape[1]
    rows_num = length // groups
    subs = rows_num // SPAN
    wide = bcbuf.shape[-1]
    me = lax.axis_index("head")
    my_hi, my_lo = me // 2, me % 2

    pairs = [
        (dg_hbm, dg), (a_hbm, a), (s_hbm, s), (x_hbm, x), (o_hbm, obuf), (step_hbm, step), (bc_hbm, bc),
        (prev_hbm, prev), (act_hbm, act), (dsc_hbm, dsc), (inn_hbm, inn), (zw_hbm, zw), (xw_hbm, xw),
        (bcw_hbm, bdw.at[:, pl.ds(0, 2 * n)]), (dtw_hbm, bdw.at[:, pl.ds(2 * n, 128)]),
    ]
    loads = [pltpu.make_async_copy(src, dst, load_sem.at[i]) for i, (src, dst) in enumerate(pairs)]
    for load in loads:
        load.start()
    for load in loads[:3]:
        load.wait()

    def gates(i, carry):
        per = rows_num // 64
        rows = pl.ds(pl.multiple_of(i * 64, 64), 64)
        d = dg[i // per, pl.ds(pl.multiple_of((i % per) * 64, 64), 64), :].astype(F32)
        a[rows, :] = (d * a[rows, :].astype(F32)).astype(BF16)
        s[rows, :] = (d * s[rows, :].astype(F32)).astype(BF16)
        return carry

    lax.fori_loop(0, length // 64, gates, 0)
    meet(
        [("batch", partner("batch", b)) for b in range(count)]
        + [("head", partner("head", b)) for b in range(group_bits)]
    )

    ports = Ports(send, recv)
    up = list(range(1, count))
    orders = [up, up[::-1]]
    cols_num = channels // 2

    def own_at():
        return place(count, dict(enumerate(bits_of("batch", count))))

    def keep(src, dst, sem):
        def step():
            copy = pltpu.make_async_copy(src(), dst(), store_sem.at[sem])
            copy.start()
            copy.wait()

        return [step]

    def grads(i):
        part = (slice(None),) * (count + 1) + (pl.ds((i % 2) * cols_num, cols_num),)
        view = lambda: (z_out, x_out)[i // 2].at[part]
        buf = lambda: (zg, zw)[i // 2].at[part]
        order = orders[i % 2]
        return Stream(
            halving(ports, "batch", buf, zx_slots[i], [0] + order),
            keep(lambda: buf().at[own_at()], lambda: view().at[own_at()], i),
            spreading(ports, "batch", view, order[::-1] + [0]),
        )

    streams = [grads(i) for i in range(4)]
    def state_part(i):
        part = (slice(None),) * (count + 1) + ((pl.ds(n, n + 128), pl.ds(0, n))[i],)
        buf = lambda: bcbuf.at[part]
        view = lambda: bc_out.at[part]
        return Stream(
            halving(ports, "batch", buf, bc_slots[i], [0] + orders[i]),
            exchanging(
                ports, "head", lambda: bcbuf.at[own_at() + (slice(None), pl.ds((n, 0)[i], n))], bc_head[i],
                range(group_bits),
            ),
            keep(lambda: buf().at[own_at()], lambda: view().at[own_at()], (4, 6)[i]),
            spreading(ports, "batch", view, orders[i][::-1] + [0]),
        )

    state = [state_part(i) for i in range(2)]
    vectors = Stream(
        exchanging(ports, "batch", lambda: small, small_slots, range(count)),
        exchanging(ports, "head", lambda: small.at[pl.ds(0, 8)], small_head, range(group_bits)),
    )
    half = model // 2

    def head_own():
        return place(group_bits, dict(enumerate(bits_of("head", group_bits))))

    def o_view(i):
        return o_out.at[(slice(None),) * (count + 1) + (pl.ds(i * half, half),)]

    outs = Stream(
        halving(ports, "head", lambda: obuf, o_slots, list(range(group_bits))),
        keep(lambda: obuf.at[head_own()], lambda: o_out.at[own_at()], 5),
    )
    spread = [Stream(spreading(ports, "batch", lambda i=i: o_view(i), orders[i] + [0])) for i in range(2)]

    for load in loads[3:5]:
        load.wait()
    outs.advance()
    tile = 256
    block_rows = model >> count

    def put(target, t, value):
        for k in range(tile // min(block_rows, tile)):
            p = (t * tile) // block_rows + k
            index = tuple((p // 2**b) % 2 for b in reversed(range(count)))
            if block_rows <= tile:
                target[index] = value[k * block_rows : (k + 1) * block_rows].astype(BF16)
            else:
                first = pl.multiple_of((t * tile) % block_rows, tile)
                target[index + (pl.ds(first, tile), slice(None))] = value.astype(BF16)

    def take(source, t):
        if block_rows >= tile:
            p = (t * tile) // block_rows
            index = tuple((p // 2**b) % 2 for b in reversed(range(count)))
            return source[index + (pl.ds(pl.multiple_of((t * tile) % block_rows, tile), tile), slice(None))]
        found = []
        for k in range(tile // block_rows):
            p = (t * tile) // block_rows + k
            found.append(source[tuple((p // 2**b) % 2 for b in reversed(range(count)))])
        return jnp.concatenate(found, axis=0)

    def weight_grad(right, target):
        def one(t, carry):
            put(target, t, mm_tn(x[:, pl.ds(pl.multiple_of(t * tile, tile), tile)], right[...]))
            return carry

        lax.fori_loop(0, model // tile, one, 0)

    weight_grad(a, zg)
    advance_all(streams[:2])
    for load in loads[5:]:
        load.wait()

    lam[...] = jnp.zeros_like(lam)
    dconv[rows_num:, :] = jnp.zeros((8, channels), F32)
    vec_s[...] = jnp.zeros_like(vec_s)
    head_s[...] = jnp.zeros_like(head_s)
    draw_s[...] = jnp.zeros_like(draw_s)
    pre_s[...] = jnp.zeros_like(pre_s)
    rate = -jnp.exp(alog_ref[...])
    lower = lower_mask((SPAN, SPAN))
    lower_f = lower.astype(F32)
    lower_b = lower.astype(BF16)
    row_at = lax.broadcasted_iota(jnp.int32, (SPAN, SPAN), 0)
    col_at = lax.broadcasted_iota(jnp.int32, (SPAN, SPAN), 1)
    upper = row_at <= col_at
    strict = row_at < col_at
    strict_f = strict.astype(F32)
    left = lax.broadcasted_iota(jnp.int32, (SPAN, 128), 1) < 64

    def block(at, local):
        rows = pl.ds(pl.multiple_of(at * SPAN, SPAN), SPAN)
        local_rows = pl.ds(pl.multiple_of(local * SPAN, SPAN), SPAN)
        raw = step[rows, :] + dtb_ref[...]
        delta = softplus(raw)
        cum = mm_exact(lower_f, delta * rate)
        cum_t = cum.T
        delta_t = delta.T
        slope_t = sigmoid(raw).T
        rate_t = jnp.broadcast_to(rate, (SPAN, 128)).T
        b_val = bc[rows, :n]
        c_val = bc[rows, n:]
        inner = jnp.where(upper, mm_nt(b_val, c_val), 0.0)
        before = prev[at]
        lam_b = lam[...].astype(BF16)
        across = mm(c_val, before)
        dtail = mm(b_val, lam_b)
        d_inner_prod = jnp.zeros((SPAN, SPAN), F32)
        for pair in range(channels // 128):
            cols = slice(pair * 128, pair * 128 + 128)
            c0, c1, ce = pair_columns(cum, pair, left)
            _, _, de = pair_columns(delta, pair, left)
            tot = ce[SPAN - 1 : SPAN, :]
            e_cum = jnp.exp(ce)
            e_tail = jnp.exp(tot - ce)
            dy_b = s[rows, cols]
            dy = dy_b.astype(F32)
            act_p = act[rows, cols].astype(F32)
            vec_s[5:6, cols] += jnp.sum(dy * act_p, axis=0, keepdims=True)
            u = act_p * de
            u_b = u.astype(BF16)
            zero = jnp.zeros_like(dy_b)
            dy01 = jnp.concatenate([jnp.where(left, dy_b, zero), jnp.where(left, zero, dy_b)], axis=0)
            m0 = jnp.exp(jnp.minimum(cum_t[2 * pair : 2 * pair + 1, :] - c0, 0.0))
            m1 = jnp.exp(jnp.minimum(cum_t[2 * pair + 1 : 2 * pair + 2, :] - c1, 0.0))
            p0 = m0 * inner
            p1 = m1 * inner
            du = mm(jnp.concatenate([p0.astype(BF16), p1.astype(BF16)], axis=1), dy01)
            dp = mm_nt(u_b, dy01)
            dp0, dp1 = dp[:, :SPAN], dp[:, SPAN:]
            d_inner_prod += dp0 * m0 + dp1 * m1
            e01 = jnp.concatenate([(dp0 * p0).astype(BF16), (dp1 * p1).astype(BF16)], axis=0)
            spans = mm(e01, lower_b)
            da_s[2 * pair : 2 * pair + 1, :] = jnp.sum(
                jnp.where(strict, spans[:SPAN], 0.0), axis=0, keepdims=True
            )
            da_s[2 * pair + 1 : 2 * pair + 2, :] = jnp.sum(
                jnp.where(strict, spans[SPAN:], 0.0), axis=0, keepdims=True
            )
            dut = dtail[:, cols] * e_tail
            du = du + dut
            dye = dy * e_cum
            dyc_s[:, cols] = dye.astype(BF16)
            vt_s[:, cols] = (u * e_tail).astype(BF16)
            q_s[:, cols] = (dye * across[:, cols]).astype(BF16)
            v_s[:, cols] = (u * dut).astype(BF16)
            w_s[:, cols] = (act_p * du).astype(BF16)
            etot_s[:, cols] = jnp.exp(tot)
            d_act = de * du + skip_ref[:, cols] * dy
            dconv[local_rows, cols] = d_act * dsc[rows, cols].astype(F32)
        hot = hot_ref[...]
        over = jnp.sum(lam[...] * before.astype(F32), axis=0, keepdims=True) * etot_s[...]
        over = jnp.broadcast_to(over, (128, channels))
        over = lax.dot_general(
            hot.astype(F32), over, (((1,), (1,)), ((), ())), preferred_element_type=F32, precision=HIGHEST
        )
        da = (
            da_s[...]
            + mm_exact(mm_nt(hot, q_s[...]), lower_f)
            + mm_exact(mm_nt(hot, v_s[...]), strict_f)
            + over
        )
        d_step = mm_nt(hot, w_s[...]) + rate_t[:heads] * da
        d_raw = d_step * slope_t[:heads]
        head_s[0:heads, :] += d_raw
        head_s[heads : 2 * heads, :] += delta_t[:heads] * da * rate_t[:heads]
        draw_s[0:heads, :] = d_raw
        dg_b = jnp.where(upper, d_inner_prod, 0.0)
        dbs[rows, :n] = (mm(dg_b.astype(BF16), c_val) + mm_nt(vt_s[...], lam_b)).astype(BF16)
        dbs[rows, n : 2 * n] = (mm(dg_b.T.astype(BF16), b_val) + mm_nt(dyc_s[...], before)).astype(BF16)
        dbs[rows, 2 * n :] = draw_s[...].T.astype(BF16)
        lam[...] = lam[...] * etot_s[...] + mm(bc[rows, n:].astype(F32).T.astype(BF16), dyc_s[...])

    def near_copy(hi, h):
        at = 2 * hi + h
        return pltpu.make_async_remote_copy(
            src_ref=rows_s.at[hi, 1 - my_lo, h], dst_ref=dg.at[at], send_sem=rsend.at[at], recv_sem=rrecv.at[at],
            device_id={"head": partner("head", 0)}, device_id_type=pl.DeviceIdType.MESH,
        )

    def far_copy(h):
        return pltpu.make_async_remote_copy(
            src_ref=rows_s.at[1 - my_hi, my_lo, h], dst_ref=far_s.at[h], send_sem=rsend.at[4 + h],
            recv_sem=rrecv.at[4 + h],
            device_id={"head": partner("head", 1)}, device_id_type=pl.DeviceIdType.MESH,
        )

    def join_near(hi, h):
        near_copy(hi, h).wait()
        add_block(rows_s, (hi, my_lo, h), dg.at[2 * hi + h], ())

        @pl.when(my_hi != hi)
        def _():
            far_copy(h).start()

    def quarter_step(i, carry):
        q = groups - 1 - i
        rows = pl.ds(pl.multiple_of(q * rows_num, rows_num), rows_num)

        def one(j, inner_carry):
            block(q * subs + subs - 1 - j, subs - 1 - j)
            return inner_carry

        lax.fori_loop(0, subs, one, 0)
        for k in range(groups):
            @pl.when(i == k)
            def _():
                for action in plan[k, "a"]:
                    action()

        for c in range(0, channels, 128):
            cols = slice(c, c + 128)
            inner_v = inn[rows, cols].astype(F32)
            d_in = jnp.zeros((rows_num, 128), F32)
            for k in range(4):
                shifted = dconv[3 - k : 3 - k + rows_num, cols]
                d_in += convw_ref[k : k + 1, cols] * shifted
                vec_s[k : k + 1, cols] += jnp.sum(inner_v * shifted, axis=0, keepdims=True)
            vec_s[4:5, cols] += jnp.sum(dconv[0:rows_num, cols], axis=0, keepdims=True)
            inn[rows, cols] = d_in.astype(BF16)
        dconv[rows_num:, :] = dconv[0:8, :]

        def columns(t, inner_carry):
            cols = pl.ds(pl.multiple_of(t * tile, tile), tile)
            value = mm_nt(a[rows, :], take(zw, t)) + mm_nt(inn[rows, :], xw[cols, :]) + mm_nt(dbs[rows, :], bdw[cols, :])
            pre_s[:, cols] += jnp.sum(value * x[rows, cols].astype(F32), axis=0, keepdims=True)
            per = model // 2 // tile
            rows_s[q // 2, q % 2, t // per, :, pl.ds(pl.multiple_of((t % per) * tile, tile), tile)] = value.astype(BF16)
            return inner_carry

        lax.fori_loop(0, model // tile, columns, 0)

        @pl.when(q % 2 != my_lo)
        def _():
            for h in range(2):
                near_copy(q // 2, h).start()

        for k in range(groups):
            @pl.when(i == k)
            def _():
                for action in plan[k, "b"]:
                    action()

        return carry

    plan = {(k, half_at): [] for k in range(groups) for half_at in "ab"}

    def book(stream, slots):
        for slot in slots:
            if stream.steps:
                plan[slot].append(stream.steps.pop(0))

    for st in streams[:2]:
        book(st, [(0, "a"), (1, "a"), (2, "a"), (2, "b"), (3, "b")])
    book(outs, [(1, "a"), (2, "b")])
    for st in spread:
        book(st, [(2, "b"), (3, "a"), (3, "b")])
    plan[3, "b"] += [lambda h=h: join_near(1, h) for h in range(2)]
    lax.fori_loop(0, groups, quarter_step, 0)

    weight_grad(inn, zw)
    advance_all(streams[2:])

    def state_grad(t, carry):
        put(bcbuf, t, mm_tn(x[:, pl.ds(pl.multiple_of(t * tile, tile), tile)], dbs[...]))
        return carry

    lax.fori_loop(0, model // tile, state_grad, 0)
    advance_all(state)
    small[...] = jnp.zeros_like(small)
    for j in range(groups):
        small[j : j + 1, :] = gain_ref[j]
    for j in range(model // channels):
        small[groups + j : groups + j + 1, :] = pre_s[:, j * channels : (j + 1) * channels]
    small[8:14, :] = vec_s[0:6, :]
    totals = lax.dot_general(
        jnp.ones((8, SPAN), F32), head_s[...], (((1,), (1,)), ((), ())),
        preferred_element_type=F32, precision=HIGHEST,
    )
    small[14:15, 0:128] = totals[0:1]
    vectors.advance()
    advance_all(streams)
    advance_all(spread)
    join_near(0, 0)
    advance_all(state + [vectors])
    join_near(0, 1)
    drain(streams + spread + state + [vectors, outs])
    for h in range(2):
        far_copy(h).wait()
    small_out[...] = small[...]

    def total(r, carry):
        rs = pl.ds(pl.multiple_of(r * 32, 32), 32)
        for h in range(2):
            own_out[rs, h * half : (h + 1) * half] = rows_s[my_hi, my_lo, h, rs, :].astype(F32) + far_s[h, rs, :].astype(F32)
        return carry

    lax.fori_loop(0, rows_num // 32, total, 0)


def back_call(dg, res, x, bc, step, prev, zw, xw, bcw, dtw, out_part, gain_grad, convw, dtb, alog, skip, hot, groups, batches):
    length, model = x.shape
    channels = xw.shape[1]
    n = bc.shape[1] // 2
    heads = hot.shape[0]
    rows_num = length // groups
    count = log2(batches)
    group_bits = log2(groups)
    lead = (2,) * count
    part = channels // batches
    rows = model // batches
    wide = 2 * n + 128
    block = (rows, channels // 2)
    hbm = pl.BlockSpec(memory_space=pl.ANY)
    vmem = pl.BlockSpec(memory_space=pltpu.VMEM)
    dma = pltpu.SemaphoreType.DMA
    copies = 4 * 2 * count + 2 * (2 * count + group_bits) + (count + group_bits) + group_bits + 2 * count
    tall = lambda w, t: pltpu.VMEM((length, w), t)
    span = pltpu.VMEM((SPAN, channels), BF16)
    z, xg, o, bcg, small, own = pl.pallas_call(
        functools.partial(back_kernel, count, group_bits),
        in_specs=[hbm] * 15 + [vmem] * 6,
        out_specs=[hbm] * 4 + [vmem] * 2,
        out_shape=[
            jax.ShapeDtypeStruct(lead + (rows, channels), BF16),
            jax.ShapeDtypeStruct(lead + (rows, channels), BF16),
            jax.ShapeDtypeStruct(lead + (part, model), BF16),
            jax.ShapeDtypeStruct(lead + (rows, wide), BF16),
            jax.ShapeDtypeStruct((16, channels), F32),
            jax.ShapeDtypeStruct((rows_num, model), F32),
        ],
        scratch_shapes=[pltpu.VMEM((groups, rows_num, model // 2), BF16)] + [tall(channels, BF16)] * 5
        + [
            tall(model, BF16), tall(2 * n, BF16), tall(128, F32), pltpu.VMEM(prev.shape, BF16),
            pltpu.VMEM(lead + (rows, channels), BF16), pltpu.VMEM(xw.shape, BF16), pltpu.VMEM((model, wide), BF16),
            pltpu.VMEM((2,) * group_bits + (part, model), BF16),
            pltpu.VMEM((n, channels), F32), pltpu.VMEM((rows_num + 8, channels), F32),
        ]
        + [span] * 5
        + [
            pltpu.VMEM((heads, SPAN), F32), pltpu.VMEM((1, channels), F32), pltpu.VMEM((128, SPAN), F32),
            pltpu.VMEM((128, SPAN), F32), pltpu.VMEM((8, channels), F32), pltpu.VMEM((1, model), F32),
            tall(wide, BF16),
            pltpu.VMEM((2, 2, 2, rows_num, model // 2), BF16), pltpu.VMEM((2, rows_num, model // 2), BF16),
            pltpu.VMEM(lead + (rows, channels), BF16), pltpu.VMEM(lead + (rows, wide), BF16),
            pltpu.VMEM((16, channels), F32),
        ]
        + [s for _ in range(4) for s in halving_slots(count, block, BF16)]
        + halving_slots(count, (rows, n + 128), BF16)
        + halving_slots(count, (rows, n), BF16)
        + [pltpu.VMEM((rows, n), BF16)] * (2 * group_bits)
        + [pltpu.VMEM((16, channels), F32)] * count
        + [pltpu.VMEM((8, channels), F32)] * group_bits
        + halving_slots(group_bits, (part, model), BF16)
        + [dma((15,)), dma((7,)), dma((6,)), dma((6,)), dma((copies,)), dma((copies,))],
        compiler_params=pltpu.CompilerParams(
            collective_id=3, has_side_effects=True, vmem_limit_bytes=BACK_VMEM_BYTES
        ),
        cost_estimate=pl.CostEstimate(
            flops=10 * length * model * channels, bytes_accessed=300 * 2**20, transcendentals=0
        ),
        name="back",
    )(
        dg, *res, x, bc, step, prev, zw.reshape(lead + (rows, channels)), xw, bcw, dtw, out_part.reshape((2,) * group_bits + (part, model)),
        gain_grad, convw, dtb, alog, skip, hot,
    )
    return (
        z.reshape(model, channels), xg.reshape(model, channels), o.reshape(channels, model),
        bcg.reshape(model, wide), small, own,
    )


def finish_kernel(
    z_ref, x_ref, o_ref, bc_ref, small_ref, own_ref, tok_ref, cot_ref, pre_ref,
    zf_ref, xf_ref, of_ref, bcf_ref, dt_ref, grad_ref, convw_ref, convb_ref, skip_ref, gain_ref, pre_out, dtb_ref, alog_ref,
):
    zf_ref[...] = z_ref[...].astype(F32)
    xf_ref[...] = x_ref[...].astype(F32)
    of_ref[...] = o_ref[...].astype(F32)
    width = bcf_ref.shape[1]
    heads = dt_ref.shape[1]
    bcf_ref[...] = bc_ref[:, :width].astype(F32)
    dt_ref[...] = bc_ref[:, width : width + 128].astype(F32)[:, :heads]
    tok = tok_ref[...].astype(F32)
    recip = lax.rsqrt(jnp.mean(tok * tok, axis=-1, keepdims=True) + EPSILON)
    scaled = pre_ref[...] * own_ref[...]
    mean = jnp.mean(tok * scaled, axis=-1, keepdims=True)
    passed = sum(cot_ref[w].astype(F32) for w in range(4))
    grad_ref[...] = (passed + recip * scaled - tok * recip**3 * mean).astype(BF16)

    @pl.when(pl.program_id(0) == 0)
    def _():
        groups = small_ref.shape[0] // 4
        channels = small_ref.shape[1]
        convw_ref[...] = small_ref[8:12, :]
        convb_ref[...] = small_ref[12:13, :]
        skip_ref[...] = small_ref[13:14, :]
        me = lax.axis_index("head")
        gain = small_ref[0:1, :]
        for j in range(1, groups):
            gain = jnp.where(me == j, small_ref[j : j + 1, :], gain)
        gain_ref[...] = gain
        for j in range(pre_out.shape[1] // channels):
            cols = slice(j * channels, (j + 1) * channels)
            pre_out[:, cols] = small_ref[groups + j : groups + j + 1, :] / pre_ref[:, cols]
        dtb_ref[...] = small_ref[14:15, 0:heads]
        alog_ref[...] = small_ref[14:15, heads : 2 * heads]


def finish_call(z, x, o, bc, small, own, tok, cot, pre_gain, heads):
    model, channels = z.shape
    rows_num = tok.shape[0]
    steps = 8
    wide = bc.shape[1]
    rows = lambda r, w: pl.BlockSpec((r // steps, w), lambda i: (i, 0))
    fixed = lambda shape: pl.BlockSpec(shape, lambda i: (0, 0))
    shapes = [
        ((model, channels), F32), ((model, channels), F32), ((channels, model), F32), ((model, wide - 128), F32),
        ((model, heads), F32), ((rows_num, model), BF16),
    ]
    flat = [(4, channels), (1, channels), (1, channels), (1, channels), (1, model), (1, heads), (1, heads)]
    return pl.pallas_call(
        finish_kernel,
        grid=(steps,),
        in_specs=[
            rows(model, channels), rows(model, channels), rows(channels, model), rows(model, wide),
            fixed(small.shape), rows(rows_num, model), rows(rows_num, model),
            pl.BlockSpec((4, rows_num // steps, model), lambda i: (0, i, 0)), fixed((1, model)),
        ],
        out_specs=[rows(*shape) for shape, _ in shapes] + [fixed(shape) for shape in flat],
        out_shape=[jax.ShapeDtypeStruct(shape, t) for shape, t in shapes]
        + [jax.ShapeDtypeStruct(shape, F32) for shape in flat],
        compiler_params=pltpu.CompilerParams(vmem_limit_bytes=VMEM_BYTES),
        cost_estimate=pl.CostEstimate(flops=0, bytes_accessed=46 * 2**20, transcendentals=0),
        name="finish",
    )(z, x, o, bc, small, own, tok, cot, pre_gain[None])


def per_device(
    tokens, z_weight, x_weight, bc_weight, dt_weight, conv_weight, conv_bias, dt_bias,
    a_log, skip, norm_gain, pre_gain, out_weight, cotangent,
):
    groups = lax.axis_size("head")
    batches = lax.axis_size("batch")
    _, own_len, model = tokens.shape
    tokens = tokens[0]
    cot = cotangent[:, 0]
    channels = z_weight.shape[1]
    heads = dt_weight.shape[1]
    pad = lambda v: jnp.pad(v, ((0, 0), (0, 128 - heads)))
    dtb = pad(dt_bias[None])
    alog = pad(a_log[None])
    skip_r = skip[None]
    dtw = pad(dt_weight)
    x, res, bc, step, prev, gated, w_all, gain_all = front_call(
        tokens, pre_gain, z_weight, x_weight, bc_weight, dtw, out_weight, norm_gain,
        conv_weight, conv_bias[None], dtb, alog, skip_r, groups, batches,
    )
    outputs, d_gated, out_part, gain_grad = middle_call(gated, w_all, gain_all, tokens, cot, batches)
    hot = (jnp.arange(channels)[None] // (channels // heads) == jnp.arange(heads)[:, None]).astype(BF16)
    z_grad, x_grad, out_grad, bcdt_grad, small, d_own = back_call(
        d_gated, res, x, bc, step, prev, z_weight, x_weight, bc_weight, dtw, out_part, gain_grad,
        conv_weight, dtb, alog, skip_r, hot, groups, batches,
    )
    z_grad, x_grad, out_grad, bc_grad, dt_grad, tokens_grad, convw, convb, skip_g, gain_g, pre_g, dtb_g, alog_g = finish_call(
        z_grad, x_grad, out_grad, bcdt_grad, small, d_own, tokens, cot, pre_gain, heads
    )
    flat = lambda v: v.reshape(-1)
    return (
        outputs[:, None], tokens_grad[None], z_grad, x_grad, bc_grad, dt_grad, convw, flat(convb), flat(dtb_g),
        flat(alog_g), flat(skip_g), flat(gain_g), flat(pre_g), out_grad,
    )


def solution(mesh):
    head_cols = P(None, "head")
    rows4 = P(None, "batch", "head", None)
    return jax.shard_map(
        per_device,
        mesh=mesh,
        in_specs=(
            P("batch", "head", None), head_cols, head_cols, P(), head_cols, head_cols, P("head"),
            P("head"), P("head"), P("head"), P("head"), P(), P("head", None), rows4,
        ),
        out_specs=(
            rows4, P("batch", "head", None), head_cols, head_cols, P(), head_cols, head_cols,
            P("head"), P("head"), P("head"), P("head"), P("head"), P(), P("head", None),
        ),
        check_vma=False,
    )
```

```python
import functools
import itertools

import jax
import jax.numpy as jnp
from jax import lax
from jax.experimental import pallas as pl
from jax.experimental.pallas import tpu as pltpu
from jax.sharding import PartitionSpec as P

SPAN = 128
HEAD_PARTS = 2
ROW_CHUNKS = 4
BACK_PARTS = 1
X_STREAMS = 4
EPSILON = 1e-05
BF16 = jnp.bfloat16
F32 = jnp.float32
HIGHEST = lax.Precision.HIGHEST
VMEM_BYTES = 60 * 1024 * 1024
BACK_VMEM_BYTES = 63 * 1024 * 1024


def mm(a, b):
    return lax.dot_general(a, b, (((1,), (0,)), ((), ())), preferred_element_type=F32)


def mm_nt(a, b):
    return lax.dot_general(a, b, (((1,), (1,)), ((), ())), preferred_element_type=F32)


def mm_tn(a, b):
    return lax.dot_general(a, b, (((0,), (0,)), ((), ())), preferred_element_type=F32)


def mm_exact(a, b):
    return lax.dot_general(
        a, b, (((1,), (0,)), ((), ())), preferred_element_type=F32, precision=HIGHEST
    )


def lower_mask(shape):
    return lax.broadcasted_iota(jnp.int32, shape, 0) >= lax.broadcasted_iota(jnp.int32, shape, 1)


def softplus(v):
    return jnp.maximum(v, 0.0) + jnp.log1p(jnp.exp(-jnp.abs(v)))


def sigmoid(v):
    return 1.0 / (1.0 + jnp.exp(-v))


def pair_columns(values, pair, left):
    shape = (SPAN, 128)
    one = jnp.broadcast_to(values[:, 2 * pair : 2 * pair + 1], shape)
    two = jnp.broadcast_to(values[:, 2 * pair + 1 : 2 * pair + 2], shape)
    return one, two, jnp.where(left, one, two)


def segments(channels):
    ends = [channels * 2**w // 8 for w in range(4)]
    return list(zip([0] + ends[:-1], ends))


def partner(axis, bit):
    me = lax.axis_index(axis)
    return me + (1 - 2 * ((me // 2**bit) % 2)) * 2**bit


def bits_of(axis, count):
    me = lax.axis_index(axis)
    return [(me // 2**b) % 2 for b in range(count)]


def log2(value):
    return value.bit_length() - 1


def place(bits, fixed):
    bits = range(bits) if isinstance(bits, int) else sorted(bits)
    return tuple(fixed[b] if b in fixed else slice(None) for b in reversed(bits))


class Links:
    def __init__(self, send, recv):
        self.send, self.recv, self.used = send, recv, 0

    def copy(self, src, dst, axis, to):
        at = self.used
        self.used += 1
        return pltpu.make_async_remote_copy(
            src_ref=src, dst_ref=dst, send_sem=self.send.at[at], recv_sem=self.recv.at[at],
            device_id={axis: to}, device_id_type=pl.DeviceIdType.MESH,
        )


def meet(peers):
    barrier = pltpu.get_barrier_semaphore()
    for axis, to in peers:
        pl.semaphore_signal(barrier, inc=1, device_id={axis: to}, device_id_type=pl.DeviceIdType.MESH)
    pl.semaphore_wait(barrier, len(peers))


def add_block(buf, index, slot, at):
    rows = slot.shape[-2]
    step = min(rows, 32)
    index = index + (slice(None),) * (len(buf.shape) - len(index))
    free = [i for i, v in enumerate(index[:-2]) if isinstance(v, slice)]
    full = list(index[:-2])
    for i, v in zip(free, at):
        full[i] = v
    full = tuple(full)

    def piece(r, carry):
        rs = pl.ds(pl.multiple_of(r * step, step), step)
        total = buf[full + (rs, index[-1])].astype(F32) + slot[tuple(at) + (rs, slice(None))].astype(F32)
        buf[full + (rs, index[-1])] = total.astype(buf.dtype)
        return carry

    lax.fori_loop(0, rows // step, piece, 0)


def halving_slots(count, block, dtype):
    return [pltpu.VMEM((2,) * (count - 1 - i) + tuple(block), dtype) for i in range(count)]


class Stream:
    def __init__(self, *parts):
        self.steps = []
        for part in parts:
            if self.steps and part:
                last, first = self.steps.pop(), part[0]
                self.steps.append(lambda last=last, first=first: (last(), first()))
                part = part[1:]
            self.steps.extend(part)

    def advance(self):
        if self.steps:
            self.steps.pop(0)()


def advance_all(streams):
    for s in streams:
        s.advance()


def drain(streams):
    while any(s.steps for s in streams):
        advance_all(streams)


class Ports:
    def __init__(self, send, recv):
        self.send, self.recv, self.used = send, recv, 0

    def make(self, src, dst, axis, to):
        at = self.used
        self.used += 1

        def describe():
            return pltpu.make_async_remote_copy(
                src_ref=src(), dst_ref=dst(), send_sem=self.send.at[at], recv_sem=self.recv.at[at],
                device_id={axis: to()}, device_id_type=pl.DeviceIdType.MESH,
            )

        return describe


def linked(copies, work):
    steps = []
    for i in range(len(copies) + 1):
        def step(i=i):
            if i:
                copies[i - 1]().wait()
                work(i - 1)
            if i < len(copies):
                copies[i]().start()

        steps.append(step)
    return steps


def halving(ports, axis, buf, slots, order):
    count = len(order)

    def fixed(i, give):
        mine = bits_of(axis, max(order) + 1)
        out = {b: mine[b] for b in order[: i + 1]}
        if give:
            out[order[i]] = 1 - out[order[i]]
        return out

    copies = [
        ports.make(
            lambda i=i: buf().at[place(order, fixed(i, True))], lambda i=i: slots[i],
            axis, lambda i=i: partner(axis, order[i]),
        )
        for i in range(count)
    ]

    def work(i):
        for at in itertools.product(*(range(d) for d in slots[i].shape[:-2])):
            add_block(buf(), place(order, fixed(i, False)), slots[i], at)

    return linked(copies, work)


def spreading(ports, axis, view, order, own, sem):
    count = len(order)

    def at(i):
        mine = bits_of(axis, count)
        return view().at[place(count, {b: mine[b] for b in order[i:]})]

    copies = [
        ports.make(
            (lambda i=i: at(i)) if i else own, lambda i=i: at(i), axis, lambda i=i: partner(axis, order[i])
        )
        for i in range(count)
    ]

    def kept():
        return pltpu.make_async_copy(own(), at(0), sem)

    def work(i):
        if i == 0:
            kept().wait()

    steps = linked(copies, work)
    first = steps[0]
    steps[0] = lambda: (kept().start(), first())
    return steps


def exchanging(ports, axis, buf, slots, order):
    copies = [
        ports.make(buf, lambda i=i: slots[i], axis, lambda i=i: partner(axis, order[i])) for i in range(len(order))
    ]

    def work(i):
        ref = buf()
        ref[...] = (ref[...].astype(F32) + slots[i][...].astype(F32)).astype(ref.dtype)

    return linked(copies, work)


PIECE_POLLS = (
    ("a", 0), ("a", 1), ("a", 2), ("c", 0), ("d", 1), ("e", 2), ("e", 0), (1, 1), (3, 2), (3, 0), (5, 1), (7, 2),
)


def front_kernel(
    count, tok_ref, pre_ref, zw_hbm, xw_hbm, bcw_hbm, dtw_hbm, w_hbm, gain_hbm,
    convw_ref, convb_ref, dtb_ref, alog_ref, skip_ref,
    x_out, a_out, s_out, act_out, dsc_out, inn_out, bc_out, step_out, prev_out, gated_out, all_ref, gains_ref,
    xs, zw, xw, bcw, dtw, wv, gate_s, a_s, s_s, act_s, dsc_s, inn_s, inner_s, bc_s, bcb_s, step_s, prev_s, gated_s, state, tails,
    cum_s, cum_t_s, inner_prod_s, b_t_s, pad_s, load_sem, local_sem, store_sem, away_sem, here_sem, send, recv, send2, recv2,
):
    rows_num, channels = gated_s.shape[1:]
    groups = gated_s.shape[0]
    length = groups * rows_num
    n = state.shape[0]
    model = tok_ref.shape[1]
    chunks = 2
    chunk = rows_num // chunks
    me = lax.axis_index("head")
    hi, lo = me // 2, me % 2
    near = partner("head", 0)
    far = partner("head", 1)
    others = [near, far, near + far - me]
    links = Links(send, recv)

    loads = [
        pltpu.make_async_copy(src, dst, load_sem.at[i])
        for i, (src, dst) in enumerate(((zw_hbm, zw), (xw_hbm, xw), (bcw_hbm, bcw), (dtw_hbm, dtw), (w_hbm, wv)))
    ]
    for load in loads:
        load.start()
    tok = tok_ref[...].astype(F32)
    recip = lax.rsqrt(jnp.mean(tok * tok, axis=-1, keepdims=True) + EPSILON)
    xs[hi, lo] = (tok * recip * pre_ref[...]).astype(BF16)
    meet([("head", z) for z in others] + [("batch", partner("batch", b)) for b in range(count)])

    own_rows = xs.at[hi, lo]
    to_far = []
    for c in range(chunks):
        part = xs.at[hi, lo, pl.ds(c * chunk, chunk)]
        to_far.append(links.copy(part, part, "head", far))
        to_far[-1].start()
    to_near = links.copy(own_rows, own_rows, "head", near)
    to_near.start()
    half = w_hbm.shape[-1] // 2

    def pieces(z, cols, order):
        def own_piece(ref):
            return ref.at[place(count, dict(enumerate(bits_of("batch", count)))) + (slice(None), cols)]

        first = ports.make(
            lambda: own_piece(w_hbm), lambda: own_piece(all_ref.at[lax.axis_index("head")]), "head", z
        )

        def at(i):
            bits = bits_of("batch", count)
            return all_ref.at[(z(),) + place(count, {b: bits[b] for b in order[i:]}) + (slice(None), cols)]

        rest = [
            ports.make(lambda i=i: at(i), lambda i=i: at(i), "batch", lambda i=i: partner("batch", order[i]))
            for i in range(count)
        ]
        return Stream(linked([first] + rest, lambda i: None))

    up = list(range(1, count))
    ports = Ports(send2, recv2)
    near_at = lambda: partner("head", 0)
    far_at = lambda: partner("head", 1)
    streams = []
    for z in (near_at, far_at, lambda: near_at() + far_at() - lax.axis_index("head")):
        streams.append(pieces(z, pl.ds(0, half), up + [0]))
        streams.append(pieces(z, pl.ds(half, half), up[::-1] + [0]))
    plan = [[] for _ in range(HEAD_PARTS * groups)]
    early = {spot: [] for spot in "abcde"}
    for spot, group in PIECE_POLLS:
        for st in streams[2 * group : 2 * group + 2]:
            if st.steps:
                (early[spot] if spot in early else plan[spot]).append(st.steps.pop(0))

    def poll(spot):
        for action in early[spot]:
            action()

    poll("a")
    keep = [pltpu.make_async_copy(gain_hbm, gains_ref.at[me], local_sem.at[1])]
    keep[0].start()
    inner_s[0:8, :] = jnp.zeros((8, channels), F32)
    state[...] = jnp.zeros_like(state)
    step_s[...] = jnp.zeros_like(step_s)
    pad_s[...] = jnp.zeros_like(pad_s)
    pad_s[0:1, 0 : dtw.shape[0]] = dtb_ref[...]
    pad_s[1:2, 0 : dtw.shape[0]] = alog_ref[...]
    for load in loads:
        load.wait()
    keep.append(pltpu.make_async_copy(wv, all_ref.at[me], local_sem.at[0]))
    keep[-1].start()

    def project(at_hi, at_lo):
        first = pl.multiple_of((2 * at_hi + at_lo) * rows_num, rows_num)
        rows = pl.ds(first, rows_num)
        inner_rows = pl.ds(pl.multiple_of(first + 8, 8), rows_num)
        tile = 256

        def columns(t, carry):
            cols = pl.ds(pl.multiple_of(t * tile, tile), tile)
            x = xs[at_hi, at_lo]
            gate_s[rows, cols] = mm(x, zw[:, cols])
            inner_s[inner_rows, cols] = mm(x, xw[:, cols])
            return carry

        lax.fori_loop(0, channels // tile, columns, 0)
        x = xs[at_hi, at_lo]
        bc_s[rows, :] = mm(x, bcw[...])
        step_s[rows, 0 : dtw.shape[0]] = mm_nt(x, dtw[...])

    project(hi, lo)
    to_near.wait()
    project(hi, 1 - lo)
    poll("b")
    onward = []
    for c in range(chunks):
        to_far[c].wait()
        part = xs.at[1 - hi, lo, pl.ds(c * chunk, chunk)]
        onward.append(links.copy(part, part, "head", near))
        onward[-1].start()

    poll("c")
    gain_sends = [links.copy(gain_hbm, gains_ref.at[me], "head", z) for z in others]
    for item in gain_sends:
        item.start()

    project(1 - hi, lo)
    poll("d")
    for item in onward:
        item.wait()
    project(1 - hi, 1 - lo)
    poll("e")

    rate = -jnp.exp(pad_s[1:2, :])
    lower = lower_mask((SPAN, SPAN))
    lower_f = lower.astype(F32)
    left = lax.broadcasted_iota(jnp.int32, (SPAN, 128), 1) < 64

    span_num = channels // HEAD_PARTS

    def block(at, part):
        first = pl.multiple_of(at * SPAN, SPAN)
        rows = pl.ds(first, SPAN)
        if part == 0:
            delta = softplus(step_s[rows, :] + pad_s[0:1, :])
            cum = mm_exact(lower_f, delta * rate)
            cum_t = cum.T
            bcb_s[rows, :] = bc_s[rows, :].astype(BF16)
            inner = jnp.where(lower, mm_nt(bcb_s[rows, n:], bcb_s[rows, :n]), 0.0)
            b_t = bc_s[rows, :n].T.astype(BF16)
            step_s[rows, :] = delta
            cum_s[at], cum_t_s[at], inner_prod_s[at], b_t_s[at] = cum, cum_t, inner, b_t
        else:
            delta = step_s[rows, :]
            cum, cum_t, inner, b_t = cum_s[at], cum_t_s[at], inner_prod_s[at], b_t_s[at]
        span_cols = pl.ds(part * span_num, span_num)
        before = state[:, span_cols].astype(BF16)
        prev_s[at, :, span_cols] = before
        across = mm(bcb_s[rows, n:], before)
        quarter = at // (rows_num // SPAN)
        sub = pl.ds(pl.multiple_of((at % (rows_num // SPAN)) * SPAN, SPAN), SPAN)
        for pair in range(part * span_num // 128, (part + 1) * span_num // 128):
            cols = slice(pair * 128, pair * 128 + 128)
            local = slice(pair * 128 - part * span_num, pair * 128 + 128 - part * span_num)
            c0, c1, ce = pair_columns(cum, pair, left)
            _, _, de = pair_columns(delta, pair, left)
            tot = ce[SPAN - 1 : SPAN, :]
            window = inner_s[pl.ds(first, SPAN + 8), cols]
            conv_p = convb_ref[:, cols] + sum(
                convw_ref[k : k + 1, cols] * window[5 + k : 5 + k + SPAN] for k in range(4)
            )
            inn_s[rows, cols] = window[8:].astype(BF16)
            sc = sigmoid(conv_p)
            act = conv_p * sc
            act_s[rows, cols] = act.astype(BF16)
            dsc_s[rows, cols] = (sc + act * (1.0 - sc)).astype(BF16)
            u = act * de
            tails[:, local] = (u * jnp.exp(tot - ce)).astype(BF16)
            u0 = jnp.where(left, u, 0.0).astype(BF16)
            u1 = jnp.where(left, 0.0, u).astype(BF16)
            p0 = (jnp.exp(jnp.minimum(c0 - cum_t[2 * pair : 2 * pair + 1, :], 0.0)) * inner).astype(BF16)
            p1 = (jnp.exp(jnp.minimum(c1 - cum_t[2 * pair + 1 : 2 * pair + 2, :], 0.0)) * inner).astype(BF16)
            within = mm(jnp.concatenate([p0, p1], axis=1), jnp.concatenate([u0, u1], axis=0))
            y = within + across[:, local] * jnp.exp(ce) + skip_ref[:, cols] * act
            gate = gate_s[rows, cols]
            sg = sigmoid(gate)
            sl = gate * sg
            s_s[rows, cols] = sl.astype(BF16)
            a_s[rows, cols] = (y * (sg + sl * (1.0 - sg))).astype(BF16)
            gated_s[quarter, sub, cols] = (y * sl).astype(BF16)
            state[:, cols] = state[:, cols] * jnp.exp(tot)
        state[:, span_cols] += mm(b_t, tails[...])

    def leave(q, part):
        cols = pl.ds(part * span_num, span_num)
        return pltpu.make_async_remote_copy(
            src_ref=gated_s.at[q, :, cols], dst_ref=gated_out.at[me, :, cols],
            send_sem=away_sem.at[part, q], recv_sem=here_sem.at[part, me],
            device_id={"head": q}, device_id_type=pl.DeviceIdType.MESH,
        )

    def arrive(q, part):
        cols = pl.ds(part * span_num, span_num)
        return pltpu.make_async_remote_copy(
            src_ref=gated_s.at[q, :, cols], dst_ref=gated_out.at[q, :, cols],
            send_sem=away_sem.at[part, q], recv_sem=here_sem.at[part, q],
            device_id={"head": q}, device_id_type=pl.DeviceIdType.MESH,
        )

    subs = rows_num // SPAN

    def stores(q):
        rows = pl.ds(pl.multiple_of(q * rows_num, rows_num), rows_num)
        pairs = (
            (xs.at[q // 2, q % 2], x_out.at[rows]),
            (a_s.at[rows], a_out.at[rows]),
            (s_s.at[rows], s_out.at[rows]),
            (act_s.at[rows], act_out.at[rows]),
            (dsc_s.at[rows], dsc_out.at[rows]),
            (inn_s.at[rows], inn_out.at[rows]),
            (bcb_s.at[rows], bc_out.at[rows]),
            (step_s.at[rows], step_out.at[rows]),
            (prev_s.at[pl.ds(q * subs, subs)], prev_out.at[pl.ds(q * subs, subs)]),
        )
        return [pltpu.make_async_copy(src, dst, store_sem.at[i, q]) for i, (src, dst) in enumerate(pairs)]

    for part in range(HEAD_PARTS):
        def quarter_step(q, carry):
            def one(at, inner_carry):
                block(at, part)
                return inner_carry

            lax.fori_loop(q * subs, (q + 1) * subs, one, 0)

            @pl.when(q != me)
            def _():
                leave(q, part).start()

            if part == HEAD_PARTS - 1:
                for item in stores(q):
                    item.start()
            for k in range(groups):
                @pl.when(q == k)
                def _():
                    for action in plan[part * groups + k]:
                        action()
            return carry

        lax.fori_loop(0, groups, quarter_step, 0)
    stay = pltpu.make_async_copy(gated_s.at[me], gated_out.at[me], local_sem.at[2])
    stay.start()
    drain(streams)
    for item in gain_sends:
        item.wait()
    for item in keep:
        item.wait()
    stay.wait()

    def finish(q, carry):
        @pl.when(q != me)
        def _():
            for part in range(HEAD_PARTS):
                leave(q, part).wait_send()
                arrive(q, part).wait_recv()

        for item in stores(q):
            item.wait()
        return carry

    lax.fori_loop(0, groups, finish, 0)


def front_call(tokens, pre_gain, zw, xw, bcw, dtw, out_weight, norm_gain, convw, convb, dtb, alog, skip, groups, batches):
    rows_num, model = tokens.shape
    channels = zw.shape[1]
    n = bcw.shape[1] // 2
    length = rows_num * groups
    count = log2(batches)
    part = channels // batches
    copies = 5 + groups - 1
    piece_copies = 2 * (groups - 1) * (1 + count)
    hbm = pl.BlockSpec(memory_space=pl.ANY)
    vmem = pl.BlockSpec(memory_space=pltpu.VMEM)
    wide = jax.ShapeDtypeStruct((length, channels), BF16)
    outs = [
        jax.ShapeDtypeStruct((length, model), BF16), wide, wide, wide, wide, wide,
        jax.ShapeDtypeStruct((length, 2 * n), BF16),
        jax.ShapeDtypeStruct((length, 128), F32),
        jax.ShapeDtypeStruct((length // SPAN, n, channels), BF16),
        jax.ShapeDtypeStruct((groups, rows_num, channels), BF16),
        jax.ShapeDtypeStruct((groups,) + (2,) * count + (part, model), BF16),
        jax.ShapeDtypeStruct((groups, 1, channels), F32),
    ]
    dma = pltpu.SemaphoreType.DMA
    result = pl.pallas_call(
        functools.partial(front_kernel, count),
        in_specs=[vmem, vmem] + [hbm] * 6 + [vmem] * 5,
        out_specs=[hbm] * len(outs),
        out_shape=outs,
        scratch_shapes=[
            pltpu.VMEM((2, 2, rows_num, model), BF16),
            pltpu.VMEM(zw.shape, BF16), pltpu.VMEM(xw.shape, BF16),
            pltpu.VMEM(bcw.shape, BF16), pltpu.VMEM(dtw.shape, BF16),
            pltpu.VMEM((2,) * count + (part, model), BF16),
            pltpu.VMEM((length, channels), F32),
            pltpu.VMEM((length, channels), BF16), pltpu.VMEM((length, channels), BF16),
            pltpu.VMEM((length, channels), BF16), pltpu.VMEM((length, channels), BF16),
            pltpu.VMEM((length, channels), BF16), pltpu.VMEM((length + 8, channels), F32),
            pltpu.VMEM((length, 2 * n), F32), pltpu.VMEM((length, 2 * n), BF16),
            pltpu.VMEM((length, 128), F32), pltpu.VMEM((length // SPAN, n, channels), BF16),
            pltpu.VMEM((groups, rows_num, channels), BF16),
            pltpu.VMEM((n, channels), F32), pltpu.VMEM((SPAN, channels // HEAD_PARTS), BF16),
            pltpu.VMEM((length // SPAN, SPAN, 128), F32), pltpu.VMEM((length // SPAN, 128, SPAN), F32),
            pltpu.VMEM((length // SPAN, SPAN, SPAN), F32), pltpu.VMEM((length // SPAN, n, SPAN), BF16),
            pltpu.VMEM((8, 128), F32),
            dma((5,)), dma((3,)), dma((9, groups)), dma((HEAD_PARTS, groups)), dma((HEAD_PARTS, groups)), dma((copies,)), dma((copies,)),
            dma((piece_copies,)), dma((piece_copies,)),
        ],
        compiler_params=pltpu.CompilerParams(
            collective_id=1, has_side_effects=True, vmem_limit_bytes=VMEM_BYTES
        ),
        cost_estimate=pl.CostEstimate(
            flops=4 * length * model * channels, bytes_accessed=400 * 2**20, transcendentals=0
        ),
        name="front",
    )(
        tokens, pre_gain[None], zw, xw, bcw, dtw, out_weight.reshape((2,) * count + (part, model)),
        norm_gain[None], convw, convb, dtb, alog, skip,
    )
    x, a, s, act, dsc, inn, bc, step, prev, gated, w_all, gains = result
    return x, (a, s, act, dsc, inn), bc, step, prev, gated, w_all.reshape(groups, channels, model), gains


def middle_kernel(
    count, g_hbm, w_hbm, cot_hbm, gain_ref, tok_ref,
    out_hbm, dg_out, own_ref, part_ref, ggrad_ref,
    g_s, w_s, cot_s, dy_s, gg_s, out_s, dg_s, give_s, kept_s, obuf, oslot0, oslot1, *refs,
):
    slots = [refs[i * (count - 1) : (i + 1) * (count - 1)] for i in range(4)]
    load_sem, store_sem, away_sem, here_sem, send, recv = refs[4 * (count - 1) :]
    groups, rows_num, channels = g_s.shape
    model = tok_ref.shape[1]
    part, half = kept_s.shape[-2:]
    pairs_num = groups // 2
    segs = segments(channels)
    tile = 512
    tiles = model // tile
    me = lax.axis_index("head")

    def w_load(t):
        cols = pl.ds(pl.multiple_of(t * tile, tile), tile)
        return pltpu.make_async_copy(w_hbm.at[:, :, cols], w_s.at[:, :, cols], load_sem.at[2 + t])

    loads = [
        pltpu.make_async_copy(g_hbm, g_s, load_sem.at[0]), pltpu.make_async_copy(cot_hbm, cot_s, load_sem.at[1]),
    ]
    for load in loads:
        load.start()
    for t in range(tiles):
        w_load(t).start()
    loads[0].wait()
    sums = [jnp.zeros((rows_num, 1), F32) for _ in segs]
    for j in range(groups):
        for w, (lo, hi) in enumerate(segs):
            g = g_s[j, :, lo:hi].astype(F32)
            gg_s[j, :, lo:hi] = (g * gain_ref[j, 0:1, lo:hi]).astype(BF16)
            sums[w] += jnp.sum(g * g, axis=1, keepdims=True)
    recips = []
    total = jnp.zeros((rows_num, 1), F32)
    for w, (lo, hi) in enumerate(segs):
        total = total + sums[w]
        recips.append(lax.rsqrt(total / (hi * groups) + EPSILON))
    meet(
        [("batch", partner("batch", b)) for b in range(count)]
        + [("head", z) for z in (partner("head", 0), partner("head", 1), partner("head", 0) + partner("head", 1) - me)]
    )
    loads[1].wait()

    def out_store(t):
        cols = pl.ds(pl.multiple_of(t * tile, tile), tile)
        return pltpu.make_async_copy(out_s.at[:, :, cols], out_hbm.at[:, :, cols], store_sem.at[t])

    def forward(t, dots):
        cols = pl.ds(pl.multiple_of(t * tile, tile), tile)
        w_load(t).wait()
        acc = jnp.zeros((rows_num, tile), F32)
        tok = tok_ref[:, cols].astype(F32)
        new = []
        for w, (lo, hi) in enumerate(segs):
            acc += mm(
                jnp.concatenate([gg_s[j, :, lo:hi] for j in range(groups)], axis=1),
                jnp.concatenate([w_s[j, lo:hi, cols] for j in range(groups)], axis=0),
            )
            out_s[w, :, cols] = (tok + recips[w] * acc).astype(BF16)
            new.append(dots[w] + jnp.sum(cot_s[w, :, cols].astype(F32) * acc, axis=1, keepdims=True))
        out_store(t).start()
        return tuple(new)

    def combine(t, carry):
        cols = pl.ds(pl.multiple_of(t * tile, tile), tile)
        combined = jnp.zeros((rows_num, tile), F32)
        for w in reversed(range(4)):
            combined += recips[w] * cot_s[w, :, cols].astype(F32)
            dy_s[w, :, cols] = combined.astype(BF16)
        return carry

    lax.fori_loop(0, tiles, combine, 0)

    def leave(j):
        return pltpu.make_async_remote_copy(
            src_ref=dg_s.at[j], dst_ref=dg_out.at[me], send_sem=away_sem.at[j], recv_sem=here_sem.at[me],
            device_id={"head": j}, device_id_type=pl.DeviceIdType.MESH,
        )

    def arrive(j):
        return pltpu.make_async_remote_copy(
            src_ref=dg_s.at[j], dst_ref=dg_out.at[j], send_sem=away_sem.at[j], recv_sem=here_sem.at[j],
            device_id={"head": j}, device_id_type=pl.DeviceIdType.MESH,
        )

    def back(k, carry):
        j = (me + 1 + k) % groups
        for w, (lo, hi) in enumerate(segs):
            dn = mm_nt(dy_s[w], w_s[j, lo:hi, :])
            g = g_s[j, :, lo:hi].astype(F32)
            ggrad_ref[j, :, lo:hi] = jnp.sum(g * dn, axis=0, keepdims=True)
            dg_s[j, :, lo:hi] = (gain_ref[j, 0:1, lo:hi] * dn - g * scales[w]).astype(BF16)

        @pl.when(j != me)
        def _():
            leave(j).start()

        return carry

    ports = Ports(send, recv)
    up = list(range(1, count))
    core = bits_of("batch", 1)[0]

    def upper_index(p):
        return tuple((p >> b) & 1 for b in reversed(range(1, count)))

    def terms(s, bit, use):
        g0, c0 = (s % 2) * pairs_num, (s // 2) * half
        if part % 128 == 0:
            for q in range(2 ** (count - 1)):
                at = pl.ds(pl.multiple_of((2 * q + bit) * part, part), part)
                left = jnp.concatenate([gg_s[g0 + j, :, at] for j in range(pairs_num)], axis=1)
                owners = [[w for w, (lo, hi) in enumerate(segs) if lo <= (2 * q + c) * part < hi][0] for c in range(2)]
                w = owners[0] + (owners[1] - owners[0]) * bit
                term = mm_tn(left, dy_s[w, :, c0 : c0 + half])
                for j in range(pairs_num):
                    use(upper_index(2 * q), j, term[j * part : (j + 1) * part])
            return
        for j in range(pairs_num):
            for w, (lo, hi) in enumerate(segs):
                term = mm_tn(gg_s[g0 + j, :, lo:hi], dy_s[w, :, c0 : c0 + half])
                for p in range(lo // part, hi // part):
                    @pl.when(bit == p % 2)
                    def _():
                        use(upper_index(p), j, term[p * part - lo : (p + 1) * part - lo])

    def to_core(s):
        return pltpu.make_async_remote_copy(
            src_ref=give_s.at[s], dst_ref=kept_s.at[s], send_sem=send.at[s], recv_sem=recv.at[s],
            device_id={"batch": partner("batch", 0)}, device_id_type=pl.DeviceIdType.MESH,
        )

    def give(s):
        def use(index, j, rows):
            give_s[(s,) + index + (j,)] = rows.astype(BF16)

        terms(s, 1 - core, use)
        to_core(s).start()

    def keep(s):
        to_core(s).wait()

        def use(index, j, rows):
            at = (s,) + index + (j,)
            kept_s[at] = (kept_s[at].astype(F32) + rows).astype(BF16)

        terms(s, core, use)

    ports.used = 4
    streams = [
        Stream(halving(ports, "batch", lambda s=s: kept_s.at[s], slots[s], up if s % 2 == 0 else up[::-1]))
        for s in range(4)
    ]
    mine = bits_of("batch", count)
    own = place(up, {b: mine[b] for b in up})
    head_sum = Stream(halving(ports, "head", lambda: obuf, (oslot0, oslot1), [0, 1]))
    for s in range(2):
        give(s)
    for s in range(2):
        keep(s)
        streams[s].advance()
    dots = lax.fori_loop(0, tiles, forward, tuple(jnp.zeros((rows_num, 1), F32) for _ in segs))
    scales = [None] * 4
    scale = jnp.zeros((rows_num, 1), F32)
    for w in reversed(range(4)):
        scale = scale + recips[w] ** 3 * dots[w] / (segs[w][1] * groups)
        scales[w] = scale
    lax.fori_loop(0, groups, back, 0)
    stay = pltpu.make_async_copy(dg_s.at[me], dg_out.at[me], load_sem.at[0])
    stay.start()
    for s in range(2, 4):
        give(s)
    advance_all(streams[:2])
    for s in range(2, 4):
        keep(s)
        streams[s].advance()
    drain(streams[:2])
    for s in range(2):
        for j in range(pairs_num):
            obuf[s, j] = kept_s[(s,) + own + (j,)]
    head_sum.advance()
    advance_all(streams[2:])
    head_sum.advance()
    drain(streams)
    drain([head_sum])
    own_ref[...] = obuf[place(2, dict(enumerate(bits_of("head", 2))))]
    for s in range(2, 4):
        for j in range(pairs_num):
            part_ref[s - 2, j] = kept_s[(s,) + own + (j,)]
    stay.wait()

    def finish(j, carry):
        @pl.when(j != me)
        def _():
            leave(j).wait_send()
            arrive(j).wait_recv()

        return carry

    lax.fori_loop(0, groups, finish, 0)

    def stored(t, carry):
        out_store(t).wait()
        return carry

    lax.fori_loop(0, tiles, stored, 0)


def middle_call(g, w_all, gain, tok, cot, batches):
    groups, rows_num, channels = g.shape
    model = tok.shape[1]
    count = log2(batches)
    part = channels // batches
    half = model // 2
    block = (groups // 2, part, half)
    hbm = pl.BlockSpec(memory_space=pl.ANY)
    vmem = pl.BlockSpec(memory_space=pltpu.VMEM)
    dma = pltpu.SemaphoreType.DMA
    wide = pltpu.VMEM((groups, rows_num, channels), BF16)
    tall = pltpu.VMEM((4, rows_num, model), BF16)
    halves = pltpu.VMEM((4,) + (2,) * (count - 1) + block, BF16)
    return pl.pallas_call(
        functools.partial(middle_kernel, count),
        in_specs=[hbm] * 3 + [vmem] * 2,
        out_specs=[hbm, hbm, vmem, vmem, vmem],
        out_shape=[
            jax.ShapeDtypeStruct((4, rows_num, model), BF16),
            jax.ShapeDtypeStruct(g.shape, BF16),
            jax.ShapeDtypeStruct((part, half), BF16),
            jax.ShapeDtypeStruct((2, 2, part, half), BF16),
            jax.ShapeDtypeStruct((groups, 1, channels), F32),
        ],
        scratch_shapes=[
            wide, pltpu.VMEM((groups, channels, model), BF16), tall, tall, wide, tall, wide, halves, halves,
            pltpu.VMEM((2, 2, part, half), BF16), pltpu.VMEM((2, part, half), BF16), pltpu.VMEM((part, half), BF16),
        ]
        + [s for _ in range(4) for s in halving_slots(count - 1, block, BF16)]
        + [
            dma((2 + model // 512,)), dma((model // 512,)), dma((groups,)), dma((groups,)),
            dma((4 * count + 2,)), dma((4 * count + 2,)),
        ],
        compiler_params=pltpu.CompilerParams(
            collective_id=2, has_side_effects=True, vmem_limit_bytes=BACK_VMEM_BYTES
        ),
        cost_estimate=pl.CostEstimate(
            flops=6 * groups * rows_num * channels * model, bytes_accessed=200 * 2**20, transcendentals=0
        ),
        name="nested_norm",
    )(g, w_all, cot, gain, tok)


BACK_POLLS = {
    "z": ((0, 0, "a"), (0, 1, "a"), (0, 1, "b"), (0, 2, "a"), (0, 3, "a"), (0, 3, "b")),
    "out": ((0, 0, "a"), (0, 1, "a")),
    "spread": (((0, 0, "a"), (0, 1, "a"), (0, 1, "b")), ((0, 1, "b"), (0, 2, "a"), (0, 2, "b"), (0, 3, "a"))),
    "relay": (
        ((0, 1, "a"), 3, 0, 1), ((0, 1, "b"), 3, 1, 1), ((0, 2, "a"), 3, 2, 1), ((0, 2, "a"), 3, 3, 1),
        ((0, 1, "b"), 3, 0, 2), ((0, 2, "a"), 3, 1, 2), ((0, 2, "b"), 3, 2, 2), ((0, 3, "a"), 3, 3, 2),
        ((0, 2, "b"), 2, 0, 1), ((0, 3, "a"), 2, 1, 1), ((0, 3, "b"), 2, 2, 1),
    ),
    "tail": (1, 1, 2, 2),
}
RELAY_ORDER = [(2, c, 1) for c in range(4)] + [(1, c, 1) for c in range(4)]
RELAY_ORDER += [(0, 0, 1), (0, 1, 1), (0, 0, 2), (0, 2, 1), (0, 1, 2), (0, 3, 1), (0, 2, 2), (0, 3, 2)]


def back_kernel(
    count, group_bits,
    dg_hbm, a_hbm, s_hbm, act_hbm, dsc_hbm, inn_hbm, x_hbm, bc_hbm, step_hbm, prev_hbm,
    zw_hbm, xw_hbm, bcw_hbm, dtw_hbm, o_hbm, own_hbm, gain_ref, convw_ref, alog_ref, skip_ref,
    z_out, x_out, o_out, bc_out, small_out, own_out,
    dg, a, s, act, dsc, inn, x, bc, step, prev, zw, xw, bdw, dtw, obuf, o_first, hot_ref, pad_s,
    lam, dconv, dyc_s, vt_s, q_s, v_s, w_s, da_s, etot_s, draw_s, head_s, vec_s, pre_s, dbs,
    rows_s, line_s, last_s, zg, bcbuf, small, *refs,
):
    zx_slots = [refs[i * count : (i + 1) * count] for i in range(2)]
    refs = refs[2 * count :]
    bc_slots, refs = (refs[:count], refs[count : 2 * count]), refs[2 * count :]
    bc_head, refs = (refs[:group_bits], refs[group_bits : 2 * group_bits]), refs[2 * group_bits :]
    small_slots, refs = refs[:count], refs[count:]
    small_head, refs = refs[:group_bits], refs[group_bits:]
    o_slots, refs = refs[:group_bits], refs[group_bits:]
    load_sem, store_sem, rsend, rrecv, rrecv_own, send, recv = refs
    length, channels = a.shape
    model = x.shape[1]
    n = lam.shape[0]
    heads = hot_ref.shape[0]
    groups = rows_s.shape[0] * rows_s.shape[1]
    rows_num = length // groups
    subs = rows_num // SPAN
    wide = bcbuf.shape[-1]
    me = lax.axis_index("head")

    pairs = [
        (dg_hbm.at[:, :, pl.ds(0, channels // 2)], dg.at[0]),
        (dg_hbm.at[:, :, pl.ds(channels // 2, channels // 2)], dg.at[1]), (a_hbm, a), (s_hbm, s), (x_hbm, x), (o_hbm, obuf), (own_hbm, o_first), (step_hbm, step), (bc_hbm, bc),
        (prev_hbm, prev), (act_hbm, act), (dsc_hbm, dsc), (inn_hbm, inn), (zw_hbm, zw), (xw_hbm, xw),
        (bcw_hbm, bdw.at[:, pl.ds(0, 2 * n)]), (dtw_hbm, dtw),
    ]
    loads = [pltpu.make_async_copy(src, dst, load_sem.at[i]) for i, (src, dst) in enumerate(pairs)]
    for load in loads:
        load.start()
    for load in loads[:4]:
        load.wait()

    def gates(i, carry):
        per = rows_num // 64
        rows = pl.ds(pl.multiple_of(i * 64, 64), 64)
        piece = dg.shape[-1]
        for h in range(dg.shape[0]):
            cols = slice(h * piece, (h + 1) * piece)
            d = dg[h, i // per, pl.ds(pl.multiple_of((i % per) * 64, 64), 64), :].astype(F32)
            a[rows, cols] = (d * a[rows, cols].astype(F32)).astype(BF16)
            s[rows, cols] = (d * s[rows, cols].astype(F32)).astype(BF16)
        return carry

    lax.fori_loop(0, length // 64, gates, 0)
    meet(
        [("batch", partner("batch", b)) for b in range(count)]
        + [("head", partner("head", b)) for b in range(group_bits)]
    )

    ports = Ports(send, recv)
    up = list(range(1, count))
    orders = [up, up[::-1]]

    def own_at():
        return place(count, dict(enumerate(bits_of("batch", count))))

    def grads(i, out, slots, first, width):
        part = (slice(None),) * (count + 1) + (pl.ds(first, width),)
        view = lambda: out.at[part]
        buf = lambda: zg.at[part]
        order = orders[i % 2]
        return Stream(
            halving(ports, "batch", buf, slots, [0] + order),
            spreading(
                ports, "batch", view, order[::-1] + [0], lambda: buf().at[own_at()], store_sem.at[2 + i]
            ),
        )

    z_width, x_width = channels // 2, channels // X_STREAMS
    streams = [grads(i, z_out, zx_slots[i], i * z_width, z_width) for i in range(2)]
    per = z_width // x_width
    for i in range(X_STREAMS):
        cols = pl.ds((i % per) * x_width, x_width)
        slots = [ref.at[(slice(None),) * (len(ref.shape) - 1) + (cols,)] for ref in zx_slots[i // per]]
        streams.append(grads(2 + i, x_out, slots, i * x_width, x_width))

    def state_part(i):
        part = (slice(None),) * (count + 1) + ((pl.ds(n, n + 128), pl.ds(0, n))[i],)
        buf = lambda: bcbuf.at[part]
        view = lambda: bc_out.at[part]
        return Stream(
            halving(ports, "batch", buf, bc_slots[i], [0] + orders[i]),
            exchanging(
                ports, "head", lambda: bcbuf.at[own_at() + (slice(None), pl.ds((n, 0)[i], n))], bc_head[i],
                range(group_bits),
            ),
            spreading(
                ports, "batch", view, orders[i][::-1] + [0], lambda: buf().at[own_at()], store_sem.at[i]
            ),
        )

    state = [state_part(i) for i in range(2)]
    vectors = Stream(
        exchanging(ports, "batch", lambda: small, small_slots, range(count)),
        exchanging(ports, "head", lambda: small.at[pl.ds(0, 8)], small_head, range(group_bits)),
    )
    half = model // 2

    def head_own():
        return place(group_bits, dict(enumerate(bits_of("head", group_bits))))

    def o_view(i):
        return o_out.at[(slice(None),) * (count + 1) + (pl.ds(i * half, half),)]

    outs = Stream(halving(ports, "head", lambda: obuf, o_slots, list(range(group_bits))))

    def o_own(i):
        return obuf.at[head_own()] if i else o_first

    spread = [
        Stream(spreading(
            ports, "batch", lambda i=i: o_view(i), orders[i] + [0], lambda i=i: o_own(i),
            store_sem.at[2 + 2 + X_STREAMS + i],
        ))
        for i in range(2)
    ]

    for load in loads[4:7]:
        load.wait()
    outs.advance()
    spread[0].advance()
    tile = 256
    block_rows = model >> count

    def put(target, t, value):
        for k in range(tile // min(block_rows, tile)):
            p = (t * tile) // block_rows + k
            index = tuple((p // 2**b) % 2 for b in reversed(range(count)))
            if block_rows <= tile:
                target[index] = value[k * block_rows : (k + 1) * block_rows].astype(BF16)
            else:
                first = pl.multiple_of((t * tile) % block_rows, tile)
                target[index + (pl.ds(first, tile), slice(None))] = value.astype(BF16)

    def weight_grad(right, target):
        def one(t, carry):
            put(target, t, mm_tn(x[:, pl.ds(pl.multiple_of(t * tile, tile), tile)], right[...]))
            return carry

        lax.fori_loop(0, model // tile, one, 0)

    weight_grad(a, zg)
    advance_all(streams[:2])
    for load in loads[7:]:
        load.wait()
    bdw[:, 2 * n :] = jnp.concatenate([dtw[...], jnp.zeros((128 - heads, model), BF16)], axis=0).T
    pad_s[...] = jnp.zeros_like(pad_s)
    pad_s[0:1, 0:heads] = alog_ref[...]
    hot_ref[...] = (
        lax.broadcasted_iota(jnp.int32, hot_ref.shape, 1) // (channels // heads)
        == lax.broadcasted_iota(jnp.int32, hot_ref.shape, 0)
    ).astype(F32).astype(BF16)

    lam[...] = jnp.zeros_like(lam)
    dconv[rows_num:, :] = jnp.zeros((8, channels), F32)
    vec_s[...] = jnp.zeros_like(vec_s)
    head_s[...] = jnp.zeros_like(head_s)
    draw_s[...] = jnp.zeros_like(draw_s)
    pre_s[...] = jnp.zeros_like(pre_s)
    rate = -jnp.exp(pad_s[0:1, :])
    lower = lower_mask((SPAN, SPAN))
    lower_f = lower.astype(F32)
    lower_b = lower.astype(BF16)
    row_at = lax.broadcasted_iota(jnp.int32, (SPAN, SPAN), 0)
    col_at = lax.broadcasted_iota(jnp.int32, (SPAN, SPAN), 1)
    upper = row_at <= col_at
    strict = row_at < col_at
    strict_f = strict.astype(F32)
    left = lax.broadcasted_iota(jnp.int32, (SPAN, 128), 1) < 64

    span_num = channels // BACK_PARTS
    span_heads = heads // BACK_PARTS

    def block(at, local, part):
        rows = pl.ds(pl.multiple_of(at * SPAN, SPAN), SPAN)
        local_rows = pl.ds(pl.multiple_of(local * SPAN, SPAN), SPAN)
        delta = step[rows, :]
        cum = mm_exact(lower_f, delta * rate)
        cum_t = cum.T
        delta_t = delta.T
        series = delta_t * (1.0 - delta_t * (0.5 - delta_t * (1.0 / 6.0 - delta_t / 24.0)))
        slope_t = jnp.where(delta_t < 0.04, series, 1.0 - jnp.exp(-delta_t))
        rate_t = jnp.broadcast_to(rate, (SPAN, 128)).T
        b_val = bc[rows, :n]
        c_val = bc[rows, n:]
        inner = jnp.where(upper, mm_nt(b_val, c_val), 0.0)
        span_cols = pl.ds(part * span_num, span_num)
        before = prev[at, :, span_cols]
        lam_b = lam[:, span_cols].astype(BF16)
        across = mm(c_val, before)
        dtail = mm(b_val, lam_b)
        d_inner_prod = jnp.zeros((SPAN, SPAN), F32)
        for pair in range(part * span_num // 128, (part + 1) * span_num // 128):
            cols = slice(pair * 128, pair * 128 + 128)
            own = pair - part * span_num // 128
            here = slice(own * 128, own * 128 + 128)
            c0, c1, ce = pair_columns(cum, pair, left)
            _, _, de = pair_columns(delta, pair, left)
            tot = ce[SPAN - 1 : SPAN, :]
            e_cum = jnp.exp(ce)
            e_tail = jnp.exp(tot - ce)
            dy_b = s[rows, cols]
            dy = dy_b.astype(F32)
            act_p = act[rows, cols].astype(F32)
            vec_s[5:6, cols] += jnp.sum(dy * act_p, axis=0, keepdims=True)
            u = act_p * de
            u_b = u.astype(BF16)
            zero = jnp.zeros_like(dy_b)
            dy01 = jnp.concatenate([jnp.where(left, dy_b, zero), jnp.where(left, zero, dy_b)], axis=0)
            m0 = jnp.exp(jnp.minimum(cum_t[2 * pair : 2 * pair + 1, :] - c0, 0.0))
            m1 = jnp.exp(jnp.minimum(cum_t[2 * pair + 1 : 2 * pair + 2, :] - c1, 0.0))
            p0 = m0 * inner
            p1 = m1 * inner
            du = mm(jnp.concatenate([p0.astype(BF16), p1.astype(BF16)], axis=1), dy01)
            dp = mm_nt(u_b, dy01)
            dp0, dp1 = dp[:, :SPAN], dp[:, SPAN:]
            d_inner_prod += dp0 * m0 + dp1 * m1
            e01 = jnp.concatenate([(dp0 * p0).astype(BF16), (dp1 * p1).astype(BF16)], axis=0)
            spans = mm(e01, lower_b)
            da_s[2 * own : 2 * own + 1, :] = jnp.sum(
                jnp.where(strict, spans[:SPAN], 0.0), axis=0, keepdims=True
            )
            da_s[2 * own + 1 : 2 * own + 2, :] = jnp.sum(
                jnp.where(strict, spans[SPAN:], 0.0), axis=0, keepdims=True
            )
            dut = dtail[:, here] * e_tail
            du = du + dut
            dye = dy * e_cum
            dyc_s[:, here] = dye.astype(BF16)
            vt_s[:, here] = (u * e_tail).astype(BF16)
            q_s[:, here] = (dye * across[:, here]).astype(BF16)
            v_s[:, here] = (u * dut).astype(BF16)
            w_s[:, here] = (act_p * du).astype(BF16)
            etot_s[:, here] = jnp.exp(tot)
            d_act = de * du + skip_ref[:, cols] * dy
            dconv[local_rows, cols] = d_act * dsc[rows, cols].astype(F32)
        hot = hot_ref[:span_heads, :span_num]
        these = slice(part * span_heads, (part + 1) * span_heads)
        over = jnp.sum(lam[:, span_cols] * before.astype(F32), axis=0, keepdims=True) * etot_s[...]
        over = jnp.broadcast_to(over, (128, span_num))
        over = lax.dot_general(
            hot.astype(F32), over, (((1,), (1,)), ((), ())), preferred_element_type=F32, precision=HIGHEST
        )
        da = (
            da_s[...]
            + mm_exact(mm_nt(hot, q_s[...]), lower_f)
            + mm_exact(mm_nt(hot, v_s[...]), strict_f)
            + over
        )
        d_step = mm_nt(hot, w_s[...]) + rate_t[these] * da
        d_raw = d_step * slope_t[these]
        head_s[these, :] += d_raw
        head_s[heads + part * span_heads : heads + (part + 1) * span_heads, :] += delta_t[these] * da * rate_t[these]
        draw_s[these, :] = d_raw
        dg_b = jnp.where(upper, d_inner_prod, 0.0)
        d_b = mm(dg_b.astype(BF16), c_val) + mm_nt(vt_s[...], lam_b)
        d_c = mm(dg_b.T.astype(BF16), b_val) + mm_nt(dyc_s[...], before)
        d_t = draw_s[...].T
        if part:
            d_b += dbs[rows, :n].astype(F32)
            d_c += dbs[rows, n : 2 * n].astype(F32)
            d_t += dbs[rows, 2 * n :].astype(F32)
        dbs[rows, :n] = d_b.astype(BF16)
        dbs[rows, n : 2 * n] = d_c.astype(BF16)
        dbs[rows, 2 * n :] = d_t.astype(BF16)
        lam[:, span_cols] = lam[:, span_cols] * etot_s[...] + mm(bc[rows, n:].astype(F32).T.astype(BF16), dyc_s[...])

    top = groups - 1

    def slot(q, c):
        return dg.at[q, c] if q < 2 else line_s.at[q - 2, c]

    def hop(q, c, dst, sem, to):
        return pltpu.make_async_remote_copy(
            src_ref=rows_s.at[q // 2, q % 2, c], dst_ref=dst, send_sem=rsend.at[q, c], recv_sem=sem,
            device_id={"head": to}, device_id_type=pl.DeviceIdType.MESH,
        )

    def send_up(q, c):
        @pl.when(me + 1 < q)
        def _():
            hop(q, c, slot(q, c), rrecv.at[q, c], me + 1).start()

        @pl.when(me + 1 == q)
        def _():
            hop(q, c, last_s.at[c], rrecv_own.at[c], me + 1).start()

    def send_down(q, c):
        hop(q, c, slot(q, c), rrecv.at[q, c], me - 1).start()

    def arrived(q, c):
        hop(q, c, slot(q, c), rrecv.at[q, c], me).wait_recv()

    def arrived_last(q, c):
        hop(q, c, last_s.at[c], rrecv_own.at[c], me).wait_recv()

    def begin(q):
        for c in range(ROW_CHUNKS):
            if q > 0:
                @pl.when(me == 0)
                def _():
                    send_up(q, c)
            if q < top:
                @pl.when(me == top)
                def _():
                    send_down(q, c)

    def relay(q, c, distance):
        if distance < q:
            @pl.when(me == distance)
            def _():
                arrived(q, c)
                add_block(rows_s, (q // 2, q % 2, c), slot(q, c), ())
                send_up(q, c)
        if top - distance > q:
            @pl.when(me == top - distance)
            def _():
                arrived(q, c)
                add_block(rows_s, (q // 2, q % 2, c), slot(q, c), ())
                send_down(q, c)

    def conv_back(rows, part):
        for c in range(part * span_num, (part + 1) * span_num, 128):
            cols = slice(c, c + 128)
            inner_v = inn[rows, cols].astype(F32)
            d_in = jnp.zeros((rows_num, 128), F32)
            for k in range(4):
                shifted = dconv[3 - k : 3 - k + rows_num, cols]
                d_in += convw_ref[k : k + 1, cols] * shifted
                vec_s[k : k + 1, cols] += jnp.sum(inner_v * shifted, axis=0, keepdims=True)
            vec_s[4:5, cols] += jnp.sum(dconv[0:rows_num, cols], axis=0, keepdims=True)
            inn[rows, cols] = d_in.astype(BF16)
        kept = pl.ds(part * span_num, span_num)
        dconv[rows_num:, kept] = dconv[0:8, kept]

    def row_grads(q, rows):
        per = model // ROW_CHUNKS // tile

        def columns(t, carry):
            cols = pl.ds(pl.multiple_of(t * tile, tile), tile)
            value = mm_nt(a[rows, :], zw[cols, :]) + mm_nt(inn[rows, :], xw[cols, :]) + mm_nt(dbs[rows, :], bdw[cols, :])
            pre_s[:, cols] += jnp.sum(value * x[rows, cols].astype(F32), axis=0, keepdims=True)
            rows_s[q // 2, q % 2, t // per, :, pl.ds(pl.multiple_of((t % per) * tile, tile), tile)] = value.astype(BF16)
            return carry

        lax.fori_loop(0, model // tile, columns, 0)

    plan = {(part, k, spot): [] for part in range(BACK_PARTS) for k in range(groups) for spot in "ab"}

    def book(stream, slots):
        for slot in slots:
            if stream.steps:
                plan[slot].append(stream.steps.pop(0))

    for st in streams[:2]:
        book(st, BACK_POLLS["z"])
    book(outs, BACK_POLLS["out"])
    for i, st in enumerate(spread):
        book(st, BACK_POLLS["spread"][i])
    last = BACK_PARTS - 1
    for k in range(groups):
        plan[last, k, "b"].insert(0, lambda q=top - k: begin(q))
    for spot, q, c, distance in BACK_POLLS["relay"]:
        plan[spot].append(lambda q=q, c=c, distance=distance: relay(q, c, distance))

    for part in range(BACK_PARTS):
        def quarter_step(i, carry):
            q = groups - 1 - i
            rows = pl.ds(pl.multiple_of(q * rows_num, rows_num), rows_num)

            def one(j, inner_carry):
                block(q * subs + subs - 1 - j, subs - 1 - j, part)
                return inner_carry

            lax.fori_loop(0, subs, one, 0)

            def polls(spot):
                for k in range(groups):
                    if plan[part, k, spot]:
                        @pl.when(i == k)
                        def _():
                            for action in plan[part, k, spot]:
                                action()

            polls("a")
            conv_back(rows, part)
            if part == last:
                row_grads(q, rows)
            polls("b")
            return carry

        lax.fori_loop(0, groups, quarter_step, 0)

    drain(streams[:2])
    tail = list(BACK_POLLS["tail"])
    booked = {key[1:] for key in BACK_POLLS["relay"]}
    relays = [r for r in RELAY_ORDER if r not in booked]

    def relay_some(number):
        for _ in range(number):
            if relays:
                relay(*relays.pop(0))

    per = X_STREAMS // 2
    for h in range(2):
        weight_grad(inn.at[:, pl.ds(h * z_width, z_width)], zg.at[(slice(None),) * (count + 1) + (pl.ds(h * z_width, z_width),)])
        advance_all(streams[2 + h * per : 2 + (h + 1) * per])
        relay_some(tail.pop(0))

    def state_grad(t, carry):
        put(bcbuf, t, mm_tn(x[:, pl.ds(pl.multiple_of(t * tile, tile), tile)], dbs[...]))
        return carry

    lax.fori_loop(0, model // tile, state_grad, 0)
    advance_all(state)
    small[...] = jnp.zeros_like(small)
    for j in range(groups):
        small[j : j + 1, :] = gain_ref[j]
    for j in range(model // channels):
        small[groups + j : groups + j + 1, :] = pre_s[:, j * channels : (j + 1) * channels]
    small[8:14, :] = vec_s[0:6, :]
    totals = lax.dot_general(
        jnp.ones((8, SPAN), F32), head_s[...], (((1,), (1,)), ((), ())),
        preferred_element_type=F32, precision=HIGHEST,
    )
    small[14:15, 0:128] = totals[0:1]
    vectors.advance()
    while relays:
        advance_all(streams[2 : 2 + per])
        relay_some(tail.pop(0) if tail else 1)
        advance_all(streams[2 + per :] + spread)
        relay_some(tail.pop(0) if tail else 1)
        advance_all(state + [vectors])
    drain(streams + spread + state + [vectors, outs])
    small_out[...] = small[...]

    piece = model // ROW_CHUNKS
    for c in range(ROW_CHUNKS):
        for q in range(groups):
            @pl.when(me == q)
            def _():
                if q > 0:
                    arrived_last(q, c)
                if q < top:
                    arrived(q, c)

                def total(r, carry):
                    rs = pl.ds(pl.multiple_of(r * 32, 32), 32)
                    value = rows_s[q // 2, q % 2, c, rs, :].astype(F32)
                    if q > 0:
                        value += last_s[c, rs, :].astype(F32)
                    if q < top:
                        value += slot(q, c)[rs, :].astype(F32)
                    own_out[rs, c * piece : (c + 1) * piece] = value
                    return carry

                lax.fori_loop(0, rows_num // 32, total, 0)

            @pl.when(me != q)
            def _():
                hop(q, c, slot(q, c), rrecv.at[q, c], me).wait_send()


def back_call(dg, res, x, bc, step, prev, zw, xw, bcw, dtw, out_part, out_own, gain_grad, convw, alog, skip, groups, batches):
    length, model = x.shape
    channels = xw.shape[1]
    n = bc.shape[1] // 2
    heads = dtw.shape[0]
    rows_num = length // groups
    count = log2(batches)
    group_bits = log2(groups)
    lead = (2,) * count
    part = channels // batches
    rows = model // batches
    wide = 2 * n + 128
    hbm = pl.BlockSpec(memory_space=pl.ANY)
    vmem = pl.BlockSpec(memory_space=pltpu.VMEM)
    dma = pltpu.SemaphoreType.DMA
    copies = (2 + X_STREAMS) * 2 * count + 2 * (2 * count + group_bits) + (count + group_bits) + group_bits + 2 * count
    tall = lambda w, t: pltpu.VMEM((length, w), t)
    span = pltpu.VMEM((SPAN, channels // BACK_PARTS), BF16)
    z, xg, o, bcg, small, own = pl.pallas_call(
        functools.partial(back_kernel, count, group_bits),
        in_specs=[hbm] * 16 + [vmem] * 4,
        out_specs=[hbm] * 4 + [vmem] * 2,
        out_shape=[
            jax.ShapeDtypeStruct(lead + (rows, channels), BF16),
            jax.ShapeDtypeStruct(lead + (rows, channels), BF16),
            jax.ShapeDtypeStruct(lead + (part, model), BF16),
            jax.ShapeDtypeStruct(lead + (rows, wide), BF16),
            jax.ShapeDtypeStruct((16, channels), F32),
            jax.ShapeDtypeStruct((rows_num, model), F32),
        ],
        scratch_shapes=[pltpu.VMEM((2, groups, rows_num, channels // 2), BF16)] + [tall(channels, BF16)] * 5
        + [
            tall(model, BF16), tall(2 * n, BF16), tall(128, F32), pltpu.VMEM(prev.shape, BF16),
            pltpu.VMEM(zw.shape, BF16), pltpu.VMEM(xw.shape, BF16), pltpu.VMEM((model, wide), BF16),
            pltpu.VMEM(dtw.shape, BF16),
            pltpu.VMEM((2,) * group_bits + (part, model // 2), BF16), pltpu.VMEM((part, model // 2), BF16),
            pltpu.VMEM((heads, channels), BF16), pltpu.VMEM((8, 128), F32),
            pltpu.VMEM((n, channels), F32), pltpu.VMEM((rows_num + 8, channels), F32),
        ]
        + [span] * 5
        + [
            pltpu.VMEM((heads // BACK_PARTS, SPAN), F32), pltpu.VMEM((1, channels // BACK_PARTS), F32),
            pltpu.VMEM((128, SPAN), F32),
            pltpu.VMEM((128, SPAN), F32), pltpu.VMEM((8, channels), F32), pltpu.VMEM((1, model), F32),
            tall(wide, BF16),
            pltpu.VMEM((2, 2, ROW_CHUNKS, rows_num, model // ROW_CHUNKS), BF16),
            pltpu.VMEM((2, ROW_CHUNKS, rows_num, model // ROW_CHUNKS), BF16),
            pltpu.VMEM((ROW_CHUNKS, rows_num, model // ROW_CHUNKS), BF16),
            pltpu.VMEM(lead + (rows, channels), BF16), pltpu.VMEM(lead + (rows, wide), BF16),
            pltpu.VMEM((16, channels), F32),
        ]
        + [s for _ in range(2) for s in halving_slots(count, (rows, channels // 2), BF16)]
        + halving_slots(count, (rows, n + 128), BF16)
        + halving_slots(count, (rows, n), BF16)
        + [pltpu.VMEM((rows, n), BF16)] * (2 * group_bits)
        + [pltpu.VMEM((16, channels), F32)] * count
        + [pltpu.VMEM((8, channels), F32)] * group_bits
        + halving_slots(group_bits, (part, model // 2), BF16)
        + [dma((17,)), dma((6 + X_STREAMS,)),
            dma((groups, ROW_CHUNKS)), dma((groups, ROW_CHUNKS)), dma((ROW_CHUNKS,)), dma((copies,)), dma((copies,))],
        compiler_params=pltpu.CompilerParams(
            collective_id=3, has_side_effects=True, vmem_limit_bytes=BACK_VMEM_BYTES
        ),
        cost_estimate=pl.CostEstimate(
            flops=10 * length * model * channels, bytes_accessed=300 * 2**20, transcendentals=0
        ),
        name="back",
    )(
        dg, *res, x, bc, step, prev, zw, xw, bcw, dtw, out_part, out_own,
        gain_grad, convw, alog, skip,
    )
    return (
        z.reshape(model, channels), xg.reshape(model, channels), o.reshape(channels, model),
        bcg.reshape(model, wide), small, own,
    )


def finish_kernel(
    z_ref, x_ref, o_ref, bc_ref, small_ref, own_ref, tok_ref, cot_ref, pre_ref, out_ref,
    zf_ref, xf_ref, of_ref, bcf_ref, dt_ref, grad_ref, outf_ref, convw_ref, convb_ref, skip_ref, gain_ref, pre_out, dtb_ref, alog_ref,
):
    zf_ref[...] = z_ref[...].astype(F32)
    xf_ref[...] = x_ref[...].astype(F32)
    of_ref[...] = o_ref[...].astype(F32)
    width = bcf_ref.shape[1]
    heads = dt_ref.shape[0]
    outf_ref[...] = out_ref[...]
    bcf_ref[...] = bc_ref[:, :width].astype(F32)
    dt_ref[...] = bc_ref[:, width : width + 128].astype(F32).T[:heads]
    tok = tok_ref[...].astype(F32)
    recip = lax.rsqrt(jnp.mean(tok * tok, axis=-1, keepdims=True) + EPSILON)
    scaled = pre_ref[...] * own_ref[...]
    mean = jnp.mean(tok * scaled, axis=-1, keepdims=True)
    passed = sum(cot_ref[w].astype(F32) for w in range(4))
    grad_ref[...] = (passed + recip * scaled - tok * recip**3 * mean).astype(BF16)

    @pl.when(pl.program_id(0) == 0)
    def _():
        groups = small_ref.shape[0] // 4
        channels = small_ref.shape[1]
        convw_ref[...] = small_ref[8:12, :]
        convb_ref[...] = small_ref[12:13, :]
        skip_ref[...] = small_ref[13:14, :]
        me = lax.axis_index("head")
        gain = small_ref[0:1, :]
        for j in range(1, groups):
            gain = jnp.where(me == j, small_ref[j : j + 1, :], gain)
        gain_ref[...] = gain
        for j in range(pre_out.shape[1] // channels):
            cols = slice(j * channels, (j + 1) * channels)
            pre_out[:, cols] = small_ref[groups + j : groups + j + 1, :] / pre_ref[:, cols]
        dtb_ref[...] = small_ref[14:15, 0:heads]
        alog_ref[...] = small_ref[14:15, heads : 2 * heads]


def finish_call(z, x, o, bc, small, own, tok, cot, pre_gain, out, heads):
    model, channels = z.shape
    rows_num = tok.shape[0]
    steps = 16
    wide = bc.shape[1]
    rows = lambda r, w: pl.BlockSpec((r // steps, w), lambda i: (i, 0))
    fixed = lambda shape: pl.BlockSpec(shape, lambda i: (0, 0))
    shapes = [
        ((model, channels), F32), ((model, channels), F32), ((channels, model), F32), ((model, wide - 128), F32),
    ]
    wide4 = pl.BlockSpec((4, rows_num // steps, model), lambda i: (0, i, 0))
    flat = [(4, channels), (1, channels), (1, channels), (1, channels), (1, model), (1, heads), (1, heads)]
    return pl.pallas_call(
        finish_kernel,
        grid=(steps,),
        in_specs=[
            rows(model, channels), rows(model, channels), rows(channels, model), rows(model, wide),
            fixed(small.shape), rows(rows_num, model), rows(rows_num, model),
            wide4, fixed((1, model)), wide4,
        ],
        out_specs=[rows(*shape) for shape, _ in shapes]
        + [pl.BlockSpec((heads, model // steps), lambda i: (0, i)), rows(rows_num, model), wide4]
        + [fixed(shape) for shape in flat],
        out_shape=[jax.ShapeDtypeStruct(shape, t) for shape, t in shapes]
        + [
            jax.ShapeDtypeStruct((heads, model), F32), jax.ShapeDtypeStruct((rows_num, model), BF16),
            jax.ShapeDtypeStruct(out.shape, BF16),
        ]
        + [jax.ShapeDtypeStruct(shape, F32) for shape in flat],
        compiler_params=pltpu.CompilerParams(vmem_limit_bytes=VMEM_BYTES),
        cost_estimate=pl.CostEstimate(flops=0, bytes_accessed=46 * 2**20, transcendentals=0),
        name="finish",
    )(z, x, o, bc, small, own, tok, cot, pre_gain[None], out)


def per_device(
    tokens, z_weight, x_weight, bc_weight, dt_weight, conv_weight, conv_bias, dt_bias,
    a_log, skip, norm_gain, pre_gain, out_weight, cotangent,
):
    groups = lax.axis_size("head")
    batches = lax.axis_size("batch")
    _, own_len, model = tokens.shape
    tokens = tokens[0]
    cot = cotangent[:, 0]
    channels = z_weight.shape[1]
    heads = dt_weight.shape[1]
    dtw = dt_weight.T
    alog = a_log[None]
    skip_r = skip[None]
    x, res, bc, step, prev, gated, w_all, gain_all = front_call(
        tokens, pre_gain, z_weight, x_weight, bc_weight, dtw, out_weight, norm_gain,
        conv_weight, conv_bias[None], dt_bias[None], alog, skip_r, groups, batches,
    )
    outputs, d_gated, out_own, out_part, gain_grad = middle_call(gated, w_all, gain_all, tokens, cot, batches)
    z_grad, x_grad, out_grad, bcdt_grad, small, d_own = back_call(
        d_gated, res, x, bc, step, prev, z_weight, x_weight, bc_weight, dtw, out_part, out_own, gain_grad,
        conv_weight, alog, skip_r, groups, batches,
    )
    (
        z_grad, x_grad, out_grad, bc_grad, dt_grad, tokens_grad, outputs, convw, convb, skip_g, gain_g, pre_g, dtb_g, alog_g,
    ) = finish_call(z_grad, x_grad, out_grad, bcdt_grad, small, d_own, tokens, cot, pre_gain, outputs, heads)
    flat = lambda v: v.reshape(-1)
    return (
        outputs[:, None], tokens_grad[None], z_grad, x_grad, bc_grad, dt_grad.T, convw, flat(convb), flat(dtb_g),
        flat(alog_g), flat(skip_g), flat(gain_g), flat(pre_g), out_grad,
    )


def solution(mesh):
    head_cols = P(None, "head")
    rows4 = P(None, "batch", "head", None)
    return jax.shard_map(
        per_device,
        mesh=mesh,
        in_specs=(
            P("batch", "head", None), head_cols, head_cols, P(), head_cols, head_cols, P("head"),
            P("head"), P("head"), P("head"), P("head"), P(), P("head", None), rows4,
        ),
        out_specs=(
            rows4, P("batch", "head", None), head_cols, head_cols, P(), head_cols, head_cols,
            P("head"), P("head"), P("head"), P("head"), P("head"), P(), P("head", None),
        ),
        check_vma=False,
    )
```

```python
import functools
import itertools

import jax
import jax.numpy as jnp
from jax import lax
from jax.experimental import pallas as pl
from jax.experimental.pallas import tpu as pltpu
from jax.sharding import PartitionSpec as P

SPAN = 128
HEAD_PARTS = 2
ROW_CHUNKS = 4
BACK_PARTS = 1
X_STREAMS = 4
EPSILON = 1e-05
BF16 = jnp.bfloat16
F32 = jnp.float32
HIGHEST = lax.Precision.HIGHEST
VMEM_BYTES = 60 * 1024 * 1024
BACK_VMEM_BYTES = 63 * 1024 * 1024


def mm(a, b):
    return lax.dot_general(a, b, (((1,), (0,)), ((), ())), preferred_element_type=F32)


def mm_nt(a, b):
    return lax.dot_general(a, b, (((1,), (1,)), ((), ())), preferred_element_type=F32)


def mm_tn(a, b):
    return lax.dot_general(a, b, (((0,), (0,)), ((), ())), preferred_element_type=F32)


def mm_exact(a, b):
    return lax.dot_general(
        a, b, (((1,), (0,)), ((), ())), preferred_element_type=F32, precision=HIGHEST
    )


def lower_mask(shape):
    return lax.broadcasted_iota(jnp.int32, shape, 0) >= lax.broadcasted_iota(jnp.int32, shape, 1)


def softplus(v):
    return jnp.maximum(v, 0.0) + jnp.log1p(jnp.exp(-jnp.abs(v)))


def sigmoid(v):
    return 1.0 / (1.0 + jnp.exp(-v))


def pair_columns(values, pair, left):
    shape = (SPAN, 128)
    one = jnp.broadcast_to(values[:, 2 * pair : 2 * pair + 1], shape)
    two = jnp.broadcast_to(values[:, 2 * pair + 1 : 2 * pair + 2], shape)
    return one, two, jnp.where(left, one, two)


def segments(channels):
    ends = [channels * 2**w // 8 for w in range(4)]
    return list(zip([0] + ends[:-1], ends))


def partner(axis, bit):
    me = lax.axis_index(axis)
    return me + (1 - 2 * ((me // 2**bit) % 2)) * 2**bit


def bits_of(axis, count):
    me = lax.axis_index(axis)
    return [(me // 2**b) % 2 for b in range(count)]


def log2(value):
    return value.bit_length() - 1


def place(bits, fixed):
    bits = range(bits) if isinstance(bits, int) else sorted(bits)
    return tuple(fixed[b] if b in fixed else slice(None) for b in reversed(bits))


class Links:
    def __init__(self, send, recv):
        self.send, self.recv, self.used = send, recv, 0

    def copy(self, src, dst, axis, to):
        at = self.used
        self.used += 1
        return pltpu.make_async_remote_copy(
            src_ref=src, dst_ref=dst, send_sem=self.send.at[at], recv_sem=self.recv.at[at],
            device_id={axis: to}, device_id_type=pl.DeviceIdType.MESH,
        )


def meet(peers):
    barrier = pltpu.get_barrier_semaphore()
    for axis, to in peers:
        pl.semaphore_signal(barrier, inc=1, device_id={axis: to}, device_id_type=pl.DeviceIdType.MESH)
    pl.semaphore_wait(barrier, len(peers))


def add_block(buf, index, slot, at):
    rows = slot.shape[-2]
    step = min(rows, 32)
    index = index + (slice(None),) * (len(buf.shape) - len(index))
    free = [i for i, v in enumerate(index[:-2]) if isinstance(v, slice)]
    full = list(index[:-2])
    for i, v in zip(free, at):
        full[i] = v
    full = tuple(full)

    def piece(r, carry):
        rs = pl.ds(pl.multiple_of(r * step, step), step)
        total = buf[full + (rs, index[-1])].astype(F32) + slot[tuple(at) + (rs, slice(None))].astype(F32)
        buf[full + (rs, index[-1])] = total.astype(buf.dtype)
        return carry

    lax.fori_loop(0, rows // step, piece, 0)


def halving_slots(count, block, dtype):
    return [pltpu.VMEM((2,) * (count - 1 - i) + tuple(block), dtype) for i in range(count)]


class Stream:
    def __init__(self, *parts):
        self.steps = []
        for part in parts:
            if self.steps and part:
                last, first = self.steps.pop(), part[0]
                self.steps.append(lambda last=last, first=first: (last(), first()))
                part = part[1:]
            self.steps.extend(part)

    def advance(self):
        if self.steps:
            self.steps.pop(0)()


def advance_all(streams):
    for s in streams:
        s.advance()


def drain(streams):
    while any(s.steps for s in streams):
        advance_all(streams)


def exchanging_once(ports, axis, bits, buf, slots):
    def to(k):
        return lax.axis_index(axis) + sum(
            (1 - 2 * b) * 2**i for i, b in enumerate(bits_of(axis, bits)) if k & 2**i
        )

    copies = [
        ports.make(buf, lambda k=k: slots[k - 1], axis, lambda k=k: to(k)) for k in range(1, 2**bits)
    ]

    def start():
        for copy in copies:
            copy().start()

    def finish():
        for copy in copies:
            copy().wait()
        ref = buf()
        ref[...] = (ref[...].astype(F32) + sum(slot[...].astype(F32) for slot in slots)).astype(ref.dtype)

    return [start, finish]


class Ports:
    def __init__(self, send, recv):
        self.send, self.recv, self.used = send, recv, 0

    def make(self, src, dst, axis, to):
        at = self.used
        self.used += 1

        def describe():
            return pltpu.make_async_remote_copy(
                src_ref=src(), dst_ref=dst(), send_sem=self.send.at[at], recv_sem=self.recv.at[at],
                device_id={axis: to()}, device_id_type=pl.DeviceIdType.MESH,
            )

        return describe


def linked(copies, work):
    steps = []
    for i in range(len(copies) + 1):
        def step(i=i):
            if i:
                copies[i - 1]().wait()
                work(i - 1)
            if i < len(copies):
                copies[i]().start()

        steps.append(step)
    return steps


def halving(ports, axis, buf, slots, order):
    count = len(order)

    def fixed(i, give):
        mine = bits_of(axis, max(order) + 1)
        out = {b: mine[b] for b in order[: i + 1]}
        if give:
            out[order[i]] = 1 - out[order[i]]
        return out

    copies = [
        ports.make(
            lambda i=i: buf().at[place(order, fixed(i, True))], lambda i=i: slots[i],
            axis, lambda i=i: partner(axis, order[i]),
        )
        for i in range(count)
    ]

    def work(i):
        for at in itertools.product(*(range(d) for d in slots[i].shape[:-2])):
            add_block(buf(), place(order, fixed(i, False)), slots[i], at)

    return linked(copies, work)


def spreading(ports, axis, view, order, own, sem):
    count = len(order)

    def at(i):
        mine = bits_of(axis, count)
        return view().at[place(count, {b: mine[b] for b in order[i:]})]

    copies = [
        ports.make(
            (lambda i=i: at(i)) if i else own, lambda i=i: at(i), axis, lambda i=i: partner(axis, order[i])
        )
        for i in range(count)
    ]

    def kept():
        return pltpu.make_async_copy(own(), at(0), sem)

    def work(i):
        if i == 0:
            kept().wait()

    steps = linked(copies, work)
    first = steps[0]
    steps[0] = lambda: (kept().start(), first())
    return steps


def exchanging(ports, axis, buf, slots, order):
    copies = [
        ports.make(buf, lambda i=i: slots[i], axis, lambda i=i: partner(axis, order[i])) for i in range(len(order))
    ]

    def work(i):
        ref = buf()
        ref[...] = (ref[...].astype(F32) + slots[i][...].astype(F32)).astype(ref.dtype)

    return linked(copies, work)


PIECE_POLLS = (
    ("a", 0), ("a", 1), ("c", 2), ("c", 0), ("d", 1), ("e", 0), (1, 1), (2, 2), (3, 0), (4, 1), (5, 2), (7, 2),
)


def front_kernel(
    count, tok_ref, pre_ref, zw_hbm, xw_hbm, bcw_hbm, dtw_hbm, w_hbm, gain_hbm,
    convw_ref, convb_ref, dtb_ref, alog_ref, skip_ref,
    x_out, a_out, s_out, act_out, dsc_out, inn_out, bc_out, step_out, prev_out, gated_out, all_ref, gains_ref,
    xs, zw, xw, bcw, dtw, wv, gate_s, a_s, s_s, act_s, dsc_s, inn_s, inner_s, bc_s, bcb_s, step_s, prev_s, gated_s, state, tails,
    cum_s, cum_t_s, inner_prod_s, b_t_s, pad_s, load_sem, local_sem, store_sem, away_sem, here_sem, send, recv, send2, recv2,
):
    rows_num, channels = gated_s.shape[1:]
    groups = gated_s.shape[0]
    length = groups * rows_num
    n = state.shape[0]
    model = tok_ref.shape[1]
    chunks = 2
    chunk = rows_num // chunks
    me = lax.axis_index("head")
    hi, lo = me // 2, me % 2
    near = partner("head", 0)
    far = partner("head", 1)
    others = [near, far, near + far - me]
    links = Links(send, recv)

    loads = [
        pltpu.make_async_copy(src, dst, load_sem.at[i])
        for i, (src, dst) in enumerate(((zw_hbm, zw), (xw_hbm, xw), (bcw_hbm, bcw), (dtw_hbm, dtw), (w_hbm, wv)))
    ]
    for load in loads:
        load.start()
    tok = tok_ref[...].astype(F32)
    recip = lax.rsqrt(jnp.mean(tok * tok, axis=-1, keepdims=True) + EPSILON)
    xs[hi, lo] = (tok * recip * pre_ref[...]).astype(BF16)
    meet([("head", z) for z in others] + [("batch", partner("batch", b)) for b in range(count)])

    own_rows = xs.at[hi, lo]
    to_far = []
    for c in range(chunks):
        part = xs.at[hi, lo, pl.ds(c * chunk, chunk)]
        to_far.append(links.copy(part, part, "head", far))
        to_far[-1].start()
    to_near = links.copy(own_rows, own_rows, "head", near)
    to_near.start()
    half = w_hbm.shape[-1] // 2

    def pieces(z, cols, order):
        def own_piece(ref):
            return ref.at[place(count, dict(enumerate(bits_of("batch", count)))) + (slice(None), cols)]

        first = ports.make(
            lambda: own_piece(w_hbm), lambda: own_piece(all_ref.at[lax.axis_index("head")]), "head", z
        )

        def at(i):
            bits = bits_of("batch", count)
            return all_ref.at[(z(),) + place(count, {b: bits[b] for b in order[i:]}) + (slice(None), cols)]

        rest = [
            ports.make(lambda i=i: at(i), lambda i=i: at(i), "batch", lambda i=i: partner("batch", order[i]))
            for i in range(count)
        ]
        return Stream(linked([first] + rest, lambda i: None))

    up = list(range(1, count))
    ports = Ports(send2, recv2)
    near_at = lambda: partner("head", 0)
    far_at = lambda: partner("head", 1)
    streams = []
    for z in (near_at, far_at, lambda: near_at() + far_at() - lax.axis_index("head")):
        streams.append(pieces(z, pl.ds(0, half), up + [0]))
        streams.append(pieces(z, pl.ds(half, half), up[::-1] + [0]))
    plan = [[] for _ in range(HEAD_PARTS * groups)]
    early = {spot: [] for spot in "abcde"}
    for spot, group in PIECE_POLLS:
        for st in streams[2 * group : 2 * group + 2]:
            if st.steps:
                (early[spot] if spot in early else plan[spot]).append(st.steps.pop(0))

    def poll(spot):
        for action in early[spot]:
            action()

    poll("a")
    keep = [pltpu.make_async_copy(gain_hbm, gains_ref.at[me], local_sem.at[1])]
    keep[0].start()
    inner_s[0:8, :] = jnp.zeros((8, channels), F32)
    state[...] = jnp.zeros_like(state)
    step_s[...] = jnp.zeros_like(step_s)
    pad_s[...] = jnp.zeros_like(pad_s)
    pad_s[0:1, 0 : dtw.shape[0]] = dtb_ref[...]
    pad_s[1:2, 0 : dtw.shape[0]] = alog_ref[...]
    for load in loads:
        load.wait()
    keep.append(pltpu.make_async_copy(wv, all_ref.at[me], local_sem.at[0]))
    keep[-1].start()

    def project(at_hi, at_lo):
        first = pl.multiple_of((2 * at_hi + at_lo) * rows_num, rows_num)
        rows = pl.ds(first, rows_num)
        inner_rows = pl.ds(pl.multiple_of(first + 8, 8), rows_num)
        tile = 256

        def columns(t, carry):
            cols = pl.ds(pl.multiple_of(t * tile, tile), tile)
            x = xs[at_hi, at_lo]
            gate_s[rows, cols] = mm(x, zw[:, cols])
            inner_s[inner_rows, cols] = mm(x, xw[:, cols])
            return carry

        lax.fori_loop(0, channels // tile, columns, 0)
        x = xs[at_hi, at_lo]
        bc_s[rows, :] = mm(x, bcw[...])
        step_s[rows, 0 : dtw.shape[0]] = mm_nt(x, dtw[...])

    project(hi, lo)
    to_near.wait()
    project(hi, 1 - lo)
    poll("b")
    onward = []
    for c in range(chunks):
        to_far[c].wait()
        part = xs.at[1 - hi, lo, pl.ds(c * chunk, chunk)]
        onward.append(links.copy(part, part, "head", near))
        onward[-1].start()

    poll("c")
    gain_sends = [links.copy(gain_hbm, gains_ref.at[me], "head", z) for z in others]
    for item in gain_sends:
        item.start()

    project(1 - hi, lo)
    poll("d")
    for item in onward:
        item.wait()
    project(1 - hi, 1 - lo)
    poll("e")

    rate = -jnp.exp(pad_s[1:2, :])
    lower = lower_mask((SPAN, SPAN))
    lower_f = lower.astype(F32)
    left = lax.broadcasted_iota(jnp.int32, (SPAN, 128), 1) < 64

    span_num = channels // HEAD_PARTS

    def block(at, part):
        first = pl.multiple_of(at * SPAN, SPAN)
        rows = pl.ds(first, SPAN)
        if part == 0:
            delta = softplus(step_s[rows, :] + pad_s[0:1, :])
            cum = mm_exact(lower_f, delta * rate)
            cum_t = cum.T
            bcb_s[rows, :] = bc_s[rows, :].astype(BF16)
            inner = jnp.where(lower, mm_nt(bcb_s[rows, n:], bcb_s[rows, :n]), 0.0)
            b_t = bc_s[rows, :n].T.astype(BF16)
            step_s[rows, :] = delta
            cum_s[at], cum_t_s[at], inner_prod_s[at], b_t_s[at] = cum, cum_t, inner, b_t
        else:
            delta = step_s[rows, :]
            cum, cum_t, inner, b_t = cum_s[at], cum_t_s[at], inner_prod_s[at], b_t_s[at]
        span_cols = pl.ds(part * span_num, span_num)
        before = state[:, span_cols].astype(BF16)
        prev_s[at, :, span_cols] = before
        across = mm(bcb_s[rows, n:], before)
        quarter = at // (rows_num // SPAN)
        sub = pl.ds(pl.multiple_of((at % (rows_num // SPAN)) * SPAN, SPAN), SPAN)
        for pair in range(part * span_num // 128, (part + 1) * span_num // 128):
            cols = slice(pair * 128, pair * 128 + 128)
            local = slice(pair * 128 - part * span_num, pair * 128 + 128 - part * span_num)
            c0, c1, ce = pair_columns(cum, pair, left)
            _, _, de = pair_columns(delta, pair, left)
            tot = ce[SPAN - 1 : SPAN, :]
            window = inner_s[pl.ds(first, SPAN + 8), cols]
            conv_p = convb_ref[:, cols] + sum(
                convw_ref[k : k + 1, cols] * window[5 + k : 5 + k + SPAN] for k in range(4)
            )
            inn_s[rows, cols] = window[8:].astype(BF16)
            sc = sigmoid(conv_p)
            act = conv_p * sc
            act_s[rows, cols] = act.astype(BF16)
            dsc_s[rows, cols] = (sc + act * (1.0 - sc)).astype(BF16)
            u = act * de
            tails[:, local] = (u * jnp.exp(tot - ce)).astype(BF16)
            u0 = jnp.where(left, u, 0.0).astype(BF16)
            u1 = jnp.where(left, 0.0, u).astype(BF16)
            p0 = (jnp.exp(jnp.minimum(c0 - cum_t[2 * pair : 2 * pair + 1, :], 0.0)) * inner).astype(BF16)
            p1 = (jnp.exp(jnp.minimum(c1 - cum_t[2 * pair + 1 : 2 * pair + 2, :], 0.0)) * inner).astype(BF16)
            within = mm(jnp.concatenate([p0, p1], axis=1), jnp.concatenate([u0, u1], axis=0))
            y = within + across[:, local] * jnp.exp(ce) + skip_ref[:, cols] * act
            gate = gate_s[rows, cols]
            sg = sigmoid(gate)
            sl = gate * sg
            s_s[rows, cols] = sl.astype(BF16)
            a_s[rows, cols] = (y * (sg + sl * (1.0 - sg))).astype(BF16)
            gated_s[quarter, sub, cols] = (y * sl).astype(BF16)
            state[:, cols] = state[:, cols] * jnp.exp(tot)
        state[:, span_cols] += mm(b_t, tails[...])

    def leave(q, part):
        cols = pl.ds(part * span_num, span_num)
        return pltpu.make_async_remote_copy(
            src_ref=gated_s.at[q, :, cols], dst_ref=gated_out.at[me, :, cols],
            send_sem=away_sem.at[part, q], recv_sem=here_sem.at[part, me],
            device_id={"head": q}, device_id_type=pl.DeviceIdType.MESH,
        )

    def arrive(q, part):
        cols = pl.ds(part * span_num, span_num)
        return pltpu.make_async_remote_copy(
            src_ref=gated_s.at[q, :, cols], dst_ref=gated_out.at[q, :, cols],
            send_sem=away_sem.at[part, q], recv_sem=here_sem.at[part, q],
            device_id={"head": q}, device_id_type=pl.DeviceIdType.MESH,
        )

    subs = rows_num // SPAN

    def stores(q):
        rows = pl.ds(pl.multiple_of(q * rows_num, rows_num), rows_num)
        pairs = (
            (xs.at[q // 2, q % 2], x_out.at[rows]),
            (a_s.at[rows], a_out.at[rows]),
            (s_s.at[rows], s_out.at[rows]),
            (act_s.at[rows], act_out.at[rows]),
            (dsc_s.at[rows], dsc_out.at[rows]),
            (inn_s.at[rows], inn_out.at[rows]),
            (bcb_s.at[rows], bc_out.at[rows]),
            (step_s.at[rows], step_out.at[rows]),
            (prev_s.at[pl.ds(q * subs, subs)], prev_out.at[pl.ds(q * subs, subs)]),
        )
        return [pltpu.make_async_copy(src, dst, store_sem.at[i, q]) for i, (src, dst) in enumerate(pairs)]

    for part in range(HEAD_PARTS):
        def quarter_step(q, carry):
            def one(at, inner_carry):
                block(at, part)
                return inner_carry

            lax.fori_loop(q * subs, (q + 1) * subs, one, 0)

            @pl.when(q != me)
            def _():
                leave(q, part).start()

            if part == HEAD_PARTS - 1:
                for item in stores(q):
                    item.start()
            for k in range(groups):
                @pl.when(q == k)
                def _():
                    for action in plan[part * groups + k]:
                        action()
            return carry

        lax.fori_loop(0, groups, quarter_step, 0)
    stay = pltpu.make_async_copy(gated_s.at[me], gated_out.at[me], local_sem.at[2])
    stay.start()
    drain(streams)
    for item in gain_sends:
        item.wait()
    for item in keep:
        item.wait()
    stay.wait()

    def finish(q, carry):
        @pl.when(q != me)
        def _():
            for part in range(HEAD_PARTS):
                leave(q, part).wait_send()
                arrive(q, part).wait_recv()

        for item in stores(q):
            item.wait()
        return carry

    lax.fori_loop(0, groups, finish, 0)


def front_call(tokens, pre_gain, zw, xw, bcw, dtw, out_weight, norm_gain, convw, convb, dtb, alog, skip, groups, batches):
    rows_num, model = tokens.shape
    channels = zw.shape[1]
    n = bcw.shape[1] // 2
    length = rows_num * groups
    count = log2(batches)
    part = channels // batches
    copies = 5 + groups - 1
    piece_copies = 2 * (groups - 1) * (1 + count)
    hbm = pl.BlockSpec(memory_space=pl.ANY)
    vmem = pl.BlockSpec(memory_space=pltpu.VMEM)
    wide = jax.ShapeDtypeStruct((length, channels), BF16)
    outs = [
        jax.ShapeDtypeStruct((length, model), BF16), wide, wide, wide, wide, wide,
        jax.ShapeDtypeStruct((length, 2 * n), BF16),
        jax.ShapeDtypeStruct((length, 128), F32),
        jax.ShapeDtypeStruct((length // SPAN, n, channels), BF16),
        jax.ShapeDtypeStruct((groups, rows_num, channels), BF16),
        jax.ShapeDtypeStruct((groups,) + (2,) * count + (part, model), BF16),
        jax.ShapeDtypeStruct((groups, 1, channels), F32),
    ]
    dma = pltpu.SemaphoreType.DMA
    result = pl.pallas_call(
        functools.partial(front_kernel, count),
        in_specs=[vmem, vmem] + [hbm] * 6 + [vmem] * 5,
        out_specs=[hbm] * len(outs),
        out_shape=outs,
        scratch_shapes=[
            pltpu.VMEM((2, 2, rows_num, model), BF16),
            pltpu.VMEM(zw.shape, BF16), pltpu.VMEM(xw.shape, BF16),
            pltpu.VMEM(bcw.shape, BF16), pltpu.VMEM(dtw.shape, BF16),
            pltpu.VMEM((2,) * count + (part, model), BF16),
            pltpu.VMEM((length, channels), F32),
            pltpu.VMEM((length, channels), BF16), pltpu.VMEM((length, channels), BF16),
            pltpu.VMEM((length, channels), BF16), pltpu.VMEM((length, channels), BF16),
            pltpu.VMEM((length, channels), BF16), pltpu.VMEM((length + 8, channels), F32),
            pltpu.VMEM((length, 2 * n), F32), pltpu.VMEM((length, 2 * n), BF16),
            pltpu.VMEM((length, 128), F32), pltpu.VMEM((length // SPAN, n, channels), BF16),
            pltpu.VMEM((groups, rows_num, channels), BF16),
            pltpu.VMEM((n, channels), F32), pltpu.VMEM((SPAN, channels // HEAD_PARTS), BF16),
            pltpu.VMEM((length // SPAN, SPAN, 128), F32), pltpu.VMEM((length // SPAN, 128, SPAN), F32),
            pltpu.VMEM((length // SPAN, SPAN, SPAN), F32), pltpu.VMEM((length // SPAN, n, SPAN), BF16),
            pltpu.VMEM((8, 128), F32),
            dma((5,)), dma((3,)), dma((9, groups)), dma((HEAD_PARTS, groups)), dma((HEAD_PARTS, groups)), dma((copies,)), dma((copies,)),
            dma((piece_copies,)), dma((piece_copies,)),
        ],
        compiler_params=pltpu.CompilerParams(
            collective_id=1, has_side_effects=True, vmem_limit_bytes=VMEM_BYTES
        ),
        cost_estimate=pl.CostEstimate(
            flops=4 * length * model * channels, bytes_accessed=400 * 2**20, transcendentals=0
        ),
        name="front",
    )(
        tokens, pre_gain[None], zw, xw, bcw, dtw, out_weight.reshape((2,) * count + (part, model)),
        norm_gain[None], convw, convb, dtb, alog, skip,
    )
    x, a, s, act, dsc, inn, bc, step, prev, gated, w_all, gains = result
    return x, (a, s, act, dsc, inn), bc, step, prev, gated, w_all.reshape(groups, channels, model), gains


def middle_kernel(
    count, g_hbm, w_hbm, cot_hbm, gain_ref, tok_ref,
    out_hbm, dg_out, own_ref, part_ref, ggrad_ref,
    g_s, w_s, cot_s, dy_s, gg_s, out_s, dg_s, give_s, kept_s, obuf, oslot0, oslot1, *refs,
):
    slots = [refs[i * (count - 1) : (i + 1) * (count - 1)] for i in range(4)]
    load_sem, store_sem, away_sem, here_sem, send, recv = refs[4 * (count - 1) :]
    groups, rows_num, channels = g_s.shape
    model = tok_ref.shape[1]
    part, half = kept_s.shape[-2:]
    pairs_num = groups // 2
    segs = segments(channels)
    tile = 512
    tiles = model // tile
    me = lax.axis_index("head")

    def w_load(t):
        cols = pl.ds(pl.multiple_of(t * tile, tile), tile)
        return pltpu.make_async_copy(w_hbm.at[:, :, cols], w_s.at[:, :, cols], load_sem.at[2 + t])

    loads = [
        pltpu.make_async_copy(g_hbm, g_s, load_sem.at[0]), pltpu.make_async_copy(cot_hbm, cot_s, load_sem.at[1]),
    ]
    for load in loads:
        load.start()
    for t in range(tiles):
        w_load(t).start()
    loads[0].wait()
    sums = [jnp.zeros((rows_num, 1), F32) for _ in segs]
    for j in range(groups):
        for w, (lo, hi) in enumerate(segs):
            g = g_s[j, :, lo:hi].astype(F32)
            gg_s[j, :, lo:hi] = (g * gain_ref[j, 0:1, lo:hi]).astype(BF16)
            sums[w] += jnp.sum(g * g, axis=1, keepdims=True)
    recips = []
    total = jnp.zeros((rows_num, 1), F32)
    for w, (lo, hi) in enumerate(segs):
        total = total + sums[w]
        recips.append(lax.rsqrt(total / (hi * groups) + EPSILON))
    meet(
        [("batch", partner("batch", b)) for b in range(count)]
        + [("head", z) for z in (partner("head", 0), partner("head", 1), partner("head", 0) + partner("head", 1) - me)]
    )
    loads[1].wait()

    def out_store(t):
        cols = pl.ds(pl.multiple_of(t * tile, tile), tile)
        return pltpu.make_async_copy(out_s.at[:, :, cols], out_hbm.at[:, :, cols], store_sem.at[t])

    def forward(t, dots):
        cols = pl.ds(pl.multiple_of(t * tile, tile), tile)
        w_load(t).wait()
        acc = jnp.zeros((rows_num, tile), F32)
        tok = tok_ref[:, cols].astype(F32)
        new = []
        for w, (lo, hi) in enumerate(segs):
            acc += mm(
                jnp.concatenate([gg_s[j, :, lo:hi] for j in range(groups)], axis=1),
                jnp.concatenate([w_s[j, lo:hi, cols] for j in range(groups)], axis=0),
            )
            out_s[w, :, cols] = (tok + recips[w] * acc).astype(BF16)
            new.append(dots[w] + jnp.sum(cot_s[w, :, cols].astype(F32) * acc, axis=1, keepdims=True))
        out_store(t).start()
        return tuple(new)

    def combine(t, carry):
        cols = pl.ds(pl.multiple_of(t * tile, tile), tile)
        combined = jnp.zeros((rows_num, tile), F32)
        for w in reversed(range(4)):
            combined += recips[w] * cot_s[w, :, cols].astype(F32)
            dy_s[w, :, cols] = combined.astype(BF16)
        return carry

    lax.fori_loop(0, tiles, combine, 0)

    def leave(j):
        return pltpu.make_async_remote_copy(
            src_ref=dg_s.at[j], dst_ref=dg_out.at[me], send_sem=away_sem.at[j], recv_sem=here_sem.at[me],
            device_id={"head": j}, device_id_type=pl.DeviceIdType.MESH,
        )

    def arrive(j):
        return pltpu.make_async_remote_copy(
            src_ref=dg_s.at[j], dst_ref=dg_out.at[j], send_sem=away_sem.at[j], recv_sem=here_sem.at[j],
            device_id={"head": j}, device_id_type=pl.DeviceIdType.MESH,
        )

    def back(k, carry):
        j = (me + 1 + k) % groups
        for w, (lo, hi) in enumerate(segs):
            dn = mm_nt(dy_s[w], w_s[j, lo:hi, :])
            g = g_s[j, :, lo:hi].astype(F32)
            ggrad_ref[j, :, lo:hi] = jnp.sum(g * dn, axis=0, keepdims=True)
            dg_s[j, :, lo:hi] = (gain_ref[j, 0:1, lo:hi] * dn - g * scales[w]).astype(BF16)

        @pl.when(j != me)
        def _():
            leave(j).start()

        return carry

    ports = Ports(send, recv)
    up = list(range(1, count))
    core = bits_of("batch", 1)[0]

    def upper_index(p):
        return tuple((p >> b) & 1 for b in reversed(range(1, count)))

    def terms(s, bit, use):
        g0, c0 = (s % 2) * pairs_num, (s // 2) * half
        if part % 128 == 0:
            for q in range(2 ** (count - 1)):
                at = pl.ds(pl.multiple_of((2 * q + bit) * part, part), part)
                left = jnp.concatenate([gg_s[g0 + j, :, at] for j in range(pairs_num)], axis=1)
                owners = [[w for w, (lo, hi) in enumerate(segs) if lo <= (2 * q + c) * part < hi][0] for c in range(2)]
                w = owners[0] + (owners[1] - owners[0]) * bit
                term = mm_tn(left, dy_s[w, :, c0 : c0 + half])
                for j in range(pairs_num):
                    use(upper_index(2 * q), j, term[j * part : (j + 1) * part])
            return
        for j in range(pairs_num):
            for w, (lo, hi) in enumerate(segs):
                term = mm_tn(gg_s[g0 + j, :, lo:hi], dy_s[w, :, c0 : c0 + half])
                for p in range(lo // part, hi // part):
                    @pl.when(bit == p % 2)
                    def _():
                        use(upper_index(p), j, term[p * part - lo : (p + 1) * part - lo])

    def to_core(s):
        return pltpu.make_async_remote_copy(
            src_ref=give_s.at[s], dst_ref=kept_s.at[s], send_sem=send.at[s], recv_sem=recv.at[s],
            device_id={"batch": partner("batch", 0)}, device_id_type=pl.DeviceIdType.MESH,
        )

    def give(s):
        def use(index, j, rows):
            give_s[(s,) + index + (j,)] = rows.astype(BF16)

        terms(s, 1 - core, use)
        to_core(s).start()

    def keep(s):
        to_core(s).wait()

        def use(index, j, rows):
            at = (s,) + index + (j,)
            kept_s[at] = (kept_s[at].astype(F32) + rows).astype(BF16)

        terms(s, core, use)

    ports.used = 4
    streams = [
        Stream(halving(ports, "batch", lambda s=s: kept_s.at[s], slots[s], up if s % 2 == 0 else up[::-1]))
        for s in range(4)
    ]
    mine = bits_of("batch", count)
    own = place(up, {b: mine[b] for b in up})
    head_sum = Stream(halving(ports, "head", lambda: obuf, (oslot0, oslot1), [0, 1]))
    for s in range(2):
        give(s)
    for s in range(2):
        keep(s)
        streams[s].advance()
    dots = lax.fori_loop(0, tiles, forward, tuple(jnp.zeros((rows_num, 1), F32) for _ in segs))
    scales = [None] * 4
    scale = jnp.zeros((rows_num, 1), F32)
    for w in reversed(range(4)):
        scale = scale + recips[w] ** 3 * dots[w] / (segs[w][1] * groups)
        scales[w] = scale
    lax.fori_loop(0, groups, back, 0)
    stay = pltpu.make_async_copy(dg_s.at[me], dg_out.at[me], load_sem.at[0])
    stay.start()
    for s in range(2, 4):
        give(s)
    advance_all(streams[:2])
    for s in range(2, 4):
        keep(s)
        streams[s].advance()
    drain(streams[:2])
    for s in range(2):
        for j in range(pairs_num):
            obuf[s, j] = kept_s[(s,) + own + (j,)]
    head_sum.advance()
    advance_all(streams[2:])
    head_sum.advance()
    drain(streams)
    drain([head_sum])
    own_ref[...] = obuf[place(2, dict(enumerate(bits_of("head", 2))))]
    for s in range(2, 4):
        for j in range(pairs_num):
            part_ref[s - 2, j] = kept_s[(s,) + own + (j,)]
    stay.wait()

    def finish(j, carry):
        @pl.when(j != me)
        def _():
            leave(j).wait_send()
            arrive(j).wait_recv()

        return carry

    lax.fori_loop(0, groups, finish, 0)

    def stored(t, carry):
        out_store(t).wait()
        return carry

    lax.fori_loop(0, tiles, stored, 0)


def middle_call(g, w_all, gain, tok, cot, batches):
    groups, rows_num, channels = g.shape
    model = tok.shape[1]
    count = log2(batches)
    part = channels // batches
    half = model // 2
    block = (groups // 2, part, half)
    hbm = pl.BlockSpec(memory_space=pl.ANY)
    vmem = pl.BlockSpec(memory_space=pltpu.VMEM)
    dma = pltpu.SemaphoreType.DMA
    wide = pltpu.VMEM((groups, rows_num, channels), BF16)
    tall = pltpu.VMEM((4, rows_num, model), BF16)
    halves = pltpu.VMEM((4,) + (2,) * (count - 1) + block, BF16)
    return pl.pallas_call(
        functools.partial(middle_kernel, count),
        in_specs=[hbm] * 3 + [vmem] * 2,
        out_specs=[hbm, hbm, vmem, vmem, vmem],
        out_shape=[
            jax.ShapeDtypeStruct((4, rows_num, model), BF16),
            jax.ShapeDtypeStruct(g.shape, BF16),
            jax.ShapeDtypeStruct((part, half), BF16),
            jax.ShapeDtypeStruct((2, 2, part, half), BF16),
            jax.ShapeDtypeStruct((groups, 1, channels), F32),
        ],
        scratch_shapes=[
            wide, pltpu.VMEM((groups, channels, model), BF16), tall, tall, wide, tall, wide, halves, halves,
            pltpu.VMEM((2, 2, part, half), BF16), pltpu.VMEM((2, part, half), BF16), pltpu.VMEM((part, half), BF16),
        ]
        + [s for _ in range(4) for s in halving_slots(count - 1, block, BF16)]
        + [
            dma((2 + model // 512,)), dma((model // 512,)), dma((groups,)), dma((groups,)),
            dma((4 * count + 2,)), dma((4 * count + 2,)),
        ],
        compiler_params=pltpu.CompilerParams(
            collective_id=2, has_side_effects=True, vmem_limit_bytes=BACK_VMEM_BYTES
        ),
        cost_estimate=pl.CostEstimate(
            flops=6 * groups * rows_num * channels * model, bytes_accessed=200 * 2**20, transcendentals=0
        ),
        name="nested_norm",
    )(g, w_all, cot, gain, tok)


BACK_POLLS = {
    "z": ((0, 0, "a"), (0, 1, "a"), (0, 1, "b"), (0, 2, "a"), (0, 3, "a"), (0, 3, "b")),
    "out": ((0, 0, "a"), (0, 1, "a")),
    "spread": (((0, 2, "a"), (0, 2, "b"), (0, 3, "b")), ((0, 2, "a"), (0, 2, "b"), (0, 3, "b"))),
    "relay": (
        ((0, 1, "a"), 3, 0, 1), ((0, 1, "b"), 3, 1, 1), ((0, 2, "a"), 3, 2, 1), ((0, 2, "a"), 3, 3, 1),
        ((0, 1, "b"), 3, 0, 2), ((0, 2, "a"), 3, 1, 2), ((0, 2, "b"), 3, 2, 2), ((0, 3, "a"), 3, 3, 2),
        ((0, 2, "b"), 2, 0, 1), ((0, 3, "a"), 2, 1, 1), ((0, 3, "b"), 2, 2, 1),
    ),
    "tail": (1, 1, 2, 2),
}
RELAY_ORDER = [(2, c, 1) for c in range(4)] + [(1, c, 1) for c in range(4)]
RELAY_ORDER += [(0, 0, 1), (0, 1, 1), (0, 0, 2), (0, 2, 1), (0, 1, 2), (0, 3, 1), (0, 2, 2), (0, 3, 2)]


def back_kernel(
    count, group_bits,
    dg_hbm, a_hbm, s_hbm, act_hbm, dsc_hbm, inn_hbm, x_hbm, bc_hbm, step_hbm, prev_hbm,
    zw_hbm, xw_hbm, bcw_hbm, dtw_hbm, o_hbm, own_hbm, gain_ref, convw_ref, alog_ref, skip_ref,
    z_out, x_out, o_out, bc_out, small_out, own_out,
    dg, a, s, act, dsc, inn, x, bc, step, prev, zw, xw, bdw, dtw, obuf, o_first, hot_ref, pad_s,
    lam, dconv, dyc_s, vt_s, q_s, v_s, w_s, da_s, etot_s, draw_s, head_s, vec_s, pre_s, dbs,
    rows_s, line_s, last_s, zg, bcbuf, small, *refs,
):
    groups = rows_s.shape[0] * rows_s.shape[1]
    zx_slots = [refs[i * count : (i + 1) * count] for i in range(2)]
    refs = refs[2 * count :]
    bc_slots, refs = (refs[:count], refs[count : 2 * count]), refs[2 * count :]
    bc_head, refs = (refs[: groups - 1], refs[groups - 1 : 2 * (groups - 1)]), refs[2 * (groups - 1) :]
    small_slots, refs = refs[:count], refs[count:]
    small_head, refs = refs[:group_bits], refs[group_bits:]
    o_slots, refs = refs[:group_bits], refs[group_bits:]
    load_sem, store_sem, rsend, rrecv, rrecv_own, send, recv = refs
    length, channels = a.shape
    model = x.shape[1]
    n = lam.shape[0]
    heads = hot_ref.shape[0]
    rows_num = length // groups
    subs = rows_num // SPAN
    wide = bcbuf.shape[-1]
    me = lax.axis_index("head")

    pairs = [
        (dg_hbm.at[:, :, pl.ds(0, channels // 2)], dg.at[0]),
        (dg_hbm.at[:, :, pl.ds(channels // 2, channels // 2)], dg.at[1]), (a_hbm, a), (s_hbm, s), (x_hbm, x), (o_hbm, obuf), (own_hbm, o_first), (step_hbm, step), (bc_hbm, bc),
        (prev_hbm, prev), (act_hbm, act), (dsc_hbm, dsc), (inn_hbm, inn), (zw_hbm, zw), (xw_hbm, xw),
        (bcw_hbm, bdw.at[:, pl.ds(0, 2 * n)]), (dtw_hbm, dtw),
    ]
    loads = [pltpu.make_async_copy(src, dst, load_sem.at[i]) for i, (src, dst) in enumerate(pairs)]
    for load in loads:
        load.start()
    for load in loads[:4]:
        load.wait()

    def gates(i, carry):
        per = rows_num // 64
        rows = pl.ds(pl.multiple_of(i * 64, 64), 64)
        piece = dg.shape[-1]
        for h in range(dg.shape[0]):
            cols = slice(h * piece, (h + 1) * piece)
            d = dg[h, i // per, pl.ds(pl.multiple_of((i % per) * 64, 64), 64), :].astype(F32)
            a[rows, cols] = (d * a[rows, cols].astype(F32)).astype(BF16)
            s[rows, cols] = (d * s[rows, cols].astype(F32)).astype(BF16)
        return carry

    lax.fori_loop(0, length // 64, gates, 0)
    near, far = partner("head", 0), partner("head", 1)
    meet(
        [("batch", partner("batch", b)) for b in range(count)]
        + [("head", to) for to in (near, far, near + far - me)]
    )

    ports = Ports(send, recv)
    up = list(range(1, count))
    orders = [up, up[::-1]]

    def own_at():
        return place(count, dict(enumerate(bits_of("batch", count))))

    def grads(i, out, slots, first, width):
        part = (slice(None),) * (count + 1) + (pl.ds(first, width),)
        view = lambda: out.at[part]
        buf = lambda: zg.at[part]
        order = orders[i % 2]
        return Stream(
            halving(ports, "batch", buf, slots, [0] + order),
            spreading(
                ports, "batch", view, order[::-1] + [0], lambda: buf().at[own_at()], store_sem.at[2 + i]
            ),
        )

    z_width, x_width = channels // 2, channels // X_STREAMS
    streams = [grads(i, z_out, zx_slots[i], i * z_width, z_width) for i in range(2)]
    per = z_width // x_width
    for i in range(X_STREAMS):
        cols = pl.ds((i % per) * x_width, x_width)
        slots = [ref.at[(slice(None),) * (len(ref.shape) - 1) + (cols,)] for ref in zx_slots[i // per]]
        streams.append(grads(2 + i, x_out, slots, i * x_width, x_width))

    def state_part(i):
        part = (slice(None),) * (count + 1) + ((pl.ds(n, n + 128), pl.ds(0, n))[i],)
        buf = lambda: bcbuf.at[part]
        view = lambda: bc_out.at[part]
        return Stream(
            halving(ports, "batch", buf, bc_slots[i], [0] + orders[i]),
            exchanging_once(
                ports, "head", group_bits, lambda: bcbuf.at[own_at() + (slice(None), pl.ds((n, 0)[i], n))], bc_head[i]
            ),
            spreading(
                ports, "batch", view, orders[i][::-1] + [0], lambda: buf().at[own_at()], store_sem.at[i]
            ),
        )

    state = [state_part(i) for i in range(2)]
    vectors = Stream(
        exchanging(ports, "batch", lambda: small, small_slots, range(count)),
        exchanging(ports, "head", lambda: small.at[pl.ds(0, 8)], small_head, range(group_bits)),
    )
    half = model // 2

    def head_own():
        return place(group_bits, dict(enumerate(bits_of("head", group_bits))))

    def o_view(i):
        return o_out.at[(slice(None),) * (count + 1) + (pl.ds(i * half, half),)]

    outs = Stream(halving(ports, "head", lambda: obuf, o_slots, list(range(group_bits))))

    def o_own(i):
        return obuf.at[head_own()] if i else o_first

    spread = [
        Stream(spreading(
            ports, "batch", lambda i=i: o_view(i), orders[i] + [0], lambda i=i: o_own(i),
            store_sem.at[2 + 2 + X_STREAMS + i],
        ))
        for i in range(2)
    ]

    for load in loads[4:7]:
        load.wait()
    outs.advance()
    tile = 256
    block_rows = model >> count

    def put(target, t, value):
        for k in range(tile // min(block_rows, tile)):
            p = (t * tile) // block_rows + k
            index = tuple((p // 2**b) % 2 for b in reversed(range(count)))
            if block_rows <= tile:
                target[index] = value[k * block_rows : (k + 1) * block_rows].astype(BF16)
            else:
                first = pl.multiple_of((t * tile) % block_rows, tile)
                target[index + (pl.ds(first, tile), slice(None))] = value.astype(BF16)

    def weight_grad(right, target):
        def one(t, carry):
            value = mm_tn(x[:, pl.ds(pl.multiple_of(t * 2 * tile, 2 * tile), 2 * tile)], right[...])
            for k in range(2):
                put(target, 2 * t + k, value[k * tile : (k + 1) * tile])
            return carry

        lax.fori_loop(0, model // (2 * tile), one, 0)

    weight_grad(a, zg)
    advance_all(streams[:2])
    for load in loads[7:]:
        load.wait()
    bdw[:, 2 * n :] = jnp.concatenate([dtw[...], jnp.zeros((128 - heads, model), BF16)], axis=0).T
    pad_s[...] = jnp.zeros_like(pad_s)
    pad_s[0:1, 0:heads] = alog_ref[...]
    hot_ref[...] = (
        lax.broadcasted_iota(jnp.int32, hot_ref.shape, 1) // (channels // heads)
        == lax.broadcasted_iota(jnp.int32, hot_ref.shape, 0)
    ).astype(F32).astype(BF16)

    lam[...] = jnp.zeros_like(lam)
    dconv[rows_num:, :] = jnp.zeros((8, channels), F32)
    vec_s[...] = jnp.zeros_like(vec_s)
    head_s[...] = jnp.zeros_like(head_s)
    draw_s[...] = jnp.zeros_like(draw_s)
    pre_s[...] = jnp.zeros_like(pre_s)
    rate = -jnp.exp(pad_s[0:1, :])
    lower = lower_mask((SPAN, SPAN))
    lower_f = lower.astype(F32)
    lower_b = lower.astype(BF16)
    row_at = lax.broadcasted_iota(jnp.int32, (SPAN, SPAN), 0)
    col_at = lax.broadcasted_iota(jnp.int32, (SPAN, SPAN), 1)
    upper = row_at <= col_at
    strict = row_at < col_at
    strict_f = strict.astype(F32)
    left = lax.broadcasted_iota(jnp.int32, (SPAN, 128), 1) < 64

    span_num = channels // BACK_PARTS
    span_heads = heads // BACK_PARTS

    def block(at, local, part):
        rows = pl.ds(pl.multiple_of(at * SPAN, SPAN), SPAN)
        local_rows = pl.ds(pl.multiple_of(local * SPAN, SPAN), SPAN)
        delta = step[rows, :]
        cum = mm_exact(lower_f, delta * rate)
        cum_t = cum.T
        delta_t = delta.T
        series = delta_t * (1.0 - delta_t * (0.5 - delta_t * (1.0 / 6.0 - delta_t / 24.0)))
        slope_t = jnp.where(delta_t < 0.04, series, 1.0 - jnp.exp(-delta_t))
        rate_t = jnp.broadcast_to(rate, (SPAN, 128)).T
        b_val = bc[rows, :n]
        c_val = bc[rows, n:]
        inner = jnp.where(upper, mm_nt(b_val, c_val), 0.0)
        span_cols = pl.ds(part * span_num, span_num)
        before = prev[at, :, span_cols]
        lam_b = lam[:, span_cols].astype(BF16)
        across = mm(c_val, before)
        dtail = mm(b_val, lam_b)
        d_inner_prod = jnp.zeros((SPAN, SPAN), F32)
        for pair in range(part * span_num // 128, (part + 1) * span_num // 128):
            cols = slice(pair * 128, pair * 128 + 128)
            own = pair - part * span_num // 128
            here = slice(own * 128, own * 128 + 128)
            c0, c1, ce = pair_columns(cum, pair, left)
            _, _, de = pair_columns(delta, pair, left)
            tot = ce[SPAN - 1 : SPAN, :]
            e_cum = jnp.exp(ce)
            e_tail = jnp.exp(tot - ce)
            dy_b = s[rows, cols]
            dy = dy_b.astype(F32)
            act_p = act[rows, cols].astype(F32)
            vec_s[5:6, cols] += jnp.sum(dy * act_p, axis=0, keepdims=True)
            u = act_p * de
            u_b = u.astype(BF16)
            zero = jnp.zeros_like(dy_b)
            dy01 = jnp.concatenate([jnp.where(left, dy_b, zero), jnp.where(left, zero, dy_b)], axis=0)
            m0 = jnp.exp(jnp.minimum(cum_t[2 * pair : 2 * pair + 1, :] - c0, 0.0))
            m1 = jnp.exp(jnp.minimum(cum_t[2 * pair + 1 : 2 * pair + 2, :] - c1, 0.0))
            p0 = m0 * inner
            p1 = m1 * inner
            du = mm(jnp.concatenate([p0.astype(BF16), p1.astype(BF16)], axis=1), dy01)
            dp = mm_nt(u_b, dy01)
            dp0, dp1 = dp[:, :SPAN], dp[:, SPAN:]
            d_inner_prod += dp0 * m0 + dp1 * m1
            e01 = jnp.concatenate([(dp0 * p0).astype(BF16), (dp1 * p1).astype(BF16)], axis=0)
            spans = mm(e01, lower_b)
            da_s[2 * own : 2 * own + 1, :] = jnp.sum(
                jnp.where(strict, spans[:SPAN], 0.0), axis=0, keepdims=True
            )
            da_s[2 * own + 1 : 2 * own + 2, :] = jnp.sum(
                jnp.where(strict, spans[SPAN:], 0.0), axis=0, keepdims=True
            )
            dut = dtail[:, here] * e_tail
            du = du + dut
            dye = dy * e_cum
            dyc_s[:, here] = dye.astype(BF16)
            vt_s[:, here] = (u * e_tail).astype(BF16)
            q_s[:, here] = (dye * across[:, here]).astype(BF16)
            v_s[:, here] = (u * dut).astype(BF16)
            w_s[:, here] = (act_p * du).astype(BF16)
            etot_s[:, here] = jnp.exp(tot)
            d_act = de * du + skip_ref[:, cols] * dy
            dconv[local_rows, cols] = d_act * dsc[rows, cols].astype(F32)
        hot = hot_ref[:span_heads, :span_num]
        these = slice(part * span_heads, (part + 1) * span_heads)
        over = jnp.sum(lam[:, span_cols] * before.astype(F32), axis=0, keepdims=True) * etot_s[...]
        over = jnp.broadcast_to(over, (128, span_num))
        over = lax.dot_general(
            hot.astype(F32), over, (((1,), (1,)), ((), ())), preferred_element_type=F32, precision=HIGHEST
        )
        da = (
            da_s[...]
            + mm_exact(mm_nt(hot, q_s[...]), lower_f)
            + mm_exact(mm_nt(hot, v_s[...]), strict_f)
            + over
        )
        d_step = mm_nt(hot, w_s[...]) + rate_t[these] * da
        d_raw = d_step * slope_t[these]
        head_s[these, :] += d_raw
        head_s[heads + part * span_heads : heads + (part + 1) * span_heads, :] += delta_t[these] * da * rate_t[these]
        draw_s[these, :] = d_raw
        dg_b = jnp.where(upper, d_inner_prod, 0.0)
        d_b = mm(dg_b.astype(BF16), c_val) + mm_nt(vt_s[...], lam_b)
        d_c = mm(dg_b.T.astype(BF16), b_val) + mm_nt(dyc_s[...], before)
        d_t = draw_s[...].T
        if part:
            d_b += dbs[rows, :n].astype(F32)
            d_c += dbs[rows, n : 2 * n].astype(F32)
            d_t += dbs[rows, 2 * n :].astype(F32)
        dbs[rows, :n] = d_b.astype(BF16)
        dbs[rows, n : 2 * n] = d_c.astype(BF16)
        dbs[rows, 2 * n :] = d_t.astype(BF16)
        lam[:, span_cols] = lam[:, span_cols] * etot_s[...] + mm(bc[rows, n:].astype(F32).T.astype(BF16), dyc_s[...])

    top = groups - 1

    def slot(q, c):
        return dg.at[q, c] if q < 2 else line_s.at[q - 2, c]

    def hop(q, c, dst, sem, to):
        return pltpu.make_async_remote_copy(
            src_ref=rows_s.at[q // 2, q % 2, c], dst_ref=dst, send_sem=rsend.at[q, c], recv_sem=sem,
            device_id={"head": to}, device_id_type=pl.DeviceIdType.MESH,
        )

    def send_up(q, c):
        @pl.when(me + 1 < q)
        def _():
            hop(q, c, slot(q, c), rrecv.at[q, c], me + 1).start()

        @pl.when(me + 1 == q)
        def _():
            hop(q, c, last_s.at[c], rrecv_own.at[c], me + 1).start()

    def send_down(q, c):
        hop(q, c, slot(q, c), rrecv.at[q, c], me - 1).start()

    def arrived(q, c):
        hop(q, c, slot(q, c), rrecv.at[q, c], me).wait_recv()

    def arrived_last(q, c):
        hop(q, c, last_s.at[c], rrecv_own.at[c], me).wait_recv()

    def begin(q):
        for c in range(ROW_CHUNKS):
            if q > 0:
                @pl.when(me == 0)
                def _():
                    send_up(q, c)
            if q < top:
                @pl.when(me == top)
                def _():
                    send_down(q, c)

    def relay(q, c, distance):
        if distance < q:
            @pl.when(me == distance)
            def _():
                arrived(q, c)
                add_block(rows_s, (q // 2, q % 2, c), slot(q, c), ())
                send_up(q, c)
        if top - distance > q:
            @pl.when(me == top - distance)
            def _():
                arrived(q, c)
                add_block(rows_s, (q // 2, q % 2, c), slot(q, c), ())
                send_down(q, c)

    def conv_back(rows, part):
        for c in range(part * span_num, (part + 1) * span_num, 128):
            cols = slice(c, c + 128)
            inner_v = inn[rows, cols].astype(F32)
            d_in = jnp.zeros((rows_num, 128), F32)
            for k in range(4):
                shifted = dconv[3 - k : 3 - k + rows_num, cols]
                d_in += convw_ref[k : k + 1, cols] * shifted
                vec_s[k : k + 1, cols] += jnp.sum(inner_v * shifted, axis=0, keepdims=True)
            vec_s[4:5, cols] += jnp.sum(dconv[0:rows_num, cols], axis=0, keepdims=True)
            inn[rows, cols] = d_in.astype(BF16)
        kept = pl.ds(part * span_num, span_num)
        dconv[rows_num:, kept] = dconv[0:8, kept]

    def row_grads(q, rows):
        wide_tile = 2 * tile
        per = model // ROW_CHUNKS // wide_tile

        def columns(t, carry):
            cols = pl.ds(pl.multiple_of(t * wide_tile, wide_tile), wide_tile)
            value = mm_nt(a[rows, :], zw[cols, :]) + mm_nt(inn[rows, :], xw[cols, :]) + mm_nt(dbs[rows, :], bdw[cols, :])
            pre_s[:, cols] += jnp.sum(value * x[rows, cols].astype(F32), axis=0, keepdims=True)
            rows_s[q // 2, q % 2, t // per, :, pl.ds(pl.multiple_of((t % per) * wide_tile, wide_tile), wide_tile)] = value.astype(BF16)
            return carry

        lax.fori_loop(0, model // wide_tile, columns, 0)

    plan = {(part, k, spot): [] for part in range(BACK_PARTS) for k in range(groups) for spot in "ab"}

    def book(stream, slots):
        for slot in slots:
            if stream.steps:
                plan[slot].append(stream.steps.pop(0))

    for st in streams[:2]:
        book(st, BACK_POLLS["z"])
    book(outs, BACK_POLLS["out"])
    for i, st in enumerate(spread):
        book(st, BACK_POLLS["spread"][i])
    last = BACK_PARTS - 1
    for k in range(groups):
        plan[last, k, "b"].insert(0, lambda q=top - k: begin(q))
    for spot, q, c, distance in BACK_POLLS["relay"]:
        plan[spot].append(lambda q=q, c=c, distance=distance: relay(q, c, distance))

    for part in range(BACK_PARTS):
        def quarter_step(i, carry):
            q = groups - 1 - i
            rows = pl.ds(pl.multiple_of(q * rows_num, rows_num), rows_num)

            def one(j, inner_carry):
                block(q * subs + subs - 1 - j, subs - 1 - j, part)
                return inner_carry

            lax.fori_loop(0, subs, one, 0)

            def polls(spot):
                for k in range(groups):
                    if plan[part, k, spot]:
                        @pl.when(i == k)
                        def _():
                            for action in plan[part, k, spot]:
                                action()

            polls("a")
            conv_back(rows, part)
            if part == last:
                row_grads(q, rows)
            polls("b")
            return carry

        lax.fori_loop(0, groups, quarter_step, 0)

    drain(streams[:2])
    tail = list(BACK_POLLS["tail"])
    booked = {key[1:] for key in BACK_POLLS["relay"]}
    relays = [r for r in RELAY_ORDER if r not in booked]

    def relay_some():
        for _ in range(tail.pop(0) if tail else 1):
            if relays:
                relay(*relays.pop(0))

    def state_grad(t, carry):
        put(bcbuf, t, mm_tn(x[:, pl.ds(pl.multiple_of(t * tile, tile), tile)], dbs[...]))
        return carry

    lax.fori_loop(0, model // tile, state_grad, 0)
    advance_all(state)
    per = X_STREAMS // 2
    x_pairs = [streams[2 + h * per : 2 + (h + 1) * per] for h in range(2)]
    for h in range(2):
        cols = pl.ds(h * z_width, z_width)
        weight_grad(inn.at[:, cols], zg.at[(slice(None),) * (count + 1) + (cols,)])
        advance_all(x_pairs[h])
        relay_some()
        advance_all(state)
    small[...] = jnp.zeros_like(small)
    for j in range(groups):
        small[j : j + 1, :] = gain_ref[j]
    for j in range(model // channels):
        small[groups + j : groups + j + 1, :] = pre_s[:, j * channels : (j + 1) * channels]
    small[8:14, :] = vec_s[0:6, :]
    totals = lax.dot_general(
        jnp.ones((8, SPAN), F32), head_s[...], (((1,), (1,)), ((), ())),
        preferred_element_type=F32, precision=HIGHEST,
    )
    small[14:15, 0:128] = totals[0:1]
    vectors.advance()
    while relays or any(st.steps for st in streams + state + spread + [vectors, outs]):
        advance_all(x_pairs[0])
        relay_some()
        advance_all(state + [vectors])
        advance_all(x_pairs[1])
        relay_some()
        advance_all(spread + [outs])
    small_out[...] = small[...]

    piece = model // ROW_CHUNKS
    for c in range(ROW_CHUNKS):
        for q in range(groups):
            @pl.when(me == q)
            def _():
                if q > 0:
                    arrived_last(q, c)
                if q < top:
                    arrived(q, c)

                def total(r, carry):
                    rs = pl.ds(pl.multiple_of(r * 32, 32), 32)
                    value = rows_s[q // 2, q % 2, c, rs, :].astype(F32)
                    if q > 0:
                        value += last_s[c, rs, :].astype(F32)
                    if q < top:
                        value += slot(q, c)[rs, :].astype(F32)
                    own_out[rs, c * piece : (c + 1) * piece] = value
                    return carry

                lax.fori_loop(0, rows_num // 32, total, 0)

            @pl.when(me != q)
            def _():
                hop(q, c, slot(q, c), rrecv.at[q, c], me).wait_send()


def back_call(dg, res, x, bc, step, prev, zw, xw, bcw, dtw, out_part, out_own, gain_grad, convw, alog, skip, groups, batches):
    length, model = x.shape
    channels = xw.shape[1]
    n = bc.shape[1] // 2
    heads = dtw.shape[0]
    rows_num = length // groups
    count = log2(batches)
    group_bits = log2(groups)
    lead = (2,) * count
    part = channels // batches
    rows = model // batches
    wide = 2 * n + 128
    hbm = pl.BlockSpec(memory_space=pl.ANY)
    vmem = pl.BlockSpec(memory_space=pltpu.VMEM)
    dma = pltpu.SemaphoreType.DMA
    copies = (2 + X_STREAMS) * 2 * count + 2 * (2 * count + groups - 1) + (count + group_bits) + group_bits + 2 * count
    tall = lambda w, t: pltpu.VMEM((length, w), t)
    span = pltpu.VMEM((SPAN, channels // BACK_PARTS), BF16)
    z, xg, o, bcg, small, own = pl.pallas_call(
        functools.partial(back_kernel, count, group_bits),
        in_specs=[hbm] * 16 + [vmem] * 4,
        out_specs=[hbm] * 4 + [vmem] * 2,
        out_shape=[
            jax.ShapeDtypeStruct(lead + (rows, channels), BF16),
            jax.ShapeDtypeStruct(lead + (rows, channels), BF16),
            jax.ShapeDtypeStruct(lead + (part, model), BF16),
            jax.ShapeDtypeStruct(lead + (rows, wide), BF16),
            jax.ShapeDtypeStruct((16, channels), F32),
            jax.ShapeDtypeStruct((rows_num, model), F32),
        ],
        scratch_shapes=[pltpu.VMEM((2, groups, rows_num, channels // 2), BF16)] + [tall(channels, BF16)] * 5
        + [
            tall(model, BF16), tall(2 * n, BF16), tall(128, F32), pltpu.VMEM(prev.shape, BF16),
            pltpu.VMEM(zw.shape, BF16), pltpu.VMEM(xw.shape, BF16), pltpu.VMEM((model, wide), BF16),
            pltpu.VMEM(dtw.shape, BF16),
            pltpu.VMEM((2,) * group_bits + (part, model // 2), BF16), pltpu.VMEM((part, model // 2), BF16),
            pltpu.VMEM((heads, channels), BF16), pltpu.VMEM((8, 128), F32),
            pltpu.VMEM((n, channels), F32), pltpu.VMEM((rows_num + 8, channels), F32),
        ]
        + [span] * 5
        + [
            pltpu.VMEM((heads // BACK_PARTS, SPAN), F32), pltpu.VMEM((1, channels // BACK_PARTS), F32),
            pltpu.VMEM((128, SPAN), F32),
            pltpu.VMEM((128, SPAN), F32), pltpu.VMEM((8, channels), F32), pltpu.VMEM((1, model), F32),
            tall(wide, BF16),
            pltpu.VMEM((2, 2, ROW_CHUNKS, rows_num, model // ROW_CHUNKS), BF16),
            pltpu.VMEM((2, ROW_CHUNKS, rows_num, model // ROW_CHUNKS), BF16),
            pltpu.VMEM((ROW_CHUNKS, rows_num, model // ROW_CHUNKS), BF16),
            pltpu.VMEM(lead + (rows, channels), BF16), pltpu.VMEM(lead + (rows, wide), BF16),
            pltpu.VMEM((16, channels), F32),
        ]
        + [s for _ in range(2) for s in halving_slots(count, (rows, channels // 2), BF16)]
        + halving_slots(count, (rows, n + 128), BF16)
        + halving_slots(count, (rows, n), BF16)
        + [pltpu.VMEM((rows, n), BF16)] * (2 * (groups - 1))
        + [pltpu.VMEM((16, channels), F32)] * count
        + [pltpu.VMEM((8, channels), F32)] * group_bits
        + halving_slots(group_bits, (part, model // 2), BF16)
        + [dma((17,)), dma((6 + X_STREAMS,)),
            dma((groups, ROW_CHUNKS)), dma((groups, ROW_CHUNKS)), dma((ROW_CHUNKS,)), dma((copies,)), dma((copies,))],
        compiler_params=pltpu.CompilerParams(
            collective_id=3, has_side_effects=True, vmem_limit_bytes=BACK_VMEM_BYTES
        ),
        cost_estimate=pl.CostEstimate(
            flops=10 * length * model * channels, bytes_accessed=300 * 2**20, transcendentals=0
        ),
        name="back",
    )(
        dg, *res, x, bc, step, prev, zw, xw, bcw, dtw, out_part, out_own,
        gain_grad, convw, alog, skip,
    )
    return (
        z.reshape(model, channels), xg.reshape(model, channels), o.reshape(channels, model),
        bcg.reshape(model, wide), small, own,
    )


def finish_kernel(
    z_ref, x_ref, o_ref, bc_ref, small_ref, own_ref, tok_ref, cot_ref, pre_ref, out_ref,
    zf_ref, xf_ref, of_ref, bcf_ref, dt_ref, grad_ref, outf_ref, convw_ref, convb_ref, skip_ref, gain_ref, pre_out, dtb_ref, alog_ref,
):
    zf_ref[...] = z_ref[...].astype(F32)
    xf_ref[...] = x_ref[...].astype(F32)
    of_ref[...] = o_ref[...].astype(F32)
    width = bcf_ref.shape[1]
    heads = dt_ref.shape[0]
    outf_ref[...] = out_ref[...]
    bcf_ref[...] = bc_ref[:, :width].astype(F32)
    dt_ref[...] = bc_ref[:, width : width + 128].astype(F32).T[:heads]
    tok = tok_ref[...].astype(F32)
    recip = lax.rsqrt(jnp.mean(tok * tok, axis=-1, keepdims=True) + EPSILON)
    scaled = pre_ref[...] * own_ref[...]
    mean = jnp.mean(tok * scaled, axis=-1, keepdims=True)
    passed = sum(cot_ref[w].astype(F32) for w in range(4))
    grad_ref[...] = (passed + recip * scaled - tok * recip**3 * mean).astype(BF16)

    @pl.when(pl.program_id(0) == 0)
    def _():
        groups = small_ref.shape[0] // 4
        channels = small_ref.shape[1]
        convw_ref[...] = small_ref[8:12, :]
        convb_ref[...] = small_ref[12:13, :]
        skip_ref[...] = small_ref[13:14, :]
        me = lax.axis_index("head")
        gain = small_ref[0:1, :]
        for j in range(1, groups):
            gain = jnp.where(me == j, small_ref[j : j + 1, :], gain)
        gain_ref[...] = gain
        for j in range(pre_out.shape[1] // channels):
            cols = slice(j * channels, (j + 1) * channels)
            pre_out[:, cols] = small_ref[groups + j : groups + j + 1, :] / pre_ref[:, cols]
        dtb_ref[...] = small_ref[14:15, 0:heads]
        alog_ref[...] = small_ref[14:15, heads : 2 * heads]


def finish_call(z, x, o, bc, small, own, tok, cot, pre_gain, out, heads):
    model, channels = z.shape
    rows_num = tok.shape[0]
    steps = 8
    wide = bc.shape[1]
    rows = lambda r, w: pl.BlockSpec((r // steps, w), lambda i: (i, 0))
    fixed = lambda shape: pl.BlockSpec(shape, lambda i: (0, 0))
    shapes = [
        ((model, channels), F32), ((model, channels), F32), ((channels, model), F32), ((model, wide - 128), F32),
    ]
    wide4 = pl.BlockSpec((4, rows_num // steps, model), lambda i: (0, i, 0))
    flat = [(4, channels), (1, channels), (1, channels), (1, channels), (1, model), (1, heads), (1, heads)]
    return pl.pallas_call(
        finish_kernel,
        grid=(steps,),
        in_specs=[
            rows(model, channels), rows(model, channels), rows(channels, model), rows(model, wide),
            fixed(small.shape), rows(rows_num, model), rows(rows_num, model),
            wide4, fixed((1, model)), wide4,
        ],
        out_specs=[rows(*shape) for shape, _ in shapes]
        + [pl.BlockSpec((heads, model // steps), lambda i: (0, i)), rows(rows_num, model), wide4]
        + [fixed(shape) for shape in flat],
        out_shape=[jax.ShapeDtypeStruct(shape, t) for shape, t in shapes]
        + [
            jax.ShapeDtypeStruct((heads, model), F32), jax.ShapeDtypeStruct((rows_num, model), BF16),
            jax.ShapeDtypeStruct(out.shape, BF16),
        ]
        + [jax.ShapeDtypeStruct(shape, F32) for shape in flat],
        compiler_params=pltpu.CompilerParams(vmem_limit_bytes=VMEM_BYTES),
        cost_estimate=pl.CostEstimate(flops=0, bytes_accessed=46 * 2**20, transcendentals=0),
        name="finish",
    )(z, x, o, bc, small, own, tok, cot, pre_gain[None], out)


def per_device(
    tokens, z_weight, x_weight, bc_weight, dt_weight, conv_weight, conv_bias, dt_bias,
    a_log, skip, norm_gain, pre_gain, out_weight, cotangent,
):
    groups = lax.axis_size("head")
    batches = lax.axis_size("batch")
    _, own_len, model = tokens.shape
    tokens = tokens[0]
    cot = cotangent[:, 0]
    channels = z_weight.shape[1]
    heads = dt_weight.shape[1]
    dtw = dt_weight.T
    alog = a_log[None]
    skip_r = skip[None]
    x, res, bc, step, prev, gated, w_all, gain_all = front_call(
        tokens, pre_gain, z_weight, x_weight, bc_weight, dtw, out_weight, norm_gain,
        conv_weight, conv_bias[None], dt_bias[None], alog, skip_r, groups, batches,
    )
    outputs, d_gated, out_own, out_part, gain_grad = middle_call(gated, w_all, gain_all, tokens, cot, batches)
    z_grad, x_grad, out_grad, bcdt_grad, small, d_own = back_call(
        d_gated, res, x, bc, step, prev, z_weight, x_weight, bc_weight, dtw, out_part, out_own, gain_grad,
        conv_weight, alog, skip_r, groups, batches,
    )
    (
        z_grad, x_grad, out_grad, bc_grad, dt_grad, tokens_grad, outputs, convw, convb, skip_g, gain_g, pre_g, dtb_g, alog_g,
    ) = finish_call(z_grad, x_grad, out_grad, bcdt_grad, small, d_own, tokens, cot, pre_gain, outputs, heads)
    flat = lambda v: v.reshape(-1)
    return (
        outputs[:, None], tokens_grad[None], z_grad, x_grad, bc_grad, dt_grad.T, convw, flat(convb), flat(dtb_g),
        flat(alog_g), flat(skip_g), flat(gain_g), flat(pre_g), out_grad,
    )


def solution(mesh):
    head_cols = P(None, "head")
    rows4 = P(None, "batch", "head", None)
    return jax.shard_map(
        per_device,
        mesh=mesh,
        in_specs=(
            P("batch", "head", None), head_cols, head_cols, P(), head_cols, head_cols, P("head"),
            P("head"), P("head"), P("head"), P("head"), P(), P("head", None), rows4,
        ),
        out_specs=(
            rows4, P("batch", "head", None), head_cols, head_cols, P(), head_cols, head_cols,
            P("head"), P("head"), P("head"), P("head"), P("head"), P(), P("head", None),
        ),
        check_vma=False,
    )
```

```python
import functools
import itertools

import jax
import jax.numpy as jnp
from jax import lax
from jax.experimental import pallas as pl
from jax.experimental.pallas import tpu as pltpu
from jax.sharding import PartitionSpec as P

SPAN = 128
HEAD_PARTS = 2
ROW_CHUNKS = 4
BACK_PARTS = 1
X_STREAMS = 4
EPSILON = 1e-05
BF16 = jnp.bfloat16
F32 = jnp.float32
HIGHEST = lax.Precision.HIGHEST
VMEM_BYTES = 60 * 1024 * 1024
BACK_VMEM_BYTES = 63 * 1024 * 1024


def mm(a, b):
    return lax.dot_general(a, b, (((1,), (0,)), ((), ())), preferred_element_type=F32)


def mm_nt(a, b):
    return lax.dot_general(a, b, (((1,), (1,)), ((), ())), preferred_element_type=F32)


def mm_tn(a, b):
    return lax.dot_general(a, b, (((0,), (0,)), ((), ())), preferred_element_type=F32)


def mm_exact(a, b):
    return lax.dot_general(
        a, b, (((1,), (0,)), ((), ())), preferred_element_type=F32, precision=HIGHEST
    )


def lower_mask(shape):
    return lax.broadcasted_iota(jnp.int32, shape, 0) >= lax.broadcasted_iota(jnp.int32, shape, 1)


def softplus(v):
    return jnp.maximum(v, 0.0) + jnp.log1p(jnp.exp(-jnp.abs(v)))


def sigmoid(v):
    return 1.0 / (1.0 + jnp.exp(-v))


def pair_columns(values, pair, left):
    shape = (SPAN, 128)
    one = jnp.broadcast_to(values[:, 2 * pair : 2 * pair + 1], shape)
    two = jnp.broadcast_to(values[:, 2 * pair + 1 : 2 * pair + 2], shape)
    return one, two, jnp.where(left, one, two)


def segments(channels):
    ends = [channels * 2**w // 8 for w in range(4)]
    return list(zip([0] + ends[:-1], ends))


def partner(axis, bit):
    me = lax.axis_index(axis)
    return me + (1 - 2 * ((me // 2**bit) % 2)) * 2**bit


def bits_of(axis, count):
    me = lax.axis_index(axis)
    return [(me // 2**b) % 2 for b in range(count)]


def log2(value):
    return value.bit_length() - 1


def place(bits, fixed):
    bits = range(bits) if isinstance(bits, int) else sorted(bits)
    return tuple(fixed[b] if b in fixed else slice(None) for b in reversed(bits))


class Links:
    def __init__(self, send, recv):
        self.send, self.recv, self.used = send, recv, 0

    def copy(self, src, dst, axis, to):
        at = self.used
        self.used += 1
        return pltpu.make_async_remote_copy(
            src_ref=src, dst_ref=dst, send_sem=self.send.at[at], recv_sem=self.recv.at[at],
            device_id={axis: to}, device_id_type=pl.DeviceIdType.MESH,
        )


def meet(peers):
    barrier = pltpu.get_barrier_semaphore()
    for axis, to in peers:
        pl.semaphore_signal(barrier, inc=1, device_id={axis: to}, device_id_type=pl.DeviceIdType.MESH)
    pl.semaphore_wait(barrier, len(peers))


def add_block(buf, index, slot, at):
    rows = slot.shape[-2]
    step = min(rows, 32)
    index = index + (slice(None),) * (len(buf.shape) - len(index))
    free = [i for i, v in enumerate(index[:-2]) if isinstance(v, slice)]
    full = list(index[:-2])
    for i, v in zip(free, at):
        full[i] = v
    full = tuple(full)

    def piece(r, carry):
        rs = pl.ds(pl.multiple_of(r * step, step), step)
        total = buf[full + (rs, index[-1])].astype(F32) + slot[tuple(at) + (rs, slice(None))].astype(F32)
        buf[full + (rs, index[-1])] = total.astype(buf.dtype)
        return carry

    lax.fori_loop(0, rows // step, piece, 0)


def halving_slots(count, block, dtype):
    return [pltpu.VMEM((2,) * (count - 1 - i) + tuple(block), dtype) for i in range(count)]


class Stream:
    def __init__(self, *parts):
        self.steps = []
        for part in parts:
            if self.steps and part:
                last, first = self.steps.pop(), part[0]
                self.steps.append(lambda last=last, first=first: (last(), first()))
                part = part[1:]
            self.steps.extend(part)

    def advance(self):
        if self.steps:
            self.steps.pop(0)()


def advance_all(streams):
    for s in streams:
        s.advance()


def drain(streams):
    while any(s.steps for s in streams):
        advance_all(streams)


def exchanging_once(ports, axis, bits, buf, slots):
    def to(k):
        return lax.axis_index(axis) + sum(
            (1 - 2 * b) * 2**i for i, b in enumerate(bits_of(axis, bits)) if k & 2**i
        )

    copies = [
        ports.make(buf, lambda k=k: slots[k - 1], axis, lambda k=k: to(k)) for k in range(1, 2**bits)
    ]

    def start():
        for copy in copies:
            copy().start()

    def finish():
        for copy in copies:
            copy().wait()
        ref = buf()
        ref[...] = (ref[...].astype(F32) + sum(slot[...].astype(F32) for slot in slots)).astype(ref.dtype)

    return [start, finish]


class Ports:
    def __init__(self, send, recv):
        self.send, self.recv, self.used = send, recv, 0

    def make(self, src, dst, axis, to):
        at = self.used
        self.used += 1

        def describe():
            return pltpu.make_async_remote_copy(
                src_ref=src(), dst_ref=dst(), send_sem=self.send.at[at], recv_sem=self.recv.at[at],
                device_id={axis: to()}, device_id_type=pl.DeviceIdType.MESH,
            )

        return describe


def linked(copies, work):
    steps = []
    for i in range(len(copies) + 1):
        def step(i=i):
            if i:
                copies[i - 1]().wait()
                work(i - 1)
            if i < len(copies):
                copies[i]().start()

        steps.append(step)
    return steps


def halving(ports, axis, buf, slots, order):
    count = len(order)

    def fixed(i, give):
        mine = bits_of(axis, max(order) + 1)
        out = {b: mine[b] for b in order[: i + 1]}
        if give:
            out[order[i]] = 1 - out[order[i]]
        return out

    copies = [
        ports.make(
            lambda i=i: buf().at[place(order, fixed(i, True))], lambda i=i: slots[i],
            axis, lambda i=i: partner(axis, order[i]),
        )
        for i in range(count)
    ]

    def work(i):
        for at in itertools.product(*(range(d) for d in slots[i].shape[:-2])):
            add_block(buf(), place(order, fixed(i, False)), slots[i], at)

    return linked(copies, work)


def spreading(ports, axis, view, order, own, sem):
    count = len(order)

    def at(i):
        mine = bits_of(axis, count)
        return view().at[place(count, {b: mine[b] for b in order[i:]})]

    copies = [
        ports.make(
            (lambda i=i: at(i)) if i else own, lambda i=i: at(i), axis, lambda i=i: partner(axis, order[i])
        )
        for i in range(count)
    ]

    def kept():
        return pltpu.make_async_copy(own(), at(0), sem)

    def work(i):
        if i == 0:
            kept().wait()

    steps = linked(copies, work)
    first = steps[0]
    steps[0] = lambda: (kept().start(), first())
    return steps


def exchanging(ports, axis, buf, slots, order):
    copies = [
        ports.make(buf, lambda i=i: slots[i], axis, lambda i=i: partner(axis, order[i])) for i in range(len(order))
    ]

    def work(i):
        ref = buf()
        ref[...] = (ref[...].astype(F32) + slots[i][...].astype(F32)).astype(ref.dtype)

    return linked(copies, work)


PIECE_POLLS = (
    ("a", 0), ("a", 1), ("c", 2), ("c", 0), ("d", 1), ("e", 0), (1, 1), (2, 2), (3, 0), (4, 1), (5, 2), (7, 2),
)


def front_kernel(
    count, tok_ref, pre_ref, zw_hbm, xw_hbm, bcw_hbm, dtw_hbm, w_hbm, gain_hbm,
    convw_ref, convb_ref, dtb_ref, alog_ref, skip_ref,
    x_out, a_out, s_out, act_out, dsc_out, inn_out, bc_out, step_out, prev_out, gated_out, all_ref, gains_ref,
    xs, zw, xw, bcw, dtw, wv, gate_s, a_s, s_s, act_s, dsc_s, inn_s, inner_s, bc_s, bcb_s, step_s, prev_s, gated_s, state, tails,
    cum_s, cum_t_s, inner_prod_s, b_t_s, pad_s, load_sem, local_sem, store_sem, away_sem, here_sem, send, recv, send2, recv2,
):
    rows_num, channels = gated_s.shape[1:]
    groups = gated_s.shape[0]
    length = groups * rows_num
    n = state.shape[0]
    model = tok_ref.shape[1]
    chunks = 2
    chunk = rows_num // chunks
    me = lax.axis_index("head")
    hi, lo = me // 2, me % 2
    near = partner("head", 0)
    far = partner("head", 1)
    others = [near, far, near + far - me]
    links = Links(send, recv)

    loads = [
        pltpu.make_async_copy(src, dst, load_sem.at[i])
        for i, (src, dst) in enumerate(((zw_hbm, zw), (xw_hbm, xw), (bcw_hbm, bcw), (dtw_hbm, dtw), (w_hbm, wv)))
    ]
    for load in loads:
        load.start()
    tok = tok_ref[...].astype(F32)
    recip = lax.rsqrt(jnp.mean(tok * tok, axis=-1, keepdims=True) + EPSILON)
    xs[hi, lo] = (tok * recip * pre_ref[...]).astype(BF16)
    meet([("head", z) for z in others] + [("batch", partner("batch", b)) for b in range(count)])

    own_rows = xs.at[hi, lo]
    to_far = []
    for c in range(chunks):
        part = xs.at[hi, lo, pl.ds(c * chunk, chunk)]
        to_far.append(links.copy(part, part, "head", far))
        to_far[-1].start()
    to_near = links.copy(own_rows, own_rows, "head", near)
    to_near.start()
    half = w_hbm.shape[-1] // 2

    def pieces(z, cols, order):
        def own_piece(ref):
            return ref.at[place(count, dict(enumerate(bits_of("batch", count)))) + (slice(None), cols)]

        first = ports.make(
            lambda: own_piece(w_hbm), lambda: own_piece(all_ref.at[lax.axis_index("head")]), "head", z
        )

        def at(i):
            bits = bits_of("batch", count)
            return all_ref.at[(z(),) + place(count, {b: bits[b] for b in order[i:]}) + (slice(None), cols)]

        rest = [
            ports.make(lambda i=i: at(i), lambda i=i: at(i), "batch", lambda i=i: partner("batch", order[i]))
            for i in range(count)
        ]
        return Stream(linked([first] + rest, lambda i: None))

    up = list(range(1, count))
    ports = Ports(send2, recv2)
    near_at = lambda: partner("head", 0)
    far_at = lambda: partner("head", 1)
    streams = []
    for z in (near_at, far_at, lambda: near_at() + far_at() - lax.axis_index("head")):
        streams.append(pieces(z, pl.ds(0, half), up + [0]))
        streams.append(pieces(z, pl.ds(half, half), up[::-1] + [0]))
    plan = [[] for _ in range(HEAD_PARTS * groups)]
    early = {spot: [] for spot in "abcde"}
    for spot, group in PIECE_POLLS:
        for st in streams[2 * group : 2 * group + 2]:
            if st.steps:
                (early[spot] if spot in early else plan[spot]).append(st.steps.pop(0))

    def poll(spot):
        for action in early[spot]:
            action()

    poll("a")
    keep = [pltpu.make_async_copy(gain_hbm, gains_ref.at[me], local_sem.at[1])]
    keep[0].start()
    inner_s[0:8, :] = jnp.zeros((8, channels), F32)
    state[...] = jnp.zeros_like(state)
    step_s[...] = jnp.zeros_like(step_s)
    pad_s[...] = jnp.zeros_like(pad_s)
    pad_s[0:1, 0 : dtw.shape[0]] = dtb_ref[...]
    pad_s[1:2, 0 : dtw.shape[0]] = alog_ref[...]
    for load in loads:
        load.wait()
    keep.append(pltpu.make_async_copy(wv, all_ref.at[me], local_sem.at[0]))
    keep[-1].start()

    def project(at_hi, at_lo):
        first = pl.multiple_of((2 * at_hi + at_lo) * rows_num, rows_num)
        rows = pl.ds(first, rows_num)
        inner_rows = pl.ds(pl.multiple_of(first + 8, 8), rows_num)
        tile = 256

        def columns(t, carry):
            cols = pl.ds(pl.multiple_of(t * tile, tile), tile)
            x = xs[at_hi, at_lo]
            gate_s[rows, cols] = mm(x, zw[:, cols])
            inner_s[inner_rows, cols] = mm(x, xw[:, cols])
            return carry

        lax.fori_loop(0, channels // tile, columns, 0)
        x = xs[at_hi, at_lo]
        bc_s[rows, :] = mm(x, bcw[...])
        step_s[rows, 0 : dtw.shape[0]] = mm_nt(x, dtw[...])

    project(hi, lo)
    to_near.wait()
    project(hi, 1 - lo)
    poll("b")
    onward = []
    for c in range(chunks):
        to_far[c].wait()
        part = xs.at[1 - hi, lo, pl.ds(c * chunk, chunk)]
        onward.append(links.copy(part, part, "head", near))
        onward[-1].start()

    poll("c")
    gain_sends = [links.copy(gain_hbm, gains_ref.at[me], "head", z) for z in others]
    for item in gain_sends:
        item.start()

    project(1 - hi, lo)
    poll("d")
    for item in onward:
        item.wait()
    project(1 - hi, 1 - lo)
    poll("e")

    rate = -jnp.exp(pad_s[1:2, :])
    lower = lower_mask((SPAN, SPAN))
    lower_f = lower.astype(F32)
    left = lax.broadcasted_iota(jnp.int32, (SPAN, 128), 1) < 64

    span_num = channels // HEAD_PARTS

    def block(at, part):
        first = pl.multiple_of(at * SPAN, SPAN)
        rows = pl.ds(first, SPAN)
        if part == 0:
            delta = softplus(step_s[rows, :] + pad_s[0:1, :])
            cum = mm_exact(lower_f, delta * rate)
            cum_t = cum.T
            bcb_s[rows, :] = bc_s[rows, :].astype(BF16)
            inner = jnp.where(lower, mm_nt(bcb_s[rows, n:], bcb_s[rows, :n]), 0.0)
            b_t = bc_s[rows, :n].T.astype(BF16)
            step_s[rows, :] = delta
            cum_s[at], cum_t_s[at], inner_prod_s[at], b_t_s[at] = cum, cum_t, inner, b_t
        else:
            delta = step_s[rows, :]
            cum, cum_t, inner, b_t = cum_s[at], cum_t_s[at], inner_prod_s[at], b_t_s[at]
        span_cols = pl.ds(part * span_num, span_num)
        before = state[:, span_cols].astype(BF16)
        prev_s[at, :, span_cols] = before
        across = mm(bcb_s[rows, n:], before)
        quarter = at // (rows_num // SPAN)
        sub = pl.ds(pl.multiple_of((at % (rows_num // SPAN)) * SPAN, SPAN), SPAN)
        for pair in range(part * span_num // 128, (part + 1) * span_num // 128):
            cols = slice(pair * 128, pair * 128 + 128)
            local = slice(pair * 128 - part * span_num, pair * 128 + 128 - part * span_num)
            c0, c1, ce = pair_columns(cum, pair, left)
            _, _, de = pair_columns(delta, pair, left)
            tot = ce[SPAN - 1 : SPAN, :]
            window = inner_s[pl.ds(first, SPAN + 8), cols]
            conv_p = convb_ref[:, cols] + sum(
                convw_ref[k : k + 1, cols] * window[5 + k : 5 + k + SPAN] for k in range(4)
            )
            inn_s[rows, cols] = window[8:].astype(BF16)
            sc = sigmoid(conv_p)
            act = conv_p * sc
            act_s[rows, cols] = act.astype(BF16)
            dsc_s[rows, cols] = (sc + act * (1.0 - sc)).astype(BF16)
            u = act * de
            tails[:, local] = (u * jnp.exp(tot - ce)).astype(BF16)
            u0 = jnp.where(left, u, 0.0).astype(BF16)
            u1 = jnp.where(left, 0.0, u).astype(BF16)
            p0 = (jnp.exp(jnp.minimum(c0 - cum_t[2 * pair : 2 * pair + 1, :], 0.0)) * inner).astype(BF16)
            p1 = (jnp.exp(jnp.minimum(c1 - cum_t[2 * pair + 1 : 2 * pair + 2, :], 0.0)) * inner).astype(BF16)
            within = mm(jnp.concatenate([p0, p1], axis=1), jnp.concatenate([u0, u1], axis=0))
            y = within + across[:, local] * jnp.exp(ce) + skip_ref[:, cols] * act
            gate = gate_s[rows, cols]
            sg = sigmoid(gate)
            sl = gate * sg
            s_s[rows, cols] = sl.astype(BF16)
            a_s[rows, cols] = (y * (sg + sl * (1.0 - sg))).astype(BF16)
            gated_s[quarter, sub, cols] = (y * sl).astype(BF16)
            state[:, cols] = state[:, cols] * jnp.exp(tot)
        state[:, span_cols] += mm(b_t, tails[...])

    def leave(q, part):
        cols = pl.ds(part * span_num, span_num)
        return pltpu.make_async_remote_copy(
            src_ref=gated_s.at[q, :, cols], dst_ref=gated_out.at[me, :, cols],
            send_sem=away_sem.at[part, q], recv_sem=here_sem.at[part, me],
            device_id={"head": q}, device_id_type=pl.DeviceIdType.MESH,
        )

    def arrive(q, part):
        cols = pl.ds(part * span_num, span_num)
        return pltpu.make_async_remote_copy(
            src_ref=gated_s.at[q, :, cols], dst_ref=gated_out.at[q, :, cols],
            send_sem=away_sem.at[part, q], recv_sem=here_sem.at[part, q],
            device_id={"head": q}, device_id_type=pl.DeviceIdType.MESH,
        )

    subs = rows_num // SPAN

    def stores(q):
        rows = pl.ds(pl.multiple_of(q * rows_num, rows_num), rows_num)
        pairs = (
            (xs.at[q // 2, q % 2], x_out.at[rows]),
            (a_s.at[rows], a_out.at[rows]),
            (s_s.at[rows], s_out.at[rows]),
            (act_s.at[rows], act_out.at[rows]),
            (dsc_s.at[rows], dsc_out.at[rows]),
            (inn_s.at[rows], inn_out.at[rows]),
            (bcb_s.at[rows], bc_out.at[rows]),
            (step_s.at[rows], step_out.at[rows]),
            (prev_s.at[pl.ds(q * subs, subs)], prev_out.at[pl.ds(q * subs, subs)]),
        )
        return [pltpu.make_async_copy(src, dst, store_sem.at[i, q]) for i, (src, dst) in enumerate(pairs)]

    for part in range(HEAD_PARTS):
        def quarter_step(q, carry):
            def one(at, inner_carry):
                block(at, part)
                return inner_carry

            lax.fori_loop(q * subs, (q + 1) * subs, one, 0)

            @pl.when(q != me)
            def _():
                leave(q, part).start()

            if part == HEAD_PARTS - 1:
                for item in stores(q):
                    item.start()
            for k in range(groups):
                @pl.when(q == k)
                def _():
                    for action in plan[part * groups + k]:
                        action()
            return carry

        lax.fori_loop(0, groups, quarter_step, 0)
    stay = pltpu.make_async_copy(gated_s.at[me], gated_out.at[me], local_sem.at[2])
    stay.start()
    drain(streams)
    for item in gain_sends:
        item.wait()
    for item in keep:
        item.wait()
    stay.wait()

    def finish(q, carry):
        @pl.when(q != me)
        def _():
            for part in range(HEAD_PARTS):
                leave(q, part).wait_send()
                arrive(q, part).wait_recv()

        for item in stores(q):
            item.wait()
        return carry

    lax.fori_loop(0, groups, finish, 0)


def front_call(tokens, pre_gain, zw, xw, bcw, dtw, out_weight, norm_gain, convw, convb, dtb, alog, skip, groups, batches):
    rows_num, model = tokens.shape
    channels = zw.shape[1]
    n = bcw.shape[1] // 2
    length = rows_num * groups
    count = log2(batches)
    part = channels // batches
    copies = 5 + groups - 1
    piece_copies = 2 * (groups - 1) * (1 + count)
    hbm = pl.BlockSpec(memory_space=pl.ANY)
    vmem = pl.BlockSpec(memory_space=pltpu.VMEM)
    wide = jax.ShapeDtypeStruct((length, channels), BF16)
    outs = [
        jax.ShapeDtypeStruct((length, model), BF16), wide, wide, wide, wide, wide,
        jax.ShapeDtypeStruct((length, 2 * n), BF16),
        jax.ShapeDtypeStruct((length, 128), F32),
        jax.ShapeDtypeStruct((length // SPAN, n, channels), BF16),
        jax.ShapeDtypeStruct((groups, rows_num, channels), BF16),
        jax.ShapeDtypeStruct((groups,) + (2,) * count + (part, model), BF16),
        jax.ShapeDtypeStruct((groups, 1, channels), F32),
    ]
    dma = pltpu.SemaphoreType.DMA
    result = pl.pallas_call(
        functools.partial(front_kernel, count),
        in_specs=[vmem, vmem] + [hbm] * 6 + [vmem] * 5,
        out_specs=[hbm] * len(outs),
        out_shape=outs,
        scratch_shapes=[
            pltpu.VMEM((2, 2, rows_num, model), BF16),
            pltpu.VMEM(zw.shape, BF16), pltpu.VMEM(xw.shape, BF16),
            pltpu.VMEM(bcw.shape, BF16), pltpu.VMEM(dtw.shape, BF16),
            pltpu.VMEM((2,) * count + (part, model), BF16),
            pltpu.VMEM((length, channels), F32),
            pltpu.VMEM((length, channels), BF16), pltpu.VMEM((length, channels), BF16),
            pltpu.VMEM((length, channels), BF16), pltpu.VMEM((length, channels), BF16),
            pltpu.VMEM((length, channels), BF16), pltpu.VMEM((length + 8, channels), F32),
            pltpu.VMEM((length, 2 * n), F32), pltpu.VMEM((length, 2 * n), BF16),
            pltpu.VMEM((length, 128), F32), pltpu.VMEM((length // SPAN, n, channels), BF16),
            pltpu.VMEM((groups, rows_num, channels), BF16),
            pltpu.VMEM((n, channels), F32), pltpu.VMEM((SPAN, channels // HEAD_PARTS), BF16),
            pltpu.VMEM((length // SPAN, SPAN, 128), F32), pltpu.VMEM((length // SPAN, 128, SPAN), F32),
            pltpu.VMEM((length // SPAN, SPAN, SPAN), F32), pltpu.VMEM((length // SPAN, n, SPAN), BF16),
            pltpu.VMEM((8, 128), F32),
            dma((5,)), dma((3,)), dma((9, groups)), dma((HEAD_PARTS, groups)), dma((HEAD_PARTS, groups)), dma((copies,)), dma((copies,)),
            dma((piece_copies,)), dma((piece_copies,)),
        ],
        compiler_params=pltpu.CompilerParams(
            collective_id=1, has_side_effects=True, vmem_limit_bytes=VMEM_BYTES
        ),
        cost_estimate=pl.CostEstimate(
            flops=4 * length * model * channels, bytes_accessed=400 * 2**20, transcendentals=0
        ),
        name="front",
    )(
        tokens, pre_gain[None], zw, xw, bcw, dtw, out_weight.reshape((2,) * count + (part, model)),
        norm_gain[None], convw, convb, dtb, alog, skip,
    )
    x, a, s, act, dsc, inn, bc, step, prev, gated, w_all, gains = result
    return x, (a, s, act, dsc, inn), bc, step, prev, gated, w_all.reshape(groups, channels, model), gains


def middle_kernel(
    count, g_hbm, w_hbm, cot_hbm, x_hbm, a_hbm, s_hbm, gain_ref, tok_ref,
    out_hbm, da_out, ds_out, z_out, own_ref, part_ref, ggrad_ref,
    g_s, w_s, cot_s, dy_s, gg_s, out_s, dg_s, dg_in, give_s, kept_s, obuf, oslot0, oslot1, *refs,
):
    slots = [refs[i * (count - 1) : (i + 1) * (count - 1)] for i in range(4)]
    load_sem, store_sem, away_sem, here_sem, send, recv = refs[4 * (count - 1) :]
    groups, rows_num, channels = g_s.shape
    model = tok_ref.shape[1]
    part, half = kept_s.shape[-2:]
    pairs_num = groups // 2
    segs = segments(channels)
    tile = 512
    tiles = model // tile
    me = lax.axis_index("head")

    def w_load(t):
        cols = pl.ds(pl.multiple_of(t * tile, tile), tile)
        return pltpu.make_async_copy(w_hbm.at[:, :, cols], w_s.at[:, :, cols], load_sem.at[2 + t])

    loads = [
        pltpu.make_async_copy(g_hbm, g_s, load_sem.at[0]), pltpu.make_async_copy(cot_hbm, cot_s, load_sem.at[1]),
    ]
    for load in loads:
        load.start()
    for t in range(tiles):
        w_load(t).start()
    loads[0].wait()
    sums = [jnp.zeros((rows_num, 1), F32) for _ in segs]
    for j in range(groups):
        for w, (lo, hi) in enumerate(segs):
            g = g_s[j, :, lo:hi].astype(F32)
            gg_s[j, :, lo:hi] = (g * gain_ref[j, 0:1, lo:hi]).astype(BF16)
            sums[w] += jnp.sum(g * g, axis=1, keepdims=True)
    recips = []
    total = jnp.zeros((rows_num, 1), F32)
    for w, (lo, hi) in enumerate(segs):
        total = total + sums[w]
        recips.append(lax.rsqrt(total / (hi * groups) + EPSILON))
    meet(
        [("batch", partner("batch", b)) for b in range(count)]
        + [("head", z) for z in (partner("head", 0), partner("head", 1), partner("head", 0) + partner("head", 1) - me)]
    )
    loads[1].wait()

    out_tile = tile // 2

    def out_store(t, h):
        cols = pl.ds(pl.multiple_of(t * tile + h * out_tile, out_tile), out_tile)
        return pltpu.make_async_copy(out_s.at[h], out_hbm.at[:, :, cols], store_sem.at[t, h])

    def forward(t, dots):
        cols = pl.ds(pl.multiple_of(t * tile, tile), tile)
        w_load(t).wait()

        @pl.when(t >= 1)
        def _():
            for h in range(2):
                out_store(t - 1, h).wait()

        acc = jnp.zeros((rows_num, tile), F32)
        tok = tok_ref[:, cols].astype(F32)
        new = []
        for w, (lo, hi) in enumerate(segs):
            acc += mm(
                jnp.concatenate([gg_s[j, :, lo:hi] for j in range(groups)], axis=1),
                jnp.concatenate([w_s[j, lo:hi, cols] for j in range(groups)], axis=0),
            )
            value = (tok + recips[w] * acc).astype(BF16)
            for h in range(2):
                out_s[h, w] = value[:, h * out_tile : (h + 1) * out_tile]
            new.append(dots[w] + jnp.sum(cot_s[w, :, cols].astype(F32) * acc, axis=1, keepdims=True))
        for h in range(2):
            out_store(t, h).start()
        return tuple(new)

    def combine(t, carry):
        cols = pl.ds(pl.multiple_of(t * tile, tile), tile)
        combined = jnp.zeros((rows_num, tile), F32)
        for w in reversed(range(4)):
            combined += recips[w] * cot_s[w, :, cols].astype(F32)
            dy_s[w, :, cols] = combined.astype(BF16)
        return carry

    lax.fori_loop(0, tiles, combine, 0)

    def leave(j):
        return pltpu.make_async_remote_copy(
            src_ref=dg_s.at[j], dst_ref=dg_in.at[me], send_sem=away_sem.at[j], recv_sem=here_sem.at[me],
            device_id={"head": j}, device_id_type=pl.DeviceIdType.MESH,
        )

    def arrive(j):
        return pltpu.make_async_remote_copy(
            src_ref=dg_s.at[j], dst_ref=dg_in.at[j], send_sem=away_sem.at[j], recv_sem=here_sem.at[j],
            device_id={"head": j}, device_id_type=pl.DeviceIdType.MESH,
        )

    def back(k, carry):
        j = (me + 1 + k) % groups
        for w, (lo, hi) in enumerate(segs):
            dn = mm_nt(dy_s[w], w_s[j, lo:hi, :])
            g = g_s[j, :, lo:hi].astype(F32)
            ggrad_ref[j, :, lo:hi] = jnp.sum(g * dn, axis=0, keepdims=True)
            dg_s[j, :, lo:hi] = (gain_ref[j, 0:1, lo:hi] * dn - g * scales[w]).astype(BF16)

        @pl.when(j != me)
        def _():
            leave(j).start()

        return carry

    ports = Ports(send, recv)
    up = list(range(1, count))
    core = bits_of("batch", 1)[0]

    def upper_index(p):
        return tuple((p >> b) & 1 for b in reversed(range(1, count)))

    def terms(s, bit, use):
        g0, c0 = (s % 2) * pairs_num, (s // 2) * half
        if part % 128 == 0:
            for q in range(2 ** (count - 1)):
                at = pl.ds(pl.multiple_of((2 * q + bit) * part, part), part)
                left = jnp.concatenate([gg_s[g0 + j, :, at] for j in range(pairs_num)], axis=1)
                owners = [[w for w, (lo, hi) in enumerate(segs) if lo <= (2 * q + c) * part < hi][0] for c in range(2)]
                w = owners[0] + (owners[1] - owners[0]) * bit
                term = mm_tn(left, dy_s[w, :, c0 : c0 + half])
                for j in range(pairs_num):
                    use(upper_index(2 * q), j, term[j * part : (j + 1) * part])
            return
        for j in range(pairs_num):
            for w, (lo, hi) in enumerate(segs):
                term = mm_tn(gg_s[g0 + j, :, lo:hi], dy_s[w, :, c0 : c0 + half])
                for p in range(lo // part, hi // part):
                    @pl.when(bit == p % 2)
                    def _():
                        use(upper_index(p), j, term[p * part - lo : (p + 1) * part - lo])

    def to_core(s):
        return pltpu.make_async_remote_copy(
            src_ref=give_s.at[s], dst_ref=kept_s.at[s], send_sem=send.at[s], recv_sem=recv.at[s],
            device_id={"batch": partner("batch", 0)}, device_id_type=pl.DeviceIdType.MESH,
        )

    def give(s):
        def use(index, j, rows):
            give_s[(s,) + index + (j,)] = rows.astype(BF16)

        terms(s, 1 - core, use)
        to_core(s).start()

    def keep(s):
        to_core(s).wait()

        def use(index, j, rows):
            at = (s,) + index + (j,)
            kept_s[at] = (kept_s[at].astype(F32) + rows).astype(BF16)

        terms(s, core, use)

    ports.used = 4
    streams = [
        Stream(halving(ports, "batch", lambda s=s: kept_s.at[s], slots[s], up if s % 2 == 0 else up[::-1]))
        for s in range(4)
    ]
    mine = bits_of("batch", count)
    own = place(up, {b: mine[b] for b in up})
    head_sum = Stream(halving(ports, "head", lambda: obuf, (oslot0, oslot1), [0, 1]))
    for s in range(2):
        give(s)
    for s in range(2):
        keep(s)
        streams[s].advance()
    dots = lax.fori_loop(0, tiles, forward, tuple(jnp.zeros((rows_num, 1), F32) for _ in segs))
    scales = [None] * 4
    scale = jnp.zeros((rows_num, 1), F32)
    for w in reversed(range(4)):
        scale = scale + recips[w] ** 3 * dots[w] / (segs[w][1] * groups)
        scales[w] = scale
    lax.fori_loop(0, groups, back, 0)
    stay = pltpu.make_async_copy(dg_s.at[me], dg_in.at[me], load_sem.at[0])
    stay.start()
    x_s, factors, z_s = w_s.at[0], w_s.at[1], w_s.at[2]
    wide_at = [pl.ds(h * channels, channels) for h in range(2)]
    late = [
        pltpu.make_async_copy(x_hbm, x_s, load_sem.at[2]),
        pltpu.make_async_copy(a_hbm, factors.at[:, wide_at[0]], load_sem.at[3]),
        pltpu.make_async_copy(s_hbm, factors.at[:, wide_at[1]], load_sem.at[4]),
    ]
    for load in late:
        load.start()
    for s in range(2, 4):
        give(s)
    advance_all(streams[:2])
    for s in range(2, 4):
        keep(s)
        streams[s].advance()
    drain(streams[:2])
    for s in range(2):
        for j in range(pairs_num):
            obuf[s, j] = kept_s[(s,) + own + (j,)]
    head_sum.advance()
    advance_all(streams[2:])

    def taken(j, carry):
        @pl.when(j != me)
        def _():
            leave(j).wait_send()
            arrive(j).wait_recv()

        return carry

    lax.fori_loop(0, groups, taken, 0)
    stay.wait()
    for load in late:
        load.wait()
    length = groups * rows_num
    rows_at = 64

    def gates(i, carry):
        per = rows_num // rows_at
        rows = pl.ds(pl.multiple_of(i * rows_at, rows_at), rows_at)
        d = dg_in[i // per, pl.ds(pl.multiple_of((i % per) * rows_at, rows_at), rows_at), :].astype(F32)
        for at in wide_at:
            factors[rows, at] = (d * factors[rows, at].astype(F32)).astype(BF16)
        return carry

    lax.fori_loop(0, length // rows_at, gates, 0)
    stores = [
        pltpu.make_async_copy(factors.at[:, wide_at[0]], da_out, load_sem.at[0]),
        pltpu.make_async_copy(factors.at[:, wide_at[1]], ds_out, load_sem.at[1]),
    ]
    for item in stores:
        item.start()
    head_sum.advance()
    per_half = model // tile // 2

    def z_store(t):
        first = pl.multiple_of((t % per_half) * tile, tile)
        cols = pl.ds(pl.multiple_of((t // per_half) * channels, channels), channels)
        rows = pl.ds(pl.multiple_of(t * tile, tile), tile)
        return pltpu.make_async_copy(z_s.at[pl.ds(first, tile), cols], z_out.at[rows], load_sem.at[2 + t])

    def z_grad(t, carry):
        value = mm_tn(x_s[:, pl.ds(pl.multiple_of(t * tile, tile), tile)], factors[:, wide_at[0]])
        first = pl.multiple_of((t % per_half) * tile, tile)
        cols = pl.ds(pl.multiple_of((t // per_half) * channels, channels), channels)
        z_s[pl.ds(first, tile), cols] = value.astype(BF16)
        z_store(t).start()
        return carry

    lax.fori_loop(0, tiles, z_grad, 0)
    drain(streams)
    drain([head_sum])
    for item in stores:
        item.wait()

    def z_stored(t, carry):
        z_store(t).wait()
        return carry

    lax.fori_loop(0, tiles, z_stored, 0)
    own_ref[...] = obuf[place(2, dict(enumerate(bits_of("head", 2))))]
    for s in range(2, 4):
        for j in range(pairs_num):
            part_ref[s - 2, j] = kept_s[(s,) + own + (j,)]
    for h in range(2):
        out_store(tiles - 1, h).wait()


def middle_call(g, w_all, gain, tok, cot, x, a, s, batches):
    groups, rows_num, channels = g.shape
    model = tok.shape[1]
    count = log2(batches)
    part = channels // batches
    half = model // 2
    block = (groups // 2, part, half)
    hbm = pl.BlockSpec(memory_space=pl.ANY)
    vmem = pl.BlockSpec(memory_space=pltpu.VMEM)
    dma = pltpu.SemaphoreType.DMA
    wide = pltpu.VMEM((groups, rows_num, channels), BF16)
    tall = pltpu.VMEM((4, rows_num, model), BF16)
    halves = pltpu.VMEM((4,) + (2,) * (count - 1) + block, BF16)
    return pl.pallas_call(
        functools.partial(middle_kernel, count),
        in_specs=[hbm] * 6 + [vmem] * 2,
        out_specs=[hbm] * 4 + [vmem] * 3,
        out_shape=[
            jax.ShapeDtypeStruct((4, rows_num, model), BF16),
            jax.ShapeDtypeStruct(a.shape, BF16),
            jax.ShapeDtypeStruct(s.shape, BF16),
            jax.ShapeDtypeStruct((model, channels), BF16),
            jax.ShapeDtypeStruct((part, half), BF16),
            jax.ShapeDtypeStruct((2, 2, part, half), BF16),
            jax.ShapeDtypeStruct((groups, 1, channels), F32),
        ],
        scratch_shapes=[
            wide, pltpu.VMEM((groups, channels, model), BF16), tall, tall, wide,
            pltpu.VMEM((2, 4, rows_num, 256), BF16), wide, wide, halves, halves,
            pltpu.VMEM((2, 2, part, half), BF16), pltpu.VMEM((2, part, half), BF16), pltpu.VMEM((part, half), BF16),
        ]
        + [s for _ in range(4) for s in halving_slots(count - 1, block, BF16)]
        + [
            dma((2 + model // 512,)), dma((model // 512, 2)), dma((groups,)), dma((groups,)),
            dma((4 * count + 2,)), dma((4 * count + 2,)),
        ],
        compiler_params=pltpu.CompilerParams(
            collective_id=2, has_side_effects=True, vmem_limit_bytes=BACK_VMEM_BYTES
        ),
        cost_estimate=pl.CostEstimate(
            flops=6 * groups * rows_num * channels * model, bytes_accessed=200 * 2**20, transcendentals=0
        ),
        name="nested_norm",
    )(g, w_all, cot, x, a, s, gain, tok)


BACK_POLLS = {
    "z": ((0, 0, "a"), (0, 1, "a"), (0, 1, "b"), (0, 2, "a"), (0, 3, "a"), (0, 3, "b")),
    "out": ((0, 0, "a"), (0, 1, "a")),
    "spread": (((0, 3, "b"),), ((0, 3, "b"),)),
    "relay": (
        ((0, 1, "a"), 3, 0, 1), ((0, 1, "b"), 3, 1, 1), ((0, 1, "b"), 3, 2, 1), ((0, 2, "a"), 3, 3, 1),
        ((0, 1, "b"), 3, 0, 2), ((0, 2, "a"), 3, 1, 2), ((0, 2, "a"), 3, 2, 2), ((0, 2, "b"), 3, 3, 2),
        ((0, 2, "b"), 2, 0, 1), ((0, 2, "b"), 2, 1, 1), ((0, 3, "a"), 2, 2, 1), ((0, 3, "b"), 2, 3, 1),
        ((0, 3, "b"), 1, 0, 1),
    ),
    "tail": (1, 1, 2, 2),
}
RELAY_ORDER = [(2, c, 1) for c in range(4)] + [(1, c, 1) for c in range(4)]
RELAY_ORDER += [(0, 0, 1), (0, 1, 1), (0, 0, 2), (0, 2, 1), (0, 1, 2), (0, 3, 1), (0, 2, 2), (0, 3, 2)]


def back_kernel(
    count, group_bits,
    zg_hbm, a_hbm, s_hbm, act_hbm, dsc_hbm, inn_hbm, x_hbm, bc_hbm, step_hbm, prev_hbm,
    zw_hbm, xw_hbm, bcw_hbm, dtw_hbm, o_hbm, own_hbm, gain_ref, convw_ref, alog_ref, skip_ref,
    z_out, x_out, o_out, bc_out, small_out, own_out,
    dg, a, s, act, dsc, inn, x, bc, step, prev, zw, xw, bdw, dtw, obuf, o_first, hot_ref, pad_s,
    lam, dconv, dyc_s, vt_s, q_s, v_s, w_s, da_s, etot_s, draw_s, head_s, vec_s, pre_s, dbs,
    rows_s, line_s, last_s, zg, bcbuf, small, *refs,
):
    groups = rows_s.shape[0] * rows_s.shape[1]
    zx_slots = [refs[i * count : (i + 1) * count] for i in range(2)]
    refs = refs[2 * count :]
    bc_slots, refs = (refs[:count], refs[count : 2 * count]), refs[2 * count :]
    bc_head, refs = (refs[: groups - 1], refs[groups - 1 : 2 * (groups - 1)]), refs[2 * (groups - 1) :]
    small_slots, refs = refs[:count], refs[count:]
    small_head, refs = refs[:group_bits], refs[group_bits:]
    o_slots, refs = refs[:group_bits], refs[group_bits:]
    load_sem, store_sem, rsend, rrecv, rrecv_own, send, recv = refs
    length, channels = a.shape
    model = x.shape[1]
    n = lam.shape[0]
    heads = hot_ref.shape[0]
    rows_num = length // groups
    subs = rows_num // SPAN
    wide = bcbuf.shape[-1]
    me = lax.axis_index("head")

    pairs = [
        (zg_hbm, zg), (o_hbm, obuf), (own_hbm, o_first), (step_hbm, step), (bc_hbm, bc), (prev_hbm, prev),
        (s_hbm, s), (act_hbm, act), (dsc_hbm, dsc), (inn_hbm, inn), (a_hbm, a), (zw_hbm, zw), (xw_hbm, xw),
        (x_hbm, x), (bcw_hbm, bdw.at[:, pl.ds(0, 2 * n)]), (dtw_hbm, dtw),
    ]
    loads = [pltpu.make_async_copy(src, dst, load_sem.at[i]) for i, (src, dst) in enumerate(pairs)]
    for load in loads:
        load.start()
    near, far = partner("head", 0), partner("head", 1)
    meet(
        [("batch", partner("batch", b)) for b in range(count)]
        + [("head", to) for to in (near, far, near + far - me)]
    )

    ports = Ports(send, recv)
    up = list(range(1, count))
    orders = [up, up[::-1]]

    def own_at():
        return place(count, dict(enumerate(bits_of("batch", count))))

    def grads(i, out, slots, first, width):
        part = (slice(None),) * (count + 1) + (pl.ds(first, width),)
        view = lambda: out.at[part]
        buf = lambda: zg.at[part]
        order = orders[i % 2]
        return Stream(
            halving(ports, "batch", buf, slots, [0] + order),
            spreading(
                ports, "batch", view, order[::-1] + [0], lambda: buf().at[own_at()], store_sem.at[2 + i]
            ),
        )

    z_width, x_width = channels // 2, channels // X_STREAMS
    streams = [grads(i, z_out, zx_slots[i], i * z_width, z_width) for i in range(2)]
    per = z_width // x_width
    for i in range(X_STREAMS):
        cols = pl.ds((i % per) * x_width, x_width)
        slots = [ref.at[(slice(None),) * (len(ref.shape) - 1) + (cols,)] for ref in zx_slots[i // per]]
        streams.append(grads(2 + i, x_out, slots, i * x_width, x_width))

    def state_part(i):
        part = (slice(None),) * (count + 1) + ((pl.ds(n, n + 128), pl.ds(0, n))[i],)
        buf = lambda: bcbuf.at[part]
        view = lambda: bc_out.at[part]
        return Stream(
            halving(ports, "batch", buf, bc_slots[i], [0] + orders[i]),
            exchanging_once(
                ports, "head", group_bits, lambda: bcbuf.at[own_at() + (slice(None), pl.ds((n, 0)[i], n))], bc_head[i]
            ),
            spreading(
                ports, "batch", view, orders[i][::-1] + [0], lambda: buf().at[own_at()], store_sem.at[i]
            ),
        )

    state = [state_part(i) for i in range(2)]
    vectors = Stream(
        exchanging(ports, "batch", lambda: small, small_slots, range(count)),
        exchanging(ports, "head", lambda: small.at[pl.ds(0, 8)], small_head, range(group_bits)),
    )
    half = model // 2

    def head_own():
        return place(group_bits, dict(enumerate(bits_of("head", group_bits))))

    def o_view(i):
        return o_out.at[(slice(None),) * (count + 1) + (pl.ds(i * half, half),)]

    outs = Stream(halving(ports, "head", lambda: obuf, o_slots, list(range(group_bits))))

    def o_own(i):
        return obuf.at[head_own()] if i else o_first

    spread = [
        Stream(spreading(
            ports, "batch", lambda i=i: o_view(i), orders[i] + [0], lambda i=i: o_own(i),
            store_sem.at[2 + 2 + X_STREAMS + i],
        ))
        for i in range(2)
    ]

    loads[0].wait()
    advance_all(streams[:2])
    for load in loads[1:3]:
        load.wait()
    outs.advance()
    tile = 256
    block_rows = model >> count

    def put(target, t, value):
        for k in range(tile // min(block_rows, tile)):
            p = (t * tile) // block_rows + k
            index = tuple((p // 2**b) % 2 for b in reversed(range(count)))
            if block_rows <= tile:
                target[index] = value[k * block_rows : (k + 1) * block_rows].astype(BF16)
            else:
                first = pl.multiple_of((t * tile) % block_rows, tile)
                target[index + (pl.ds(first, tile), slice(None))] = value.astype(BF16)

    def weight_grad(right, target):
        def one(t, carry):
            value = mm_tn(x[:, pl.ds(pl.multiple_of(t * 2 * tile, 2 * tile), 2 * tile)], right[...])
            for k in range(2):
                put(target, 2 * t + k, value[k * tile : (k + 1) * tile])
            return carry

        lax.fori_loop(0, model // (2 * tile), one, 0)

    for load in loads[3:10]:
        load.wait()

    def late_loads():
        for load in loads[10:]:
            load.wait()
        bdw[:, 2 * n :] = jnp.concatenate([dtw[...], jnp.zeros((128 - heads, model), BF16)], axis=0).T

    pad_s[...] = jnp.zeros_like(pad_s)
    pad_s[0:1, 0:heads] = alog_ref[...]
    hot_ref[...] = (
        lax.broadcasted_iota(jnp.int32, hot_ref.shape, 1) // (channels // heads)
        == lax.broadcasted_iota(jnp.int32, hot_ref.shape, 0)
    ).astype(F32).astype(BF16)

    lam[...] = jnp.zeros_like(lam)
    dconv[rows_num:, :] = jnp.zeros((8, channels), F32)
    vec_s[...] = jnp.zeros_like(vec_s)
    head_s[...] = jnp.zeros_like(head_s)
    draw_s[...] = jnp.zeros_like(draw_s)
    pre_s[...] = jnp.zeros_like(pre_s)
    rate = -jnp.exp(pad_s[0:1, :])
    lower = lower_mask((SPAN, SPAN))
    lower_f = lower.astype(F32)
    lower_b = lower.astype(BF16)
    row_at = lax.broadcasted_iota(jnp.int32, (SPAN, SPAN), 0)
    col_at = lax.broadcasted_iota(jnp.int32, (SPAN, SPAN), 1)
    upper = row_at <= col_at
    strict = row_at < col_at
    strict_f = strict.astype(F32)
    left = lax.broadcasted_iota(jnp.int32, (SPAN, 128), 1) < 64

    span_num = channels // BACK_PARTS
    span_heads = heads // BACK_PARTS

    def block(at, local, part):
        rows = pl.ds(pl.multiple_of(at * SPAN, SPAN), SPAN)
        local_rows = pl.ds(pl.multiple_of(local * SPAN, SPAN), SPAN)
        delta = step[rows, :]
        cum = mm_exact(lower_f, delta * rate)
        cum_t = cum.T
        delta_t = delta.T
        series = delta_t * (1.0 - delta_t * (0.5 - delta_t * (1.0 / 6.0 - delta_t / 24.0)))
        slope_t = jnp.where(delta_t < 0.04, series, 1.0 - jnp.exp(-delta_t))
        rate_t = jnp.broadcast_to(rate, (SPAN, 128)).T
        b_val = bc[rows, :n]
        c_val = bc[rows, n:]
        inner = jnp.where(upper, mm_nt(b_val, c_val), 0.0)
        span_cols = pl.ds(part * span_num, span_num)
        before = prev[at, :, span_cols]
        lam_b = lam[:, span_cols].astype(BF16)
        across = mm(c_val, before)
        dtail = mm(b_val, lam_b)
        d_inner_prod = jnp.zeros((SPAN, SPAN), F32)
        for pair in range(part * span_num // 128, (part + 1) * span_num // 128):
            cols = slice(pair * 128, pair * 128 + 128)
            own = pair - part * span_num // 128
            here = slice(own * 128, own * 128 + 128)
            c0, c1, ce = pair_columns(cum, pair, left)
            _, _, de = pair_columns(delta, pair, left)
            tot = ce[SPAN - 1 : SPAN, :]
            e_cum = jnp.exp(ce)
            e_tail = jnp.exp(tot - ce)
            dy_b = s[rows, cols]
            dy = dy_b.astype(F32)
            act_p = act[rows, cols].astype(F32)
            vec_s[5:6, cols] += jnp.sum(dy * act_p, axis=0, keepdims=True)
            u = act_p * de
            u_b = u.astype(BF16)
            zero = jnp.zeros_like(dy_b)
            dy01 = jnp.concatenate([jnp.where(left, dy_b, zero), jnp.where(left, zero, dy_b)], axis=0)
            m0 = jnp.exp(jnp.minimum(cum_t[2 * pair : 2 * pair + 1, :] - c0, 0.0))
            m1 = jnp.exp(jnp.minimum(cum_t[2 * pair + 1 : 2 * pair + 2, :] - c1, 0.0))
            p0 = m0 * inner
            p1 = m1 * inner
            du = mm(jnp.concatenate([p0.astype(BF16), p1.astype(BF16)], axis=1), dy01)
            dp = mm_nt(u_b, dy01)
            dp0, dp1 = dp[:, :SPAN], dp[:, SPAN:]
            d_inner_prod += dp0 * m0 + dp1 * m1
            e01 = jnp.concatenate([(dp0 * p0).astype(BF16), (dp1 * p1).astype(BF16)], axis=0)
            spans = mm(e01, lower_b)
            da_s[2 * own : 2 * own + 1, :] = jnp.sum(
                jnp.where(strict, spans[:SPAN], 0.0), axis=0, keepdims=True
            )
            da_s[2 * own + 1 : 2 * own + 2, :] = jnp.sum(
                jnp.where(strict, spans[SPAN:], 0.0), axis=0, keepdims=True
            )
            dut = dtail[:, here] * e_tail
            du = du + dut
            dye = dy * e_cum
            dyc_s[:, here] = dye.astype(BF16)
            vt_s[:, here] = (u * e_tail).astype(BF16)
            q_s[:, here] = (dye * across[:, here]).astype(BF16)
            v_s[:, here] = (u * dut).astype(BF16)
            w_s[:, here] = (act_p * du).astype(BF16)
            etot_s[:, here] = jnp.exp(tot)
            d_act = de * du + skip_ref[:, cols] * dy
            dconv[local_rows, cols] = d_act * dsc[rows, cols].astype(F32)
        hot = hot_ref[:span_heads, :span_num]
        these = slice(part * span_heads, (part + 1) * span_heads)
        over = jnp.sum(lam[:, span_cols] * before.astype(F32), axis=0, keepdims=True) * etot_s[...]
        over = jnp.broadcast_to(over, (128, span_num))
        over = lax.dot_general(
            hot.astype(F32), over, (((1,), (1,)), ((), ())), preferred_element_type=F32, precision=HIGHEST
        )
        da = (
            da_s[...]
            + mm_exact(mm_nt(hot, q_s[...]), lower_f)
            + mm_exact(mm_nt(hot, v_s[...]), strict_f)
            + over
        )
        d_step = mm_nt(hot, w_s[...]) + rate_t[these] * da
        d_raw = d_step * slope_t[these]
        head_s[these, :] += d_raw
        head_s[heads + part * span_heads : heads + (part + 1) * span_heads, :] += delta_t[these] * da * rate_t[these]
        draw_s[these, :] = d_raw
        dg_b = jnp.where(upper, d_inner_prod, 0.0)
        d_b = mm(dg_b.astype(BF16), c_val) + mm_nt(vt_s[...], lam_b)
        d_c = mm(dg_b.T.astype(BF16), b_val) + mm_nt(dyc_s[...], before)
        d_t = draw_s[...].T
        if part:
            d_b += dbs[rows, :n].astype(F32)
            d_c += dbs[rows, n : 2 * n].astype(F32)
            d_t += dbs[rows, 2 * n :].astype(F32)
        dbs[rows, :n] = d_b.astype(BF16)
        dbs[rows, n : 2 * n] = d_c.astype(BF16)
        dbs[rows, 2 * n :] = d_t.astype(BF16)
        lam[:, span_cols] = lam[:, span_cols] * etot_s[...] + mm(bc[rows, n:].astype(F32).T.astype(BF16), dyc_s[...])

    top = groups - 1

    def slot(q, c):
        return dg.at[q, c] if q < 2 else line_s.at[q - 2, c]

    def hop(q, c, dst, sem, to):
        return pltpu.make_async_remote_copy(
            src_ref=rows_s.at[q // 2, q % 2, c], dst_ref=dst, send_sem=rsend.at[q, c], recv_sem=sem,
            device_id={"head": to}, device_id_type=pl.DeviceIdType.MESH,
        )

    def send_up(q, c):
        @pl.when(me + 1 < q)
        def _():
            hop(q, c, slot(q, c), rrecv.at[q, c], me + 1).start()

        @pl.when(me + 1 == q)
        def _():
            hop(q, c, last_s.at[c], rrecv_own.at[c], me + 1).start()

    def send_down(q, c):
        hop(q, c, slot(q, c), rrecv.at[q, c], me - 1).start()

    def arrived(q, c):
        hop(q, c, slot(q, c), rrecv.at[q, c], me).wait_recv()

    def arrived_last(q, c):
        hop(q, c, last_s.at[c], rrecv_own.at[c], me).wait_recv()

    def begin(q):
        for c in range(ROW_CHUNKS):
            if q > 0:
                @pl.when(me == 0)
                def _():
                    send_up(q, c)
            if q < top:
                @pl.when(me == top)
                def _():
                    send_down(q, c)

    def relay(q, c, distance):
        if distance < q:
            @pl.when(me == distance)
            def _():
                arrived(q, c)
                add_block(rows_s, (q // 2, q % 2, c), slot(q, c), ())
                send_up(q, c)
        if top - distance > q:
            @pl.when(me == top - distance)
            def _():
                arrived(q, c)
                add_block(rows_s, (q // 2, q % 2, c), slot(q, c), ())
                send_down(q, c)

    def conv_back(rows, part):
        for c in range(part * span_num, (part + 1) * span_num, 128):
            cols = slice(c, c + 128)
            inner_v = inn[rows, cols].astype(F32)
            d_in = jnp.zeros((rows_num, 128), F32)
            for k in range(4):
                shifted = dconv[3 - k : 3 - k + rows_num, cols]
                d_in += convw_ref[k : k + 1, cols] * shifted
                vec_s[k : k + 1, cols] += jnp.sum(inner_v * shifted, axis=0, keepdims=True)
            vec_s[4:5, cols] += jnp.sum(dconv[0:rows_num, cols], axis=0, keepdims=True)
            inn[rows, cols] = d_in.astype(BF16)
        kept = pl.ds(part * span_num, span_num)
        dconv[rows_num:, kept] = dconv[0:8, kept]

    def row_grads(q, rows):
        wide_tile = 2 * tile
        per = model // ROW_CHUNKS // wide_tile

        def columns(t, carry):
            cols = pl.ds(pl.multiple_of(t * wide_tile, wide_tile), wide_tile)
            value = mm_nt(a[rows, :], zw[cols, :]) + mm_nt(inn[rows, :], xw[cols, :]) + mm_nt(dbs[rows, :], bdw[cols, :])
            pre_s[:, cols] += jnp.sum(value * x[rows, cols].astype(F32), axis=0, keepdims=True)
            rows_s[q // 2, q % 2, t // per, :, pl.ds(pl.multiple_of((t % per) * wide_tile, wide_tile), wide_tile)] = value.astype(BF16)
            return carry

        lax.fori_loop(0, model // wide_tile, columns, 0)

    plan = {(part, k, spot): [] for part in range(BACK_PARTS) for k in range(groups) for spot in "ab"}

    def book(stream, slots):
        for slot in slots:
            if stream.steps:
                plan[slot].append(stream.steps.pop(0))

    plan[0, 0, "a"].append(late_loads)
    for st in streams[:2]:
        book(st, BACK_POLLS["z"])
    book(outs, BACK_POLLS["out"])
    for i, st in enumerate(spread):
        book(st, BACK_POLLS["spread"][i])
    last = BACK_PARTS - 1
    for k in range(groups):
        plan[last, k, "b"].insert(0, lambda q=top - k: begin(q))
    for spot, q, c, distance in BACK_POLLS["relay"]:
        plan[spot].append(lambda q=q, c=c, distance=distance: relay(q, c, distance))

    for part in range(BACK_PARTS):
        def quarter_step(i, carry):
            q = groups - 1 - i
            rows = pl.ds(pl.multiple_of(q * rows_num, rows_num), rows_num)

            def one(j, inner_carry):
                block(q * subs + subs - 1 - j, subs - 1 - j, part)
                return inner_carry

            lax.fori_loop(0, subs, one, 0)

            def polls(spot):
                for k in range(groups):
                    if plan[part, k, spot]:
                        @pl.when(i == k)
                        def _():
                            for action in plan[part, k, spot]:
                                action()

            polls("a")
            conv_back(rows, part)
            if part == last:
                row_grads(q, rows)
            polls("b")
            return carry

        lax.fori_loop(0, groups, quarter_step, 0)

    drain(streams[:2])
    tail = list(BACK_POLLS["tail"])
    booked = {key[1:] for key in BACK_POLLS["relay"]}
    relays = [r for r in RELAY_ORDER if r not in booked]

    def relay_some():
        for _ in range(tail.pop(0) if tail else 1):
            if relays:
                relay(*relays.pop(0))

    def state_grad(t, carry):
        put(bcbuf, t, mm_tn(x[:, pl.ds(pl.multiple_of(t * tile, tile), tile)], dbs[...]))
        return carry

    lax.fori_loop(0, model // tile, state_grad, 0)
    advance_all(state)
    per = X_STREAMS // 2
    x_pairs = [streams[2 + h * per : 2 + (h + 1) * per] for h in range(2)]
    for h in range(2):
        cols = pl.ds(h * z_width, z_width)
        weight_grad(inn.at[:, cols], zg.at[(slice(None),) * (count + 1) + (cols,)])
        advance_all(x_pairs[h])
        relay_some()
        advance_all(state)
    small[...] = jnp.zeros_like(small)
    for j in range(groups):
        small[j : j + 1, :] = gain_ref[j]
    for j in range(model // channels):
        small[groups + j : groups + j + 1, :] = pre_s[:, j * channels : (j + 1) * channels]
    small[8:14, :] = vec_s[0:6, :]
    totals = lax.dot_general(
        jnp.ones((8, SPAN), F32), head_s[...], (((1,), (1,)), ((), ())),
        preferred_element_type=F32, precision=HIGHEST,
    )
    small[14:15, 0:128] = totals[0:1]
    vectors.advance()
    while relays or any(st.steps for st in streams + state + spread + [vectors, outs]):
        advance_all(x_pairs[0])
        relay_some()
        advance_all(state + [vectors])
        advance_all(x_pairs[1])
        relay_some()
        advance_all(spread + [outs])
    small_out[...] = small[...]

    piece = model // ROW_CHUNKS
    for c in range(ROW_CHUNKS):
        for q in range(groups):
            @pl.when(me == q)
            def _():
                if q > 0:
                    arrived_last(q, c)
                if q < top:
                    arrived(q, c)

                def total(r, carry):
                    rs = pl.ds(pl.multiple_of(r * 32, 32), 32)
                    value = rows_s[q // 2, q % 2, c, rs, :].astype(F32)
                    if q > 0:
                        value += last_s[c, rs, :].astype(F32)
                    if q < top:
                        value += slot(q, c)[rs, :].astype(F32)
                    own_out[rs, c * piece : (c + 1) * piece] = value
                    return carry

                lax.fori_loop(0, rows_num // 32, total, 0)

            @pl.when(me != q)
            def _():
                hop(q, c, slot(q, c), rrecv.at[q, c], me).wait_send()


def back_call(z_grad, res, x, bc, step, prev, zw, xw, bcw, dtw, out_part, out_own, gain_grad, convw, alog, skip, groups, batches):
    length, model = x.shape
    channels = xw.shape[1]
    n = bc.shape[1] // 2
    heads = dtw.shape[0]
    rows_num = length // groups
    count = log2(batches)
    group_bits = log2(groups)
    lead = (2,) * count
    part = channels // batches
    rows = model // batches
    wide = 2 * n + 128
    hbm = pl.BlockSpec(memory_space=pl.ANY)
    vmem = pl.BlockSpec(memory_space=pltpu.VMEM)
    dma = pltpu.SemaphoreType.DMA
    copies = (2 + X_STREAMS) * 2 * count + 2 * (2 * count + groups - 1) + (count + group_bits) + group_bits + 2 * count
    tall = lambda w, t: pltpu.VMEM((length, w), t)
    span = pltpu.VMEM((SPAN, channels // BACK_PARTS), BF16)
    z, xg, o, bcg, small, own = pl.pallas_call(
        functools.partial(back_kernel, count, group_bits),
        in_specs=[hbm] * 16 + [vmem] * 4,
        out_specs=[hbm] * 4 + [vmem] * 2,
        out_shape=[
            jax.ShapeDtypeStruct(lead + (rows, channels), BF16),
            jax.ShapeDtypeStruct(lead + (rows, channels), BF16),
            jax.ShapeDtypeStruct(lead + (part, model), BF16),
            jax.ShapeDtypeStruct(lead + (rows, wide), BF16),
            jax.ShapeDtypeStruct((16, channels), F32),
            jax.ShapeDtypeStruct((rows_num, model), F32),
        ],
        scratch_shapes=[pltpu.VMEM((2, groups, rows_num, channels // 2), BF16)] + [tall(channels, BF16)] * 5
        + [
            tall(model, BF16), tall(2 * n, BF16), tall(128, F32), pltpu.VMEM(prev.shape, BF16),
            pltpu.VMEM(zw.shape, BF16), pltpu.VMEM(xw.shape, BF16), pltpu.VMEM((model, wide), BF16),
            pltpu.VMEM(dtw.shape, BF16),
            pltpu.VMEM((2,) * group_bits + (part, model // 2), BF16), pltpu.VMEM((part, model // 2), BF16),
            pltpu.VMEM((heads, channels), BF16), pltpu.VMEM((8, 128), F32),
            pltpu.VMEM((n, channels), F32), pltpu.VMEM((rows_num + 8, channels), F32),
        ]
        + [span] * 5
        + [
            pltpu.VMEM((heads // BACK_PARTS, SPAN), F32), pltpu.VMEM((1, channels // BACK_PARTS), F32),
            pltpu.VMEM((128, SPAN), F32),
            pltpu.VMEM((128, SPAN), F32), pltpu.VMEM((8, channels), F32), pltpu.VMEM((1, model), F32),
            tall(wide, BF16),
            pltpu.VMEM((2, 2, ROW_CHUNKS, rows_num, model // ROW_CHUNKS), BF16),
            pltpu.VMEM((2, ROW_CHUNKS, rows_num, model // ROW_CHUNKS), BF16),
            pltpu.VMEM((ROW_CHUNKS, rows_num, model // ROW_CHUNKS), BF16),
            pltpu.VMEM(lead + (rows, channels), BF16), pltpu.VMEM(lead + (rows, wide), BF16),
            pltpu.VMEM((16, channels), F32),
        ]
        + [s for _ in range(2) for s in halving_slots(count, (rows, channels // 2), BF16)]
        + halving_slots(count, (rows, n + 128), BF16)
        + halving_slots(count, (rows, n), BF16)
        + [pltpu.VMEM((rows, n), BF16)] * (2 * (groups - 1))
        + [pltpu.VMEM((16, channels), F32)] * count
        + [pltpu.VMEM((8, channels), F32)] * group_bits
        + halving_slots(group_bits, (part, model // 2), BF16)
        + [dma((17,)), dma((6 + X_STREAMS,)),
            dma((groups, ROW_CHUNKS)), dma((groups, ROW_CHUNKS)), dma((ROW_CHUNKS,)), dma((copies,)), dma((copies,))],
        compiler_params=pltpu.CompilerParams(
            collective_id=3, has_side_effects=True, vmem_limit_bytes=BACK_VMEM_BYTES
        ),
        cost_estimate=pl.CostEstimate(
            flops=10 * length * model * channels, bytes_accessed=300 * 2**20, transcendentals=0
        ),
        name="back",
    )(
        z_grad.reshape(lead + (rows, channels)), *res, x, bc, step, prev, zw, xw, bcw, dtw, out_part, out_own,
        gain_grad, convw, alog, skip,
    )
    return (
        z.reshape(model, channels), xg.reshape(model, channels), o.reshape(channels, model),
        bcg.reshape(model, wide), small, own,
    )


def finish_kernel(
    z_ref, x_ref, o_ref, bc_ref, small_ref, own_ref, tok_ref, cot_ref, pre_ref, out_ref,
    zf_ref, xf_ref, of_ref, bcf_ref, dt_ref, grad_ref, outf_ref, convw_ref, convb_ref, skip_ref, gain_ref, pre_out, dtb_ref, alog_ref,
):
    zf_ref[...] = z_ref[...].astype(F32)
    xf_ref[...] = x_ref[...].astype(F32)
    of_ref[...] = o_ref[...].astype(F32)
    width = bcf_ref.shape[1]
    heads = dt_ref.shape[0]
    outf_ref[...] = out_ref[...]
    bcf_ref[...] = bc_ref[:, :width].astype(F32)
    dt_ref[...] = bc_ref[:, width : width + 128].astype(F32).T[:heads]
    tok = tok_ref[...].astype(F32)
    recip = lax.rsqrt(jnp.mean(tok * tok, axis=-1, keepdims=True) + EPSILON)
    scaled = pre_ref[...] * own_ref[...]
    mean = jnp.mean(tok * scaled, axis=-1, keepdims=True)
    passed = sum(cot_ref[w].astype(F32) for w in range(4))
    grad_ref[...] = (passed + recip * scaled - tok * recip**3 * mean).astype(BF16)

    @pl.when(pl.program_id(0) == 0)
    def _():
        groups = small_ref.shape[0] // 4
        channels = small_ref.shape[1]
        convw_ref[...] = small_ref[8:12, :]
        convb_ref[...] = small_ref[12:13, :]
        skip_ref[...] = small_ref[13:14, :]
        me = lax.axis_index("head")
        gain = small_ref[0:1, :]
        for j in range(1, groups):
            gain = jnp.where(me == j, small_ref[j : j + 1, :], gain)
        gain_ref[...] = gain
        for j in range(pre_out.shape[1] // channels):
            cols = slice(j * channels, (j + 1) * channels)
            pre_out[:, cols] = small_ref[groups + j : groups + j + 1, :] / pre_ref[:, cols]
        dtb_ref[...] = small_ref[14:15, 0:heads]
        alog_ref[...] = small_ref[14:15, heads : 2 * heads]


def finish_call(z, x, o, bc, small, own, tok, cot, pre_gain, out, heads):
    model, channels = z.shape
    rows_num = tok.shape[0]
    steps = 8
    wide = bc.shape[1]
    rows = lambda r, w: pl.BlockSpec((r // steps, w), lambda i: (i, 0))
    fixed = lambda shape: pl.BlockSpec(shape, lambda i: (0, 0))
    shapes = [
        ((model, channels), F32), ((model, channels), F32), ((channels, model), F32), ((model, wide - 128), F32),
    ]
    wide4 = pl.BlockSpec((4, rows_num // steps, model), lambda i: (0, i, 0))
    flat = [(4, channels), (1, channels), (1, channels), (1, channels), (1, model), (1, heads), (1, heads)]
    return pl.pallas_call(
        finish_kernel,
        grid=(steps,),
        in_specs=[
            rows(model, channels), rows(model, channels), rows(channels, model), rows(model, wide),
            fixed(small.shape), rows(rows_num, model), rows(rows_num, model),
            wide4, fixed((1, model)), wide4,
        ],
        out_specs=[rows(*shape) for shape, _ in shapes]
        + [pl.BlockSpec((heads, model // steps), lambda i: (0, i)), rows(rows_num, model), wide4]
        + [fixed(shape) for shape in flat],
        out_shape=[jax.ShapeDtypeStruct(shape, t) for shape, t in shapes]
        + [
            jax.ShapeDtypeStruct((heads, model), F32), jax.ShapeDtypeStruct((rows_num, model), BF16),
            jax.ShapeDtypeStruct(out.shape, BF16),
        ]
        + [jax.ShapeDtypeStruct(shape, F32) for shape in flat],
        compiler_params=pltpu.CompilerParams(vmem_limit_bytes=VMEM_BYTES),
        cost_estimate=pl.CostEstimate(flops=0, bytes_accessed=46 * 2**20, transcendentals=0),
        name="finish",
    )(z, x, o, bc, small, own, tok, cot, pre_gain[None], out)


def per_device(
    tokens, z_weight, x_weight, bc_weight, dt_weight, conv_weight, conv_bias, dt_bias,
    a_log, skip, norm_gain, pre_gain, out_weight, cotangent,
):
    groups = lax.axis_size("head")
    batches = lax.axis_size("batch")
    _, own_len, model = tokens.shape
    tokens = tokens[0]
    cot = cotangent[:, 0]
    channels = z_weight.shape[1]
    heads = dt_weight.shape[1]
    dtw = dt_weight.T
    alog = a_log[None]
    skip_r = skip[None]
    x, res, bc, step, prev, gated, w_all, gain_all = front_call(
        tokens, pre_gain, z_weight, x_weight, bc_weight, dtw, out_weight, norm_gain,
        conv_weight, conv_bias[None], dt_bias[None], alog, skip_r, groups, batches,
    )
    outputs, d_gate, d_scanned, z_grad, out_own, out_part, gain_grad = middle_call(
        gated, w_all, gain_all, tokens, cot, x, res[0], res[1], batches
    )
    z_grad, x_grad, out_grad, bcdt_grad, small, d_own = back_call(
        z_grad, (d_gate, d_scanned) + res[2:], x, bc, step, prev, z_weight, x_weight, bc_weight, dtw, out_part, out_own, gain_grad,
        conv_weight, alog, skip_r, groups, batches,
    )
    (
        z_grad, x_grad, out_grad, bc_grad, dt_grad, tokens_grad, outputs, convw, convb, skip_g, gain_g, pre_g, dtb_g, alog_g,
    ) = finish_call(z_grad, x_grad, out_grad, bcdt_grad, small, d_own, tokens, cot, pre_gain, outputs, heads)
    flat = lambda v: v.reshape(-1)
    return (
        outputs[:, None], tokens_grad[None], z_grad, x_grad, bc_grad, dt_grad.T, convw, flat(convb), flat(dtb_g),
        flat(alog_g), flat(skip_g), flat(gain_g), flat(pre_g), out_grad,
    )


def solution(mesh):
    head_cols = P(None, "head")
    rows4 = P(None, "batch", "head", None)
    return jax.shard_map(
        per_device,
        mesh=mesh,
        in_specs=(
            P("batch", "head", None), head_cols, head_cols, P(), head_cols, head_cols, P("head"),
            P("head"), P("head"), P("head"), P("head"), P(), P("head", None), rows4,
        ),
        out_specs=(
            rows4, P("batch", "head", None), head_cols, head_cols, P(), head_cols, head_cols,
            P("head"), P("head"), P("head"), P("head"), P("head"), P(), P("head", None),
        ),
        check_vma=False,
    )
```

```python
import functools
import itertools

import jax
import jax.numpy as jnp
from jax import lax
from jax.experimental import pallas as pl
from jax.experimental.pallas import tpu as pltpu
from jax.sharding import PartitionSpec as P

SPAN = 128
HEAD_PARTS = 2
ROW_CHUNKS = 4
BACK_PARTS = 1
X_STREAMS = 4
EPSILON = 1e-05
BF16 = jnp.bfloat16
F32 = jnp.float32
HIGHEST = lax.Precision.HIGHEST
VMEM_BYTES = 60 * 1024 * 1024
BACK_VMEM_BYTES = 63 * 1024 * 1024


def mm(a, b):
    return lax.dot_general(a, b, (((1,), (0,)), ((), ())), preferred_element_type=F32)


def mm_nt(a, b):
    return lax.dot_general(a, b, (((1,), (1,)), ((), ())), preferred_element_type=F32)


def mm_tn(a, b):
    return lax.dot_general(a, b, (((0,), (0,)), ((), ())), preferred_element_type=F32)


def mm_exact(a, b):
    return lax.dot_general(
        a, b, (((1,), (0,)), ((), ())), preferred_element_type=F32, precision=HIGHEST
    )


def lower_mask(shape):
    return lax.broadcasted_iota(jnp.int32, shape, 0) >= lax.broadcasted_iota(jnp.int32, shape, 1)


def softplus(v):
    return jnp.maximum(v, 0.0) + jnp.log1p(jnp.exp(-jnp.abs(v)))


def sigmoid(v):
    return 1.0 / (1.0 + jnp.exp(-v))


def pair_columns(values, pair, left):
    shape = (SPAN, 128)
    one = jnp.broadcast_to(values[:, 2 * pair : 2 * pair + 1], shape)
    two = jnp.broadcast_to(values[:, 2 * pair + 1 : 2 * pair + 2], shape)
    return one, two, jnp.where(left, one, two)


def segments(channels):
    ends = [channels * 2**w // 8 for w in range(4)]
    return list(zip([0] + ends[:-1], ends))


def partner(axis, bit):
    me = lax.axis_index(axis)
    return me + (1 - 2 * ((me // 2**bit) % 2)) * 2**bit


def bits_of(axis, count):
    me = lax.axis_index(axis)
    return [(me // 2**b) % 2 for b in range(count)]


def log2(value):
    return value.bit_length() - 1


def place(bits, fixed):
    bits = range(bits) if isinstance(bits, int) else sorted(bits)
    return tuple(fixed[b] if b in fixed else slice(None) for b in reversed(bits))


class Links:
    def __init__(self, send, recv):
        self.send, self.recv, self.used = send, recv, 0

    def copy(self, src, dst, axis, to):
        at = self.used
        self.used += 1
        return pltpu.make_async_remote_copy(
            src_ref=src, dst_ref=dst, send_sem=self.send.at[at], recv_sem=self.recv.at[at],
            device_id={axis: to}, device_id_type=pl.DeviceIdType.MESH,
        )


def meet(peers):
    barrier = pltpu.get_barrier_semaphore()
    for axis, to in peers:
        pl.semaphore_signal(barrier, inc=1, device_id={axis: to}, device_id_type=pl.DeviceIdType.MESH)
    pl.semaphore_wait(barrier, len(peers))


def add_block(buf, index, slot, at):
    rows = slot.shape[-2]
    step = min(rows, 32)
    index = index + (slice(None),) * (len(buf.shape) - len(index))
    free = [i for i, v in enumerate(index[:-2]) if isinstance(v, slice)]
    full = list(index[:-2])
    for i, v in zip(free, at):
        full[i] = v
    full = tuple(full)

    def piece(r, carry):
        rs = pl.ds(pl.multiple_of(r * step, step), step)
        total = buf[full + (rs, index[-1])].astype(F32) + slot[tuple(at) + (rs, slice(None))].astype(F32)
        buf[full + (rs, index[-1])] = total.astype(buf.dtype)
        return carry

    lax.fori_loop(0, rows // step, piece, 0)


def halving_slots(count, block, dtype):
    return [pltpu.VMEM((2,) * (count - 1 - i) + tuple(block), dtype) for i in range(count)]


class Stream:
    def __init__(self, *parts):
        self.steps = []
        for part in parts:
            if self.steps and part:
                last, first = self.steps.pop(), part[0]
                self.steps.append(lambda last=last, first=first: (last(), first()))
                part = part[1:]
            self.steps.extend(part)

    def advance(self):
        if self.steps:
            self.steps.pop(0)()


def advance_all(streams):
    for s in streams:
        s.advance()


def drain(streams):
    while any(s.steps for s in streams):
        advance_all(streams)


def exchanging_once(ports, axis, bits, buf, slots):
    def to(k):
        return lax.axis_index(axis) + sum(
            (1 - 2 * b) * 2**i for i, b in enumerate(bits_of(axis, bits)) if k & 2**i
        )

    copies = [
        ports.make(buf, lambda k=k: slots[k - 1], axis, lambda k=k: to(k)) for k in range(1, 2**bits)
    ]

    def start():
        for copy in copies:
            copy().start()

    def finish():
        for copy in copies:
            copy().wait()
        ref = buf()
        ref[...] = (ref[...].astype(F32) + sum(slot[...].astype(F32) for slot in slots)).astype(ref.dtype)

    return [start, finish]


class Ports:
    def __init__(self, send, recv):
        self.send, self.recv, self.used = send, recv, 0

    def make(self, src, dst, axis, to):
        at = self.used
        self.used += 1

        def describe():
            return pltpu.make_async_remote_copy(
                src_ref=src(), dst_ref=dst(), send_sem=self.send.at[at], recv_sem=self.recv.at[at],
                device_id={axis: to()}, device_id_type=pl.DeviceIdType.MESH,
            )

        return describe


def linked(copies, work):
    steps = []
    for i in range(len(copies) + 1):
        def step(i=i):
            if i:
                copies[i - 1]().wait()
                work(i - 1)
            if i < len(copies):
                copies[i]().start()

        steps.append(step)
    return steps


def halving(ports, axis, buf, slots, order):
    count = len(order)

    def fixed(i, give):
        mine = bits_of(axis, max(order) + 1)
        out = {b: mine[b] for b in order[: i + 1]}
        if give:
            out[order[i]] = 1 - out[order[i]]
        return out

    copies = [
        ports.make(
            lambda i=i: buf().at[place(order, fixed(i, True))], lambda i=i: slots[i],
            axis, lambda i=i: partner(axis, order[i]),
        )
        for i in range(count)
    ]

    def work(i):
        for at in itertools.product(*(range(d) for d in slots[i].shape[:-2])):
            add_block(buf(), place(order, fixed(i, False)), slots[i], at)

    return linked(copies, work)


def spreading(ports, axis, view, order, own, sem):
    count = len(order)

    def at(i):
        mine = bits_of(axis, count)
        return view().at[place(count, {b: mine[b] for b in order[i:]})]

    copies = [
        ports.make(
            (lambda i=i: at(i)) if i else own, lambda i=i: at(i), axis, lambda i=i: partner(axis, order[i])
        )
        for i in range(count)
    ]

    def kept():
        return pltpu.make_async_copy(own(), at(0), sem)

    def work(i):
        if i == 0:
            kept().wait()

    steps = linked(copies, work)
    first = steps[0]
    steps[0] = lambda: (kept().start(), first())
    return steps


def exchanging(ports, axis, buf, slots, order):
    copies = [
        ports.make(buf, lambda i=i: slots[i], axis, lambda i=i: partner(axis, order[i])) for i in range(len(order))
    ]

    def work(i):
        ref = buf()
        ref[...] = (ref[...].astype(F32) + slots[i][...].astype(F32)).astype(ref.dtype)

    return linked(copies, work)


PIECE_POLLS = (
    ("a", 0), ("a", 1), ("c", 2), ("c", 0), ("d", 1), ("e", 0), (1, 1), (2, 2), (3, 0), (4, 1), (5, 2), (7, 2),
)


def front_kernel(
    count, tok_ref, pre_ref, zw_hbm, xw_hbm, bcw_hbm, dtw_hbm, w_hbm, gain_hbm,
    convw_ref, convb_ref, dtb_ref, alog_ref, skip_ref,
    x_out, a_out, s_out, act_out, dsc_out, inn_out, bc_out, step_out, prev_out, gated_out, all_ref, gains_ref,
    xs, zw, xw, bcw, dtw, wv, gate_s, a_s, s_s, act_s, dsc_s, inn_s, inner_s, bc_s, bcb_s, step_s, prev_s, gated_s, state, tails,
    cum_s, cum_t_s, inner_prod_s, b_t_s, pad_s, load_sem, local_sem, store_sem, away_sem, here_sem, send, recv, send2, recv2,
):
    rows_num, channels = gated_s.shape[1:]
    groups = gated_s.shape[0]
    length = groups * rows_num
    n = state.shape[0]
    model = tok_ref.shape[1]
    chunks = 2
    chunk = rows_num // chunks
    me = lax.axis_index("head")
    hi, lo = me // 2, me % 2
    near = partner("head", 0)
    far = partner("head", 1)
    others = [near, far, near + far - me]
    links = Links(send, recv)

    loads = [
        pltpu.make_async_copy(src, dst, load_sem.at[i])
        for i, (src, dst) in enumerate(((zw_hbm, zw), (xw_hbm, xw), (bcw_hbm, bcw), (dtw_hbm, dtw), (w_hbm, wv)))
    ]
    for load in loads:
        load.start()
    tok = tok_ref[...].astype(F32)
    recip = lax.rsqrt(jnp.mean(tok * tok, axis=-1, keepdims=True) + EPSILON)
    xs[hi, lo] = (tok * recip * pre_ref[...]).astype(BF16)
    meet([("head", z) for z in others] + [("batch", partner("batch", b)) for b in range(count)])

    own_rows = xs.at[hi, lo]
    to_far = []
    for c in range(chunks):
        part = xs.at[hi, lo, pl.ds(c * chunk, chunk)]
        to_far.append(links.copy(part, part, "head", far))
        to_far[-1].start()
    to_near = links.copy(own_rows, own_rows, "head", near)
    to_near.start()
    half = w_hbm.shape[-1] // 2

    def pieces(z, cols, order):
        def own_piece(ref):
            return ref.at[place(count, dict(enumerate(bits_of("batch", count)))) + (slice(None), cols)]

        first = ports.make(
            lambda: own_piece(w_hbm), lambda: own_piece(all_ref.at[lax.axis_index("head")]), "head", z
        )

        def at(i):
            bits = bits_of("batch", count)
            return all_ref.at[(z(),) + place(count, {b: bits[b] for b in order[i:]}) + (slice(None), cols)]

        rest = [
            ports.make(lambda i=i: at(i), lambda i=i: at(i), "batch", lambda i=i: partner("batch", order[i]))
            for i in range(count)
        ]
        return Stream(linked([first] + rest, lambda i: None))

    up = list(range(1, count))
    ports = Ports(send2, recv2)
    near_at = lambda: partner("head", 0)
    far_at = lambda: partner("head", 1)
    streams = []
    for z in (near_at, far_at, lambda: near_at() + far_at() - lax.axis_index("head")):
        streams.append(pieces(z, pl.ds(0, half), up + [0]))
        streams.append(pieces(z, pl.ds(half, half), up[::-1] + [0]))
    plan = [[] for _ in range(HEAD_PARTS * groups)]
    early = {spot: [] for spot in "abcde"}
    for spot, group in PIECE_POLLS:
        for st in streams[2 * group : 2 * group + 2]:
            if st.steps:
                (early[spot] if spot in early else plan[spot]).append(st.steps.pop(0))

    def poll(spot):
        for action in early[spot]:
            action()

    poll("a")
    keep = [pltpu.make_async_copy(gain_hbm, gains_ref.at[me], local_sem.at[1])]
    keep[0].start()
    inner_s[0:8, :] = jnp.zeros((8, channels), F32)
    state[...] = jnp.zeros_like(state)
    step_s[...] = jnp.zeros_like(step_s)
    pad_s[...] = jnp.zeros_like(pad_s)
    pad_s[0:1, 0 : dtw.shape[0]] = dtb_ref[...]
    pad_s[1:2, 0 : dtw.shape[0]] = alog_ref[...]
    for load in loads:
        load.wait()
    keep.append(pltpu.make_async_copy(wv, all_ref.at[me], local_sem.at[0]))
    keep[-1].start()

    def project(at_hi, at_lo):
        first = pl.multiple_of((2 * at_hi + at_lo) * rows_num, rows_num)
        rows = pl.ds(first, rows_num)
        inner_rows = pl.ds(pl.multiple_of(first + 8, 8), rows_num)
        tile = 256

        def columns(t, carry):
            cols = pl.ds(pl.multiple_of(t * tile, tile), tile)
            x = xs[at_hi, at_lo]
            gate_s[rows, cols] = mm(x, zw[:, cols])
            inner_s[inner_rows, cols] = mm(x, xw[:, cols])
            return carry

        lax.fori_loop(0, channels // tile, columns, 0)
        x = xs[at_hi, at_lo]
        bc_s[rows, :] = mm(x, bcw[...])
        step_s[rows, 0 : dtw.shape[0]] = mm_nt(x, dtw[...])

    project(hi, lo)
    to_near.wait()
    project(hi, 1 - lo)
    poll("b")
    onward = []
    for c in range(chunks):
        to_far[c].wait()
        part = xs.at[1 - hi, lo, pl.ds(c * chunk, chunk)]
        onward.append(links.copy(part, part, "head", near))
        onward[-1].start()

    poll("c")
    gain_sends = [links.copy(gain_hbm, gains_ref.at[me], "head", z) for z in others]
    for item in gain_sends:
        item.start()

    project(1 - hi, lo)
    poll("d")
    for item in onward:
        item.wait()
    project(1 - hi, 1 - lo)
    poll("e")

    rate = -jnp.exp(pad_s[1:2, :])
    lower = lower_mask((SPAN, SPAN))
    lower_f = lower.astype(F32)
    left = lax.broadcasted_iota(jnp.int32, (SPAN, 128), 1) < 64

    span_num = channels // HEAD_PARTS

    def block(at, part):
        first = pl.multiple_of(at * SPAN, SPAN)
        rows = pl.ds(first, SPAN)
        if part == 0:
            delta = softplus(step_s[rows, :] + pad_s[0:1, :])
            cum = mm_exact(lower_f, delta * rate)
            cum_t = cum.T
            bcb_s[rows, :] = bc_s[rows, :].astype(BF16)
            inner = jnp.where(lower, mm_nt(bcb_s[rows, n:], bcb_s[rows, :n]), 0.0)
            b_t = bc_s[rows, :n].T.astype(BF16)
            step_s[rows, :] = delta
            cum_s[at], cum_t_s[at], inner_prod_s[at], b_t_s[at] = cum, cum_t, inner, b_t
        else:
            delta = step_s[rows, :]
            cum, cum_t, inner, b_t = cum_s[at], cum_t_s[at], inner_prod_s[at], b_t_s[at]
        span_cols = pl.ds(part * span_num, span_num)
        before = state[:, span_cols].astype(BF16)
        prev_s[at, :, span_cols] = before
        across = mm(bcb_s[rows, n:], before)
        quarter = at // (rows_num // SPAN)
        sub = pl.ds(pl.multiple_of((at % (rows_num // SPAN)) * SPAN, SPAN), SPAN)
        for pair in range(part * span_num // 128, (part + 1) * span_num // 128):
            cols = slice(pair * 128, pair * 128 + 128)
            local = slice(pair * 128 - part * span_num, pair * 128 + 128 - part * span_num)
            c0, c1, ce = pair_columns(cum, pair, left)
            _, _, de = pair_columns(delta, pair, left)
            tot = ce[SPAN - 1 : SPAN, :]
            window = inner_s[pl.ds(first, SPAN + 8), cols]
            conv_p = convb_ref[:, cols] + sum(
                convw_ref[k : k + 1, cols] * window[5 + k : 5 + k + SPAN] for k in range(4)
            )
            inn_s[rows, cols] = window[8:].astype(BF16)
            sc = sigmoid(conv_p)
            act = conv_p * sc
            act_s[rows, cols] = act.astype(BF16)
            dsc_s[rows, cols] = (sc + act * (1.0 - sc)).astype(BF16)
            u = act * de
            tails[:, local] = (u * jnp.exp(tot - ce)).astype(BF16)
            u0 = jnp.where(left, u, 0.0).astype(BF16)
            u1 = jnp.where(left, 0.0, u).astype(BF16)
            p0 = (jnp.exp(jnp.minimum(c0 - cum_t[2 * pair : 2 * pair + 1, :], 0.0)) * inner).astype(BF16)
            p1 = (jnp.exp(jnp.minimum(c1 - cum_t[2 * pair + 1 : 2 * pair + 2, :], 0.0)) * inner).astype(BF16)
            within = mm(jnp.concatenate([p0, p1], axis=1), jnp.concatenate([u0, u1], axis=0))
            y = within + across[:, local] * jnp.exp(ce) + skip_ref[:, cols] * act
            gate = gate_s[rows, cols]
            sg = sigmoid(gate)
            sl = gate * sg
            s_s[rows, cols] = sl.astype(BF16)
            a_s[rows, cols] = (y * (sg + sl * (1.0 - sg))).astype(BF16)
            gated_s[quarter, sub, cols] = (y * sl).astype(BF16)
            state[:, cols] = state[:, cols] * jnp.exp(tot)
        state[:, span_cols] += mm(b_t, tails[...])

    def leave(q, part):
        cols = pl.ds(part * span_num, span_num)
        return pltpu.make_async_remote_copy(
            src_ref=gated_s.at[q, :, cols], dst_ref=gated_out.at[me, :, cols],
            send_sem=away_sem.at[part, q], recv_sem=here_sem.at[part, me],
            device_id={"head": q}, device_id_type=pl.DeviceIdType.MESH,
        )

    def arrive(q, part):
        cols = pl.ds(part * span_num, span_num)
        return pltpu.make_async_remote_copy(
            src_ref=gated_s.at[q, :, cols], dst_ref=gated_out.at[q, :, cols],
            send_sem=away_sem.at[part, q], recv_sem=here_sem.at[part, q],
            device_id={"head": q}, device_id_type=pl.DeviceIdType.MESH,
        )

    subs = rows_num // SPAN

    def stores(q):
        rows = pl.ds(pl.multiple_of(q * rows_num, rows_num), rows_num)
        pairs = (
            (xs.at[q // 2, q % 2], x_out.at[rows]),
            (a_s.at[rows], a_out.at[rows]),
            (s_s.at[rows], s_out.at[rows]),
            (act_s.at[rows], act_out.at[rows]),
            (dsc_s.at[rows], dsc_out.at[rows]),
            (inn_s.at[rows], inn_out.at[rows]),
            (bcb_s.at[rows], bc_out.at[rows]),
            (step_s.at[rows], step_out.at[rows]),
            (prev_s.at[pl.ds(q * subs, subs)], prev_out.at[pl.ds(q * subs, subs)]),
        )
        return [pltpu.make_async_copy(src, dst, store_sem.at[i, q]) for i, (src, dst) in enumerate(pairs)]

    for part in range(HEAD_PARTS):
        def quarter_step(q, carry):
            def one(at, inner_carry):
                block(at, part)
                return inner_carry

            lax.fori_loop(q * subs, (q + 1) * subs, one, 0)

            @pl.when(q != me)
            def _():
                leave(q, part).start()

            if part == HEAD_PARTS - 1:
                for item in stores(q):
                    item.start()
            for k in range(groups):
                @pl.when(q == k)
                def _():
                    for action in plan[part * groups + k]:
                        action()
            return carry

        lax.fori_loop(0, groups, quarter_step, 0)
    stay = pltpu.make_async_copy(gated_s.at[me], gated_out.at[me], local_sem.at[2])
    stay.start()
    drain(streams)
    for item in gain_sends:
        item.wait()
    for item in keep:
        item.wait()
    stay.wait()

    def finish(q, carry):
        @pl.when(q != me)
        def _():
            for part in range(HEAD_PARTS):
                leave(q, part).wait_send()
                arrive(q, part).wait_recv()

        for item in stores(q):
            item.wait()
        return carry

    lax.fori_loop(0, groups, finish, 0)


def front_call(tokens, pre_gain, zw, xw, bcw, dtw, out_weight, norm_gain, convw, convb, dtb, alog, skip, groups, batches):
    rows_num, model = tokens.shape
    channels = zw.shape[1]
    n = bcw.shape[1] // 2
    length = rows_num * groups
    count = log2(batches)
    part = channels // batches
    copies = 5 + groups - 1
    piece_copies = 2 * (groups - 1) * (1 + count)
    hbm = pl.BlockSpec(memory_space=pl.ANY)
    vmem = pl.BlockSpec(memory_space=pltpu.VMEM)
    wide = jax.ShapeDtypeStruct((length, channels), BF16)
    outs = [
        jax.ShapeDtypeStruct((length, model), BF16), wide, wide, wide, wide, wide,
        jax.ShapeDtypeStruct((length, 2 * n), BF16),
        jax.ShapeDtypeStruct((length, 128), F32),
        jax.ShapeDtypeStruct((length // SPAN, n, channels), BF16),
        jax.ShapeDtypeStruct((groups, rows_num, channels), BF16),
        jax.ShapeDtypeStruct((groups,) + (2,) * count + (part, model), BF16),
        jax.ShapeDtypeStruct((groups, 1, channels), F32),
    ]
    dma = pltpu.SemaphoreType.DMA
    result = pl.pallas_call(
        functools.partial(front_kernel, count),
        in_specs=[vmem, vmem] + [hbm] * 6 + [vmem] * 5,
        out_specs=[hbm] * len(outs),
        out_shape=outs,
        scratch_shapes=[
            pltpu.VMEM((2, 2, rows_num, model), BF16),
            pltpu.VMEM(zw.shape, BF16), pltpu.VMEM(xw.shape, BF16),
            pltpu.VMEM(bcw.shape, BF16), pltpu.VMEM(dtw.shape, BF16),
            pltpu.VMEM((2,) * count + (part, model), BF16),
            pltpu.VMEM((length, channels), F32),
            pltpu.VMEM((length, channels), BF16), pltpu.VMEM((length, channels), BF16),
            pltpu.VMEM((length, channels), BF16), pltpu.VMEM((length, channels), BF16),
            pltpu.VMEM((length, channels), BF16), pltpu.VMEM((length + 8, channels), F32),
            pltpu.VMEM((length, 2 * n), F32), pltpu.VMEM((length, 2 * n), BF16),
            pltpu.VMEM((length, 128), F32), pltpu.VMEM((length // SPAN, n, channels), BF16),
            pltpu.VMEM((groups, rows_num, channels), BF16),
            pltpu.VMEM((n, channels), F32), pltpu.VMEM((SPAN, channels // HEAD_PARTS), BF16),
            pltpu.VMEM((length // SPAN, SPAN, 128), F32), pltpu.VMEM((length // SPAN, 128, SPAN), F32),
            pltpu.VMEM((length // SPAN, SPAN, SPAN), F32), pltpu.VMEM((length // SPAN, n, SPAN), BF16),
            pltpu.VMEM((8, 128), F32),
            dma((5,)), dma((3,)), dma((9, groups)), dma((HEAD_PARTS, groups)), dma((HEAD_PARTS, groups)), dma((copies,)), dma((copies,)),
            dma((piece_copies,)), dma((piece_copies,)),
        ],
        compiler_params=pltpu.CompilerParams(
            collective_id=1, has_side_effects=True, vmem_limit_bytes=VMEM_BYTES
        ),
        cost_estimate=pl.CostEstimate(
            flops=4 * length * model * channels, bytes_accessed=400 * 2**20, transcendentals=0
        ),
        name="front",
    )(
        tokens, pre_gain[None], zw, xw, bcw, dtw, out_weight.reshape((2,) * count + (part, model)),
        norm_gain[None], convw, convb, dtb, alog, skip,
    )
    x, a, s, act, dsc, inn, bc, step, prev, gated, w_all, gains = result
    return x, (a, s, act, dsc, inn), bc, step, prev, gated, w_all.reshape(groups, channels, model), gains


def middle_kernel(
    count, g_hbm, w_hbm, cot_hbm, gain_ref, tok_ref,
    out_hbm, dg_out, own_ref, part_ref, ggrad_ref,
    g_s, w_s, cot_s, dy_s, gg_s, out_s, dg_s, give_s, kept_s, obuf, oslot0, oslot1, *refs,
):
    slots = [refs[i * (count - 1) : (i + 1) * (count - 1)] for i in range(4)]
    load_sem, store_sem, away_sem, here_sem, send, recv = refs[4 * (count - 1) :]
    groups, rows_num, channels = g_s.shape
    model = tok_ref.shape[1]
    part, half = kept_s.shape[-2:]
    pairs_num = groups // 2
    segs = segments(channels)
    tile = 512
    tiles = model // tile
    me = lax.axis_index("head")

    def w_load(t):
        cols = pl.ds(pl.multiple_of(t * tile, tile), tile)
        return pltpu.make_async_copy(w_hbm.at[:, :, cols], w_s.at[:, :, cols], load_sem.at[2 + t])

    loads = [
        pltpu.make_async_copy(g_hbm, g_s, load_sem.at[0]), pltpu.make_async_copy(cot_hbm, cot_s, load_sem.at[1]),
    ]
    for load in loads:
        load.start()
    for t in range(tiles):
        w_load(t).start()
    loads[0].wait()
    sums = [jnp.zeros((rows_num, 1), F32) for _ in segs]
    for j in range(groups):
        for w, (lo, hi) in enumerate(segs):
            g = g_s[j, :, lo:hi].astype(F32)
            gg_s[j, :, lo:hi] = (g * gain_ref[j, 0:1, lo:hi]).astype(BF16)
            sums[w] += jnp.sum(g * g, axis=1, keepdims=True)
    recips = []
    total = jnp.zeros((rows_num, 1), F32)
    for w, (lo, hi) in enumerate(segs):
        total = total + sums[w]
        recips.append(lax.rsqrt(total / (hi * groups) + EPSILON))
    meet(
        [("batch", partner("batch", b)) for b in range(count)]
        + [("head", z) for z in (partner("head", 0), partner("head", 1), partner("head", 0) + partner("head", 1) - me)]
    )
    loads[1].wait()

    def out_store(t):
        cols = pl.ds(pl.multiple_of(t * tile, tile), tile)
        return pltpu.make_async_copy(out_s.at[:, :, cols], out_hbm.at[:, :, cols], store_sem.at[t])

    def forward(t, dots):
        cols = pl.ds(pl.multiple_of(t * tile, tile), tile)
        w_load(t).wait()
        acc = jnp.zeros((rows_num, tile), F32)
        tok = tok_ref[:, cols].astype(F32)
        new = []
        for w, (lo, hi) in enumerate(segs):
            acc += mm(
                jnp.concatenate([gg_s[j, :, lo:hi] for j in range(groups)], axis=1),
                jnp.concatenate([w_s[j, lo:hi, cols] for j in range(groups)], axis=0),
            )
            out_s[w, :, cols] = (tok + recips[w] * acc).astype(BF16)
            new.append(dots[w] + jnp.sum(cot_s[w, :, cols].astype(F32) * acc, axis=1, keepdims=True))
        out_store(t).start()
        return tuple(new)

    def combine(t, carry):
        cols = pl.ds(pl.multiple_of(t * tile, tile), tile)
        combined = jnp.zeros((rows_num, tile), F32)
        for w in reversed(range(4)):
            combined += recips[w] * cot_s[w, :, cols].astype(F32)
            dy_s[w, :, cols] = combined.astype(BF16)
        return carry

    lax.fori_loop(0, tiles, combine, 0)

    def leave(j):
        return pltpu.make_async_remote_copy(
            src_ref=dg_s.at[j], dst_ref=dg_out.at[me], send_sem=away_sem.at[j], recv_sem=here_sem.at[me],
            device_id={"head": j}, device_id_type=pl.DeviceIdType.MESH,
        )

    def arrive(j):
        return pltpu.make_async_remote_copy(
            src_ref=dg_s.at[j], dst_ref=dg_out.at[j], send_sem=away_sem.at[j], recv_sem=here_sem.at[j],
            device_id={"head": j}, device_id_type=pl.DeviceIdType.MESH,
        )

    def back(k, carry):
        j = (me + 1 + k) % groups
        for w, (lo, hi) in enumerate(segs):
            dn = mm_nt(dy_s[w], w_s[j, lo:hi, :])
            g = g_s[j, :, lo:hi].astype(F32)
            ggrad_ref[j, :, lo:hi] = jnp.sum(g * dn, axis=0, keepdims=True)
            dg_s[j, :, lo:hi] = (gain_ref[j, 0:1, lo:hi] * dn - g * scales[w]).astype(BF16)

        @pl.when(j != me)
        def _():
            leave(j).start()

        return carry

    ports = Ports(send, recv)
    up = list(range(1, count))
    core = bits_of("batch", 1)[0]

    def upper_index(p):
        return tuple((p >> b) & 1 for b in reversed(range(1, count)))

    def terms(s, bit, use):
        g0, c0 = (s % 2) * pairs_num, (s // 2) * half
        if part % 128 == 0:
            for q in range(2 ** (count - 1)):
                at = pl.ds(pl.multiple_of((2 * q + bit) * part, part), part)
                left = jnp.concatenate([gg_s[g0 + j, :, at] for j in range(pairs_num)], axis=1)
                owners = [[w for w, (lo, hi) in enumerate(segs) if lo <= (2 * q + c) * part < hi][0] for c in range(2)]
                w = owners[0] + (owners[1] - owners[0]) * bit
                term = mm_tn(left, dy_s[w, :, c0 : c0 + half])
                for j in range(pairs_num):
                    use(upper_index(2 * q), j, term[j * part : (j + 1) * part])
            return
        for j in range(pairs_num):
            for w, (lo, hi) in enumerate(segs):
                term = mm_tn(gg_s[g0 + j, :, lo:hi], dy_s[w, :, c0 : c0 + half])
                for p in range(lo // part, hi // part):
                    @pl.when(bit == p % 2)
                    def _():
                        use(upper_index(p), j, term[p * part - lo : (p + 1) * part - lo])

    def to_core(s):
        return pltpu.make_async_remote_copy(
            src_ref=give_s.at[s], dst_ref=kept_s.at[s], send_sem=send.at[s], recv_sem=recv.at[s],
            device_id={"batch": partner("batch", 0)}, device_id_type=pl.DeviceIdType.MESH,
        )

    def give(s):
        def use(index, j, rows):
            give_s[(s,) + index + (j,)] = rows.astype(BF16)

        terms(s, 1 - core, use)
        to_core(s).start()

    def keep(s):
        to_core(s).wait()

        def use(index, j, rows):
            at = (s,) + index + (j,)
            kept_s[at] = (kept_s[at].astype(F32) + rows).astype(BF16)

        terms(s, core, use)

    ports.used = 4
    streams = [
        Stream(halving(ports, "batch", lambda s=s: kept_s.at[s], slots[s], up if s % 2 == 0 else up[::-1]))
        for s in range(4)
    ]
    mine = bits_of("batch", count)
    own = place(up, {b: mine[b] for b in up})
    head_sum = Stream(halving(ports, "head", lambda: obuf, (oslot0, oslot1), [0, 1]))
    for s in range(2):
        give(s)
    for s in range(2):
        keep(s)
        streams[s].advance()
    dots = lax.fori_loop(0, tiles, forward, tuple(jnp.zeros((rows_num, 1), F32) for _ in segs))
    scales = [None] * 4
    scale = jnp.zeros((rows_num, 1), F32)
    for w in reversed(range(4)):
        scale = scale + recips[w] ** 3 * dots[w] / (segs[w][1] * groups)
        scales[w] = scale
    lax.fori_loop(0, groups, back, 0)
    stay = pltpu.make_async_copy(dg_s.at[me], dg_out.at[me], load_sem.at[0])
    stay.start()
    for s in range(2, 4):
        give(s)
    advance_all(streams[:2])
    for s in range(2, 4):
        keep(s)
        streams[s].advance()
    drain(streams[:2])
    for s in range(2):
        for j in range(pairs_num):
            obuf[s, j] = kept_s[(s,) + own + (j,)]
    head_sum.advance()
    advance_all(streams[2:])
    head_sum.advance()
    drain(streams)
    drain([head_sum])
    own_ref[...] = obuf[place(2, dict(enumerate(bits_of("head", 2))))]
    for s in range(2, 4):
        for j in range(pairs_num):
            part_ref[s - 2, j] = kept_s[(s,) + own + (j,)]
    stay.wait()

    def finish(j, carry):
        @pl.when(j != me)
        def _():
            leave(j).wait_send()
            arrive(j).wait_recv()

        return carry

    lax.fori_loop(0, groups, finish, 0)

    def stored(t, carry):
        out_store(t).wait()
        return carry

    lax.fori_loop(0, tiles, stored, 0)


def middle_call(g, w_all, gain, tok, cot, batches):
    groups, rows_num, channels = g.shape
    model = tok.shape[1]
    count = log2(batches)
    part = channels // batches
    half = model // 2
    block = (groups // 2, part, half)
    hbm = pl.BlockSpec(memory_space=pl.ANY)
    vmem = pl.BlockSpec(memory_space=pltpu.VMEM)
    dma = pltpu.SemaphoreType.DMA
    wide = pltpu.VMEM((groups, rows_num, channels), BF16)
    tall = pltpu.VMEM((4, rows_num, model), BF16)
    halves = pltpu.VMEM((4,) + (2,) * (count - 1) + block, BF16)
    return pl.pallas_call(
        functools.partial(middle_kernel, count),
        in_specs=[hbm] * 3 + [vmem] * 2,
        out_specs=[hbm, hbm, vmem, vmem, vmem],
        out_shape=[
            jax.ShapeDtypeStruct((4, rows_num, model), BF16),
            jax.ShapeDtypeStruct(g.shape, BF16),
            jax.ShapeDtypeStruct((part, half), BF16),
            jax.ShapeDtypeStruct((2, 2, part, half), BF16),
            jax.ShapeDtypeStruct((groups, 1, channels), F32),
        ],
        scratch_shapes=[
            wide, pltpu.VMEM((groups, channels, model), BF16), tall, tall, wide, tall, wide, halves, halves,
            pltpu.VMEM((2, 2, part, half), BF16), pltpu.VMEM((2, part, half), BF16), pltpu.VMEM((part, half), BF16),
        ]
        + [s for _ in range(4) for s in halving_slots(count - 1, block, BF16)]
        + [
            dma((2 + model // 512,)), dma((model // 512,)), dma((groups,)), dma((groups,)),
            dma((4 * count + 2,)), dma((4 * count + 2,)),
        ],
        compiler_params=pltpu.CompilerParams(
            collective_id=2, has_side_effects=True, vmem_limit_bytes=BACK_VMEM_BYTES
        ),
        cost_estimate=pl.CostEstimate(
            flops=6 * groups * rows_num * channels * model, bytes_accessed=200 * 2**20, transcendentals=0
        ),
        name="nested_norm",
    )(g, w_all, cot, gain, tok)


BACK_POLLS = {
    "z": ((0, 0, "a"), (0, 1, "a"), (0, 1, "b"), (0, 2, "a"), (0, 3, "a"), (0, 3, "b")),
    "out": ((0, 0, "a"), (0, 1, "a")),
    "spread": (((0, 3, "b"),), ((0, 3, "b"),)),
    "relay": (
        ((0, 1, "a"), 3, 0, 1), ((0, 1, "b"), 3, 1, 1), ((0, 1, "b"), 3, 2, 1), ((0, 2, "a"), 3, 3, 1),
        ((0, 1, "b"), 3, 0, 2), ((0, 2, "a"), 3, 1, 2), ((0, 2, "a"), 3, 2, 2), ((0, 2, "b"), 3, 3, 2),
        ((0, 2, "b"), 2, 0, 1), ((0, 2, "b"), 2, 1, 1), ((0, 3, "a"), 2, 2, 1), ((0, 3, "b"), 2, 3, 1),
        ((0, 3, "b"), 1, 0, 1),
    ),
    "tail": (1, 1, 2, 2),
}
RELAY_ORDER = [(2, c, 1) for c in range(4)] + [(1, c, 1) for c in range(4)]
RELAY_ORDER += [(0, 0, 1), (0, 1, 1), (0, 0, 2), (0, 2, 1), (0, 1, 2), (0, 3, 1), (0, 2, 2), (0, 3, 2)]


def back_kernel(
    count, group_bits,
    dg_hbm, a_hbm, s_hbm, act_hbm, dsc_hbm, inn_hbm, x_hbm, bc_hbm, step_hbm, prev_hbm,
    zw_hbm, xw_hbm, bcw_hbm, dtw_hbm, o_hbm, own_hbm, gain_ref, convw_ref, alog_ref, skip_ref,
    z_out, x_out, o_out, bc_out, small_out, own_out,
    dg, a, s, act, dsc, inn, x, bc, step, prev, zw, xw, bdw, dtw, obuf, o_first, hot_ref, pad_s,
    lam, dconv, dyc_s, vt_s, q_s, v_s, w_s, da_s, etot_s, draw_s, head_s, vec_s, pre_s, dbs,
    rows_s, line_s, last_s, zg, bcbuf, small, *refs,
):
    groups = rows_s.shape[0] * rows_s.shape[1]
    zx_slots = [refs[i * count : (i + 1) * count] for i in range(2)]
    refs = refs[2 * count :]
    bc_slots, refs = (refs[:count], refs[count : 2 * count]), refs[2 * count :]
    bc_head, refs = (refs[: groups - 1], refs[groups - 1 : 2 * (groups - 1)]), refs[2 * (groups - 1) :]
    small_slots, refs = refs[:count], refs[count:]
    small_head, refs = refs[:group_bits], refs[group_bits:]
    o_slots, refs = refs[:group_bits], refs[group_bits:]
    load_sem, store_sem, rsend, rrecv, rrecv_own, send, recv = refs
    length, channels = a.shape
    model = x.shape[1]
    n = lam.shape[0]
    heads = hot_ref.shape[0]
    rows_num = length // groups
    subs = rows_num // SPAN
    wide = bcbuf.shape[-1]
    me = lax.axis_index("head")

    pairs = [
        (dg_hbm.at[:, :, pl.ds(0, channels // 2)], dg.at[0]),
        (dg_hbm.at[:, :, pl.ds(channels // 2, channels // 2)], dg.at[1]), (a_hbm, a), (s_hbm, s), (x_hbm, x), (o_hbm, obuf), (own_hbm, o_first), (step_hbm, step), (bc_hbm, bc),
        (prev_hbm, prev), (act_hbm, act), (dsc_hbm, dsc), (inn_hbm, inn), (zw_hbm, zw), (xw_hbm, xw),
        (bcw_hbm, bdw.at[:, pl.ds(0, 2 * n)]), (dtw_hbm, dtw),
    ]
    loads = [pltpu.make_async_copy(src, dst, load_sem.at[i]) for i, (src, dst) in enumerate(pairs)]
    for load in loads:
        load.start()
    for load in loads[:4]:
        load.wait()

    def gates(i, carry):
        per = rows_num // 64
        rows = pl.ds(pl.multiple_of(i * 64, 64), 64)
        piece = dg.shape[-1]
        for h in range(dg.shape[0]):
            cols = slice(h * piece, (h + 1) * piece)
            d = dg[h, i // per, pl.ds(pl.multiple_of((i % per) * 64, 64), 64), :].astype(F32)
            a[rows, cols] = (d * a[rows, cols].astype(F32)).astype(BF16)
            s[rows, cols] = (d * s[rows, cols].astype(F32)).astype(BF16)
        return carry

    lax.fori_loop(0, length // 64, gates, 0)
    near, far = partner("head", 0), partner("head", 1)
    meet(
        [("batch", partner("batch", b)) for b in range(count)]
        + [("head", to) for to in (near, far, near + far - me)]
    )

    ports = Ports(send, recv)
    up = list(range(1, count))
    orders = [up, up[::-1]]

    def own_at():
        return place(count, dict(enumerate(bits_of("batch", count))))

    def grads(i, out, slots, first, width):
        part = (slice(None),) * (count + 1) + (pl.ds(first, width),)
        view = lambda: out.at[part]
        buf = lambda: zg.at[part]
        order = orders[i % 2]
        return Stream(
            halving(ports, "batch", buf, slots, [0] + order),
            spreading(
                ports, "batch", view, order[::-1] + [0], lambda: buf().at[own_at()], store_sem.at[2 + i]
            ),
        )

    z_width, x_width = channels // 2, channels // X_STREAMS
    streams = [grads(i, z_out, zx_slots[i], i * z_width, z_width) for i in range(2)]
    per = z_width // x_width
    for i in range(X_STREAMS):
        cols = pl.ds((i % per) * x_width, x_width)
        slots = [ref.at[(slice(None),) * (len(ref.shape) - 1) + (cols,)] for ref in zx_slots[i // per]]
        streams.append(grads(2 + i, x_out, slots, i * x_width, x_width))

    def state_part(i):
        part = (slice(None),) * (count + 1) + ((pl.ds(n, n + 128), pl.ds(0, n))[i],)
        buf = lambda: bcbuf.at[part]
        view = lambda: bc_out.at[part]
        return Stream(
            halving(ports, "batch", buf, bc_slots[i], [0] + orders[i]),
            exchanging_once(
                ports, "head", group_bits, lambda: bcbuf.at[own_at() + (slice(None), pl.ds((n, 0)[i], n))], bc_head[i]
            ),
            spreading(
                ports, "batch", view, orders[i][::-1] + [0], lambda: buf().at[own_at()], store_sem.at[i]
            ),
        )

    state = [state_part(i) for i in range(2)]
    vectors = Stream(
        exchanging(ports, "batch", lambda: small, small_slots, range(count)),
        exchanging(ports, "head", lambda: small.at[pl.ds(0, 8)], small_head, range(group_bits)),
    )
    half = model // 2

    def head_own():
        return place(group_bits, dict(enumerate(bits_of("head", group_bits))))

    def o_view(i):
        return o_out.at[(slice(None),) * (count + 1) + (pl.ds(i * half, half),)]

    outs = Stream(halving(ports, "head", lambda: obuf, o_slots, list(range(group_bits))))

    def o_own(i):
        return obuf.at[head_own()] if i else o_first

    spread = [
        Stream(spreading(
            ports, "batch", lambda i=i: o_view(i), orders[i] + [0], lambda i=i: o_own(i),
            store_sem.at[2 + 2 + X_STREAMS + i],
        ))
        for i in range(2)
    ]

    for load in loads[4:7]:
        load.wait()
    outs.advance()
    tile = 256
    block_rows = model >> count

    def put(target, t, value):
        for k in range(tile // min(block_rows, tile)):
            p = (t * tile) // block_rows + k
            index = tuple((p // 2**b) % 2 for b in reversed(range(count)))
            if block_rows <= tile:
                target[index] = value[k * block_rows : (k + 1) * block_rows].astype(BF16)
            else:
                first = pl.multiple_of((t * tile) % block_rows, tile)
                target[index + (pl.ds(first, tile), slice(None))] = value.astype(BF16)

    def weight_grad(right, target):
        def one(t, carry):
            value = mm_tn(x[:, pl.ds(pl.multiple_of(t * 2 * tile, 2 * tile), 2 * tile)], right[...])
            for k in range(2):
                put(target, 2 * t + k, value[k * tile : (k + 1) * tile])
            return carry

        lax.fori_loop(0, model // (2 * tile), one, 0)

    weight_grad(a, zg)
    advance_all(streams[:2])
    for load in loads[7:]:
        load.wait()
    bdw[:, 2 * n :] = jnp.concatenate([dtw[...], jnp.zeros((128 - heads, model), BF16)], axis=0).T
    pad_s[...] = jnp.zeros_like(pad_s)
    pad_s[0:1, 0:heads] = alog_ref[...]
    hot_ref[...] = (
        lax.broadcasted_iota(jnp.int32, hot_ref.shape, 1) // (channels // heads)
        == lax.broadcasted_iota(jnp.int32, hot_ref.shape, 0)
    ).astype(F32).astype(BF16)

    lam[...] = jnp.zeros_like(lam)
    dconv[rows_num:, :] = jnp.zeros((8, channels), F32)
    vec_s[...] = jnp.zeros_like(vec_s)
    head_s[...] = jnp.zeros_like(head_s)
    draw_s[...] = jnp.zeros_like(draw_s)
    pre_s[...] = jnp.zeros_like(pre_s)
    rate = -jnp.exp(pad_s[0:1, :])
    lower = lower_mask((SPAN, SPAN))
    lower_f = lower.astype(F32)
    lower_b = lower.astype(BF16)
    row_at = lax.broadcasted_iota(jnp.int32, (SPAN, SPAN), 0)
    col_at = lax.broadcasted_iota(jnp.int32, (SPAN, SPAN), 1)
    upper = row_at <= col_at
    strict = row_at < col_at
    strict_f = strict.astype(F32)
    left = lax.broadcasted_iota(jnp.int32, (SPAN, 128), 1) < 64

    span_num = channels // BACK_PARTS
    span_heads = heads // BACK_PARTS

    def block(at, local, part):
        rows = pl.ds(pl.multiple_of(at * SPAN, SPAN), SPAN)
        local_rows = pl.ds(pl.multiple_of(local * SPAN, SPAN), SPAN)
        delta = step[rows, :]
        cum = mm_exact(lower_f, delta * rate)
        cum_t = cum.T
        delta_t = delta.T
        series = delta_t * (1.0 - delta_t * (0.5 - delta_t * (1.0 / 6.0 - delta_t / 24.0)))
        slope_t = jnp.where(delta_t < 0.04, series, 1.0 - jnp.exp(-delta_t))
        rate_t = jnp.broadcast_to(rate, (SPAN, 128)).T
        b_val = bc[rows, :n]
        c_val = bc[rows, n:]
        inner = jnp.where(upper, mm_nt(b_val, c_val), 0.0)
        span_cols = pl.ds(part * span_num, span_num)
        before = prev[at, :, span_cols]
        lam_b = lam[:, span_cols].astype(BF16)
        across = mm(c_val, before)
        dtail = mm(b_val, lam_b)
        d_inner_prod = jnp.zeros((SPAN, SPAN), F32)
        for pair in range(part * span_num // 128, (part + 1) * span_num // 128):
            cols = slice(pair * 128, pair * 128 + 128)
            own = pair - part * span_num // 128
            here = slice(own * 128, own * 128 + 128)
            c0, c1, ce = pair_columns(cum, pair, left)
            _, _, de = pair_columns(delta, pair, left)
            tot = ce[SPAN - 1 : SPAN, :]
            e_cum = jnp.exp(ce)
            e_tail = jnp.exp(tot - ce)
            dy_b = s[rows, cols]
            dy = dy_b.astype(F32)
            act_p = act[rows, cols].astype(F32)
            vec_s[5:6, cols] += jnp.sum(dy * act_p, axis=0, keepdims=True)
            u = act_p * de
            u_b = u.astype(BF16)
            zero = jnp.zeros_like(dy_b)
            dy01 = jnp.concatenate([jnp.where(left, dy_b, zero), jnp.where(left, zero, dy_b)], axis=0)
            m0 = jnp.exp(jnp.minimum(cum_t[2 * pair : 2 * pair + 1, :] - c0, 0.0))
            m1 = jnp.exp(jnp.minimum(cum_t[2 * pair + 1 : 2 * pair + 2, :] - c1, 0.0))
            p0 = m0 * inner
            p1 = m1 * inner
            du = mm(jnp.concatenate([p0.astype(BF16), p1.astype(BF16)], axis=1), dy01)
            dp = mm_nt(u_b, dy01)
            dp0, dp1 = dp[:, :SPAN], dp[:, SPAN:]
            d_inner_prod += dp0 * m0 + dp1 * m1
            e01 = jnp.concatenate([(dp0 * p0).astype(BF16), (dp1 * p1).astype(BF16)], axis=0)
            spans = mm(e01, lower_b)
            da_s[2 * own : 2 * own + 1, :] = jnp.sum(
                jnp.where(strict, spans[:SPAN], 0.0), axis=0, keepdims=True
            )
            da_s[2 * own + 1 : 2 * own + 2, :] = jnp.sum(
                jnp.where(strict, spans[SPAN:], 0.0), axis=0, keepdims=True
            )
            dut = dtail[:, here] * e_tail
            du = du + dut
            dye = dy * e_cum
            dyc_s[:, here] = dye.astype(BF16)
            vt_s[:, here] = (u * e_tail).astype(BF16)
            q_s[:, here] = (dye * across[:, here]).astype(BF16)
            v_s[:, here] = (u * dut).astype(BF16)
            w_s[:, here] = (act_p * du).astype(BF16)
            etot_s[:, here] = jnp.exp(tot)
            d_act = de * du + skip_ref[:, cols] * dy
            dconv[local_rows, cols] = d_act * dsc[rows, cols].astype(F32)
        hot = hot_ref[:span_heads, :span_num]
        these = slice(part * span_heads, (part + 1) * span_heads)
        over = jnp.sum(lam[:, span_cols] * before.astype(F32), axis=0, keepdims=True) * etot_s[...]
        over = jnp.broadcast_to(over, (128, span_num))
        over = lax.dot_general(
            hot.astype(F32), over, (((1,), (1,)), ((), ())), preferred_element_type=F32, precision=HIGHEST
        )
        da = (
            da_s[...]
            + mm_exact(mm_nt(hot, q_s[...]), lower_f)
            + mm_exact(mm_nt(hot, v_s[...]), strict_f)
            + over
        )
        d_step = mm_nt(hot, w_s[...]) + rate_t[these] * da
        d_raw = d_step * slope_t[these]
        head_s[these, :] += d_raw
        head_s[heads + part * span_heads : heads + (part + 1) * span_heads, :] += delta_t[these] * da * rate_t[these]
        draw_s[these, :] = d_raw
        dg_b = jnp.where(upper, d_inner_prod, 0.0)
        d_b = mm(dg_b.astype(BF16), c_val) + mm_nt(vt_s[...], lam_b)
        d_c = mm(dg_b.T.astype(BF16), b_val) + mm_nt(dyc_s[...], before)
        d_t = draw_s[...].T
        if part:
            d_b += dbs[rows, :n].astype(F32)
            d_c += dbs[rows, n : 2 * n].astype(F32)
            d_t += dbs[rows, 2 * n :].astype(F32)
        dbs[rows, :n] = d_b.astype(BF16)
        dbs[rows, n : 2 * n] = d_c.astype(BF16)
        dbs[rows, 2 * n :] = d_t.astype(BF16)
        lam[:, span_cols] = lam[:, span_cols] * etot_s[...] + mm(bc[rows, n:].astype(F32).T.astype(BF16), dyc_s[...])

    top = groups - 1

    def slot(q, c):
        return dg.at[q, c] if q < 2 else line_s.at[q - 2, c]

    def hop(q, c, dst, sem, to):
        return pltpu.make_async_remote_copy(
            src_ref=rows_s.at[q // 2, q % 2, c], dst_ref=dst, send_sem=rsend.at[q, c], recv_sem=sem,
            device_id={"head": to}, device_id_type=pl.DeviceIdType.MESH,
        )

    def send_up(q, c):
        @pl.when(me + 1 < q)
        def _():
            hop(q, c, slot(q, c), rrecv.at[q, c], me + 1).start()

        @pl.when(me + 1 == q)
        def _():
            hop(q, c, last_s.at[c], rrecv_own.at[c], me + 1).start()

    def send_down(q, c):
        hop(q, c, slot(q, c), rrecv.at[q, c], me - 1).start()

    def arrived(q, c):
        hop(q, c, slot(q, c), rrecv.at[q, c], me).wait_recv()

    def arrived_last(q, c):
        hop(q, c, last_s.at[c], rrecv_own.at[c], me).wait_recv()

    def begin(q):
        for c in range(ROW_CHUNKS):
            if q > 0:
                @pl.when(me == 0)
                def _():
                    send_up(q, c)
            if q < top:
                @pl.when(me == top)
                def _():
                    send_down(q, c)

    def relay(q, c, distance):
        if distance < q:
            @pl.when(me == distance)
            def _():
                arrived(q, c)
                add_block(rows_s, (q // 2, q % 2, c), slot(q, c), ())
                send_up(q, c)
        if top - distance > q:
            @pl.when(me == top - distance)
            def _():
                arrived(q, c)
                add_block(rows_s, (q // 2, q % 2, c), slot(q, c), ())
                send_down(q, c)

    def conv_back(rows, part):
        for c in range(part * span_num, (part + 1) * span_num, 128):
            cols = slice(c, c + 128)
            inner_v = inn[rows, cols].astype(F32)
            d_in = jnp.zeros((rows_num, 128), F32)
            for k in range(4):
                shifted = dconv[3 - k : 3 - k + rows_num, cols]
                d_in += convw_ref[k : k + 1, cols] * shifted
                vec_s[k : k + 1, cols] += jnp.sum(inner_v * shifted, axis=0, keepdims=True)
            vec_s[4:5, cols] += jnp.sum(dconv[0:rows_num, cols], axis=0, keepdims=True)
            inn[rows, cols] = d_in.astype(BF16)
        kept = pl.ds(part * span_num, span_num)
        dconv[rows_num:, kept] = dconv[0:8, kept]

    def row_grads(q, rows):
        wide_tile = 2 * tile
        per = model // ROW_CHUNKS // wide_tile

        def columns(t, carry):
            cols = pl.ds(pl.multiple_of(t * wide_tile, wide_tile), wide_tile)
            value = mm_nt(a[rows, :], zw[cols, :]) + mm_nt(inn[rows, :], xw[cols, :]) + mm_nt(dbs[rows, :], bdw[cols, :])
            pre_s[:, cols] += jnp.sum(value * x[rows, cols].astype(F32), axis=0, keepdims=True)
            rows_s[q // 2, q % 2, t // per, :, pl.ds(pl.multiple_of((t % per) * wide_tile, wide_tile), wide_tile)] = value.astype(BF16)
            return carry

        lax.fori_loop(0, model // wide_tile, columns, 0)

    plan = {(part, k, spot): [] for part in range(BACK_PARTS) for k in range(groups) for spot in "ab"}

    def book(stream, slots):
        for slot in slots:
            if stream.steps:
                plan[slot].append(stream.steps.pop(0))

    for st in streams[:2]:
        book(st, BACK_POLLS["z"])
    book(outs, BACK_POLLS["out"])
    for i, st in enumerate(spread):
        book(st, BACK_POLLS["spread"][i])
    last = BACK_PARTS - 1
    for k in range(groups):
        plan[last, k, "b"].insert(0, lambda q=top - k: begin(q))
    for spot, q, c, distance in BACK_POLLS["relay"]:
        plan[spot].append(lambda q=q, c=c, distance=distance: relay(q, c, distance))

    for part in range(BACK_PARTS):
        def quarter_step(i, carry):
            q = groups - 1 - i
            rows = pl.ds(pl.multiple_of(q * rows_num, rows_num), rows_num)

            def one(j, inner_carry):
                block(q * subs + subs - 1 - j, subs - 1 - j, part)
                return inner_carry

            lax.fori_loop(0, subs, one, 0)

            def polls(spot):
                for k in range(groups):
                    if plan[part, k, spot]:
                        @pl.when(i == k)
                        def _():
                            for action in plan[part, k, spot]:
                                action()

            polls("a")
            conv_back(rows, part)
            if part == last:
                row_grads(q, rows)
            polls("b")
            return carry

        lax.fori_loop(0, groups, quarter_step, 0)

    drain(streams[:2])
    tail = list(BACK_POLLS["tail"])
    booked = {key[1:] for key in BACK_POLLS["relay"]}
    relays = [r for r in RELAY_ORDER if r not in booked]

    def relay_some():
        for _ in range(tail.pop(0) if tail else 1):
            if relays:
                relay(*relays.pop(0))

    def state_grad(t, carry):
        put(bcbuf, t, mm_tn(x[:, pl.ds(pl.multiple_of(t * tile, tile), tile)], dbs[...]))
        return carry

    lax.fori_loop(0, model // tile, state_grad, 0)
    advance_all(state)
    per = X_STREAMS // 2
    x_pairs = [streams[2 + h * per : 2 + (h + 1) * per] for h in range(2)]
    for h in range(2):
        cols = pl.ds(h * z_width, z_width)
        weight_grad(inn.at[:, cols], zg.at[(slice(None),) * (count + 1) + (cols,)])
        advance_all(x_pairs[h])
        relay_some()
        advance_all(state)
    small[...] = jnp.zeros_like(small)
    for j in range(groups):
        small[j : j + 1, :] = gain_ref[j]
    for j in range(model // channels):
        small[groups + j : groups + j + 1, :] = pre_s[:, j * channels : (j + 1) * channels]
    small[8:14, :] = vec_s[0:6, :]
    totals = lax.dot_general(
        jnp.ones((8, SPAN), F32), head_s[...], (((1,), (1,)), ((), ())),
        preferred_element_type=F32, precision=HIGHEST,
    )
    small[14:15, 0:128] = totals[0:1]
    vectors.advance()
    while relays or any(st.steps for st in streams + state + spread + [vectors, outs]):
        advance_all(x_pairs[0])
        relay_some()
        advance_all(state + [vectors])
        advance_all(x_pairs[1])
        relay_some()
        advance_all(spread + [outs])
    small_out[...] = small[...]

    piece = model // ROW_CHUNKS
    for c in range(ROW_CHUNKS):
        for q in range(groups):
            @pl.when(me == q)
            def _():
                if q > 0:
                    arrived_last(q, c)
                if q < top:
                    arrived(q, c)

                def total(r, carry):
                    rs = pl.ds(pl.multiple_of(r * 32, 32), 32)
                    value = rows_s[q // 2, q % 2, c, rs, :].astype(F32)
                    if q > 0:
                        value += last_s[c, rs, :].astype(F32)
                    if q < top:
                        value += slot(q, c)[rs, :].astype(F32)
                    own_out[rs, c * piece : (c + 1) * piece] = value
                    return carry

                lax.fori_loop(0, rows_num // 32, total, 0)

            @pl.when(me != q)
            def _():
                hop(q, c, slot(q, c), rrecv.at[q, c], me).wait_send()


def back_call(dg, res, x, bc, step, prev, zw, xw, bcw, dtw, out_part, out_own, gain_grad, convw, alog, skip, groups, batches):
    length, model = x.shape
    channels = xw.shape[1]
    n = bc.shape[1] // 2
    heads = dtw.shape[0]
    rows_num = length // groups
    count = log2(batches)
    group_bits = log2(groups)
    lead = (2,) * count
    part = channels // batches
    rows = model // batches
    wide = 2 * n + 128
    hbm = pl.BlockSpec(memory_space=pl.ANY)
    vmem = pl.BlockSpec(memory_space=pltpu.VMEM)
    dma = pltpu.SemaphoreType.DMA
    copies = (2 + X_STREAMS) * 2 * count + 2 * (2 * count + groups - 1) + (count + group_bits) + group_bits + 2 * count
    tall = lambda w, t: pltpu.VMEM((length, w), t)
    span = pltpu.VMEM((SPAN, channels // BACK_PARTS), BF16)
    z, xg, o, bcg, small, own = pl.pallas_call(
        functools.partial(back_kernel, count, group_bits),
        in_specs=[hbm] * 16 + [vmem] * 4,
        out_specs=[hbm] * 4 + [vmem] * 2,
        out_shape=[
            jax.ShapeDtypeStruct(lead + (rows, channels), BF16),
            jax.ShapeDtypeStruct(lead + (rows, channels), BF16),
            jax.ShapeDtypeStruct(lead + (part, model), BF16),
            jax.ShapeDtypeStruct(lead + (rows, wide), BF16),
            jax.ShapeDtypeStruct((16, channels), F32),
            jax.ShapeDtypeStruct((rows_num, model), F32),
        ],
        scratch_shapes=[pltpu.VMEM((2, groups, rows_num, channels // 2), BF16)] + [tall(channels, BF16)] * 5
        + [
            tall(model, BF16), tall(2 * n, BF16), tall(128, F32), pltpu.VMEM(prev.shape, BF16),
            pltpu.VMEM(zw.shape, BF16), pltpu.VMEM(xw.shape, BF16), pltpu.VMEM((model, wide), BF16),
            pltpu.VMEM(dtw.shape, BF16),
            pltpu.VMEM((2,) * group_bits + (part, model // 2), BF16), pltpu.VMEM((part, model // 2), BF16),
            pltpu.VMEM((heads, channels), BF16), pltpu.VMEM((8, 128), F32),
            pltpu.VMEM((n, channels), F32), pltpu.VMEM((rows_num + 8, channels), F32),
        ]
        + [span] * 5
        + [
            pltpu.VMEM((heads // BACK_PARTS, SPAN), F32), pltpu.VMEM((1, channels // BACK_PARTS), F32),
            pltpu.VMEM((128, SPAN), F32),
            pltpu.VMEM((128, SPAN), F32), pltpu.VMEM((8, channels), F32), pltpu.VMEM((1, model), F32),
            tall(wide, BF16),
            pltpu.VMEM((2, 2, ROW_CHUNKS, rows_num, model // ROW_CHUNKS), BF16),
            pltpu.VMEM((2, ROW_CHUNKS, rows_num, model // ROW_CHUNKS), BF16),
            pltpu.VMEM((ROW_CHUNKS, rows_num, model // ROW_CHUNKS), BF16),
            pltpu.VMEM(lead + (rows, channels), BF16), pltpu.VMEM(lead + (rows, wide), BF16),
            pltpu.VMEM((16, channels), F32),
        ]
        + [s for _ in range(2) for s in halving_slots(count, (rows, channels // 2), BF16)]
        + halving_slots(count, (rows, n + 128), BF16)
        + halving_slots(count, (rows, n), BF16)
        + [pltpu.VMEM((rows, n), BF16)] * (2 * (groups - 1))
        + [pltpu.VMEM((16, channels), F32)] * count
        + [pltpu.VMEM((8, channels), F32)] * group_bits
        + halving_slots(group_bits, (part, model // 2), BF16)
        + [dma((17,)), dma((6 + X_STREAMS,)),
            dma((groups, ROW_CHUNKS)), dma((groups, ROW_CHUNKS)), dma((ROW_CHUNKS,)), dma((copies,)), dma((copies,))],
        compiler_params=pltpu.CompilerParams(
            collective_id=3, has_side_effects=True, vmem_limit_bytes=BACK_VMEM_BYTES
        ),
        cost_estimate=pl.CostEstimate(
            flops=10 * length * model * channels, bytes_accessed=300 * 2**20, transcendentals=0
        ),
        name="back",
    )(
        dg, *res, x, bc, step, prev, zw, xw, bcw, dtw, out_part, out_own,
        gain_grad, convw, alog, skip,
    )
    return (
        z.reshape(model, channels), xg.reshape(model, channels), o.reshape(channels, model),
        bcg.reshape(model, wide), small, own,
    )


def finish_kernel(
    z_ref, x_ref, o_ref, bc_ref, small_ref, own_ref, tok_ref, cot_ref, pre_ref, out_ref,
    zf_ref, xf_ref, of_ref, bcf_ref, dt_ref, grad_ref, outf_ref, convw_ref, convb_ref, skip_ref, gain_ref, pre_out, dtb_ref, alog_ref,
):
    zf_ref[...] = z_ref[...].astype(F32)
    xf_ref[...] = x_ref[...].astype(F32)
    of_ref[...] = o_ref[...].astype(F32)
    width = bcf_ref.shape[1]
    heads = dt_ref.shape[0]
    outf_ref[...] = out_ref[...]
    bcf_ref[...] = bc_ref[:, :width].astype(F32)
    dt_ref[...] = bc_ref[:, width : width + 128].astype(F32).T[:heads]
    tok = tok_ref[...].astype(F32)
    recip = lax.rsqrt(jnp.mean(tok * tok, axis=-1, keepdims=True) + EPSILON)
    scaled = pre_ref[...] * own_ref[...]
    mean = jnp.mean(tok * scaled, axis=-1, keepdims=True)
    passed = sum(cot_ref[w].astype(F32) for w in range(4))
    grad_ref[...] = (passed + recip * scaled - tok * recip**3 * mean).astype(BF16)

    @pl.when(pl.program_id(0) == 0)
    def _():
        groups = small_ref.shape[0] // 4
        channels = small_ref.shape[1]
        convw_ref[...] = small_ref[8:12, :]
        convb_ref[...] = small_ref[12:13, :]
        skip_ref[...] = small_ref[13:14, :]
        me = lax.axis_index("head")
        gain = small_ref[0:1, :]
        for j in range(1, groups):
            gain = jnp.where(me == j, small_ref[j : j + 1, :], gain)
        gain_ref[...] = gain
        for j in range(pre_out.shape[1] // channels):
            cols = slice(j * channels, (j + 1) * channels)
            pre_out[:, cols] = small_ref[groups + j : groups + j + 1, :] / pre_ref[:, cols]
        dtb_ref[...] = small_ref[14:15, 0:heads]
        alog_ref[...] = small_ref[14:15, heads : 2 * heads]


def finish_call(z, x, o, bc, small, own, tok, cot, pre_gain, out, heads):
    model, channels = z.shape
    rows_num = tok.shape[0]
    steps = 8
    wide = bc.shape[1]
    rows = lambda r, w: pl.BlockSpec((r // steps, w), lambda i: (i, 0))
    fixed = lambda shape: pl.BlockSpec(shape, lambda i: (0, 0))
    shapes = [
        ((model, channels), F32), ((model, channels), F32), ((channels, model), F32), ((model, wide - 128), F32),
    ]
    wide4 = pl.BlockSpec((4, rows_num // steps, model), lambda i: (0, i, 0))
    flat = [(4, channels), (1, channels), (1, channels), (1, channels), (1, model), (1, heads), (1, heads)]
    return pl.pallas_call(
        finish_kernel,
        grid=(steps,),
        in_specs=[
            rows(model, channels), rows(model, channels), rows(channels, model), rows(model, wide),
            fixed(small.shape), rows(rows_num, model), rows(rows_num, model),
            wide4, fixed((1, model)), wide4,
        ],
        out_specs=[rows(*shape) for shape, _ in shapes]
        + [pl.BlockSpec((heads, model // steps), lambda i: (0, i)), rows(rows_num, model), wide4]
        + [fixed(shape) for shape in flat],
        out_shape=[jax.ShapeDtypeStruct(shape, t) for shape, t in shapes]
        + [
            jax.ShapeDtypeStruct((heads, model), F32), jax.ShapeDtypeStruct((rows_num, model), BF16),
            jax.ShapeDtypeStruct(out.shape, BF16),
        ]
        + [jax.ShapeDtypeStruct(shape, F32) for shape in flat],
        compiler_params=pltpu.CompilerParams(vmem_limit_bytes=VMEM_BYTES),
        cost_estimate=pl.CostEstimate(flops=0, bytes_accessed=46 * 2**20, transcendentals=0),
        name="finish",
    )(z, x, o, bc, small, own, tok, cot, pre_gain[None], out)


def per_device(
    tokens, z_weight, x_weight, bc_weight, dt_weight, conv_weight, conv_bias, dt_bias,
    a_log, skip, norm_gain, pre_gain, out_weight, cotangent,
):
    groups = lax.axis_size("head")
    batches = lax.axis_size("batch")
    _, own_len, model = tokens.shape
    tokens = tokens[0]
    cot = cotangent[:, 0]
    channels = z_weight.shape[1]
    heads = dt_weight.shape[1]
    dtw = dt_weight.T
    alog = a_log[None]
    skip_r = skip[None]
    x, res, bc, step, prev, gated, w_all, gain_all = front_call(
        tokens, pre_gain, z_weight, x_weight, bc_weight, dtw, out_weight, norm_gain,
        conv_weight, conv_bias[None], dt_bias[None], alog, skip_r, groups, batches,
    )
    outputs, d_gated, out_own, out_part, gain_grad = middle_call(gated, w_all, gain_all, tokens, cot, batches)
    z_grad, x_grad, out_grad, bcdt_grad, small, d_own = back_call(
        d_gated, res, x, bc, step, prev, z_weight, x_weight, bc_weight, dtw, out_part, out_own, gain_grad,
        conv_weight, alog, skip_r, groups, batches,
    )
    (
        z_grad, x_grad, out_grad, bc_grad, dt_grad, tokens_grad, outputs, convw, convb, skip_g, gain_g, pre_g, dtb_g, alog_g,
    ) = finish_call(z_grad, x_grad, out_grad, bcdt_grad, small, d_own, tokens, cot, pre_gain, outputs, heads)
    flat = lambda v: v.reshape(-1)
    return (
        outputs[:, None], tokens_grad[None], z_grad, x_grad, bc_grad, dt_grad.T, convw, flat(convb), flat(dtb_g),
        flat(alog_g), flat(skip_g), flat(gain_g), flat(pre_g), out_grad,
    )


def solution(mesh):
    head_cols = P(None, "head")
    rows4 = P(None, "batch", "head", None)
    return jax.shard_map(
        per_device,
        mesh=mesh,
        in_specs=(
            P("batch", "head", None), head_cols, head_cols, P(), head_cols, head_cols, P("head"),
            P("head"), P("head"), P("head"), P("head"), P(), P("head", None), rows4,
        ),
        out_specs=(
            rows4, P("batch", "head", None), head_cols, head_cols, P(), head_cols, head_cols,
            P("head"), P("head"), P("head"), P("head"), P("head"), P(), P("head", None),
        ),
        check_vma=False,
    )
```

```python
import functools
import itertools

import jax
import jax.numpy as jnp
from jax import lax
from jax.experimental import pallas as pl
from jax.experimental.pallas import tpu as pltpu
from jax.sharding import PartitionSpec as P

SPAN = 128
HEAD_PARTS = 2
ROW_CHUNKS = 4
BACK_PARTS = 1
X_STREAMS = 4
EPSILON = 1e-05
BF16 = jnp.bfloat16
F32 = jnp.float32
HIGHEST = lax.Precision.HIGHEST
VMEM_BYTES = 60 * 1024 * 1024
BACK_VMEM_BYTES = 63 * 1024 * 1024


def mm(a, b):
    return lax.dot_general(a, b, (((1,), (0,)), ((), ())), preferred_element_type=F32)


def mm_nt(a, b):
    return lax.dot_general(a, b, (((1,), (1,)), ((), ())), preferred_element_type=F32)


def mm_tn(a, b):
    return lax.dot_general(a, b, (((0,), (0,)), ((), ())), preferred_element_type=F32)


def mm_exact(a, b):
    return lax.dot_general(
        a, b, (((1,), (0,)), ((), ())), preferred_element_type=F32, precision=HIGHEST
    )


def lower_mask(shape):
    return lax.broadcasted_iota(jnp.int32, shape, 0) >= lax.broadcasted_iota(jnp.int32, shape, 1)


def softplus(v):
    return jnp.maximum(v, 0.0) + jnp.log1p(jnp.exp(-jnp.abs(v)))


def sigmoid(v):
    return 1.0 / (1.0 + jnp.exp(-v))


def pair_columns(values, pair, left):
    shape = (SPAN, 128)
    one = jnp.broadcast_to(values[:, 2 * pair : 2 * pair + 1], shape)
    two = jnp.broadcast_to(values[:, 2 * pair + 1 : 2 * pair + 2], shape)
    return one, two, jnp.where(left, one, two)


def segments(channels):
    ends = [channels * 2**w // 8 for w in range(4)]
    return list(zip([0] + ends[:-1], ends))


def partner(axis, bit):
    me = lax.axis_index(axis)
    return me + (1 - 2 * ((me // 2**bit) % 2)) * 2**bit


def bits_of(axis, count):
    me = lax.axis_index(axis)
    return [(me // 2**b) % 2 for b in range(count)]


def log2(value):
    return value.bit_length() - 1


def place(bits, fixed):
    bits = range(bits) if isinstance(bits, int) else sorted(bits)
    return tuple(fixed[b] if b in fixed else slice(None) for b in reversed(bits))


class Links:
    def __init__(self, send, recv):
        self.send, self.recv, self.used = send, recv, 0

    def copy(self, src, dst, axis, to):
        at = self.used
        self.used += 1
        return pltpu.make_async_remote_copy(
            src_ref=src, dst_ref=dst, send_sem=self.send.at[at], recv_sem=self.recv.at[at],
            device_id={axis: to}, device_id_type=pl.DeviceIdType.MESH,
        )


def meet(peers):
    barrier = pltpu.get_barrier_semaphore()
    for axis, to in peers:
        pl.semaphore_signal(barrier, inc=1, device_id={axis: to}, device_id_type=pl.DeviceIdType.MESH)
    pl.semaphore_wait(barrier, len(peers))


def add_block(buf, index, slot, at):
    rows = slot.shape[-2]
    step = min(rows, 32)
    index = index + (slice(None),) * (len(buf.shape) - len(index))
    free = [i for i, v in enumerate(index[:-2]) if isinstance(v, slice)]
    full = list(index[:-2])
    for i, v in zip(free, at):
        full[i] = v
    full = tuple(full)

    def piece(r, carry):
        rs = pl.ds(pl.multiple_of(r * step, step), step)
        total = buf[full + (rs, index[-1])].astype(F32) + slot[tuple(at) + (rs, slice(None))].astype(F32)
        buf[full + (rs, index[-1])] = total.astype(buf.dtype)
        return carry

    lax.fori_loop(0, rows // step, piece, 0)


def halving_slots(count, block, dtype):
    return [pltpu.VMEM((2,) * (count - 1 - i) + tuple(block), dtype) for i in range(count)]


class Stream:
    def __init__(self, *parts):
        self.steps = []
        for part in parts:
            if self.steps and part:
                last, first = self.steps.pop(), part[0]
                self.steps.append(lambda last=last, first=first: (last(), first()))
                part = part[1:]
            self.steps.extend(part)

    def advance(self):
        if self.steps:
            self.steps.pop(0)()


def advance_all(streams):
    for s in streams:
        s.advance()


def drain(streams):
    while any(s.steps for s in streams):
        advance_all(streams)


def exchanging_once(ports, axis, bits, buf, slots):
    def to(k):
        return lax.axis_index(axis) + sum(
            (1 - 2 * b) * 2**i for i, b in enumerate(bits_of(axis, bits)) if k & 2**i
        )

    copies = [
        ports.make(buf, lambda k=k: slots[k - 1], axis, lambda k=k: to(k)) for k in range(1, 2**bits)
    ]

    def start():
        for copy in copies:
            copy().start()

    def finish():
        for copy in copies:
            copy().wait()
        ref = buf()
        ref[...] = (ref[...].astype(F32) + sum(slot[...].astype(F32) for slot in slots)).astype(ref.dtype)

    return [start, finish]


class Ports:
    def __init__(self, send, recv):
        self.send, self.recv, self.used = send, recv, 0

    def make(self, src, dst, axis, to):
        at = self.used
        self.used += 1

        def describe():
            return pltpu.make_async_remote_copy(
                src_ref=src(), dst_ref=dst(), send_sem=self.send.at[at], recv_sem=self.recv.at[at],
                device_id={axis: to()}, device_id_type=pl.DeviceIdType.MESH,
            )

        return describe


def linked(copies, work):
    steps = []
    for i in range(len(copies) + 1):
        def step(i=i):
            if i:
                copies[i - 1]().wait()
                work(i - 1)
            if i < len(copies):
                copies[i]().start()

        steps.append(step)
    return steps


def halving(ports, axis, buf, slots, order):
    count = len(order)

    def fixed(i, give):
        mine = bits_of(axis, max(order) + 1)
        out = {b: mine[b] for b in order[: i + 1]}
        if give:
            out[order[i]] = 1 - out[order[i]]
        return out

    copies = [
        ports.make(
            lambda i=i: buf().at[place(order, fixed(i, True))], lambda i=i: slots[i],
            axis, lambda i=i: partner(axis, order[i]),
        )
        for i in range(count)
    ]

    def work(i):
        for at in itertools.product(*(range(d) for d in slots[i].shape[:-2])):
            add_block(buf(), place(order, fixed(i, False)), slots[i], at)

    return linked(copies, work)


def spreading(ports, axis, view, order, own, sem):
    count = len(order)

    def at(i):
        mine = bits_of(axis, count)
        return view().at[place(count, {b: mine[b] for b in order[i:]})]

    copies = [
        ports.make(
            (lambda i=i: at(i)) if i else own, lambda i=i: at(i), axis, lambda i=i: partner(axis, order[i])
        )
        for i in range(count)
    ]

    def kept():
        return pltpu.make_async_copy(own(), at(0), sem)

    def work(i):
        if i == 0:
            kept().wait()

    steps = linked(copies, work)
    first = steps[0]
    steps[0] = lambda: (kept().start(), first())
    return steps


def exchanging(ports, axis, buf, slots, order):
    copies = [
        ports.make(buf, lambda i=i: slots[i], axis, lambda i=i: partner(axis, order[i])) for i in range(len(order))
    ]

    def work(i):
        ref = buf()
        ref[...] = (ref[...].astype(F32) + slots[i][...].astype(F32)).astype(ref.dtype)

    return linked(copies, work)


PIECE_POLLS = (
    ("a", 0), ("a", 1), ("c", 2), ("c", 0), ("d", 1), ("e", 0), (1, 1), (2, 2), (3, 0), (4, 1), (5, 2), (7, 2),
)


def front_kernel(
    count, tok_ref, pre_ref, zw_hbm, xw_hbm, bcw_hbm, dtw_hbm, w_hbm, gain_hbm,
    convw_ref, convb_ref, dtb_ref, alog_ref, skip_ref,
    x_out, a_out, s_out, act_out, dsc_out, inn_out, bc_out, step_out, prev_out, gated_out, all_ref, gains_ref,
    xs, zw, xw, bcw, dtw, wv, gate_s, a_s, s_s, act_s, dsc_s, inn_s, inner_s, bc_s, bcb_s, step_s, prev_s, gated_s, state, tails,
    cum_s, cum_t_s, inner_prod_s, b_t_s, pad_s, load_sem, local_sem, store_sem, away_sem, here_sem, send, recv, send2, recv2,
):
    rows_num, channels = gated_s.shape[1:]
    groups = gated_s.shape[0]
    length = groups * rows_num
    n = state.shape[0]
    model = tok_ref.shape[1]
    chunks = 2
    chunk = rows_num // chunks
    me = lax.axis_index("head")
    hi, lo = me // 2, me % 2
    near = partner("head", 0)
    far = partner("head", 1)
    others = [near, far, near + far - me]
    links = Links(send, recv)

    loads = [
        pltpu.make_async_copy(src, dst, load_sem.at[i])
        for i, (src, dst) in enumerate(((zw_hbm, zw), (xw_hbm, xw), (bcw_hbm, bcw), (dtw_hbm, dtw), (w_hbm, wv)))
    ]
    for load in loads:
        load.start()
    tok = tok_ref[...].astype(F32)
    recip = lax.rsqrt(jnp.mean(tok * tok, axis=-1, keepdims=True) + EPSILON)
    xs[hi, lo] = (tok * recip * pre_ref[...]).astype(BF16)
    meet([("head", z) for z in others] + [("batch", partner("batch", b)) for b in range(count)])

    own_rows = xs.at[hi, lo]
    to_far = []
    for c in range(chunks):
        part = xs.at[hi, lo, pl.ds(c * chunk, chunk)]
        to_far.append(links.copy(part, part, "head", far))
        to_far[-1].start()
    to_near = links.copy(own_rows, own_rows, "head", near)
    to_near.start()
    half = w_hbm.shape[-1] // 2

    def pieces(z, cols, order):
        def own_piece(ref):
            return ref.at[place(count, dict(enumerate(bits_of("batch", count)))) + (slice(None), cols)]

        first = ports.make(
            lambda: own_piece(w_hbm), lambda: own_piece(all_ref.at[lax.axis_index("head")]), "head", z
        )

        def at(i):
            bits = bits_of("batch", count)
            return all_ref.at[(z(),) + place(count, {b: bits[b] for b in order[i:]}) + (slice(None), cols)]

        rest = [
            ports.make(lambda i=i: at(i), lambda i=i: at(i), "batch", lambda i=i: partner("batch", order[i]))
            for i in range(count)
        ]
        return Stream(linked([first] + rest, lambda i: None))

    up = list(range(1, count))
    ports = Ports(send2, recv2)
    near_at = lambda: partner("head", 0)
    far_at = lambda: partner("head", 1)
    streams = []
    for z in (near_at, far_at, lambda: near_at() + far_at() - lax.axis_index("head")):
        streams.append(pieces(z, pl.ds(0, half), up + [0]))
        streams.append(pieces(z, pl.ds(half, half), up[::-1] + [0]))
    plan = [[] for _ in range(HEAD_PARTS * groups)]
    early = {spot: [] for spot in "abcde"}
    for spot, group in PIECE_POLLS:
        for st in streams[2 * group : 2 * group + 2]:
            if st.steps:
                (early[spot] if spot in early else plan[spot]).append(st.steps.pop(0))

    def poll(spot):
        for action in early[spot]:
            action()

    poll("a")
    keep = [pltpu.make_async_copy(gain_hbm, gains_ref.at[me], local_sem.at[1])]
    keep[0].start()
    inner_s[0:8, :] = jnp.zeros((8, channels), F32)
    state[...] = jnp.zeros_like(state)
    step_s[...] = jnp.zeros_like(step_s)
    pad_s[...] = jnp.zeros_like(pad_s)
    pad_s[0:1, 0 : dtw.shape[0]] = dtb_ref[...]
    pad_s[1:2, 0 : dtw.shape[0]] = alog_ref[...]
    for load in loads:
        load.wait()
    keep.append(pltpu.make_async_copy(wv, all_ref.at[me], local_sem.at[0]))
    keep[-1].start()

    def project(at_hi, at_lo):
        first = pl.multiple_of((2 * at_hi + at_lo) * rows_num, rows_num)
        rows = pl.ds(first, rows_num)
        inner_rows = pl.ds(pl.multiple_of(first + 8, 8), rows_num)
        tile = 256

        def columns(t, carry):
            cols = pl.ds(pl.multiple_of(t * tile, tile), tile)
            x = xs[at_hi, at_lo]
            gate_s[rows, cols] = mm(x, zw[:, cols])
            inner_s[inner_rows, cols] = mm(x, xw[:, cols])
            return carry

        lax.fori_loop(0, channels // tile, columns, 0)
        x = xs[at_hi, at_lo]
        bc_s[rows, :] = mm(x, bcw[...])
        step_s[rows, 0 : dtw.shape[0]] = mm_nt(x, dtw[...])

    project(hi, lo)
    to_near.wait()
    project(hi, 1 - lo)
    poll("b")
    onward = []
    for c in range(chunks):
        to_far[c].wait()
        part = xs.at[1 - hi, lo, pl.ds(c * chunk, chunk)]
        onward.append(links.copy(part, part, "head", near))
        onward[-1].start()

    poll("c")
    gain_sends = [links.copy(gain_hbm, gains_ref.at[me], "head", z) for z in others]
    for item in gain_sends:
        item.start()

    project(1 - hi, lo)
    poll("d")
    for item in onward:
        item.wait()
    project(1 - hi, 1 - lo)
    poll("e")

    rate = -jnp.exp(pad_s[1:2, :])
    lower = lower_mask((SPAN, SPAN))
    lower_f = lower.astype(F32)
    left = lax.broadcasted_iota(jnp.int32, (SPAN, 128), 1) < 64

    span_num = channels // HEAD_PARTS

    def block(at, part):
        first = pl.multiple_of(at * SPAN, SPAN)
        rows = pl.ds(first, SPAN)
        if part == 0:
            delta = softplus(step_s[rows, :] + pad_s[0:1, :])
            cum = mm_exact(lower_f, delta * rate)
            cum_t = cum.T
            bcb_s[rows, :] = bc_s[rows, :].astype(BF16)
            inner = jnp.where(lower, mm_nt(bcb_s[rows, n:], bcb_s[rows, :n]), 0.0)
            b_t = bc_s[rows, :n].T.astype(BF16)
            step_s[rows, :] = delta
            cum_s[at], cum_t_s[at], inner_prod_s[at], b_t_s[at] = cum, cum_t, inner, b_t
        else:
            delta = step_s[rows, :]
            cum, cum_t, inner, b_t = cum_s[at], cum_t_s[at], inner_prod_s[at], b_t_s[at]
        span_cols = pl.ds(part * span_num, span_num)
        before = state[:, span_cols].astype(BF16)
        prev_s[at, :, span_cols] = before
        across = mm(bcb_s[rows, n:], before)
        quarter = at // (rows_num // SPAN)
        sub = pl.ds(pl.multiple_of((at % (rows_num // SPAN)) * SPAN, SPAN), SPAN)
        for pair in range(part * span_num // 128, (part + 1) * span_num // 128):
            cols = slice(pair * 128, pair * 128 + 128)
            local = slice(pair * 128 - part * span_num, pair * 128 + 128 - part * span_num)
            c0, c1, ce = pair_columns(cum, pair, left)
            _, _, de = pair_columns(delta, pair, left)
            tot = ce[SPAN - 1 : SPAN, :]
            window = inner_s[pl.ds(first, SPAN + 8), cols]
            conv_p = convb_ref[:, cols] + sum(
                convw_ref[k : k + 1, cols] * window[5 + k : 5 + k + SPAN] for k in range(4)
            )
            inn_s[rows, cols] = window[8:].astype(BF16)
            sc = sigmoid(conv_p)
            act = conv_p * sc
            act_s[rows, cols] = act.astype(BF16)
            dsc_s[rows, cols] = (sc + act * (1.0 - sc)).astype(BF16)
            u = act * de
            tails[:, local] = (u * jnp.exp(tot - ce)).astype(BF16)
            u0 = jnp.where(left, u, 0.0).astype(BF16)
            u1 = jnp.where(left, 0.0, u).astype(BF16)
            p0 = (jnp.exp(jnp.minimum(c0 - cum_t[2 * pair : 2 * pair + 1, :], 0.0)) * inner).astype(BF16)
            p1 = (jnp.exp(jnp.minimum(c1 - cum_t[2 * pair + 1 : 2 * pair + 2, :], 0.0)) * inner).astype(BF16)
            within = mm(jnp.concatenate([p0, p1], axis=1), jnp.concatenate([u0, u1], axis=0))
            y = within + across[:, local] * jnp.exp(ce) + skip_ref[:, cols] * act
            gate = gate_s[rows, cols]
            sg = sigmoid(gate)
            sl = gate * sg
            s_s[rows, cols] = sl.astype(BF16)
            a_s[rows, cols] = (y * (sg + sl * (1.0 - sg))).astype(BF16)
            gated_s[quarter, sub, cols] = (y * sl).astype(BF16)
            state[:, cols] = state[:, cols] * jnp.exp(tot)
        state[:, span_cols] += mm(b_t, tails[...])

    def leave(q, part):
        cols = pl.ds(part * span_num, span_num)
        return pltpu.make_async_remote_copy(
            src_ref=gated_s.at[q, :, cols], dst_ref=gated_out.at[me, :, cols],
            send_sem=away_sem.at[part, q], recv_sem=here_sem.at[part, me],
            device_id={"head": q}, device_id_type=pl.DeviceIdType.MESH,
        )

    def arrive(q, part):
        cols = pl.ds(part * span_num, span_num)
        return pltpu.make_async_remote_copy(
            src_ref=gated_s.at[q, :, cols], dst_ref=gated_out.at[q, :, cols],
            send_sem=away_sem.at[part, q], recv_sem=here_sem.at[part, q],
            device_id={"head": q}, device_id_type=pl.DeviceIdType.MESH,
        )

    subs = rows_num // SPAN

    def stores(q):
        rows = pl.ds(pl.multiple_of(q * rows_num, rows_num), rows_num)
        pairs = (
            (xs.at[q // 2, q % 2], x_out.at[rows]),
            (a_s.at[rows], a_out.at[rows]),
            (s_s.at[rows], s_out.at[rows]),
            (act_s.at[rows], act_out.at[rows]),
            (dsc_s.at[rows], dsc_out.at[rows]),
            (inn_s.at[rows], inn_out.at[rows]),
            (bcb_s.at[rows], bc_out.at[rows]),
            (step_s.at[rows], step_out.at[rows]),
            (prev_s.at[pl.ds(q * subs, subs)], prev_out.at[pl.ds(q * subs, subs)]),
        )
        return [pltpu.make_async_copy(src, dst, store_sem.at[i, q]) for i, (src, dst) in enumerate(pairs)]

    for part in range(HEAD_PARTS):
        def quarter_step(q, carry):
            def one(at, inner_carry):
                block(at, part)
                return inner_carry

            lax.fori_loop(q * subs, (q + 1) * subs, one, 0)

            @pl.when(q != me)
            def _():
                leave(q, part).start()

            if part == HEAD_PARTS - 1:
                for item in stores(q):
                    item.start()
            for k in range(groups):
                @pl.when(q == k)
                def _():
                    for action in plan[part * groups + k]:
                        action()
            return carry

        lax.fori_loop(0, groups, quarter_step, 0)
    stay = pltpu.make_async_copy(gated_s.at[me], gated_out.at[me], local_sem.at[2])
    stay.start()
    drain(streams)
    for item in gain_sends:
        item.wait()
    for item in keep:
        item.wait()
    stay.wait()

    def finish(q, carry):
        @pl.when(q != me)
        def _():
            for part in range(HEAD_PARTS):
                leave(q, part).wait_send()
                arrive(q, part).wait_recv()

        for item in stores(q):
            item.wait()
        return carry

    lax.fori_loop(0, groups, finish, 0)


def front_call(tokens, pre_gain, zw, xw, bcw, dtw, out_weight, norm_gain, convw, convb, dtb, alog, skip, groups, batches):
    rows_num, model = tokens.shape
    channels = zw.shape[1]
    n = bcw.shape[1] // 2
    length = rows_num * groups
    count = log2(batches)
    part = channels // batches
    copies = 5 + groups - 1
    piece_copies = 2 * (groups - 1) * (1 + count)
    hbm = pl.BlockSpec(memory_space=pl.ANY)
    vmem = pl.BlockSpec(memory_space=pltpu.VMEM)
    wide = jax.ShapeDtypeStruct((length, channels), BF16)
    outs = [
        jax.ShapeDtypeStruct((length, model), BF16), wide, wide, wide, wide, wide,
        jax.ShapeDtypeStruct((length, 2 * n), BF16),
        jax.ShapeDtypeStruct((length, 128), F32),
        jax.ShapeDtypeStruct((length // SPAN, n, channels), BF16),
        jax.ShapeDtypeStruct((groups, rows_num, channels), BF16),
        jax.ShapeDtypeStruct((groups,) + (2,) * count + (part, model), BF16),
        jax.ShapeDtypeStruct((groups, 1, channels), F32),
    ]
    dma = pltpu.SemaphoreType.DMA
    result = pl.pallas_call(
        functools.partial(front_kernel, count),
        in_specs=[vmem, vmem] + [hbm] * 6 + [vmem] * 5,
        out_specs=[hbm] * len(outs),
        out_shape=outs,
        scratch_shapes=[
            pltpu.VMEM((2, 2, rows_num, model), BF16),
            pltpu.VMEM(zw.shape, BF16), pltpu.VMEM(xw.shape, BF16),
            pltpu.VMEM(bcw.shape, BF16), pltpu.VMEM(dtw.shape, BF16),
            pltpu.VMEM((2,) * count + (part, model), BF16),
            pltpu.VMEM((length, channels), F32),
            pltpu.VMEM((length, channels), BF16), pltpu.VMEM((length, channels), BF16),
            pltpu.VMEM((length, channels), BF16), pltpu.VMEM((length, channels), BF16),
            pltpu.VMEM((length, channels), BF16), pltpu.VMEM((length + 8, channels), F32),
            pltpu.VMEM((length, 2 * n), F32), pltpu.VMEM((length, 2 * n), BF16),
            pltpu.VMEM((length, 128), F32), pltpu.VMEM((length // SPAN, n, channels), BF16),
            pltpu.VMEM((groups, rows_num, channels), BF16),
            pltpu.VMEM((n, channels), F32), pltpu.VMEM((SPAN, channels // HEAD_PARTS), BF16),
            pltpu.VMEM((length // SPAN, SPAN, 128), F32), pltpu.VMEM((length // SPAN, 128, SPAN), F32),
            pltpu.VMEM((length // SPAN, SPAN, SPAN), F32), pltpu.VMEM((length // SPAN, n, SPAN), BF16),
            pltpu.VMEM((8, 128), F32),
            dma((5,)), dma((3,)), dma((9, groups)), dma((HEAD_PARTS, groups)), dma((HEAD_PARTS, groups)), dma((copies,)), dma((copies,)),
            dma((piece_copies,)), dma((piece_copies,)),
        ],
        compiler_params=pltpu.CompilerParams(
            collective_id=1, has_side_effects=True, vmem_limit_bytes=VMEM_BYTES
        ),
        cost_estimate=pl.CostEstimate(
            flops=4 * length * model * channels, bytes_accessed=400 * 2**20, transcendentals=0
        ),
        name="front",
    )(
        tokens, pre_gain[None], zw, xw, bcw, dtw, out_weight.reshape((2,) * count + (part, model)),
        norm_gain[None], convw, convb, dtb, alog, skip,
    )
    x, a, s, act, dsc, inn, bc, step, prev, gated, w_all, gains = result
    return x, (a, s, act, dsc, inn), bc, step, prev, gated, w_all.reshape(groups, channels, model), gains


def middle_kernel(
    count, g_hbm, w_hbm, cot_hbm, gain_ref, tok_ref,
    out_hbm, dg_out, passed_hbm, own_ref, part_ref, ggrad_ref,
    g_s, w_s, cot_s, dy_s, gg_s, out_s, dg_s, give_s, kept_s, obuf, oslot0, oslot1, *refs,
):
    slots = [refs[i * (count - 1) : (i + 1) * (count - 1)] for i in range(4)]
    load_sem, store_sem, away_sem, here_sem, send, recv = refs[4 * (count - 1) :]
    groups, rows_num, channels = g_s.shape
    model = tok_ref.shape[1]
    part, half = kept_s.shape[-2:]
    pairs_num = groups // 2
    segs = segments(channels)
    tile = 512
    tiles = model // tile
    me = lax.axis_index("head")

    def w_load(t):
        cols = pl.ds(pl.multiple_of(t * tile, tile), tile)
        return pltpu.make_async_copy(w_hbm.at[:, :, cols], w_s.at[:, :, cols], load_sem.at[2 + t])

    loads = [
        pltpu.make_async_copy(g_hbm, g_s, load_sem.at[0]), pltpu.make_async_copy(cot_hbm, cot_s, load_sem.at[1]),
    ]
    for load in loads:
        load.start()
    for t in range(tiles):
        w_load(t).start()
    loads[0].wait()
    sums = [jnp.zeros((rows_num, 1), F32) for _ in segs]
    for j in range(groups):
        for w, (lo, hi) in enumerate(segs):
            g = g_s[j, :, lo:hi].astype(F32)
            gg_s[j, :, lo:hi] = (g * gain_ref[j, 0:1, lo:hi]).astype(BF16)
            sums[w] += jnp.sum(g * g, axis=1, keepdims=True)
    recips = []
    total = jnp.zeros((rows_num, 1), F32)
    for w, (lo, hi) in enumerate(segs):
        total = total + sums[w]
        recips.append(lax.rsqrt(total / (hi * groups) + EPSILON))
    meet(
        [("batch", partner("batch", b)) for b in range(count)]
        + [("head", z) for z in (partner("head", 0), partner("head", 1), partner("head", 0) + partner("head", 1) - me)]
    )
    loads[1].wait()

    def out_store(t):
        cols = pl.ds(pl.multiple_of(t * tile, tile), tile)
        return pltpu.make_async_copy(out_s.at[:, :, cols], out_hbm.at[:, :, cols], store_sem.at[t])

    def forward(t, dots):
        cols = pl.ds(pl.multiple_of(t * tile, tile), tile)
        w_load(t).wait()
        acc = jnp.zeros((rows_num, tile), F32)
        tok = tok_ref[:, cols].astype(F32)
        new = []
        for w, (lo, hi) in enumerate(segs):
            acc += mm(
                jnp.concatenate([gg_s[j, :, lo:hi] for j in range(groups)], axis=1),
                jnp.concatenate([w_s[j, lo:hi, cols] for j in range(groups)], axis=0),
            )
            out_s[w, :, cols] = (tok + recips[w] * acc).astype(BF16)
            new.append(dots[w] + jnp.sum(cot_s[w, :, cols].astype(F32) * acc, axis=1, keepdims=True))
        out_store(t).start()
        cot_s[0, :, cols] = sum(cot_s[w, :, cols].astype(F32) for w in range(4)).astype(BF16)
        return tuple(new)

    def combine(t, carry):
        cols = pl.ds(pl.multiple_of(t * tile, tile), tile)
        combined = jnp.zeros((rows_num, tile), F32)
        for w in reversed(range(4)):
            combined += recips[w] * cot_s[w, :, cols].astype(F32)
            dy_s[w, :, cols] = combined.astype(BF16)
        return carry

    lax.fori_loop(0, tiles, combine, 0)

    def leave(j):
        return pltpu.make_async_remote_copy(
            src_ref=dg_s.at[j], dst_ref=dg_out.at[me], send_sem=away_sem.at[j], recv_sem=here_sem.at[me],
            device_id={"head": j}, device_id_type=pl.DeviceIdType.MESH,
        )

    def arrive(j):
        return pltpu.make_async_remote_copy(
            src_ref=dg_s.at[j], dst_ref=dg_out.at[j], send_sem=away_sem.at[j], recv_sem=here_sem.at[j],
            device_id={"head": j}, device_id_type=pl.DeviceIdType.MESH,
        )

    def back(k, carry):
        j = (me + 1 + k) % groups
        for w, (lo, hi) in enumerate(segs):
            dn = mm_nt(dy_s[w], w_s[j, lo:hi, :])
            g = g_s[j, :, lo:hi].astype(F32)
            ggrad_ref[j, :, lo:hi] = jnp.sum(g * dn, axis=0, keepdims=True)
            dg_s[j, :, lo:hi] = (gain_ref[j, 0:1, lo:hi] * dn - g * scales[w]).astype(BF16)

        @pl.when(j != me)
        def _():
            leave(j).start()

        return carry

    ports = Ports(send, recv)
    up = list(range(1, count))
    core = bits_of("batch", 1)[0]

    def upper_index(p):
        return tuple((p >> b) & 1 for b in reversed(range(1, count)))

    def terms(s, bit, use):
        g0, c0 = (s % 2) * pairs_num, (s // 2) * half
        if part % 128 == 0:
            for q in range(2 ** (count - 1)):
                at = pl.ds(pl.multiple_of((2 * q + bit) * part, part), part)
                left = jnp.concatenate([gg_s[g0 + j, :, at] for j in range(pairs_num)], axis=1)
                owners = [[w for w, (lo, hi) in enumerate(segs) if lo <= (2 * q + c) * part < hi][0] for c in range(2)]
                w = owners[0] + (owners[1] - owners[0]) * bit
                term = mm_tn(left, dy_s[w, :, c0 : c0 + half])
                for j in range(pairs_num):
                    use(upper_index(2 * q), j, term[j * part : (j + 1) * part])
            return
        for j in range(pairs_num):
            for w, (lo, hi) in enumerate(segs):
                term = mm_tn(gg_s[g0 + j, :, lo:hi], dy_s[w, :, c0 : c0 + half])
                for p in range(lo // part, hi // part):
                    @pl.when(bit == p % 2)
                    def _():
                        use(upper_index(p), j, term[p * part - lo : (p + 1) * part - lo])

    def to_core(s):
        return pltpu.make_async_remote_copy(
            src_ref=give_s.at[s], dst_ref=kept_s.at[s], send_sem=send.at[s], recv_sem=recv.at[s],
            device_id={"batch": partner("batch", 0)}, device_id_type=pl.DeviceIdType.MESH,
        )

    def give(s):
        def use(index, j, rows):
            give_s[(s,) + index + (j,)] = rows.astype(BF16)

        terms(s, 1 - core, use)
        to_core(s).start()

    def keep(s):
        to_core(s).wait()

        def use(index, j, rows):
            at = (s,) + index + (j,)
            kept_s[at] = (kept_s[at].astype(F32) + rows).astype(BF16)

        terms(s, core, use)

    ports.used = 4
    streams = [
        Stream(halving(ports, "batch", lambda s=s: kept_s.at[s], slots[s], up if s % 2 == 0 else up[::-1]))
        for s in range(4)
    ]
    mine = bits_of("batch", count)
    own = place(up, {b: mine[b] for b in up})
    head_sum = Stream(halving(ports, "head", lambda: obuf, (oslot0, oslot1), [0, 1]))
    for s in range(2):
        give(s)
    for s in range(2):
        keep(s)
        streams[s].advance()
    dots = lax.fori_loop(0, tiles, forward, tuple(jnp.zeros((rows_num, 1), F32) for _ in segs))
    scales = [None] * 4
    scale = jnp.zeros((rows_num, 1), F32)
    for w in reversed(range(4)):
        scale = scale + recips[w] ** 3 * dots[w] / (segs[w][1] * groups)
        scales[w] = scale
    lax.fori_loop(0, groups, back, 0)
    stay = pltpu.make_async_copy(dg_s.at[me], dg_out.at[me], load_sem.at[0])
    stay.start()
    pass_on = pltpu.make_async_copy(cot_s.at[0], passed_hbm, load_sem.at[1])
    pass_on.start()
    for s in range(2, 4):
        give(s)
    advance_all(streams[:2])
    for s in range(2, 4):
        keep(s)
        streams[s].advance()
    drain(streams[:2])
    for s in range(2):
        for j in range(pairs_num):
            obuf[s, j] = kept_s[(s,) + own + (j,)]
    head_sum.advance()
    advance_all(streams[2:])
    head_sum.advance()
    drain(streams)
    drain([head_sum])
    own_ref[...] = obuf[place(2, dict(enumerate(bits_of("head", 2))))]
    for s in range(2, 4):
        for j in range(pairs_num):
            part_ref[s - 2, j] = kept_s[(s,) + own + (j,)]
    stay.wait()
    pass_on.wait()

    def finish(j, carry):
        @pl.when(j != me)
        def _():
            leave(j).wait_send()
            arrive(j).wait_recv()

        return carry

    lax.fori_loop(0, groups, finish, 0)

    def stored(t, carry):
        out_store(t).wait()
        return carry

    lax.fori_loop(0, tiles, stored, 0)


def middle_call(g, w_all, gain, tok, cot, batches):
    groups, rows_num, channels = g.shape
    model = tok.shape[1]
    count = log2(batches)
    part = channels // batches
    half = model // 2
    block = (groups // 2, part, half)
    hbm = pl.BlockSpec(memory_space=pl.ANY)
    vmem = pl.BlockSpec(memory_space=pltpu.VMEM)
    dma = pltpu.SemaphoreType.DMA
    wide = pltpu.VMEM((groups, rows_num, channels), BF16)
    tall = pltpu.VMEM((4, rows_num, model), BF16)
    halves = pltpu.VMEM((4,) + (2,) * (count - 1) + block, BF16)
    return pl.pallas_call(
        functools.partial(middle_kernel, count),
        in_specs=[hbm] * 3 + [vmem] * 2,
        out_specs=[hbm, hbm, hbm, vmem, vmem, vmem],
        out_shape=[
            jax.ShapeDtypeStruct((4, rows_num, model), BF16),
            jax.ShapeDtypeStruct(g.shape, BF16),
            jax.ShapeDtypeStruct((rows_num, model), BF16),
            jax.ShapeDtypeStruct((part, half), BF16),
            jax.ShapeDtypeStruct((2, 2, part, half), BF16),
            jax.ShapeDtypeStruct((groups, 1, channels), F32),
        ],
        scratch_shapes=[
            wide, pltpu.VMEM((groups, channels, model), BF16), tall, tall, wide, tall, wide, halves, halves,
            pltpu.VMEM((2, 2, part, half), BF16), pltpu.VMEM((2, part, half), BF16), pltpu.VMEM((part, half), BF16),
        ]
        + [s for _ in range(4) for s in halving_slots(count - 1, block, BF16)]
        + [
            dma((2 + model // 512,)), dma((model // 512,)), dma((groups,)), dma((groups,)),
            dma((4 * count + 2,)), dma((4 * count + 2,)),
        ],
        compiler_params=pltpu.CompilerParams(
            collective_id=2, has_side_effects=True, vmem_limit_bytes=BACK_VMEM_BYTES
        ),
        cost_estimate=pl.CostEstimate(
            flops=6 * groups * rows_num * channels * model, bytes_accessed=200 * 2**20, transcendentals=0
        ),
        name="nested_norm",
    )(g, w_all, cot, gain, tok)


BACK_POLLS = {
    "z": ((0, 0, "a"), (0, 1, "a"), (0, 1, "b"), (0, 2, "a"), (0, 3, "a"), (0, 3, "b")),
    "out": ((0, 0, "a"), (0, 1, "a")),
    "spread": (((0, 3, "b"),), ((0, 3, "b"),)),
    "relay": (
        ((0, 1, "a"), 3, 0, 1), ((0, 1, "b"), 3, 1, 1), ((0, 1, "b"), 3, 2, 1), ((0, 2, "a"), 3, 3, 1),
        ((0, 1, "b"), 3, 0, 2), ((0, 2, "a"), 3, 1, 2), ((0, 2, "a"), 3, 2, 2), ((0, 2, "b"), 3, 3, 2),
        ((0, 2, "b"), 2, 0, 1), ((0, 2, "b"), 2, 1, 1), ((0, 3, "a"), 2, 2, 1), ((0, 3, "b"), 2, 3, 1),
        ((0, 3, "b"), 1, 0, 1),
    ),
    "tail": (1, 1, 2, 2),
}
RELAY_ORDER = [(2, c, 1) for c in range(4)] + [(1, c, 1) for c in range(4)]
RELAY_ORDER += [(0, 0, 1), (0, 1, 1), (0, 0, 2), (0, 2, 1), (0, 1, 2), (0, 3, 1), (0, 2, 2), (0, 3, 2)]


def back_kernel(
    count, group_bits,
    dg_hbm, a_hbm, s_hbm, act_hbm, dsc_hbm, inn_hbm, x_hbm, bc_hbm, step_hbm, prev_hbm,
    zw_hbm, xw_hbm, bcw_hbm, dtw_hbm, o_hbm, own_hbm, gain_ref, convw_ref, alog_ref, skip_ref,
    z_out, x_out, o_out, bc_out, small_out, own_out,
    dg, a, s, act, dsc, inn, x, bc, step, prev, zw, xw, bdw, dtw, obuf, o_first, hot_ref, pad_s,
    lam, dconv, dyc_s, vt_s, q_s, v_s, w_s, da_s, etot_s, draw_s, head_s, vec_s, pre_s, dbs,
    rows_s, line_s, last_s, zg, bcbuf, small, *refs,
):
    groups = rows_s.shape[0] * rows_s.shape[1]
    zx_slots = [refs[i * count : (i + 1) * count] for i in range(2)]
    refs = refs[2 * count :]
    bc_slots, refs = (refs[:count], refs[count : 2 * count]), refs[2 * count :]
    bc_head, refs = (refs[: groups - 1], refs[groups - 1 : 2 * (groups - 1)]), refs[2 * (groups - 1) :]
    small_slots, refs = refs[:count], refs[count:]
    small_head, refs = refs[:group_bits], refs[group_bits:]
    o_slots, refs = refs[:group_bits], refs[group_bits:]
    load_sem, store_sem, rsend, rrecv, rrecv_own, send, recv = refs
    length, channels = a.shape
    model = x.shape[1]
    n = lam.shape[0]
    heads = hot_ref.shape[0]
    rows_num = length // groups
    subs = rows_num // SPAN
    wide = bcbuf.shape[-1]
    me = lax.axis_index("head")

    pairs = [
        (dg_hbm.at[:, :, pl.ds(0, channels // 2)], dg.at[0]),
        (dg_hbm.at[:, :, pl.ds(channels // 2, channels // 2)], dg.at[1]), (a_hbm, a), (s_hbm, s), (x_hbm, x), (o_hbm, obuf), (own_hbm, o_first), (step_hbm, step), (bc_hbm, bc),
        (prev_hbm, prev), (act_hbm, act), (dsc_hbm, dsc), (inn_hbm, inn), (zw_hbm, zw), (xw_hbm, xw),
        (bcw_hbm, bdw.at[:, pl.ds(0, 2 * n)]), (dtw_hbm, dtw),
    ]
    loads = [pltpu.make_async_copy(src, dst, load_sem.at[i]) for i, (src, dst) in enumerate(pairs)]
    for load in loads:
        load.start()
    for load in loads[:4]:
        load.wait()

    def gates(i, carry):
        per = rows_num // 64
        rows = pl.ds(pl.multiple_of(i * 64, 64), 64)
        piece = dg.shape[-1]
        for h in range(dg.shape[0]):
            cols = slice(h * piece, (h + 1) * piece)
            d = dg[h, i // per, pl.ds(pl.multiple_of((i % per) * 64, 64), 64), :].astype(F32)
            a[rows, cols] = (d * a[rows, cols].astype(F32)).astype(BF16)
            s[rows, cols] = (d * s[rows, cols].astype(F32)).astype(BF16)
        return carry

    lax.fori_loop(0, length // 64, gates, 0)
    near, far = partner("head", 0), partner("head", 1)
    meet(
        [("batch", partner("batch", b)) for b in range(count)]
        + [("head", to) for to in (near, far, near + far - me)]
    )

    ports = Ports(send, recv)
    up = list(range(1, count))
    orders = [up, up[::-1]]

    def own_at():
        return place(count, dict(enumerate(bits_of("batch", count))))

    def grads(i, out, slots, first, width):
        part = (slice(None),) * (count + 1) + (pl.ds(first, width),)
        view = lambda: out.at[part]
        buf = lambda: zg.at[part]
        order = orders[i % 2]
        return Stream(
            halving(ports, "batch", buf, slots, [0] + order),
            spreading(
                ports, "batch", view, order[::-1] + [0], lambda: buf().at[own_at()], store_sem.at[2 + i]
            ),
        )

    z_width, x_width = channels // 2, channels // X_STREAMS
    streams = [grads(i, z_out, zx_slots[i], i * z_width, z_width) for i in range(2)]
    per = z_width // x_width
    for i in range(X_STREAMS):
        cols = pl.ds((i % per) * x_width, x_width)
        slots = [ref.at[(slice(None),) * (len(ref.shape) - 1) + (cols,)] for ref in zx_slots[i // per]]
        streams.append(grads(2 + i, x_out, slots, i * x_width, x_width))

    def state_part(i):
        part = (slice(None),) * (count + 1) + ((pl.ds(n, n + 128), pl.ds(0, n))[i],)
        buf = lambda: bcbuf.at[part]
        view = lambda: bc_out.at[part]
        return Stream(
            halving(ports, "batch", buf, bc_slots[i], [0] + orders[i]),
            exchanging_once(
                ports, "head", group_bits, lambda: bcbuf.at[own_at() + (slice(None), pl.ds((n, 0)[i], n))], bc_head[i]
            ),
            spreading(
                ports, "batch", view, orders[i][::-1] + [0], lambda: buf().at[own_at()], store_sem.at[i]
            ),
        )

    state = [state_part(i) for i in range(2)]
    vectors = Stream(
        exchanging(ports, "batch", lambda: small, small_slots, range(count)),
        exchanging(ports, "head", lambda: small.at[pl.ds(0, 8)], small_head, range(group_bits)),
    )
    half = model // 2

    def head_own():
        return place(group_bits, dict(enumerate(bits_of("head", group_bits))))

    def o_view(i):
        return o_out.at[(slice(None),) * (count + 1) + (pl.ds(i * half, half),)]

    outs = Stream(halving(ports, "head", lambda: obuf, o_slots, list(range(group_bits))))

    def o_own(i):
        return obuf.at[head_own()] if i else o_first

    spread = [
        Stream(spreading(
            ports, "batch", lambda i=i: o_view(i), orders[i] + [0], lambda i=i: o_own(i),
            store_sem.at[2 + 2 + X_STREAMS + i],
        ))
        for i in range(2)
    ]

    for load in loads[4:7]:
        load.wait()
    outs.advance()
    tile = 256
    block_rows = model >> count

    def put(target, t, value):
        for k in range(tile // min(block_rows, tile)):
            p = (t * tile) // block_rows + k
            index = tuple((p // 2**b) % 2 for b in reversed(range(count)))
            if block_rows <= tile:
                target[index] = value[k * block_rows : (k + 1) * block_rows].astype(BF16)
            else:
                first = pl.multiple_of((t * tile) % block_rows, tile)
                target[index + (pl.ds(first, tile), slice(None))] = value.astype(BF16)

    def weight_grad(right, target):
        def one(t, carry):
            value = mm_tn(x[:, pl.ds(pl.multiple_of(t * 2 * tile, 2 * tile), 2 * tile)], right[...])
            for k in range(2):
                put(target, 2 * t + k, value[k * tile : (k + 1) * tile])
            return carry

        lax.fori_loop(0, model // (2 * tile), one, 0)

    weight_grad(a, zg)
    advance_all(streams[:2])
    for load in loads[7:]:
        load.wait()
    bdw[:, 2 * n :] = jnp.concatenate([dtw[...], jnp.zeros((128 - heads, model), BF16)], axis=0).T
    pad_s[...] = jnp.zeros_like(pad_s)
    pad_s[0:1, 0:heads] = alog_ref[...]
    hot_ref[...] = (
        lax.broadcasted_iota(jnp.int32, hot_ref.shape, 1) // (channels // heads)
        == lax.broadcasted_iota(jnp.int32, hot_ref.shape, 0)
    ).astype(F32).astype(BF16)

    lam[...] = jnp.zeros_like(lam)
    dconv[rows_num:, :] = jnp.zeros((8, channels), F32)
    vec_s[...] = jnp.zeros_like(vec_s)
    head_s[...] = jnp.zeros_like(head_s)
    draw_s[...] = jnp.zeros_like(draw_s)
    pre_s[...] = jnp.zeros_like(pre_s)
    rate = -jnp.exp(pad_s[0:1, :])
    lower = lower_mask((SPAN, SPAN))
    lower_f = lower.astype(F32)
    lower_b = lower.astype(BF16)
    row_at = lax.broadcasted_iota(jnp.int32, (SPAN, SPAN), 0)
    col_at = lax.broadcasted_iota(jnp.int32, (SPAN, SPAN), 1)
    upper = row_at <= col_at
    strict = row_at < col_at
    strict_f = strict.astype(F32)
    left = lax.broadcasted_iota(jnp.int32, (SPAN, 128), 1) < 64

    span_num = channels // BACK_PARTS
    span_heads = heads // BACK_PARTS

    def block(at, local, part):
        rows = pl.ds(pl.multiple_of(at * SPAN, SPAN), SPAN)
        local_rows = pl.ds(pl.multiple_of(local * SPAN, SPAN), SPAN)
        delta = step[rows, :]
        cum = mm_exact(lower_f, delta * rate)
        cum_t = cum.T
        delta_t = delta.T
        series = delta_t * (1.0 - delta_t * (0.5 - delta_t * (1.0 / 6.0 - delta_t / 24.0)))
        slope_t = jnp.where(delta_t < 0.04, series, 1.0 - jnp.exp(-delta_t))
        rate_t = jnp.broadcast_to(rate, (SPAN, 128)).T
        b_val = bc[rows, :n]
        c_val = bc[rows, n:]
        inner = jnp.where(upper, mm_nt(b_val, c_val), 0.0)
        span_cols = pl.ds(part * span_num, span_num)
        before = prev[at, :, span_cols]
        lam_b = lam[:, span_cols].astype(BF16)
        across = mm(c_val, before)
        dtail = mm(b_val, lam_b)
        d_inner_prod = jnp.zeros((SPAN, SPAN), F32)
        for pair in range(part * span_num // 128, (part + 1) * span_num // 128):
            cols = slice(pair * 128, pair * 128 + 128)
            own = pair - part * span_num // 128
            here = slice(own * 128, own * 128 + 128)
            c0, c1, ce = pair_columns(cum, pair, left)
            _, _, de = pair_columns(delta, pair, left)
            tot = ce[SPAN - 1 : SPAN, :]
            e_cum = jnp.exp(ce)
            e_tail = jnp.exp(tot - ce)
            dy_b = s[rows, cols]
            dy = dy_b.astype(F32)
            act_p = act[rows, cols].astype(F32)
            vec_s[5:6, cols] += jnp.sum(dy * act_p, axis=0, keepdims=True)
            u = act_p * de
            u_b = u.astype(BF16)
            zero = jnp.zeros_like(dy_b)
            dy01 = jnp.concatenate([jnp.where(left, dy_b, zero), jnp.where(left, zero, dy_b)], axis=0)
            m0 = jnp.exp(jnp.minimum(cum_t[2 * pair : 2 * pair + 1, :] - c0, 0.0))
            m1 = jnp.exp(jnp.minimum(cum_t[2 * pair + 1 : 2 * pair + 2, :] - c1, 0.0))
            p0 = m0 * inner
            p1 = m1 * inner
            du = mm(jnp.concatenate([p0.astype(BF16), p1.astype(BF16)], axis=1), dy01)
            dp = mm_nt(u_b, dy01)
            dp0, dp1 = dp[:, :SPAN], dp[:, SPAN:]
            d_inner_prod += dp0 * m0 + dp1 * m1
            e01 = jnp.concatenate([(dp0 * p0).astype(BF16), (dp1 * p1).astype(BF16)], axis=0)
            spans = mm(e01, lower_b)
            da_s[2 * own : 2 * own + 1, :] = jnp.sum(
                jnp.where(strict, spans[:SPAN], 0.0), axis=0, keepdims=True
            )
            da_s[2 * own + 1 : 2 * own + 2, :] = jnp.sum(
                jnp.where(strict, spans[SPAN:], 0.0), axis=0, keepdims=True
            )
            dut = dtail[:, here] * e_tail
            du = du + dut
            dye = dy * e_cum
            dyc_s[:, here] = dye.astype(BF16)
            vt_s[:, here] = (u * e_tail).astype(BF16)
            q_s[:, here] = (dye * across[:, here]).astype(BF16)
            v_s[:, here] = (u * dut).astype(BF16)
            w_s[:, here] = (act_p * du).astype(BF16)
            etot_s[:, here] = jnp.exp(tot)
            d_act = de * du + skip_ref[:, cols] * dy
            dconv[local_rows, cols] = d_act * dsc[rows, cols].astype(F32)
        hot = hot_ref[:span_heads, :span_num]
        these = slice(part * span_heads, (part + 1) * span_heads)
        over = jnp.sum(lam[:, span_cols] * before.astype(F32), axis=0, keepdims=True) * etot_s[...]
        over = jnp.broadcast_to(over, (128, span_num))
        over = lax.dot_general(
            hot.astype(F32), over, (((1,), (1,)), ((), ())), preferred_element_type=F32, precision=HIGHEST
        )
        da = (
            da_s[...]
            + mm_exact(mm_nt(hot, q_s[...]), lower_f)
            + mm_exact(mm_nt(hot, v_s[...]), strict_f)
            + over
        )
        d_step = mm_nt(hot, w_s[...]) + rate_t[these] * da
        d_raw = d_step * slope_t[these]
        head_s[these, :] += d_raw
        head_s[heads + part * span_heads : heads + (part + 1) * span_heads, :] += delta_t[these] * da * rate_t[these]
        draw_s[these, :] = d_raw
        dg_b = jnp.where(upper, d_inner_prod, 0.0)
        d_b = mm(dg_b.astype(BF16), c_val) + mm_nt(vt_s[...], lam_b)
        d_c = mm(dg_b.T.astype(BF16), b_val) + mm_nt(dyc_s[...], before)
        d_t = draw_s[...].T
        if part:
            d_b += dbs[rows, :n].astype(F32)
            d_c += dbs[rows, n : 2 * n].astype(F32)
            d_t += dbs[rows, 2 * n :].astype(F32)
        dbs[rows, :n] = d_b.astype(BF16)
        dbs[rows, n : 2 * n] = d_c.astype(BF16)
        dbs[rows, 2 * n :] = d_t.astype(BF16)
        lam[:, span_cols] = lam[:, span_cols] * etot_s[...] + mm(bc[rows, n:].astype(F32).T.astype(BF16), dyc_s[...])

    top = groups - 1

    def slot(q, c):
        return dg.at[q, c] if q < 2 else line_s.at[q - 2, c]

    def hop(q, c, dst, sem, to):
        return pltpu.make_async_remote_copy(
            src_ref=rows_s.at[q // 2, q % 2, c], dst_ref=dst, send_sem=rsend.at[q, c], recv_sem=sem,
            device_id={"head": to}, device_id_type=pl.DeviceIdType.MESH,
        )

    def send_up(q, c):
        @pl.when(me + 1 < q)
        def _():
            hop(q, c, slot(q, c), rrecv.at[q, c], me + 1).start()

        @pl.when(me + 1 == q)
        def _():
            hop(q, c, last_s.at[c], rrecv_own.at[c], me + 1).start()

    def send_down(q, c):
        hop(q, c, slot(q, c), rrecv.at[q, c], me - 1).start()

    def arrived(q, c):
        hop(q, c, slot(q, c), rrecv.at[q, c], me).wait_recv()

    def arrived_last(q, c):
        hop(q, c, last_s.at[c], rrecv_own.at[c], me).wait_recv()

    def begin(q):
        for c in range(ROW_CHUNKS):
            if q > 0:
                @pl.when(me == 0)
                def _():
                    send_up(q, c)
            if q < top:
                @pl.when(me == top)
                def _():
                    send_down(q, c)

    def relay(q, c, distance):
        if distance < q:
            @pl.when(me == distance)
            def _():
                arrived(q, c)
                add_block(rows_s, (q // 2, q % 2, c), slot(q, c), ())
                send_up(q, c)
        if top - distance > q:
            @pl.when(me == top - distance)
            def _():
                arrived(q, c)
                add_block(rows_s, (q // 2, q % 2, c), slot(q, c), ())
                send_down(q, c)

    def conv_back(rows, part):
        for c in range(part * span_num, (part + 1) * span_num, 128):
            cols = slice(c, c + 128)
            inner_v = inn[rows, cols].astype(F32)
            d_in = jnp.zeros((rows_num, 128), F32)
            for k in range(4):
                shifted = dconv[3 - k : 3 - k + rows_num, cols]
                d_in += convw_ref[k : k + 1, cols] * shifted
                vec_s[k : k + 1, cols] += jnp.sum(inner_v * shifted, axis=0, keepdims=True)
            vec_s[4:5, cols] += jnp.sum(dconv[0:rows_num, cols], axis=0, keepdims=True)
            inn[rows, cols] = d_in.astype(BF16)
        kept = pl.ds(part * span_num, span_num)
        dconv[rows_num:, kept] = dconv[0:8, kept]

    def row_grads(q, rows):
        wide_tile = 2 * tile
        per = model // ROW_CHUNKS // wide_tile

        def columns(t, carry):
            cols = pl.ds(pl.multiple_of(t * wide_tile, wide_tile), wide_tile)
            value = mm_nt(a[rows, :], zw[cols, :]) + mm_nt(inn[rows, :], xw[cols, :]) + mm_nt(dbs[rows, :], bdw[cols, :])
            pre_s[:, cols] += jnp.sum(value * x[rows, cols].astype(F32), axis=0, keepdims=True)
            rows_s[q // 2, q % 2, t // per, :, pl.ds(pl.multiple_of((t % per) * wide_tile, wide_tile), wide_tile)] = value.astype(BF16)
            return carry

        lax.fori_loop(0, model // wide_tile, columns, 0)

    plan = {(part, k, spot): [] for part in range(BACK_PARTS) for k in range(groups) for spot in "ab"}

    def book(stream, slots):
        for slot in slots:
            if stream.steps:
                plan[slot].append(stream.steps.pop(0))

    for st in streams[:2]:
        book(st, BACK_POLLS["z"])
    book(outs, BACK_POLLS["out"])
    for i, st in enumerate(spread):
        book(st, BACK_POLLS["spread"][i])
    last = BACK_PARTS - 1
    for k in range(groups):
        plan[last, k, "b"].insert(0, lambda q=top - k: begin(q))
    for spot, q, c, distance in BACK_POLLS["relay"]:
        plan[spot].append(lambda q=q, c=c, distance=distance: relay(q, c, distance))

    for part in range(BACK_PARTS):
        def quarter_step(i, carry):
            q = groups - 1 - i
            rows = pl.ds(pl.multiple_of(q * rows_num, rows_num), rows_num)

            def one(j, inner_carry):
                block(q * subs + subs - 1 - j, subs - 1 - j, part)
                return inner_carry

            lax.fori_loop(0, subs, one, 0)

            def polls(spot):
                for k in range(groups):
                    if plan[part, k, spot]:
                        @pl.when(i == k)
                        def _():
                            for action in plan[part, k, spot]:
                                action()

            polls("a")
            conv_back(rows, part)
            if part == last:
                row_grads(q, rows)
            polls("b")
            return carry

        lax.fori_loop(0, groups, quarter_step, 0)

    drain(streams[:2])
    tail = list(BACK_POLLS["tail"])
    booked = {key[1:] for key in BACK_POLLS["relay"]}
    relays = [r for r in RELAY_ORDER if r not in booked]

    def relay_some():
        for _ in range(tail.pop(0) if tail else 1):
            if relays:
                relay(*relays.pop(0))

    def state_grad(t, carry):
        put(bcbuf, t, mm_tn(x[:, pl.ds(pl.multiple_of(t * tile, tile), tile)], dbs[...]))
        return carry

    lax.fori_loop(0, model // tile, state_grad, 0)
    advance_all(state)
    per = X_STREAMS // 2
    x_pairs = [streams[2 + h * per : 2 + (h + 1) * per] for h in range(2)]
    for h in range(2):
        cols = pl.ds(h * z_width, z_width)
        weight_grad(inn.at[:, cols], zg.at[(slice(None),) * (count + 1) + (cols,)])
        advance_all(x_pairs[h])
        relay_some()
        advance_all(state)
    small[...] = jnp.zeros_like(small)
    for j in range(groups):
        small[j : j + 1, :] = gain_ref[j]
    for j in range(model // channels):
        small[groups + j : groups + j + 1, :] = pre_s[:, j * channels : (j + 1) * channels]
    small[8:14, :] = vec_s[0:6, :]
    totals = lax.dot_general(
        jnp.ones((8, SPAN), F32), head_s[...], (((1,), (1,)), ((), ())),
        preferred_element_type=F32, precision=HIGHEST,
    )
    small[14:15, 0:128] = totals[0:1]
    vectors.advance()
    while relays or any(st.steps for st in streams + state + spread + [vectors, outs]):
        advance_all(x_pairs[0])
        relay_some()
        advance_all(state + [vectors])
        advance_all(x_pairs[1])
        relay_some()
        advance_all(spread + [outs])
    small_out[...] = small[...]

    piece = model // ROW_CHUNKS
    for c in range(ROW_CHUNKS):
        for q in range(groups):
            @pl.when(me == q)
            def _():
                if q > 0:
                    arrived_last(q, c)
                if q < top:
                    arrived(q, c)

                def total(r, carry):
                    rs = pl.ds(pl.multiple_of(r * 32, 32), 32)
                    value = rows_s[q // 2, q % 2, c, rs, :].astype(F32)
                    if q > 0:
                        value += last_s[c, rs, :].astype(F32)
                    if q < top:
                        value += slot(q, c)[rs, :].astype(F32)
                    own_out[rs, c * piece : (c + 1) * piece] = value.astype(BF16)
                    return carry

                lax.fori_loop(0, rows_num // 32, total, 0)

            @pl.when(me != q)
            def _():
                hop(q, c, slot(q, c), rrecv.at[q, c], me).wait_send()


def back_call(dg, res, x, bc, step, prev, zw, xw, bcw, dtw, out_part, out_own, gain_grad, convw, alog, skip, groups, batches):
    length, model = x.shape
    channels = xw.shape[1]
    n = bc.shape[1] // 2
    heads = dtw.shape[0]
    rows_num = length // groups
    count = log2(batches)
    group_bits = log2(groups)
    lead = (2,) * count
    part = channels // batches
    rows = model // batches
    wide = 2 * n + 128
    hbm = pl.BlockSpec(memory_space=pl.ANY)
    vmem = pl.BlockSpec(memory_space=pltpu.VMEM)
    dma = pltpu.SemaphoreType.DMA
    copies = (2 + X_STREAMS) * 2 * count + 2 * (2 * count + groups - 1) + (count + group_bits) + group_bits + 2 * count
    tall = lambda w, t: pltpu.VMEM((length, w), t)
    span = pltpu.VMEM((SPAN, channels // BACK_PARTS), BF16)
    z, xg, o, bcg, small, own = pl.pallas_call(
        functools.partial(back_kernel, count, group_bits),
        in_specs=[hbm] * 16 + [vmem] * 4,
        out_specs=[hbm] * 4 + [vmem] * 2,
        out_shape=[
            jax.ShapeDtypeStruct(lead + (rows, channels), BF16),
            jax.ShapeDtypeStruct(lead + (rows, channels), BF16),
            jax.ShapeDtypeStruct(lead + (part, model), BF16),
            jax.ShapeDtypeStruct(lead + (rows, wide), BF16),
            jax.ShapeDtypeStruct((16, channels), F32),
            jax.ShapeDtypeStruct((rows_num, model), BF16),
        ],
        scratch_shapes=[pltpu.VMEM((2, groups, rows_num, channels // 2), BF16)] + [tall(channels, BF16)] * 5
        + [
            tall(model, BF16), tall(2 * n, BF16), tall(128, F32), pltpu.VMEM(prev.shape, BF16),
            pltpu.VMEM(zw.shape, BF16), pltpu.VMEM(xw.shape, BF16), pltpu.VMEM((model, wide), BF16),
            pltpu.VMEM(dtw.shape, BF16),
            pltpu.VMEM((2,) * group_bits + (part, model // 2), BF16), pltpu.VMEM((part, model // 2), BF16),
            pltpu.VMEM((heads, channels), BF16), pltpu.VMEM((8, 128), F32),
            pltpu.VMEM((n, channels), F32), pltpu.VMEM((rows_num + 8, channels), F32),
        ]
        + [span] * 5
        + [
            pltpu.VMEM((heads // BACK_PARTS, SPAN), F32), pltpu.VMEM((1, channels // BACK_PARTS), F32),
            pltpu.VMEM((128, SPAN), F32),
            pltpu.VMEM((128, SPAN), F32), pltpu.VMEM((8, channels), F32), pltpu.VMEM((1, model), F32),
            tall(wide, BF16),
            pltpu.VMEM((2, 2, ROW_CHUNKS, rows_num, model // ROW_CHUNKS), BF16),
            pltpu.VMEM((2, ROW_CHUNKS, rows_num, model // ROW_CHUNKS), BF16),
            pltpu.VMEM((ROW_CHUNKS, rows_num, model // ROW_CHUNKS), BF16),
            pltpu.VMEM(lead + (rows, channels), BF16), pltpu.VMEM(lead + (rows, wide), BF16),
            pltpu.VMEM((16, channels), F32),
        ]
        + [s for _ in range(2) for s in halving_slots(count, (rows, channels // 2), BF16)]
        + halving_slots(count, (rows, n + 128), BF16)
        + halving_slots(count, (rows, n), BF16)
        + [pltpu.VMEM((rows, n), BF16)] * (2 * (groups - 1))
        + [pltpu.VMEM((16, channels), F32)] * count
        + [pltpu.VMEM((8, channels), F32)] * group_bits
        + halving_slots(group_bits, (part, model // 2), BF16)
        + [dma((17,)), dma((6 + X_STREAMS,)),
            dma((groups, ROW_CHUNKS)), dma((groups, ROW_CHUNKS)), dma((ROW_CHUNKS,)), dma((copies,)), dma((copies,))],
        compiler_params=pltpu.CompilerParams(
            collective_id=3, has_side_effects=True, vmem_limit_bytes=BACK_VMEM_BYTES
        ),
        cost_estimate=pl.CostEstimate(
            flops=10 * length * model * channels, bytes_accessed=300 * 2**20, transcendentals=0
        ),
        name="back",
    )(
        dg, *res, x, bc, step, prev, zw, xw, bcw, dtw, out_part, out_own,
        gain_grad, convw, alog, skip,
    )
    return (
        z.reshape(model, channels), xg.reshape(model, channels), o.reshape(channels, model),
        bcg.reshape(model, wide), small, own,
    )


def finish_kernel(
    z_ref, x_ref, o_ref, bc_ref, small_ref, own_ref, tok_ref, passed_ref, pre_ref, out_ref,
    zf_ref, xf_ref, of_ref, bcf_ref, dt_ref, grad_ref, outf_ref, convw_ref, convb_ref, skip_ref, gain_ref, pre_out, dtb_ref, alog_ref,
):
    zf_ref[...] = z_ref[...].astype(F32)
    xf_ref[...] = x_ref[...].astype(F32)
    of_ref[...] = o_ref[...].astype(F32)
    width = bcf_ref.shape[1]
    heads = dt_ref.shape[0]
    outf_ref[...] = out_ref[...]
    bcf_ref[...] = bc_ref[:, :width].astype(F32)
    dt_ref[...] = bc_ref[:, width : width + 128].astype(F32).T[:heads]
    tok = tok_ref[...].astype(F32)
    recip = lax.rsqrt(jnp.mean(tok * tok, axis=-1, keepdims=True) + EPSILON)
    scaled = pre_ref[...] * own_ref[...].astype(F32)
    mean = jnp.mean(tok * scaled, axis=-1, keepdims=True)
    grad_ref[...] = (passed_ref[...].astype(F32) + recip * scaled - tok * recip**3 * mean).astype(BF16)

    @pl.when(pl.program_id(0) == 0)
    def _():
        groups = small_ref.shape[0] // 4
        channels = small_ref.shape[1]
        convw_ref[...] = small_ref[8:12, :]
        convb_ref[...] = small_ref[12:13, :]
        skip_ref[...] = small_ref[13:14, :]
        me = lax.axis_index("head")
        gain = small_ref[0:1, :]
        for j in range(1, groups):
            gain = jnp.where(me == j, small_ref[j : j + 1, :], gain)
        gain_ref[...] = gain
        for j in range(pre_out.shape[1] // channels):
            cols = slice(j * channels, (j + 1) * channels)
            pre_out[:, cols] = small_ref[groups + j : groups + j + 1, :] / pre_ref[:, cols]
        dtb_ref[...] = small_ref[14:15, 0:heads]
        alog_ref[...] = small_ref[14:15, heads : 2 * heads]


def finish_call(z, x, o, bc, small, own, tok, passed, pre_gain, out, heads):
    model, channels = z.shape
    rows_num = tok.shape[0]
    steps = 8
    wide = bc.shape[1]
    rows = lambda r, w: pl.BlockSpec((r // steps, w), lambda i: (i, 0))
    fixed = lambda shape: pl.BlockSpec(shape, lambda i: (0, 0))
    shapes = [
        ((model, channels), F32), ((model, channels), F32), ((channels, model), F32), ((model, wide - 128), F32),
    ]
    wide4 = pl.BlockSpec((4, rows_num // steps, model), lambda i: (0, i, 0))
    flat = [(4, channels), (1, channels), (1, channels), (1, channels), (1, model), (1, heads), (1, heads)]
    return pl.pallas_call(
        finish_kernel,
        grid=(steps,),
        in_specs=[
            rows(model, channels), rows(model, channels), rows(channels, model), rows(model, wide),
            fixed(small.shape), rows(rows_num, model), rows(rows_num, model),
            rows(rows_num, model), fixed((1, model)), wide4,
        ],
        out_specs=[rows(*shape) for shape, _ in shapes]
        + [pl.BlockSpec((heads, model // steps), lambda i: (0, i)), rows(rows_num, model), wide4]
        + [fixed(shape) for shape in flat],
        out_shape=[jax.ShapeDtypeStruct(shape, t) for shape, t in shapes]
        + [
            jax.ShapeDtypeStruct((heads, model), F32), jax.ShapeDtypeStruct((rows_num, model), BF16),
            jax.ShapeDtypeStruct(out.shape, BF16),
        ]
        + [jax.ShapeDtypeStruct(shape, F32) for shape in flat],
        compiler_params=pltpu.CompilerParams(vmem_limit_bytes=VMEM_BYTES),
        cost_estimate=pl.CostEstimate(flops=0, bytes_accessed=46 * 2**20, transcendentals=0),
        name="finish",
    )(z, x, o, bc, small, own, tok, passed, pre_gain[None], out)


def per_device(
    tokens, z_weight, x_weight, bc_weight, dt_weight, conv_weight, conv_bias, dt_bias,
    a_log, skip, norm_gain, pre_gain, out_weight, cotangent,
):
    groups = lax.axis_size("head")
    batches = lax.axis_size("batch")
    _, own_len, model = tokens.shape
    tokens = tokens[0]
    cot = cotangent[:, 0]
    channels = z_weight.shape[1]
    heads = dt_weight.shape[1]
    dtw = dt_weight.T
    alog = a_log[None]
    skip_r = skip[None]
    x, res, bc, step, prev, gated, w_all, gain_all = front_call(
        tokens, pre_gain, z_weight, x_weight, bc_weight, dtw, out_weight, norm_gain,
        conv_weight, conv_bias[None], dt_bias[None], alog, skip_r, groups, batches,
    )
    outputs, d_gated, passed, out_own, out_part, gain_grad = middle_call(gated, w_all, gain_all, tokens, cot, batches)
    z_grad, x_grad, out_grad, bcdt_grad, small, d_own = back_call(
        d_gated, res, x, bc, step, prev, z_weight, x_weight, bc_weight, dtw, out_part, out_own, gain_grad,
        conv_weight, alog, skip_r, groups, batches,
    )
    (
        z_grad, x_grad, out_grad, bc_grad, dt_grad, tokens_grad, outputs, convw, convb, skip_g, gain_g, pre_g, dtb_g, alog_g,
    ) = finish_call(z_grad, x_grad, out_grad, bcdt_grad, small, d_own, tokens, passed, pre_gain, outputs, heads)
    flat = lambda v: v.reshape(-1)
    return (
        outputs[:, None], tokens_grad[None], z_grad, x_grad, bc_grad, dt_grad.T, convw, flat(convb), flat(dtb_g),
        flat(alog_g), flat(skip_g), flat(gain_g), flat(pre_g), out_grad,
    )


def solution(mesh):
    head_cols = P(None, "head")
    rows4 = P(None, "batch", "head", None)
    return jax.shard_map(
        per_device,
        mesh=mesh,
        in_specs=(
            P("batch", "head", None), head_cols, head_cols, P(), head_cols, head_cols, P("head"),
            P("head"), P("head"), P("head"), P("head"), P(), P("head", None), rows4,
        ),
        out_specs=(
            rows4, P("batch", "head", None), head_cols, head_cols, P(), head_cols, head_cols,
            P("head"), P("head"), P("head"), P("head"), P("head"), P(), P("head", None),
        ),
        check_vma=False,
    )
```
